32 devices in a mesh: shot: 2 (over x), slab: 16 (over z, y, core).
Axes of the slice: x: 2, y: 2, z: 4, core: 2. Of those that a mesh axis runs over, the one named last changes fastest.
Arguments:
- fwd_last: float32 [2, 256, 64, 128], P('shot', 'slab'), may hold values from -6 to 6
- fwd_prev: float32 [2, 256, 64, 128], P('shot', 'slab'), may hold values from -6 to 6
- velocity: float32 [256, 64, 128], P('slab'), may hold values from 0.5 to 1
- aperture: int32 [2, 64, 128], P('shot'), may hold values 0 or 1
- rec_index: int32 [2, 2048], P('shot'), may hold values from 0 to 2097151
- src_index: int32 [2], P('shot'), may hold values from 0 to 2097151
- residual: float32 [2, 32, 2048], P('shot'), may hold values from -6 to 6
Outputs:
- gradient: float32 [256, 64, 128], P('slab', 'shot')
- adjoint_field: float32 [2, 256, 64, 128], P('shot', 'slab')
The draws below stay inside these ranges and needn't reach their ends.
All inputs are finite; a program needn't handle non-finite values. No bound on the sum of `aperture` on one device may be relied on, other than what follows from the above.
Results may differ from the reference program's by a relative error of at most 0.000025.
Values sent between devices are 32-bit elements; how exact they have to be, the bound alone decides.
No kernel may reach another device: no remote copies, remote signals or barrier semaphores. Data moves between devices by JAX's collectives and lax.ppermute only.
A program may use at most 256 MiB of HBM per device.

```python
import jax
import jax.numpy as jnp
from jax import lax

NX = 64
NY = 128
STEPS = 32
NREC = 2048
NZ = 256
SHOTS = 2


def with_ends(entries, own_key, least, high):
    longest = entries.shape.index(max(entries.shape))
    spots = []
    for shift in (0, 1):
        where = [jax.random.randint(jax.random.fold_in(own_key, axis), (), 0, length) for axis, length in enumerate(entries.shape)]
        where[longest] = (where[longest] + shift) % entries.shape[longest]
        spots.append(tuple(where))
    return entries.at[spots[0]].set(least).at[spots[1]].set(high)


def shard_levels(rng, dims, split, least, high):
    factor_of, own = 1.0, jax.random.fold_in(rng, 6)
    for dim, parts in split:
        steps = jnp.exp(jax.random.uniform(jax.random.fold_in(own, dim), (parts,), jnp.float32, least / len(split), high / len(split)))
        factor_of = factor_of * jnp.repeat(steps, dims[dim] // parts).reshape([-1 if axis == dim else 1 for axis in range(len(dims))])
    return factor_of


def bell_draw(own_key, shape, width, limit, pieces=(), held_as=jnp.bfloat16):
    gain = shard_levels(own_key, shape, pieces, -0.22, 0.18) if pieces else 1.0
    drawn = jax.random.normal(own_key, shape, jnp.float32) * width * gain
    return jnp.minimum(jnp.maximum(drawn, -limit), limit).astype(held_as)


def setup_inputs(seed: int = 0) -> dict:
    keys = jax.random.split(jax.random.key(seed), 8)
    return {
        "fwd_last": bell_draw(keys[0], (SHOTS, NZ, NX, NY), 1.0, 6.0, ((0, 2), (1, 16)), jnp.float32),
        "fwd_prev": bell_draw(keys[1], (SHOTS, NZ, NX, NY), 1.0, 6.0, ((0, 2), (1, 16)), jnp.float32),
        "velocity": jnp.clip(0.5 + 0.5 * jax.random.uniform(keys[2], (NZ, NX, NY), jnp.float32) ** shard_levels(keys[2], (NZ, NX, NY), ((0, 16),), -0.2, 0.2), 0.5, 1.0),
        "aperture": with_ends((jax.random.randint(keys[3], (SHOTS, NX, NY), 0, 2) < 1).astype(jnp.int32), jax.random.fold_in(keys[3], 1), 0, 1),
        "rec_index": with_ends(jax.random.randint(keys[4], (SHOTS, NREC), 0, NZ * NX * NY), jax.random.fold_in(keys[4], 1), 0, (NZ * NX * NY) - 1).astype(jnp.int32),
        "src_index": jax.random.randint(keys[5], (SHOTS,), 0, NZ * NX * NY).astype(jnp.int32),
        "residual": bell_draw(keys[6], (SHOTS, STEPS, NREC), 1.0, 6.0, ((0, 2),), jnp.float32),
    }


COEFS = (-205.0 / 72.0, 8.0 / 5.0, -1.0 / 5.0, 8.0 / 315.0, -1.0 / 560.0)


def second_diff(padded, lower, count):
    centre = padded[:, lower:lower + count]
    total = 3.0 * COEFS[0] * centre
    for k in range(1, 5):
        total = total + COEFS[k] * (padded[:, lower + k:lower + k + count] + padded[:, lower - k:lower - k + count])
    width_x = centre.shape[2]
    width_y = centre.shape[3]
    sides = jnp.pad(centre, ((0, 0), (0, 0), (4, 4), (4, 4)))
    for k in range(1, 5):
        total = total + COEFS[k] * (sides[:, :, 4 + k:4 + k + width_x, 4:4 + width_y] + sides[:, :, 4 - k:4 - k + width_x, 4:4 + width_y])
    for k in range(1, 5):
        total = total + COEFS[k] * (sides[:, :, 4:4 + width_x, 4 + k:4 + k + width_y] + sides[:, :, 4:4 + width_x, 4 - k:4 - k + width_y])
    return total


def ricker(step):
    arg = (jnp.pi * 0.06 * (step - 10.0)) ** 2
    return 10.0 * (1.0 - 2.0 * arg) * jnp.exp(-arg)


def reference(fwd_last, fwd_prev, velocity, aperture, rec_index, src_index, residual):
    coef = (0.4 * velocity) ** 2
    total_cells = NZ * NX * NY

    def laplace(field):
        padded = jnp.pad(field[None], ((0, 0), (4, 4), (0, 0), (0, 0)))
        return second_diff(padded, 4, NZ)[0]

    def one_shot(items):
        u_next, u_cur, gate, receivers, source, trace = items
        gate_f = gate.astype(jnp.float32)[None]
        zero = jnp.zeros((NZ, NX, NY), jnp.float32)

        def advance(k, carry):
            u_next, u_cur, l_next, l_cur, acc = carry
            step = STEPS - 1 - k
            wave = ricker(step.astype(jnp.float32))
            src_field = jnp.zeros((total_cells,), jnp.float32).at[source].add(wave).reshape(NZ, NX, NY)
            rec_field = jnp.zeros((total_cells,), jnp.float32).at[receivers].add(trace[step]).reshape(NZ, NX, NY)
            u_new = 2.0 * u_cur - u_next + coef * (laplace(u_cur) + src_field)
            l_new = 2.0 * l_cur - l_next + coef * (laplace(l_cur) + rec_field)
            acc = acc + gate_f * u_cur * (l_next - 2.0 * l_cur + l_new)
            return (u_cur, u_new, l_cur, l_new, acc)

        out = lax.fori_loop(0, STEPS, advance, (u_next, u_cur, zero, zero, zero))
        return out[4], out[3]

    terms, adjoint_field = lax.map(one_shot, (fwd_last, fwd_prev, aperture, rec_index, src_index, residual))
    gradient = (-2.0 / velocity) * jnp.sum(terms, axis=0)
    return gradient, adjoint_field
```

```python
import functools

import jax
import jax.numpy as jnp
from jax import lax
from jax.experimental import pallas as pl
from jax.experimental.pallas import tpu as pltpu
from jax.sharding import PartitionSpec as P

COEFS = (-205.0 / 72.0, 8.0 / 5.0, -1.0 / 5.0, 8.0 / 315.0, -1.0 / 560.0)
REACH = 4
SHIFT = 8
VMEM_BYTES = 40 * 1024 * 1024
SUB = 8

MSG = 2 * SHIFT + REACH
REST = SHIFT + REACH
SPAN = 32
MID = 12


def ricker(step):
    arg = (jnp.pi * 0.06 * (step - 10.0)) ** 2
    return 10.0 * (1.0 - 2.0 * arg) * jnp.exp(-arg)


def tiled(field):
    layers, width_x, width_y = field.shape
    return field.reshape(layers, SUB, width_x // SUB, width_y).transpose(0, 2, 1, 3)


def untiled(field):
    layers, parts, sub, width_y = field.shape
    return field.transpose(0, 2, 1, 3).reshape(layers, sub * parts, width_y)


def lap_maker(parts, width_y):
    lane = lax.broadcasted_iota(jnp.int32, (1, SUB, width_y), 2)
    row = lax.broadcasted_iota(jnp.int32, (1, SUB, width_y), 1)
    plus = [jnp.where(lane < width_y - k, COEFS[k], 0.0).astype(jnp.float32) for k in range(1, 5)]
    minus = [jnp.where(lane >= k, COEFS[k], 0.0).astype(jnp.float32) for k in range(1, 5)]

    def lap(ref, j):
        f = ref[j]
        after = jnp.where(row == SUB - 1, 0.0, pltpu.roll(f[:REACH], SUB - 1, 1))
        before = jnp.where(row == 0, 0.0, pltpu.roll(f[parts - REACH :], 1, 1))
        wide = jnp.concatenate([before, f, after], axis=0)
        total = (3.0 * COEFS[0]) * f
        for k in range(1, 5):
            pair = (ref[j + k] + ref[j - k]) + (
                wide[REACH + k : REACH + k + parts] + wide[REACH - k : REACH - k + parts]
            )
            total = total + COEFS[k] * pair
            total = total + plus[k - 1] * pltpu.roll(f, width_y - k, 2)
            total = total + minus[k - 1] * pltpu.roll(f, k, 2)
        return f, total

    return lap


def layers_loop(first, count, body):
    def one(q, carry):
        body(first + q)
        return carry

    lax.fori_loop(0, count, one, 0, unroll=2)


def inject(rbuf, rl, ids, starts, res, level, first, last, bits, width_y):
    lane = lax.broadcasted_iota(jnp.int32, (1, width_y), 1)

    def one(r, carry):
        place = rl[r]
        who = ids[r]
        row = lax.shift_right_logical(place, bits)
        col = place & ((1 << bits) - 1)
        value = res[level, lax.shift_right_logical(who, 7), who & 127]
        spot = rbuf[pl.ds(row, 1), :]
        rbuf[pl.ds(row, 1), :] = spot + jnp.where(lane == col, value, 0.0)
        return carry

    lax.fori_loop(starts[first], starts[last], one, 0)


def block_kernel(side, is_l, bits, *refs):
    refs = list(refs)

    def take(count):
        got = refs[:count]
        del refs[:count]
        return got

    (scal,) = take(1)
    wave = rl = ids = starts = res_hbm = x_in = g_in = vmsg_in = None
    if is_l:
        rl, ids, starts, res_hbm = take(4)
    else:
        (wave,) = take(1)
    own, rest, recv, coef = take(4)
    if side == 1:
        (vmsg_in,) = take(1)
    if is_l:
        x_in, g_in = take(2)
    msg_out, rest_out = take(2)
    vmsg_out = x_out = g = None
    if side == 0:
        (vmsg_out,) = take(1)
    if is_l:
        (g,) = take(1)
    else:
        (x_out,) = take(1)
    a, b, c, p = take(4)
    rbuf = res = sem = None
    if is_l:
        rbuf, res, sem = take(3)

    parts, _, width_y = a.shape[1:]
    rows = parts * SUB
    n0, is_last, src_layer, src_part, src_row, src_lane = (scal[i] for i in range(6))
    off = MID - SHIFT if side == 0 else MID - 2 * SHIFT
    lap = lap_maker(parts, width_y)

    if is_l:
        fetch = pltpu.make_async_copy(res_hbm.at[pl.ds(n0 - 1, 3)], res, sem)
        fetch.start()
        rbuf[...] = jnp.zeros(rbuf.shape, jnp.float32)

    def bring(msg, low):
        if low:
            a[MID - SHIFT : MID] = msg[0:SHIFT]
            p[MID - REACH : MID] = msg[SHIFT : SHIFT + REACH]
            b[MID - SHIFT - REACH : MID - REACH] = msg[SHIFT + REACH : MSG]
        else:
            a[MID : MID + SHIFT] = msg[0:SHIFT]
            p[MID : MID + REACH] = msg[SHIFT : SHIFT + REACH]
            b[MID + REACH : MID + REACH + SHIFT] = msg[SHIFT + REACH : MSG]

    if side == 0:
        bring(recv, True)
        a[MID : MID + SHIFT] = rest[0:SHIFT]
        p[MID : MID + REACH] = rest[SHIFT:REST]
        b[MID + REACH : MID + REACH + SHIFT] = own[SHIFT + REACH : MSG]

        @pl.when(is_last == 1)
        def _():
            zero = jnp.zeros((REACH,) + a.shape[1:], jnp.float32)
            a[MID + SHIFT : MID + 2 * SHIFT] = own[0:SHIFT]
            p[MID + SHIFT + REACH : MID + 2 * SHIFT] = own[SHIFT : SHIFT + REACH]
            for field in (a, b, c):
                field[MID + 2 * SHIFT : MID + 2 * SHIFT + REACH] = zero
    else:
        a[MID - SHIFT : MID] = rest[0:SHIFT]
        p[MID - REACH : MID] = rest[SHIFT:REST]
        b[MID - SHIFT - REACH : MID - REACH] = own[SHIFT + REACH : MSG]

        @pl.when(is_last == 1)
        def _():
            bring(vmsg_in, False)

        @pl.when(is_last == 0)
        def _():
            bring(recv, False)

    if is_l:
        fetch.wait()

    def source(nxt, level, first, count):
        j = src_layer + off

        @pl.when((src_layer >= 0) & (j >= first) & (j < first + count))
        def _():
            lane = lax.broadcasted_iota(jnp.int32, (1, width_y), 1)
            spot = nxt[j, src_part, pl.ds(src_row, 1), :]
            gain = coef[src_layer, src_part, pl.ds(src_row, 1), :] * wave[n0 + 1 - level]
            nxt[j, src_part, pl.ds(src_row, 1), :] = spot - jnp.where(lane == src_lane, gain, 0.0)

    def advance(level, cur, nxt, first, count, x_base, outs, x_save=None):
        if is_l:
            zone = (first - off) // REACH
            inject(rbuf, rl, ids, starts, res, 2 - level, zone, zone + count // REACH, bits, width_y)
        else:
            source(nxt, level, first, count)

        def body(j):
            f, total = lap(cur, j)
            if is_l:
                at = pl.multiple_of((j - off) * rows, rows)
                total = total + rbuf[pl.ds(at, rows), :].reshape(parts, SUB, width_y)
                rbuf[pl.ds(at, rows), :] = jnp.zeros((rows, width_y), jnp.float32)
            step = coef[j - off] * total
            new = (2.0 * f - nxt[j]) + step
            for ref, shift in outs:
                ref[j + shift] = new
            if is_l:
                g[j - off] = g[j - off] + x_in[j + (x_base - first)] * step
            else:
                x_out[j + (x_base - first)] = f

        layers_loop(first, count, body)

    if is_l:
        if side == 0:
            g[2 * SHIFT : 3 * SHIFT] = g_in[2 * SHIFT : 3 * SHIFT]
            g[0 : 2 * SHIFT] = g_in[0 : 2 * SHIFT]
        else:
            g[...] = g_in[...]

    advance(0, a, p, MID - REACH, SHIFT, 0, [(b, 0)])
    if side == 0:

        @pl.when(is_last == 1)
        def _():
            advance(0, a, p, MID + SHIFT + REACH, REACH, 32, [(b, 0)])

    advance(1, b, a, MID - SHIFT, 2 * SHIFT, 8, [(c, 0)])
    if side == 0:

        @pl.when(is_last == 1)
        def _():
            advance(1, b, a, MID + SHIFT, SHIFT, 36, [(c, 0)])
            vmsg_out[0:SHIFT] = c[MID + SHIFT : MID + 2 * SHIFT]
            vmsg_out[SHIFT : SHIFT + REACH] = b[MID + SHIFT : MID + SHIFT + REACH]
            vmsg_out[SHIFT + 2 * REACH : MSG] = jnp.zeros((REACH,) + a.shape[1:], jnp.float32)

    if side == 0:
        msg_out[0:SHIFT] = c[MID - SHIFT : MID]
        msg_out[SHIFT : SHIFT + REACH] = b[MID - SHIFT : MID - REACH]
        rest_out[0:SHIFT] = c[MID : MID + SHIFT]
        rest_out[SHIFT:REST] = b[MID + REACH : MID + SHIFT]
    else:
        msg_out[0:SHIFT] = c[MID : MID + SHIFT]
        msg_out[SHIFT : SHIFT + REACH] = b[MID + REACH : MID + SHIFT]
        rest_out[0:SHIFT] = c[MID - SHIFT : MID]
        rest_out[SHIFT:REST] = b[MID - SHIFT : MID - REACH]

    @pl.when(n0 >= 2)
    def _():
        advance(2, c, b, MID - REACH, SHIFT, 24, [(msg_out, SHIFT + REACH - (MID - REACH))])
        if side == 0:

            @pl.when(is_last == 1)
            def _():
                first = MID + SHIFT + REACH
                advance(2, c, b, first, REACH, 44, [(vmsg_out, SHIFT + REACH - first)])

    @pl.when(n0 < 2)
    def _():
        msg_out[SHIFT + REACH : MSG] = jnp.zeros((SHIFT,) + a.shape[1:], jnp.float32)


def first_u_kernel(scal, wave, f0, f1, coef, msg_out, rest_out):
    depth, parts, _, width_y = f0.shape
    n0, _, src_layer, src_part, src_row, src_lane = (scal[i] for i in range(6))
    lap = lap_maker(parts, width_y)
    msg_out[0:SHIFT] = f0[depth - SHIFT : depth]
    msg_out[SHIFT : SHIFT + REACH] = f1[depth - REACH : depth]
    rest_out[0:SHIFT] = f0[0:SHIFT]
    rest_out[SHIFT:REST] = f1[0:REACH]

    def body(j):
        f, total = lap(f0, j)
        msg_out[j + SHIFT] = (2.0 * f - f1[j]) + coef[j] * total

    layers_loop(REACH, SHIFT, body)
    j = src_layer - SHIFT

    @pl.when((src_layer >= 0) & (j >= REACH) & (j < REACH + SHIFT))
    def _():
        lane = lax.broadcasted_iota(jnp.int32, (1, width_y), 1)
        spot = msg_out[j + SHIFT, src_part, pl.ds(src_row, 1), :]
        gain = coef[j, src_part, pl.ds(src_row, 1), :] * wave[n0 + 1]
        msg_out[j + SHIFT, src_part, pl.ds(src_row, 1), :] = spot + jnp.where(lane == src_lane, gain, 0.0)


def first_l_kernel(bits, scal, rl, ids, starts, res_hbm, f0, coef, msg_out, rest_out, g, rbuf, res, sem):
    depth, parts, _, width_y = f0.shape
    rows = parts * SUB
    fetch = pltpu.make_async_copy(res_hbm.at[pl.ds(scal[0] - 1, 3)], res, sem)
    fetch.start()
    rbuf[...] = jnp.zeros(rbuf.shape, jnp.float32)
    msg_out[0 : SHIFT + REACH] = jnp.zeros((SHIFT + REACH,) + f0.shape[1:], jnp.float32)
    rest_out[...] = jnp.zeros(rest_out.shape, jnp.float32)
    g[...] = jnp.zeros(g.shape, jnp.float32)
    fetch.wait()
    zone = (SHIFT + REACH) // REACH
    inject(rbuf, rl, ids, starts, res, 2, zone, zone + SHIFT // REACH, bits, width_y)

    def body(j):
        at = pl.multiple_of((j + SHIFT) * rows, rows)
        new = coef[j] * rbuf[pl.ds(at, rows), :].reshape(parts, SUB, width_y)
        msg_out[j + SHIFT] = new
        g[j + SHIFT] = f0[j] * new

    layers_loop(REACH, SHIFT, body)


def on_device(fwd_last, fwd_prev, velocity, aperture, rec_index, src_index, residual):
    _, depth, width_x, width_y = fwd_last.shape
    parts = width_x // SUB
    total_steps, receivers = residual.shape[1:]
    plane = width_x * width_y
    slabs = lax.axis_size("slab")
    slab = lax.axis_index("slab")
    up = [(i, i + 1) for i in range(slabs - 1)]
    down = [(i + 1, i) for i in range(slabs - 1)]
    bits = (width_y - 1).bit_length()
    f32 = jnp.float32

    vel_left = lax.ppermute(velocity[depth - SHIFT :], "slab", up)
    coef_own = tiled((0.4 * velocity) ** 2)
    coef = jnp.concatenate([tiled((0.4 * vel_left) ** 2), coef_own], axis=0)

    base = (slab * depth - SHIFT) * plane
    window = (depth + SHIFT) * plane
    local = rec_index[0] - base
    far = jnp.int32(2**30)
    keys = jnp.where((local >= 0) & (local < window), local, far)
    keys, ids = lax.sort((keys, lax.iota(jnp.int32, receivers)), num_keys=1, is_stable=False)

    def place_of(cell):
        layer = cell // plane
        x = (cell // width_y) % width_x
        return layer, x % parts, x // parts, cell % width_y

    layer, part, row, lane = place_of(keys)
    rl = (((layer * parts + part) * SUB + row) << bits) | lane
    zones = (depth + SHIFT) // REACH
    edges = jnp.arange(zones + 1, dtype=jnp.int32) * (REACH * plane)
    starts = jnp.sum((keys[None, :] < edges[:, None]).astype(jnp.int32), axis=1)

    src = src_index[0] - base
    src_in = (src >= 0) & (src < window)
    s_layer, s_part, s_row, s_lane = place_of(jnp.where(src_in, src, 0))
    s_layer = jnp.where(src_in, s_layer, -1)
    is_last = (slab == slabs - 1).astype(jnp.int32)

    def scal_of(n0):
        return jnp.stack([jnp.asarray(n0, jnp.int32), is_last, s_layer, s_part, s_row, s_lane])

    wave = jnp.concatenate([jnp.zeros((1,), f32), ricker(jnp.arange(total_steps, dtype=f32))])
    res = jnp.concatenate([jnp.zeros((1, receivers), f32), residual[0]]).reshape(
        total_steps + 1, receivers // 128, 128
    )

    smem = pl.BlockSpec(memory_space=pltpu.SMEM)
    vmem = pl.BlockSpec(memory_space=pltpu.VMEM)
    anym = pl.BlockSpec(memory_space=pl.ANY)

    def fields(layers):
        return jax.ShapeDtypeStruct((layers, parts, SUB, width_y), f32)

    params = pltpu.CompilerParams(vmem_limit_bytes=VMEM_BYTES)
    l_scratch = [
        pltpu.VMEM(((depth + SHIFT) * parts * SUB, width_y), f32),
        pltpu.SMEM((3, receivers // 128, 128), f32),
        pltpu.SemaphoreType.DMA(()),
    ]
    layer_bytes = 4 * plane

    def cost(layers):
        return pl.CostEstimate(
            flops=50 * layers * plane, bytes_accessed=6 * layers * layer_bytes, transcendentals=0
        )

    f0, f1 = tiled(fwd_prev[0]), tiled(fwd_last[0])
    um, ur = pl.pallas_call(
        first_u_kernel,
        out_shape=(fields(MSG), fields(REST)),
        in_specs=[smem, smem, vmem, vmem, vmem],
        out_specs=(vmem, vmem),
        compiler_params=params,
        cost_estimate=cost(SHIFT),
        name="first_u",
    )(scal_of(total_steps - 1), wave, f0, f1, coef_own)
    lm, lr, g = pl.pallas_call(
        functools.partial(first_l_kernel, bits),
        out_shape=(fields(MSG), fields(REST), fields(depth + SHIFT)),
        in_specs=[smem, smem, smem, smem, anym, vmem, vmem],
        out_specs=(vmem, vmem, vmem),
        scratch_shapes=l_scratch,
        compiler_params=params,
        cost_estimate=cost(SHIFT),
        name="first_l",
    )(scal_of(total_steps - 1), rl, ids, starts, res, f0, coef_own)

    def u_block(side, n0, own, rest, recv, *vmsg):
        outs = [fields(MSG), fields(REST)]
        if side == 0:
            outs.append(fields(MSG))
        outs.append(fields(48))
        return pl.pallas_call(
            functools.partial(block_kernel, side, False, bits),
            out_shape=outs,
            in_specs=[smem, smem] + [vmem] * (4 + len(vmsg)),
            out_specs=[vmem] * len(outs),
            scratch_shapes=[pltpu.VMEM((SPAN, parts, SUB, width_y), f32)] * 4,
            compiler_params=params,
            cost_estimate=cost(2 * depth),
            name=f"u_block{side}",
        )(scal_of(n0), wave, own, rest, recv, coef, *vmsg)

    def l_block(side, n0, own, rest, recv, vmsg, x, g):
        outs = [fields(MSG), fields(REST)]
        if side == 0:
            outs.append(fields(MSG))
        outs.append(fields(depth + SHIFT))
        return pl.pallas_call(
            functools.partial(block_kernel, side, True, bits),
            out_shape=outs,
            in_specs=[smem] * 4 + [anym] + [vmem] * (6 + len(vmsg)),
            out_specs=[vmem] * len(outs),
            scratch_shapes=[pltpu.VMEM((SPAN, parts, SUB, width_y), f32)] * 4 + l_scratch,
            compiler_params=params,
            cost_estimate=cost(2 * depth),
            name=f"l_block{side}",
        )(scal_of(n0), rl, ids, starts, res, own, rest, recv, coef, *vmsg, x, g)

    def two_blocks(i, carry):
        um, ur, u_got, lm, lr, g = carry
        n0 = total_steps - 1 - 4 * i
        l_got = lax.ppermute(lm, "slab", up)
        um, ur, uv, x = u_block(0, n0, um, ur, u_got)
        u_got = lax.ppermute(um, "slab", down)
        lm, lr, lv, g = l_block(0, n0, lm, lr, l_got, (), x, g)
        l_got = lax.ppermute(lm, "slab", down)
        um, ur, x = u_block(1, n0 - 2, um, ur, u_got, uv)
        u_got = lax.ppermute(um, "slab", up)
        lm, lr, g = l_block(1, n0 - 2, lm, lr, l_got, (lv,), x, g)
        return (um, ur, u_got, lm, lr, g)

    u_got = lax.ppermute(um, "slab", up)
    um, ur, u_got, lm, lr, g = lax.fori_loop(0, total_steps // 4, two_blocks, (um, ur, u_got, lm, lr, g))

    adjoint_field = untiled(jnp.concatenate([lr[:SHIFT], lm[:SHIFT]], axis=0))[None]
    g_right = lax.ppermute(g[:SHIFT], "slab", down)
    g = jnp.concatenate([g[SHIFT : 2 * SHIFT], g[2 * SHIFT :] + g_right], axis=0)
    g = aperture[0].astype(f32) * untiled(g)
    summed = lax.psum_scatter(g, "shot", scatter_dimension=1, tiled=True)
    block = width_x // lax.axis_size("shot")
    speed = lax.dynamic_slice_in_dim(velocity, lax.axis_index("shot") * block, block, 1)
    return ((-2.0 / speed) * summed, adjoint_field)


def solution(mesh):
    in_specs = (
        P("shot", "slab", None, None),
        P("shot", "slab", None, None),
        P("slab", None, None),
        P("shot", None, None),
        P("shot", None),
        P("shot"),
        P("shot", None, None),
    )
    out_specs = (P("slab", "shot", None), P("shot", "slab", None, None))
    return jax.shard_map(on_device, mesh=mesh, in_specs=in_specs, out_specs=out_specs, check_vma=False)
```

```python
import functools

import jax
import jax.numpy as jnp
from jax import lax
from jax.experimental import pallas as pl
from jax.experimental.pallas import tpu as pltpu
from jax.sharding import PartitionSpec as P

SCALE = 5040.0
WHOLE = (-14350.0, 8064.0, -1008.0, 128.0, -9.0)
REACH = 4
SHIFT = 8
VMEM_BYTES = 20 * 1024 * 1024
SUB = 8
PIECES = 3
CHUNK = 256

MSG = 2 * SHIFT + REACH
REST = SHIFT + REACH
SPAN = 32
MID = 12


def ricker(step):
    arg = (jnp.pi * 0.06 * (step - 10.0)) ** 2
    return 10.0 * (1.0 - 2.0 * arg) * jnp.exp(-arg)


def tiled(field):
    layers, width_x, width_y = field.shape
    return field.reshape(layers, SUB, width_x // SUB, width_y).transpose(0, 2, 1, 3)


def untiled(field):
    layers, parts, sub, width_y = field.shape
    return field.transpose(0, 2, 1, 3).reshape(layers, sub * parts, width_y)


def split3(f):
    hi = f.astype(jnp.bfloat16)
    left = f - hi.astype(jnp.float32)
    mid = left.astype(jnp.bfloat16)
    return hi, mid, (left - mid.astype(jnp.float32)).astype(jnp.bfloat16)


def lane_pass(cur, first, count, weights, pieces, ybuf):
    parts, _, width_y = cur.shape[1:]
    rows = parts * SUB

    def one(q):
        at = pl.multiple_of(q * rows, rows)
        for i, piece in enumerate(split3(cur[first + q].reshape(rows, width_y))):
            pieces[pl.ds(at, rows), i * width_y : (i + 1) * width_y] = piece

    layers_loop(0, count, one)
    for q in range(0, count, SHIFT):
        block = slice(q * rows, min(q + SHIFT, count) * rows)
        ybuf[block, :] = jnp.dot(pieces[block, :], weights[...], preferred_element_type=jnp.float32)


def lap_maker(parts, width_y):
    row = lax.broadcasted_iota(jnp.int32, (1, SUB, width_y), 1)

    def lap(ref, j, along):
        f = ref[j]
        after = jnp.where(row == SUB - 1, 0.0, pltpu.roll(f[:REACH], SUB - 1, 1))
        before = jnp.where(row == 0, 0.0, pltpu.roll(f[parts - REACH :], 1, 1))
        wide = jnp.concatenate([before, f, after], axis=0)
        total = along + (3.0 * WHOLE[0]) * f
        for k in range(1, 5):
            pair = (ref[j + k] + ref[j - k]) + (
                wide[REACH + k : REACH + k + parts] + wide[REACH - k : REACH - k + parts]
            )
            total = total + WHOLE[k] * pair
        return f, total

    return lap


def layers_loop(first, count, body):
    def one(q, carry):
        body(first + q)
        return carry

    lax.fori_loop(0, count, one, 0, unroll=2)


def inject(rbuf, rows, starts, table, level, first, last):
    low, high = starts[first], starts[last]

    def eight(i, carry):
        for q in range(8):
            r = jnp.minimum(low + i * 8 + q, high - 1)
            rbuf[pl.ds(rows[r], 1), :] = table[level, pl.ds(r, 1), :]
        return carry

    lax.fori_loop(0, (high - low + 7) // 8, eight, 0)


def chunks_of(starts):
    return (starts[starts.shape[0] - 1] + CHUNK - 1) // CHUNK


def table_kernel(starts, ids, rows_l, rows_s, lanes_s, res, out, res_cut, pieces, same, part, sem):
    steps, receivers = res.shape
    width_y = part.shape[2]
    chunks = chunks_of(starts)
    for i, piece in enumerate(split3(res[...])):
        pieces[i * steps : (i + 1) * steps, :] = piece

    def column(c, carry):
        who = lax.broadcasted_iota(jnp.int32, (receivers, CHUNK), 0) == ids[pl.ds(c, 1), :]
        moved = jnp.dot(
            pieces[...], jnp.where(who, 1.0, 0.0).astype(jnp.bfloat16), preferred_element_type=jnp.float32
        )
        total = (moved[:steps] + moved[steps : 2 * steps]) + moved[2 * steps :]
        res_cut[c] = SCALE * total
        return carry

    lax.fori_loop(0, chunks, column, 0)

    def to_chunk(c, carry):
        mine = rows_s[pl.ds(pl.multiple_of(c * CHUNK, CHUNK), CHUNK), :]

        def from_chunk(d, carry):
            same[...] = jnp.where(mine == rows_l[pl.ds(d, 1), :], 1.0, 0.0)
            at = pl.multiple_of(d * CHUNK, CHUNK)
            lane = lax.broadcasted_iota(jnp.int32, (CHUNK, width_y), 1)
            spots = jnp.where(lane == lanes_s[pl.ds(at, CHUNK), :], 1.0, 0.0).astype(jnp.bfloat16)

            def one(n, carry):
                total = jnp.zeros((CHUNK, width_y), jnp.float32)
                for piece in split3(same[...] * res_cut[d, pl.ds(n, 1), :]):
                    total = total + jnp.dot(piece, spots, preferred_element_type=jnp.float32)

                @pl.when(d == 0)
                def _():
                    part[n] = total

                @pl.when(d > 0)
                def _():
                    part[n] = part[n] + total

                return carry

            return lax.fori_loop(0, steps, one, carry)

        lax.fori_loop(0, chunks, from_chunk, 0)
        at = pl.multiple_of(c * CHUNK, CHUNK)
        write = pltpu.make_async_copy(part, out.at[:, pl.ds(at, CHUNK), :], sem)
        write.start()
        write.wait()
        return carry

    lax.fori_loop(0, chunks, to_chunk, 0)


def fetch_table(table_hbm, table, starts, sem, steps):
    def each(act):
        def one(c, carry):
            at = pl.ds(pl.multiple_of(c * CHUNK, CHUNK), CHUNK)
            for i, n in enumerate(steps):
                act(pltpu.make_async_copy(table_hbm.at[n, at, :], table.at[i, at, :], sem.at[i, c]))
            return carry

        lax.fori_loop(0, chunks_of(starts), one, 0)

    each(lambda copy: copy.start())
    return lambda: each(lambda copy: copy.wait())


def block_kernel(side, is_l, *refs):
    refs = list(refs)

    def take(count):
        got = refs[:count]
        del refs[:count]
        return got

    (scal,) = take(1)
    wave = rows_of = starts = table_hbm = x_in = g_in = vmsg_in = None
    if is_l:
        rows_of, starts, table_hbm = take(3)
    else:
        (wave,) = take(1)
    own, rest, recv, coef, weights = take(5)
    if side == 1:
        (vmsg_in,) = take(1)
    if is_l:
        x_in, g_in = take(2)
    msg_out, rest_out = take(2)
    vmsg_out = x_out = g = None
    if side == 0:
        (vmsg_out,) = take(1)
    if is_l:
        (g,) = take(1)
    else:
        (x_out,) = take(1)
    a, b, c, p, pieces, ybuf = take(6)
    rbuf = table = sem = None
    if is_l:
        rbuf, table, sem = take(3)

    parts, _, width_y = a.shape[1:]
    rows = parts * SUB
    n0, is_last, src_layer, src_part, src_row, src_lane = (scal[i] for i in range(6))
    off = MID - SHIFT if side == 0 else MID - 2 * SHIFT
    lap = lap_maker(parts, width_y)

    if is_l:
        await_table = fetch_table(table_hbm, table, starts, sem, (n0, n0 - 1, jnp.maximum(n0 - 2, 0)))
        rbuf[...] = jnp.zeros(rbuf.shape, jnp.float32)

    def bring(msg, low):
        if low:
            a[MID - SHIFT : MID] = msg[0:SHIFT]
            p[MID - REACH : MID] = msg[SHIFT : SHIFT + REACH]
            b[MID - SHIFT - REACH : MID - REACH] = msg[SHIFT + REACH : MSG]
        else:
            a[MID : MID + SHIFT] = msg[0:SHIFT]
            p[MID : MID + REACH] = msg[SHIFT : SHIFT + REACH]
            b[MID + REACH : MID + REACH + SHIFT] = msg[SHIFT + REACH : MSG]

    if side == 0:
        bring(recv, True)
        a[MID : MID + SHIFT] = rest[0:SHIFT]
        p[MID : MID + REACH] = rest[SHIFT:REST]
        b[MID + REACH : MID + REACH + SHIFT] = own[SHIFT + REACH : MSG]

        @pl.when(is_last == 1)
        def _():
            zero = jnp.zeros((REACH,) + a.shape[1:], jnp.float32)
            a[MID + SHIFT : MID + 2 * SHIFT] = own[0:SHIFT]
            p[MID + SHIFT + REACH : MID + 2 * SHIFT] = own[SHIFT : SHIFT + REACH]
            for field in (a, b, c):
                field[MID + 2 * SHIFT : MID + 2 * SHIFT + REACH] = zero
    else:
        a[MID - SHIFT : MID] = rest[0:SHIFT]
        p[MID - REACH : MID] = rest[SHIFT:REST]
        b[MID - SHIFT - REACH : MID - REACH] = own[SHIFT + REACH : MSG]

        @pl.when(is_last == 1)
        def _():
            bring(vmsg_in, False)

        @pl.when(is_last == 0)
        def _():
            bring(recv, False)

    if is_l:
        await_table()

    def source(nxt, level, first, count):
        j = src_layer + off

        @pl.when((src_layer >= 0) & (j >= first) & (j < first + count))
        def _():
            lane = lax.broadcasted_iota(jnp.int32, (1, width_y), 1)
            spot = nxt[j, src_part, pl.ds(src_row, 1), :]
            gain = coef[src_layer, src_part, pl.ds(src_row, 1), :] * wave[jnp.maximum(n0 - level, 0)]
            nxt[j, src_part, pl.ds(src_row, 1), :] = spot - jnp.where(lane == src_lane, gain, 0.0)

    def advance(level, cur, nxt, first, count, x_base, outs, x_save=None):
        if is_l:
            zone = (first - off) // REACH
            inject(rbuf, rows_of, starts, table, level, zone, zone + count // REACH)
        else:
            source(nxt, level, first, count)
        lane_pass(cur, first, count, weights, pieces, ybuf)

        def body(j):
            y_at = pl.multiple_of((j - first) * rows, rows)
            f, total = lap(cur, j, ybuf[pl.ds(y_at, rows), :].reshape(parts, SUB, width_y))
            if is_l:
                at = pl.multiple_of((j - off) * rows, rows)
                total = total + rbuf[pl.ds(at, rows), :].reshape(parts, SUB, width_y)
                rbuf[pl.ds(at, rows), :] = jnp.zeros((rows, width_y), jnp.float32)
            step = coef[j - off] * total
            new = (2.0 * f - nxt[j]) + step
            for ref, shift in outs:
                ref[j + shift] = new
            if is_l:
                g[j - off] = g[j - off] + x_in[j + (x_base - first)] * step
            else:
                x_out[j + (x_base - first)] = f

        layers_loop(first, count, body)

    if is_l:
        if side == 0:
            g[2 * SHIFT : 3 * SHIFT] = g_in[2 * SHIFT : 3 * SHIFT]
            g[0 : 2 * SHIFT] = g_in[0 : 2 * SHIFT]
        else:
            g[...] = g_in[...]

    advance(0, a, p, MID - REACH, SHIFT, 0, [(b, 0)])
    if side == 0:

        @pl.when(is_last == 1)
        def _():
            advance(0, a, p, MID + SHIFT + REACH, REACH, 32, [(b, 0)])

    advance(1, b, a, MID - SHIFT, 2 * SHIFT, 8, [(c, 0)])
    if side == 0:

        @pl.when(is_last == 1)
        def _():
            advance(1, b, a, MID + SHIFT, SHIFT, 36, [(c, 0)])
            vmsg_out[0:SHIFT] = c[MID + SHIFT : MID + 2 * SHIFT]
            vmsg_out[SHIFT : SHIFT + REACH] = b[MID + SHIFT : MID + SHIFT + REACH]
            vmsg_out[SHIFT + 2 * REACH : MSG] = jnp.zeros((REACH,) + a.shape[1:], jnp.float32)

    if side == 0:
        msg_out[0:SHIFT] = c[MID - SHIFT : MID]
        msg_out[SHIFT : SHIFT + REACH] = b[MID - SHIFT : MID - REACH]
        rest_out[0:SHIFT] = c[MID : MID + SHIFT]
        rest_out[SHIFT:REST] = b[MID + REACH : MID + SHIFT]
    else:
        msg_out[0:SHIFT] = c[MID : MID + SHIFT]
        msg_out[SHIFT : SHIFT + REACH] = b[MID + REACH : MID + SHIFT]
        rest_out[0:SHIFT] = c[MID - SHIFT : MID]
        rest_out[SHIFT:REST] = b[MID - SHIFT : MID - REACH]

    @pl.when(n0 >= 2)
    def _():
        advance(2, c, b, MID - REACH, SHIFT, 24, [(msg_out, SHIFT + REACH - (MID - REACH))])
        if side == 0:

            @pl.when(is_last == 1)
            def _():
                first = MID + SHIFT + REACH
                advance(2, c, b, first, REACH, 44, [(vmsg_out, SHIFT + REACH - first)])

    @pl.when(n0 < 2)
    def _():
        msg_out[SHIFT + REACH : MSG] = jnp.zeros((SHIFT,) + a.shape[1:], jnp.float32)


def first_u_kernel(scal, wave, f0, f1, coef, weights, msg_out, rest_out, pieces, ybuf):
    depth, parts, _, width_y = f0.shape
    rows = parts * SUB
    n0, _, src_layer, src_part, src_row, src_lane = (scal[i] for i in range(6))
    lap = lap_maker(parts, width_y)
    msg_out[0:SHIFT] = f0[depth - SHIFT : depth]
    msg_out[SHIFT : SHIFT + REACH] = f1[depth - REACH : depth]
    rest_out[0:SHIFT] = f0[0:SHIFT]
    rest_out[SHIFT:REST] = f1[0:REACH]
    lane_pass(f0, REACH, SHIFT, weights, pieces, ybuf)

    def body(j):
        y_at = pl.multiple_of((j - REACH) * rows, rows)
        f, total = lap(f0, j, ybuf[pl.ds(y_at, rows), :].reshape(parts, SUB, width_y))
        msg_out[j + SHIFT] = (2.0 * f - f1[j]) + coef[j] * total

    layers_loop(REACH, SHIFT, body)
    j = src_layer - SHIFT

    @pl.when((src_layer >= 0) & (j >= REACH) & (j < REACH + SHIFT))
    def _():
        lane = lax.broadcasted_iota(jnp.int32, (1, width_y), 1)
        spot = msg_out[j + SHIFT, src_part, pl.ds(src_row, 1), :]
        gain = coef[j, src_part, pl.ds(src_row, 1), :] * wave[n0]
        msg_out[j + SHIFT, src_part, pl.ds(src_row, 1), :] = spot + jnp.where(lane == src_lane, gain, 0.0)


def first_l_kernel(scal, rows_of, starts, table_hbm, f0, coef, msg_out, rest_out, g, rbuf, table, sem):
    depth, parts, _, width_y = f0.shape
    rows = parts * SUB
    await_table = fetch_table(table_hbm, table, starts, sem, (scal[0],))
    rbuf[...] = jnp.zeros(rbuf.shape, jnp.float32)
    msg_out[0 : SHIFT + REACH] = jnp.zeros((SHIFT + REACH,) + f0.shape[1:], jnp.float32)
    rest_out[...] = jnp.zeros(rest_out.shape, jnp.float32)
    g[...] = jnp.zeros(g.shape, jnp.float32)
    await_table()
    zone = (SHIFT + REACH) // REACH
    inject(rbuf, rows_of, starts, table, 0, zone, zone + SHIFT // REACH)

    def body(j):
        at = pl.multiple_of((j + SHIFT) * rows, rows)
        new = coef[j] * rbuf[pl.ds(at, rows), :].reshape(parts, SUB, width_y)
        msg_out[j + SHIFT] = new
        g[j + SHIFT] = f0[j] * new

    layers_loop(REACH, SHIFT, body)


def lane_weights(width_y):
    away = jnp.abs(jnp.arange(width_y)[:, None] - jnp.arange(width_y)[None, :])
    once = jnp.zeros((width_y, width_y), jnp.float32)
    for k in range(1, 5):
        once = jnp.where(away == k, WHOLE[k], once)
    return jnp.tile(once.astype(jnp.bfloat16), (PIECES, 1))


def sum_shots(g):
    shots = lax.axis_size("shot")
    if shots != 2:
        return lax.psum_scatter(g, "shot", scatter_dimension=1, tiled=True)
    block = g.shape[1] // 2
    low, high = g[:, :block], g[:, block:]
    first = lax.axis_index("shot") == 0
    other = lax.ppermute(jnp.where(first, high, low), "shot", [(0, 1), (1, 0)])
    return jnp.where(first, low, high) + other


def on_device(fwd_last, fwd_prev, velocity, aperture, rec_index, src_index, residual):
    _, depth, width_x, width_y = fwd_last.shape
    parts = width_x // SUB
    total_steps, receivers = residual.shape[1:]
    plane = width_x * width_y
    slabs = lax.axis_size("slab")
    slab = lax.axis_index("slab")
    up = [(i, i + 1) for i in range(slabs - 1)]
    down = [(i + 1, i) for i in range(slabs - 1)]
    f32 = jnp.float32

    def coef_of(speed):
        return tiled((0.4 * speed) ** 2 * (1.0 / SCALE))

    vel_left = lax.ppermute(velocity[depth - SHIFT :], "slab", up)
    coef_own = coef_of(velocity)
    coef = jnp.concatenate([coef_of(vel_left), coef_own], axis=0)
    weights = lane_weights(width_y)

    base = (slab * depth - SHIFT) * plane
    window = (depth + SHIFT) * plane
    local = rec_index[0] - base
    far = jnp.int32(2**30)
    keys = jnp.where((local >= 0) & (local < window), local, far)
    keys, ids = lax.sort((keys, lax.iota(jnp.int32, receivers)), num_keys=1, is_stable=False)

    def place_of(cell):
        layer = cell // plane
        x = (cell // width_y) % width_x
        return layer, x % parts, x // parts, cell % width_y

    layer, part, row, lane = place_of(keys)
    rows_of = (layer * parts + part) * SUB + row
    zones = (depth + SHIFT) // REACH
    edges = jnp.arange(zones + 1, dtype=jnp.int32) * (REACH * plane)
    starts = jnp.sum((keys[None, :] < edges[:, None]).astype(jnp.int32), axis=1)

    src = src_index[0] - base
    src_in = (src >= 0) & (src < window)
    s_layer, s_part, s_row, s_lane = place_of(jnp.where(src_in, src, 0))
    s_layer = jnp.where(src_in, s_layer, -1)
    is_last = (slab == slabs - 1).astype(jnp.int32)

    def scal_of(n0):
        return jnp.stack([jnp.asarray(n0, jnp.int32), is_last, s_layer, s_part, s_row, s_lane])

    wave = SCALE * ricker(jnp.arange(total_steps, dtype=f32))

    smem = pl.BlockSpec(memory_space=pltpu.SMEM)
    vmem = pl.BlockSpec(memory_space=pltpu.VMEM)
    anym = pl.BlockSpec(memory_space=pl.ANY)

    def fields(layers):
        return jax.ShapeDtypeStruct((layers, parts, SUB, width_y), f32)

    params = pltpu.CompilerParams(vmem_limit_bytes=VMEM_BYTES)
    l_scratch = [
        pltpu.VMEM(((depth + SHIFT) * parts * SUB, width_y), f32),
        pltpu.VMEM((3, receivers, width_y), f32),
        pltpu.SemaphoreType.DMA((3, receivers // CHUNK)),
    ]

    def lane_scratch(layers):
        rows = layers * parts * SUB
        return [pltpu.VMEM((rows, PIECES * width_y), jnp.bfloat16), pltpu.VMEM((rows, width_y), f32)]

    block_scratch = [pltpu.VMEM((SPAN, parts, SUB, width_y), f32)] * 4 + lane_scratch(2 * SHIFT)

    def cost(layers):
        return pl.CostEstimate(
            flops=50 * layers * plane, bytes_accessed=24 * layers * plane, transcendentals=0
        )

    f0, f1 = tiled(fwd_prev[0]), tiled(fwd_last[0])
    um, ur = pl.pallas_call(
        first_u_kernel,
        out_shape=(fields(MSG), fields(REST)),
        in_specs=[smem, smem] + [vmem] * 4,
        out_specs=(vmem, vmem),
        scratch_shapes=lane_scratch(SHIFT),
        compiler_params=params,
        cost_estimate=cost(SHIFT),
        name="first_u",
    )(scal_of(total_steps - 1), wave, f0, f1, coef_own, weights)
    u_got = lax.ppermute(um, "slab", up)

    table = pl.pallas_call(
        table_kernel,
        out_shape=jax.ShapeDtypeStruct((total_steps, receivers, width_y), f32),
        in_specs=[smem] + [vmem] * 5,
        out_specs=anym,
        scratch_shapes=[
            pltpu.VMEM((receivers // CHUNK, total_steps, CHUNK), f32),
            pltpu.VMEM((PIECES * total_steps, receivers), jnp.bfloat16),
            pltpu.VMEM((CHUNK, CHUNK), f32),
            pltpu.VMEM((total_steps, CHUNK, width_y), f32),
            pltpu.SemaphoreType.DMA(()),
        ],
        compiler_params=params,
        cost_estimate=cost(SHIFT),
        name="rec_table",
    )(
        starts,
        ids.reshape(receivers // CHUNK, CHUNK),
        rows_of.reshape(receivers // CHUNK, CHUNK),
        rows_of[:, None],
        lane[:, None],
        residual[0],
    )
    lm, lr, g = pl.pallas_call(
        first_l_kernel,
        out_shape=(fields(MSG), fields(REST), fields(depth + SHIFT)),
        in_specs=[smem, smem, smem, anym, vmem, vmem],
        out_specs=(vmem, vmem, vmem),
        scratch_shapes=l_scratch,
        compiler_params=params,
        cost_estimate=cost(SHIFT),
        name="first_l",
    )(scal_of(total_steps - 1), rows_of, starts, table, f0, coef_own)

    def u_block(side, n0, own, rest, recv, *vmsg):
        outs = [fields(MSG), fields(REST)]
        if side == 0:
            outs.append(fields(MSG))
        outs.append(fields(48))
        return pl.pallas_call(
            functools.partial(block_kernel, side, False),
            out_shape=outs,
            in_specs=[smem, smem] + [vmem] * (5 + len(vmsg)),
            out_specs=[vmem] * len(outs),
            scratch_shapes=block_scratch,
            compiler_params=params,
            cost_estimate=cost(2 * depth),
            name=f"u_block{side}",
        )(scal_of(n0), wave, own, rest, recv, coef, weights, *vmsg)

    def l_block(side, n0, own, rest, recv, vmsg, x, g):
        outs = [fields(MSG), fields(REST)]
        if side == 0:
            outs.append(fields(MSG))
        outs.append(fields(depth + SHIFT))
        return pl.pallas_call(
            functools.partial(block_kernel, side, True),
            out_shape=outs,
            in_specs=[smem] * 3 + [anym] + [vmem] * (7 + len(vmsg)),
            out_specs=[vmem] * len(outs),
            scratch_shapes=block_scratch + l_scratch,
            compiler_params=params,
            cost_estimate=cost(2 * depth),
            name=f"l_block{side}",
        )(scal_of(n0), rows_of, starts, table, own, rest, recv, coef, weights, *vmsg, x, g)

    def two_blocks(i, carry):
        um, ur, u_got, lm, lr, g = carry
        n0 = total_steps - 1 - 4 * i
        l_got = lax.ppermute(lm, "slab", up)
        um, ur, uv, x = u_block(0, n0, um, ur, u_got)
        u_got = lax.ppermute(um, "slab", down)
        lm, lr, lv, g_half = l_block(0, n0, lm, lr, l_got, (), x, g)
        l_got = lax.ppermute(lm, "slab", down)
        um, ur, x = u_block(1, n0 - 2, um, ur, u_got, uv)
        u_got = lax.ppermute(um, "slab", up)
        lm, lr, g = l_block(1, n0 - 2, lm, lr, l_got, (lv,), x, g_half)
        return (um, ur, u_got, lm, lr, g), g_half

    pairs = total_steps // 4
    carry = lax.fori_loop(0, pairs - 1, lambda i, c: two_blocks(i, c)[0], (um, ur, u_got, lm, lr, g))
    (_, _, _, lm, lr, g), g_half = two_blocks(pairs - 1, carry)

    g_right = lax.ppermute(g_half[:SHIFT], "slab", down)
    adjoint_field = untiled(jnp.concatenate([lr[:SHIFT], lm[:SHIFT]], axis=0))[None]
    g = jnp.concatenate([g[SHIFT : 2 * SHIFT], g[2 * SHIFT :] + g_right], axis=0)
    summed = sum_shots(aperture[0].astype(f32) * untiled(g))
    block = width_x // lax.axis_size("shot")
    speed = lax.dynamic_slice_in_dim(velocity, lax.axis_index("shot") * block, block, 1)
    return ((-2.0 / speed) * summed, adjoint_field)


def solution(mesh):
    in_specs = (
        P("shot", "slab", None, None),
        P("shot", "slab", None, None),
        P("slab", None, None),
        P("shot", None, None),
        P("shot", None),
        P("shot"),
        P("shot", None, None),
    )
    out_specs = (P("slab", "shot", None), P("shot", "slab", None, None))
    return jax.shard_map(on_device, mesh=mesh, in_specs=in_specs, out_specs=out_specs, check_vma=False)
```

```python
import functools

import jax
import jax.numpy as jnp
import numpy as np
from jax import lax
from jax.experimental import pallas as pl
from jax.experimental.pallas import tpu as pltpu
from jax.sharding import PartitionSpec as P

SCALE = 5040.0
WHOLE = (-14350.0, 8064.0, -1008.0, 128.0, -9.0)
REACH = 4
SHIFT = 8
VMEM_BYTES = 20 * 1024 * 1024
SUB = 8
PIECES = 3
CHUNK = 256

MSG = 2 * SHIFT + REACH
REST = SHIFT + REACH
SPAN = 32
MID = 12


def wave_of(step):
    arg = (np.pi * 0.06 * (step - 10.0)) ** 2
    return float(np.float32(SCALE * 10.0 * (1.0 - 2.0 * arg) * np.exp(-arg)))


def load_tiled(field, layer):
    parts = field.shape[1] // SUB
    return jnp.stack([field[layer, pl.ds(m, SUB, stride=parts), :] for m in range(parts)])


def store_tiled(field, layer, value, first=0, count=SUB):
    parts = value.shape[0]
    for m in range(parts):
        field[layer, pl.ds(m, count, stride=parts), :] = value[m, first : first + count]


def split3(f):
    hi = f.astype(jnp.bfloat16)
    left = f - hi.astype(jnp.float32)
    mid = left.astype(jnp.bfloat16)
    return hi, mid, (left - mid.astype(jnp.float32)).astype(jnp.bfloat16)


def put_weights(weights):
    width_y = weights.shape[1]
    square = (width_y, width_y)
    away = jnp.abs(lax.broadcasted_iota(jnp.int32, square, 0) - lax.broadcasted_iota(jnp.int32, square, 1))
    once = jnp.zeros(square, jnp.float32)
    for k in range(1, 5):
        once = jnp.where(away == k, WHOLE[k], once)
    for i in range(PIECES):
        weights[i * width_y : (i + 1) * width_y, :] = once.astype(jnp.bfloat16)


def lane_pass(cur, first, count, weights, pieces, ybuf):
    parts, _, width_y = cur.shape[1:]
    rows = parts * SUB

    def one(q):
        at = pl.multiple_of(q * rows, rows)
        for i, piece in enumerate(split3(cur[first + q].reshape(rows, width_y))):
            pieces[pl.ds(at, rows), i * width_y : (i + 1) * width_y] = piece

    layers_loop(0, count, one)
    for q in range(0, count, SHIFT):
        block = slice(q * rows, min(q + SHIFT, count) * rows)
        ybuf[block, :] = jnp.dot(pieces[block, :], weights[...], preferred_element_type=jnp.float32)


def lap_maker(parts, width_y):
    row = lax.broadcasted_iota(jnp.int32, (1, SUB, width_y), 1)

    def lap(ref, j, along):
        f = ref[j]
        after = jnp.where(row == SUB - 1, 0.0, pltpu.roll(f[:REACH], SUB - 1, 1))
        before = jnp.where(row == 0, 0.0, pltpu.roll(f[parts - REACH :], 1, 1))
        wide = jnp.concatenate([before, f, after], axis=0)
        total = along + (3.0 * WHOLE[0]) * f
        for k in range(1, 5):
            pair = (ref[j + k] + ref[j - k]) + (
                wide[REACH + k : REACH + k + parts] + wide[REACH - k : REACH - k + parts]
            )
            total = total + WHOLE[k] * pair
        return f, total

    return lap


def layers_loop(first, count, body):
    def one(q, carry):
        body(first + q)
        return carry

    lax.fori_loop(0, count, one, 0, unroll=2)


STARTS = 5
ROWS = 16


def inject(rbuf, info, table, level, first, last):
    low, high = info[STARTS + first], info[STARTS + last]

    def eight(i, carry):
        for q in range(8):
            r = jnp.minimum(low + i * 8 + q, high - 1)
            rbuf[pl.ds(info[ROWS + r], 1), :] = table[level, pl.ds(r, 1), :]
        return carry

    lax.fori_loop(0, (high - low + 7) // 8, eight, 0)


def chunks_of(info, zones):
    return (info[STARTS + zones] + CHUNK - 1) // CHUNK


def table_kernel(zones, info, ids, rows_l, rows_s, lanes_s, res, out, res_cut, pieces, same, part, sem):
    steps, receivers = res.shape
    width_y = part.shape[2]
    chunks = chunks_of(info, zones)
    for i, piece in enumerate(split3(res[...])):
        pieces[i * steps : (i + 1) * steps, :] = piece

    def column(c, carry):
        who = lax.broadcasted_iota(jnp.int32, (receivers, CHUNK), 0) == ids[pl.ds(c, 1), :]
        moved = jnp.dot(
            pieces[...], jnp.where(who, 1.0, 0.0).astype(jnp.bfloat16), preferred_element_type=jnp.float32
        )
        total = SCALE * ((moved[:steps] + moved[steps : 2 * steps]) + moved[2 * steps :])
        for i, piece in enumerate(split3(total)):
            res_cut[c, i] = piece.astype(jnp.float32)
        return carry

    lax.fori_loop(0, chunks, column, 0)

    def to_chunk(c, carry):
        mine = rows_s[pl.ds(pl.multiple_of(c * CHUNK, CHUNK), CHUNK), :]

        def from_chunk(d, carry):
            same[...] = jnp.where(mine == rows_l[pl.ds(d, 1), :], 1.0, 0.0).astype(jnp.bfloat16)
            at = pl.multiple_of(d * CHUNK, CHUNK)
            lane = lax.broadcasted_iota(jnp.int32, (CHUNK, width_y), 1)
            spots = jnp.where(lane == lanes_s[pl.ds(at, CHUNK), :], 1.0, 0.0).astype(jnp.bfloat16)

            def one(n, carry):
                total = jnp.zeros((CHUNK, width_y), jnp.float32)
                for i in range(PIECES):
                    row = jnp.broadcast_to(res_cut[d, i, pl.ds(n, 1), :], (16, CHUNK)).astype(jnp.bfloat16)
                    mixed = same[...].reshape(CHUNK // 16, 16, CHUNK) * row[None]
                    total = total + jnp.dot(
                        mixed.reshape(CHUNK, CHUNK), spots, preferred_element_type=jnp.float32
                    )

                @pl.when(d == 0)
                def _():
                    part[n] = total

                @pl.when(d > 0)
                def _():
                    part[n] = part[n] + total

                return carry

            return lax.fori_loop(0, steps, one, carry)

        lax.fori_loop(0, chunks, from_chunk, 0)
        at = pl.multiple_of(c * CHUNK, CHUNK)
        write = pltpu.make_async_copy(part, out.at[:, pl.ds(at, CHUNK), :], sem)
        write.start()
        write.wait()
        return carry

    lax.fori_loop(0, chunks, to_chunk, 0)


def fetch_table(table_hbm, table, info, zones, sem, steps):
    def each(act):
        def one(c, carry):
            at = pl.ds(pl.multiple_of(c * CHUNK, CHUNK), CHUNK)
            for i, n in enumerate(steps):
                act(pltpu.make_async_copy(table_hbm.at[n, at, :], table.at[i, at, :], sem.at[i, c]))
            return carry

        lax.fori_loop(0, chunks_of(info, zones), one, 0)

    each(lambda copy: copy.start())
    return lambda: each(lambda copy: copy.wait())


def block_kernel(side, is_l, n0, *refs):
    refs = list(refs)

    def take(count):
        got = refs[:count]
        del refs[:count]
        return got

    final = n0 == 1
    (info,) = take(1)
    table_hbm = x_in = g_in = vmsg_in = None
    if is_l:
        (table_hbm,) = take(1)
    own, rest, recv, coef = take(4)
    if side == 1:
        (vmsg_in,) = take(1)
    if is_l:
        x_in, g_in = take(2)
    msg_out = rest_out = vmsg_out = x_out = g = field_out = None
    if not final:
        msg_out, rest_out = take(2)
    if side == 0:
        (vmsg_out,) = take(1)
    if is_l:
        (g,) = take(1)
        if final:
            (field_out,) = take(1)
    else:
        (x_out,) = take(1)
    a, b, c, p, pieces, ybuf, weights = take(7)
    rbuf = table = sem = None
    if is_l:
        rbuf, table, sem = take(3)

    parts, _, width_y = a.shape[1:]
    rows = parts * SUB
    zones = coef.shape[0] // REACH
    is_last, src_layer, src_part, src_row, src_lane = (info[i] for i in range(STARTS))
    off = MID - SHIFT if side == 0 else MID - 2 * SHIFT
    lap = lap_maker(parts, width_y)

    if is_l:
        levels = tuple(range(n0, max(n0 - 3, -1), -1))
        await_table = fetch_table(table_hbm, table, info, zones, sem, levels)
        rbuf[...] = jnp.zeros(rbuf.shape, jnp.float32)
    put_weights(weights)

    def bring(msg, low):
        if low:
            a[MID - SHIFT : MID] = msg[0:SHIFT]
            p[MID - REACH : MID] = msg[SHIFT : SHIFT + REACH]
            b[MID - SHIFT - REACH : MID - REACH] = msg[SHIFT + REACH : MSG]
        else:
            a[MID : MID + SHIFT] = msg[0:SHIFT]
            p[MID : MID + REACH] = msg[SHIFT : SHIFT + REACH]
            b[MID + REACH : MID + REACH + SHIFT] = msg[SHIFT + REACH : MSG]

    if side == 0:
        bring(recv, True)
        a[MID : MID + SHIFT] = rest[0:SHIFT]
        p[MID : MID + REACH] = rest[SHIFT:REST]
        b[MID + REACH : MID + REACH + SHIFT] = own[SHIFT + REACH : MSG]

        @pl.when(is_last == 1)
        def _():
            zero = jnp.zeros((REACH,) + a.shape[1:], jnp.float32)
            a[MID + SHIFT : MID + 2 * SHIFT] = own[0:SHIFT]
            p[MID + SHIFT + REACH : MID + 2 * SHIFT] = own[SHIFT : SHIFT + REACH]
            for field in (a, b, c):
                field[MID + 2 * SHIFT : MID + 2 * SHIFT + REACH] = zero
    else:
        a[MID - SHIFT : MID] = rest[0:SHIFT]
        p[MID - REACH : MID] = rest[SHIFT:REST]
        b[MID - SHIFT - REACH : MID - REACH] = own[SHIFT + REACH : MSG]

        @pl.when(is_last == 1)
        def _():
            bring(vmsg_in, False)

        @pl.when(is_last == 0)
        def _():
            bring(recv, False)

    if is_l:
        await_table()

    def source(nxt, level, first, count):
        j = src_layer + off

        @pl.when((src_layer >= 0) & (j >= first) & (j < first + count))
        def _():
            lane = lax.broadcasted_iota(jnp.int32, (1, width_y), 1)
            spot = nxt[j, src_part, pl.ds(src_row, 1), :]
            gain = coef[src_layer, src_part, pl.ds(src_row, 1), :] * wave_of(n0 - level)
            nxt[j, src_part, pl.ds(src_row, 1), :] = spot - jnp.where(lane == src_lane, gain, 0.0)

    def advance(level, cur, nxt, first, count, x_base, outs, x_save=None):
        if is_l:
            zone = (first - off) // REACH
            inject(rbuf, info, table, level, zone, zone + count // REACH)
        else:
            source(nxt, level, first, count)
        lane_pass(cur, first, count, weights, pieces, ybuf)

        def body(j):
            y_at = pl.multiple_of((j - first) * rows, rows)
            f, total = lap(cur, j, ybuf[pl.ds(y_at, rows), :].reshape(parts, SUB, width_y))
            if is_l:
                at = pl.multiple_of((j - off) * rows, rows)
                total = total + rbuf[pl.ds(at, rows), :].reshape(parts, SUB, width_y)
                rbuf[pl.ds(at, rows), :] = jnp.zeros((rows, width_y), jnp.float32)
            step = coef[j - off] * total
            new = (2.0 * f - nxt[j]) + step
            for ref, shift in outs:
                ref[j + shift] = new
            if is_l:
                g[j - off] = g[j - off] + x_in[j + (x_base - first)] * step
            else:
                x_out[j + (x_base - first)] = f

        layers_loop(first, count, body)

    if is_l:
        if side == 0:
            g[2 * SHIFT : 3 * SHIFT] = g_in[2 * SHIFT : 3 * SHIFT]
            g[0 : 2 * SHIFT] = g_in[0 : 2 * SHIFT]
        else:
            g[...] = g_in[...]

    advance(0, a, p, MID - REACH, SHIFT, 0, [(b, 0)])
    if side == 0:

        @pl.when(is_last == 1)
        def _():
            advance(0, a, p, MID + SHIFT + REACH, REACH, 32, [(b, 0)])

    advance(1, b, a, MID - SHIFT, 2 * SHIFT, 8, [(c, 0)])
    if side == 0:

        @pl.when(is_last == 1)
        def _():
            advance(1, b, a, MID + SHIFT, SHIFT, 36, [(c, 0)])
            vmsg_out[0:SHIFT] = c[MID + SHIFT : MID + 2 * SHIFT]
            vmsg_out[SHIFT : SHIFT + REACH] = b[MID + SHIFT : MID + SHIFT + REACH]
            vmsg_out[SHIFT + 2 * REACH : MSG] = jnp.zeros((REACH,) + a.shape[1:], jnp.float32)

    if final:
        if is_l:
            for layer in range(2 * SHIFT):
                store_tiled(field_out, layer, c[MID - SHIFT + layer])
        return
    if side == 0:
        msg_out[0:SHIFT] = c[MID - SHIFT : MID]
        msg_out[SHIFT : SHIFT + REACH] = b[MID - SHIFT : MID - REACH]
        rest_out[0:SHIFT] = c[MID : MID + SHIFT]
        rest_out[SHIFT:REST] = b[MID + REACH : MID + SHIFT]
    else:
        msg_out[0:SHIFT] = c[MID : MID + SHIFT]
        msg_out[SHIFT : SHIFT + REACH] = b[MID + REACH : MID + SHIFT]
        rest_out[0:SHIFT] = c[MID - SHIFT : MID]
        rest_out[SHIFT:REST] = b[MID - SHIFT : MID - REACH]

    advance(2, c, b, MID - REACH, SHIFT, 24, [(msg_out, SHIFT + REACH - (MID - REACH))])
    if side == 0:

        @pl.when(is_last == 1)
        def _():
            first = MID + SHIFT + REACH
            advance(2, c, b, first, REACH, 44, [(vmsg_out, SHIFT + REACH - first)])


def first_u_kernel(n0, info, prev, last, speed, msg_out, rest_out, f0, coef, f1, pieces, ybuf, weights):
    depth, parts, _, width_y = f0.shape
    rows = parts * SUB
    src_layer, src_part, src_row, src_lane = (info[i] for i in range(1, STARTS))
    lap = lap_maker(parts, width_y)
    put_weights(weights)

    def bring(z):
        f0[z] = load_tiled(prev, z)
        f1[z] = load_tiled(last, z)
        coef[z] = (0.4 * load_tiled(speed, z)) ** 2 * (1.0 / SCALE)

    layers_loop(0, depth, bring)
    msg_out[0:SHIFT] = f0[depth - SHIFT : depth]
    msg_out[SHIFT : SHIFT + REACH] = f1[depth - REACH : depth]
    rest_out[0:SHIFT] = f0[0:SHIFT]
    rest_out[SHIFT:REST] = f1[0:REACH]
    lane_pass(f0, REACH, SHIFT, weights, pieces, ybuf)

    def body(j):
        y_at = pl.multiple_of((j - REACH) * rows, rows)
        f, total = lap(f0, j, ybuf[pl.ds(y_at, rows), :].reshape(parts, SUB, width_y))
        msg_out[j + SHIFT] = (2.0 * f - f1[j]) + coef[j] * total

    layers_loop(REACH, SHIFT, body)
    j = src_layer - SHIFT

    @pl.when((src_layer >= 0) & (j >= REACH) & (j < REACH + SHIFT))
    def _():
        lane = lax.broadcasted_iota(jnp.int32, (1, width_y), 1)
        spot = msg_out[j + SHIFT, src_part, pl.ds(src_row, 1), :]
        gain = coef[j, src_part, pl.ds(src_row, 1), :] * wave_of(n0)
        msg_out[j + SHIFT, src_part, pl.ds(src_row, 1), :] = spot + jnp.where(lane == src_lane, gain, 0.0)


def first_l_kernel(n0, info, table_hbm, f0, coef, msg_out, rest_out, g, rbuf, table, sem):
    depth, parts, _, width_y = f0.shape
    rows = parts * SUB
    await_table = fetch_table(table_hbm, table, info, (depth + SHIFT) // REACH, sem, (n0,))
    rbuf[...] = jnp.zeros(rbuf.shape, jnp.float32)
    msg_out[0 : SHIFT + REACH] = jnp.zeros((SHIFT + REACH,) + f0.shape[1:], jnp.float32)
    rest_out[...] = jnp.zeros(rest_out.shape, jnp.float32)
    g[...] = jnp.zeros(g.shape, jnp.float32)
    await_table()
    zone = (SHIFT + REACH) // REACH
    inject(rbuf, info, table, 0, zone, zone + SHIFT // REACH)

    def body(j):
        at = pl.multiple_of((j + SHIFT) * rows, rows)
        new = coef[j] * rbuf[pl.ds(at, rows), :].reshape(parts, SUB, width_y)
        msg_out[j + SHIFT] = new
        g[j + SHIFT] = f0[j] * new

    layers_loop(REACH, SHIFT, body)


def join_kernel(left, own, out):
    out[0:SHIFT] = left[...]
    out[SHIFT:] = own[...]


def last_kernel(g, g_right, gate, out):
    depth = out.shape[0]

    def one(z):
        store_tiled(out, z, load_tiled(gate, 0) * g[z + SHIFT])

    def shared(z):
        store_tiled(out, z, load_tiled(gate, 0) * (g[z + SHIFT] + g_right[z - SHIFT]))

    layers_loop(0, SHIFT, one)
    layers_loop(SHIFT, depth - SHIFT, shared)


def sum_shots(g):
    shots = lax.axis_size("shot")
    if shots != 2:
        return lax.psum_scatter(g, "shot", scatter_dimension=1, tiled=True)
    block = g.shape[1] // 2
    low, high = g[:, :block], g[:, block:]
    first = lax.axis_index("shot") == 0
    other = lax.ppermute(jnp.where(first, high, low), "shot", [(0, 1), (1, 0)])
    return jnp.where(first, low, high) + other


def on_device(fwd_last, fwd_prev, velocity, aperture, rec_index, src_index, residual):
    _, depth, width_x, width_y = fwd_last.shape
    parts = width_x // SUB
    total_steps, receivers = residual.shape[1:]
    plane = width_x * width_y
    slabs = lax.axis_size("slab")
    slab = lax.axis_index("slab")
    up = [(i, i + 1) for i in range(slabs - 1)]
    down = [(i + 1, i) for i in range(slabs - 1)]
    f32 = jnp.float32

    base = (slab * depth - SHIFT) * plane
    window = (depth + SHIFT) * plane
    local = rec_index[0] - base
    far = jnp.int32(2**30)
    keys = jnp.where((local >= 0) & (local < window), local, far)
    keys, ids = lax.sort((keys, lax.iota(jnp.int32, receivers)), num_keys=1, is_stable=False)

    def place_of(cell):
        layer = cell // plane
        x = (cell // width_y) % width_x
        return layer, x % parts, x // parts, cell % width_y

    layer, part, row, lane = place_of(keys)
    rows_of = (layer * parts + part) * SUB + row
    zones = (depth + SHIFT) // REACH
    edges = jnp.arange(zones + 1, dtype=jnp.int32) * (REACH * plane)
    starts = jnp.sum((keys[None, :] < edges[:, None]).astype(jnp.int32), axis=1)

    src = src_index[0] - base
    src_in = (src >= 0) & (src < window)
    s_layer, s_part, s_row, s_lane = place_of(jnp.where(src_in, src, 0))
    s_layer = jnp.where(src_in, s_layer, -1)
    is_last = (slab == slabs - 1).astype(jnp.int32)
    src_info = jnp.stack([is_last, s_layer, s_part, s_row, s_lane])
    info = jnp.concatenate([src_info, starts, jnp.zeros((ROWS - STARTS - zones - 1,), jnp.int32), rows_of])
    last_step = total_steps - 1

    smem = pl.BlockSpec(memory_space=pltpu.SMEM)
    vmem = pl.BlockSpec(memory_space=pltpu.VMEM)
    anym = pl.BlockSpec(memory_space=pl.ANY)

    def fields(layers):
        return jax.ShapeDtypeStruct((layers, parts, SUB, width_y), f32)

    params = pltpu.CompilerParams(vmem_limit_bytes=VMEM_BYTES)
    l_scratch = [
        pltpu.VMEM(((depth + SHIFT) * parts * SUB, width_y), f32),
        pltpu.VMEM((3, receivers, width_y), f32),
        pltpu.SemaphoreType.DMA((3, receivers // CHUNK)),
    ]

    def lane_scratch(layers):
        rows = layers * parts * SUB
        return [
            pltpu.VMEM((rows, PIECES * width_y), jnp.bfloat16),
            pltpu.VMEM((rows, width_y), f32),
            pltpu.VMEM((PIECES * width_y, width_y), jnp.bfloat16),
        ]

    block_scratch = [pltpu.VMEM((SPAN, parts, SUB, width_y), f32)] * 4 + lane_scratch(2 * SHIFT)

    def cost(layers):
        return pl.CostEstimate(
            flops=50 * layers * plane, bytes_accessed=24 * layers * plane, transcendentals=0
        )

    um, ur, f0, coef_own = pl.pallas_call(
        functools.partial(first_u_kernel, last_step),
        out_shape=(fields(MSG), fields(REST), fields(depth), fields(depth)),
        in_specs=[smem] + [vmem] * 3,
        out_specs=[vmem] * 4,
        scratch_shapes=[pltpu.VMEM((depth, parts, SUB, width_y), f32)] + lane_scratch(SHIFT),
        compiler_params=params,
        cost_estimate=cost(SHIFT),
        name="first_u",
    )(src_info, fwd_prev[0], fwd_last[0], velocity)
    u_got = lax.ppermute(um, "slab", up)
    coef_left = lax.ppermute(coef_own[depth - SHIFT :], "slab", up)

    table = pl.pallas_call(
        functools.partial(table_kernel, zones),
        out_shape=jax.ShapeDtypeStruct((total_steps, receivers, width_y), f32),
        in_specs=[smem] + [vmem] * 5,
        out_specs=anym,
        scratch_shapes=[
            pltpu.VMEM((receivers // CHUNK, PIECES, total_steps, CHUNK), f32),
            pltpu.VMEM((PIECES * total_steps, receivers), jnp.bfloat16),
            pltpu.VMEM((CHUNK, CHUNK), jnp.bfloat16),
            pltpu.VMEM((total_steps, CHUNK, width_y), f32),
            pltpu.SemaphoreType.DMA(()),
        ],
        compiler_params=params,
        cost_estimate=cost(SHIFT),
        name="rec_table",
    )(
        info,
        ids.reshape(receivers // CHUNK, CHUNK),
        rows_of.reshape(receivers // CHUNK, CHUNK),
        rows_of[:, None],
        lane[:, None],
        residual[0],
    )
    lm, lr, g = pl.pallas_call(
        functools.partial(first_l_kernel, last_step),
        out_shape=(fields(MSG), fields(REST), fields(depth + SHIFT)),
        in_specs=[smem, anym, vmem, vmem],
        out_specs=(vmem, vmem, vmem),
        scratch_shapes=l_scratch,
        compiler_params=params,
        cost_estimate=cost(SHIFT),
        name="first_l",
    )(info, table, f0, coef_own)
    l_got = lax.ppermute(lm, "slab", up)
    coef = pl.pallas_call(
        join_kernel,
        out_shape=fields(depth + SHIFT),
        in_specs=[vmem, vmem],
        out_specs=vmem,
        compiler_params=params,
        name="join_coef",
    )(coef_left, coef_own)

    def u_block(side, n0, own, rest, recv, *vmsg):
        outs = [fields(MSG), fields(REST)] if n0 > 1 else []
        if side == 0:
            outs.append(fields(MSG))
        outs.append(fields(48))
        return pl.pallas_call(
            functools.partial(block_kernel, side, False, n0),
            out_shape=outs,
            in_specs=[smem] + [vmem] * (4 + len(vmsg)),
            out_specs=[vmem] * len(outs),
            scratch_shapes=block_scratch,
            compiler_params=params,
            cost_estimate=cost(2 * depth),
            name=f"u_block{side}",
        )(info, own, rest, recv, coef, *vmsg)

    def l_block(side, n0, own, rest, recv, vmsg, x, g):
        outs = [fields(MSG), fields(REST)] if n0 > 1 else []
        if side == 0:
            outs.append(fields(MSG))
        outs.append(fields(depth + SHIFT))
        if n0 == 1:
            outs.append(jax.ShapeDtypeStruct((depth, width_x, width_y), f32))
        return pl.pallas_call(
            functools.partial(block_kernel, side, True, n0),
            out_shape=outs,
            in_specs=[smem, anym] + [vmem] * (6 + len(vmsg)),
            out_specs=[vmem] * len(outs),
            scratch_shapes=block_scratch + l_scratch,
            compiler_params=params,
            cost_estimate=cost(2 * depth),
            name=f"l_block{side}",
        )(info, table, own, rest, recv, coef, *vmsg, x, g)

    for n0 in range(last_step, 0, -4):
        um, ur, uv, x = u_block(0, n0, um, ur, u_got)
        u_got = lax.ppermute(um, "slab", down)
        lm, lr, lv, g = l_block(0, n0, lm, lr, l_got, (), x, g)
        l_got = lax.ppermute(lm, "slab", down)
        g_half = g
        if n0 > 3:
            um, ur, x = u_block(1, n0 - 2, um, ur, u_got, uv)
            u_got = lax.ppermute(um, "slab", up)
            lm, lr, g = l_block(1, n0 - 2, lm, lr, l_got, (lv,), x, g)
            l_got = lax.ppermute(lm, "slab", up)
        else:
            (x,) = u_block(1, n0 - 2, um, ur, u_got, uv)
            g, adjoint_field = l_block(1, n0 - 2, lm, lr, l_got, (lv,), x, g)

    g_right = lax.ppermute(g_half[:SHIFT], "slab", down)
    terms = pl.pallas_call(
        last_kernel,
        out_shape=jax.ShapeDtypeStruct((depth, width_x, width_y), f32),
        in_specs=[vmem] * 3,
        out_specs=vmem,
        compiler_params=params,
        cost_estimate=cost(2),
        name="last_terms",
    )(g, g_right, aperture.astype(f32))
    summed = sum_shots(terms)
    block = width_x // lax.axis_size("shot")
    speed = lax.dynamic_slice_in_dim(velocity, lax.axis_index("shot") * block, block, 1)
    return ((-2.0 / speed) * summed, adjoint_field[None])


def solution(mesh):
    in_specs = (
        P("shot", "slab", None, None),
        P("shot", "slab", None, None),
        P("slab", None, None),
        P("shot", None, None),
        P("shot", None),
        P("shot"),
        P("shot", None, None),
    )
    out_specs = (P("slab", "shot", None), P("shot", "slab", None, None))
    return jax.shard_map(on_device, mesh=mesh, in_specs=in_specs, out_specs=out_specs, check_vma=False)
```

```python
import functools

import jax
import jax.numpy as jnp
import numpy as np
from jax import lax
from jax.experimental import pallas as pl
from jax.experimental.pallas import tpu as pltpu
from jax.sharding import PartitionSpec as P

SCALE = 5040.0
WHOLE = (-14350.0, 8064.0, -1008.0, 128.0, -9.0)
REACH = 4
SHIFT = 8
VMEM_BYTES = 20 * 1024 * 1024
SUB = 8
PIECES = 3
CHUNK = 256

MSG = 2 * SHIFT + REACH
REST = SHIFT + REACH
SPAN = 32
MID = 12


def wave_of(step):
    arg = (np.pi * 0.06 * (step - 10.0)) ** 2
    return float(np.float32(SCALE * 10.0 * (1.0 - 2.0 * arg) * np.exp(-arg)))


def load_tiled(field, layer):
    parts = field.shape[1] // SUB
    return jnp.stack([field[layer, pl.ds(m, SUB, stride=parts), :] for m in range(parts)])


def store_tiled(field, layer, value, first=0, count=SUB):
    parts = value.shape[0]
    for m in range(parts):
        field[layer, pl.ds(m, count, stride=parts), :] = value[m, first : first + count]


def split3(f):
    hi = f.astype(jnp.bfloat16)
    left = f - hi.astype(jnp.float32)
    mid = left.astype(jnp.bfloat16)
    return hi, mid, (left - mid.astype(jnp.float32)).astype(jnp.bfloat16)


def put_weights(weights):
    width_y = weights.shape[1]
    square = (width_y, width_y)
    away = jnp.abs(lax.broadcasted_iota(jnp.int32, square, 0) - lax.broadcasted_iota(jnp.int32, square, 1))
    once = jnp.zeros(square, jnp.float32)
    for k in range(1, 5):
        once = jnp.where(away == k, WHOLE[k], once)
    for i in range(PIECES):
        weights[i * width_y : (i + 1) * width_y, :] = once.astype(jnp.bfloat16)


def lane_pass(cur, first, count, weights, pieces, ybuf):
    parts, _, width_y = cur.shape[1:]
    rows = parts * SUB

    def one(q):
        at = pl.multiple_of(q * rows, rows)
        for i, piece in enumerate(split3(cur[first + q].reshape(rows, width_y))):
            pieces[pl.ds(at, rows), i * width_y : (i + 1) * width_y] = piece

    layers_loop(0, count, one)
    for q in range(0, count, SHIFT):
        block = slice(q * rows, min(q + SHIFT, count) * rows)
        ybuf[block, :] = jnp.dot(pieces[block, :], weights[...], preferred_element_type=jnp.float32)


def lap_maker(parts, width_y):
    row = lax.broadcasted_iota(jnp.int32, (1, SUB, width_y), 1)

    def lap(ref, j, along):
        f = ref[j]
        after = jnp.where(row == SUB - 1, 0.0, pltpu.roll(f[:REACH], SUB - 1, 1))
        before = jnp.where(row == 0, 0.0, pltpu.roll(f[parts - REACH :], 1, 1))
        wide = jnp.concatenate([before, f, after], axis=0)
        total = along + (3.0 * WHOLE[0]) * f
        for k in range(1, 5):
            pair = (ref[j + k] + ref[j - k]) + (
                wide[REACH + k : REACH + k + parts] + wide[REACH - k : REACH - k + parts]
            )
            total = total + WHOLE[k] * pair
        return f, total

    return lap


def layers_loop(first, count, body):
    def one(q, carry):
        body(first + q)
        return carry

    lax.fori_loop(0, count, one, 0, unroll=2)


STARTS = 5
ROWS = 16


def inject(rbuf, info, near, table, steps, level, first, last):
    low, high = info[STARTS + first], info[STARTS + last]

    def store(low, high, row_of):
        def eight(i, carry):
            for q in range(8):
                r = jnp.minimum(low + i * 8 + q, high - 1)
                rbuf[pl.ds(info[ROWS + r], 1), :] = row_of(r)
            return carry

        lax.fori_loop(0, (high - low + 7) // 8, eight, 0)

    split = jnp.clip(CHUNK, low, high)
    store(low, split, lambda r: near[steps[level], pl.ds(r, 1), :])
    store(split, high, lambda r: table[level, pl.ds(r, 1), :])


def chunks_of(info, zones):
    return jnp.maximum((info[STARTS + zones] + CHUNK - 1) // CHUNK, 1)


def table_kernel(zones, info, ids, rows_l, rows_s, lanes_s, res, near, out, res_cut, pieces, same, part, sem):
    steps, receivers = res.shape
    width_y = part.shape[2]
    chunks = chunks_of(info, zones)
    for i, piece in enumerate(split3(res[...])):
        pieces[i * steps : (i + 1) * steps, :] = piece

    def column(c, carry):
        who = lax.broadcasted_iota(jnp.int32, (receivers, CHUNK), 0) == ids[pl.ds(c, 1), :]
        moved = jnp.dot(
            pieces[...], jnp.where(who, 1.0, 0.0).astype(jnp.bfloat16), preferred_element_type=jnp.float32
        )
        total = SCALE * ((moved[:steps] + moved[steps : 2 * steps]) + moved[2 * steps :])
        for i, piece in enumerate(split3(total)):
            res_cut[c, i] = piece.astype(jnp.float32)
        return carry

    lax.fori_loop(0, chunks, column, 0)

    def to_chunk(c, carry):
        mine = rows_s[pl.ds(pl.multiple_of(c * CHUNK, CHUNK), CHUNK), :]

        def from_chunk(d, carry):
            same[...] = jnp.where(mine == rows_l[pl.ds(d, 1), :], 1.0, 0.0).astype(jnp.bfloat16)
            at = pl.multiple_of(d * CHUNK, CHUNK)
            lane = lax.broadcasted_iota(jnp.int32, (CHUNK, width_y), 1)
            spots = jnp.where(lane == lanes_s[pl.ds(at, CHUNK), :], 1.0, 0.0).astype(jnp.bfloat16)

            def one(n, carry):
                total = jnp.zeros((CHUNK, width_y), jnp.float32)
                for i in range(PIECES):
                    row = jnp.broadcast_to(res_cut[d, i, pl.ds(n, 1), :], (16, CHUNK)).astype(jnp.bfloat16)
                    mixed = same[...].reshape(CHUNK // 16, 16, CHUNK) * row[None]
                    total = total + jnp.dot(
                        mixed.reshape(CHUNK, CHUNK), spots, preferred_element_type=jnp.float32
                    )

                @pl.when(d == 0)
                def _():
                    part[n] = total

                @pl.when(d > 0)
                def _():
                    part[n] = part[n] + total

                return carry

            return lax.fori_loop(0, steps, one, carry)

        lax.fori_loop(0, chunks, from_chunk, 0)
        return carry

    def store_chunk(c, carry):
        to_chunk(c, 0)
        at = pl.multiple_of(c * CHUNK, CHUNK)
        write = pltpu.make_async_copy(part, out.at[:, pl.ds(at, CHUNK), :], sem)
        write.start()
        write.wait()
        return carry

    to_chunk(0, 0)
    near[...] = part[...]
    lax.fori_loop(1, chunks, store_chunk, 0)


def fetch_table(table_hbm, table, info, zones, sem, steps):
    def each(act):
        def one(c, carry):
            at = pl.ds(pl.multiple_of(c * CHUNK, CHUNK), CHUNK)
            for i, n in enumerate(steps):
                act(pltpu.make_async_copy(table_hbm.at[n, at, :], table.at[i, at, :], sem.at[i, c]))
            return carry

        lax.fori_loop(1, chunks_of(info, zones), one, 0)

    each(lambda copy: copy.start())
    return lambda: each(lambda copy: copy.wait())


def block_kernel(side, is_l, n0, *refs):
    refs = list(refs)

    def take(count):
        got = refs[:count]
        del refs[:count]
        return got

    final = n0 == 1
    (info,) = take(1)
    table_hbm = x_in = g_in = vmsg_in = None
    if is_l:
        near, table_hbm = take(2)
    own, rest, recv, coef = take(4)
    if side == 1:
        (vmsg_in,) = take(1)
    if is_l:
        x_in, g_in = take(2)
    msg_out = rest_out = vmsg_out = x_out = g = field_out = None
    if not final:
        msg_out, rest_out = take(2)
    if side == 0:
        (vmsg_out,) = take(1)
    if is_l:
        (g,) = take(1)
        if final:
            (field_out,) = take(1)
    else:
        (x_out,) = take(1)
    a, b, c, p, pieces, ybuf, weights = take(7)
    rbuf = table = sem = None
    if is_l:
        rbuf, table, sem = take(3)

    parts, _, width_y = a.shape[1:]
    rows = parts * SUB
    zones = coef.shape[0] // REACH
    is_last, src_layer, src_part, src_row, src_lane = (info[i] for i in range(STARTS))
    off = MID - SHIFT if side == 0 else MID - 2 * SHIFT
    lap = lap_maker(parts, width_y)

    if is_l:
        levels = tuple(range(n0, max(n0 - 3, -1), -1))
        await_table = fetch_table(table_hbm, table, info, zones, sem, levels)
        rbuf[...] = jnp.zeros(rbuf.shape, jnp.float32)
    put_weights(weights)

    def bring(msg, low):
        if low:
            a[MID - SHIFT : MID] = msg[0:SHIFT]
            p[MID - REACH : MID] = msg[SHIFT : SHIFT + REACH]
            b[MID - SHIFT - REACH : MID - REACH] = msg[SHIFT + REACH : MSG]
        else:
            a[MID : MID + SHIFT] = msg[0:SHIFT]
            p[MID : MID + REACH] = msg[SHIFT : SHIFT + REACH]
            b[MID + REACH : MID + REACH + SHIFT] = msg[SHIFT + REACH : MSG]

    if side == 0:
        bring(recv, True)
        a[MID : MID + SHIFT] = rest[0:SHIFT]
        p[MID : MID + REACH] = rest[SHIFT:REST]
        b[MID + REACH : MID + REACH + SHIFT] = own[SHIFT + REACH : MSG]

        @pl.when(is_last == 1)
        def _():
            zero = jnp.zeros((REACH,) + a.shape[1:], jnp.float32)
            a[MID + SHIFT : MID + 2 * SHIFT] = own[0:SHIFT]
            p[MID + SHIFT + REACH : MID + 2 * SHIFT] = own[SHIFT : SHIFT + REACH]
            for field in (a, b, c):
                field[MID + 2 * SHIFT : MID + 2 * SHIFT + REACH] = zero
    else:
        a[MID - SHIFT : MID] = rest[0:SHIFT]
        p[MID - REACH : MID] = rest[SHIFT:REST]
        b[MID - SHIFT - REACH : MID - REACH] = own[SHIFT + REACH : MSG]

        @pl.when(is_last == 1)
        def _():
            bring(vmsg_in, False)

        @pl.when(is_last == 0)
        def _():
            bring(recv, False)

    if is_l:
        await_table()

    def source(nxt, level, first, count):
        j = src_layer + off

        @pl.when((src_layer >= 0) & (j >= first) & (j < first + count))
        def _():
            lane = lax.broadcasted_iota(jnp.int32, (1, width_y), 1)
            spot = nxt[j, src_part, pl.ds(src_row, 1), :]
            gain = coef[src_layer, src_part, pl.ds(src_row, 1), :] * wave_of(n0 - level)
            nxt[j, src_part, pl.ds(src_row, 1), :] = spot - jnp.where(lane == src_lane, gain, 0.0)

    def advance(level, cur, nxt, first, count, x_base, outs, x_save=None):
        if is_l:
            zone = (first - off) // REACH
            inject(rbuf, info, near, table, levels, level, zone, zone + count // REACH)
        else:
            source(nxt, level, first, count)
        lane_pass(cur, first, count, weights, pieces, ybuf)

        def body(j):
            y_at = pl.multiple_of((j - first) * rows, rows)
            f, total = lap(cur, j, ybuf[pl.ds(y_at, rows), :].reshape(parts, SUB, width_y))
            if is_l:
                at = pl.multiple_of((j - off) * rows, rows)
                total = total + rbuf[pl.ds(at, rows), :].reshape(parts, SUB, width_y)
                rbuf[pl.ds(at, rows), :] = jnp.zeros((rows, width_y), jnp.float32)
            step = coef[j - off] * total
            new = (2.0 * f - nxt[j]) + step
            for ref, shift in outs:
                ref[j + shift] = new
            if is_l:
                g[j - off] = g[j - off] + x_in[j + (x_base - first)] * step
            else:
                x_out[j + (x_base - first)] = f

        layers_loop(first, count, body)

    if is_l:
        if side == 0:
            g[2 * SHIFT : 3 * SHIFT] = g_in[2 * SHIFT : 3 * SHIFT]
            g[0 : 2 * SHIFT] = g_in[0 : 2 * SHIFT]
        else:
            g[...] = g_in[...]

    advance(0, a, p, MID - REACH, SHIFT, 0, [(b, 0)])
    if side == 0:

        @pl.when(is_last == 1)
        def _():
            advance(0, a, p, MID + SHIFT + REACH, REACH, 32, [(b, 0)])

    advance(1, b, a, MID - SHIFT, 2 * SHIFT, 8, [(c, 0)])
    if side == 0:

        @pl.when(is_last == 1)
        def _():
            advance(1, b, a, MID + SHIFT, SHIFT, 36, [(c, 0)])
            vmsg_out[0:SHIFT] = c[MID + SHIFT : MID + 2 * SHIFT]
            vmsg_out[SHIFT : SHIFT + REACH] = b[MID + SHIFT : MID + SHIFT + REACH]
            vmsg_out[SHIFT + 2 * REACH : MSG] = jnp.zeros((REACH,) + a.shape[1:], jnp.float32)

    if final:
        if is_l:
            for layer in range(2 * SHIFT):
                store_tiled(field_out, layer, c[MID - SHIFT + layer])
        return
    if side == 0:
        msg_out[0:SHIFT] = c[MID - SHIFT : MID]
        msg_out[SHIFT : SHIFT + REACH] = b[MID - SHIFT : MID - REACH]
        rest_out[0:SHIFT] = c[MID : MID + SHIFT]
        rest_out[SHIFT:REST] = b[MID + REACH : MID + SHIFT]
    else:
        msg_out[0:SHIFT] = c[MID : MID + SHIFT]
        msg_out[SHIFT : SHIFT + REACH] = b[MID + REACH : MID + SHIFT]
        rest_out[0:SHIFT] = c[MID - SHIFT : MID]
        rest_out[SHIFT:REST] = b[MID - SHIFT : MID - REACH]

    advance(2, c, b, MID - REACH, SHIFT, 24, [(msg_out, SHIFT + REACH - (MID - REACH))])
    if side == 0:

        @pl.when(is_last == 1)
        def _():
            first = MID + SHIFT + REACH
            advance(2, c, b, first, REACH, 44, [(vmsg_out, SHIFT + REACH - first)])


def first_u_kernel(n0, info, prev, last, speed, speed_left, msg_out, rest_out, f0, coef, f1, pieces, ybuf, weights):
    depth, parts, _, width_y = f0.shape
    rows = parts * SUB
    src_layer, src_part, src_row, src_lane = (info[i] for i in range(1, STARTS))
    lap = lap_maker(parts, width_y)
    put_weights(weights)

    def bring(z):
        f0[z] = load_tiled(prev, z)
        f1[z] = load_tiled(last, z)
        coef[z + SHIFT] = (0.4 * load_tiled(speed, z)) ** 2 * (1.0 / SCALE)

    def bring_left(z):
        coef[z] = (0.4 * load_tiled(speed_left, z)) ** 2 * (1.0 / SCALE)

    layers_loop(0, depth, bring)
    layers_loop(0, SHIFT, bring_left)
    msg_out[0:SHIFT] = f0[depth - SHIFT : depth]
    msg_out[SHIFT : SHIFT + REACH] = f1[depth - REACH : depth]
    rest_out[0:SHIFT] = f0[0:SHIFT]
    rest_out[SHIFT:REST] = f1[0:REACH]
    lane_pass(f0, REACH, SHIFT, weights, pieces, ybuf)

    def body(j):
        y_at = pl.multiple_of((j - REACH) * rows, rows)
        f, total = lap(f0, j, ybuf[pl.ds(y_at, rows), :].reshape(parts, SUB, width_y))
        msg_out[j + SHIFT] = (2.0 * f - f1[j]) + coef[j + SHIFT] * total

    layers_loop(REACH, SHIFT, body)
    j = src_layer - SHIFT

    @pl.when((src_layer >= 0) & (j >= REACH) & (j < REACH + SHIFT))
    def _():
        lane = lax.broadcasted_iota(jnp.int32, (1, width_y), 1)
        spot = msg_out[j + SHIFT, src_part, pl.ds(src_row, 1), :]
        gain = coef[src_layer, src_part, pl.ds(src_row, 1), :] * wave_of(n0)
        msg_out[j + SHIFT, src_part, pl.ds(src_row, 1), :] = spot + jnp.where(lane == src_lane, gain, 0.0)


def first_l_kernel(n0, info, near, table_hbm, f0, coef, msg_out, rest_out, g, rbuf, table, sem):
    depth, parts, _, width_y = f0.shape
    rows = parts * SUB
    await_table = fetch_table(table_hbm, table, info, (depth + SHIFT) // REACH, sem, (n0,))
    rbuf[...] = jnp.zeros(rbuf.shape, jnp.float32)
    msg_out[0 : SHIFT + REACH] = jnp.zeros((SHIFT + REACH,) + f0.shape[1:], jnp.float32)
    rest_out[...] = jnp.zeros(rest_out.shape, jnp.float32)
    g[...] = jnp.zeros(g.shape, jnp.float32)
    await_table()
    zone = (SHIFT + REACH) // REACH
    inject(rbuf, info, near, table, (n0,), 0, zone, zone + SHIFT // REACH)

    def body(j):
        at = pl.multiple_of((j + SHIFT) * rows, rows)
        new = coef[j + SHIFT] * rbuf[pl.ds(at, rows), :].reshape(parts, SUB, width_y)
        msg_out[j + SHIFT] = new
        g[j + SHIFT] = f0[j] * new

    layers_loop(REACH, SHIFT, body)


def last_kernel(g, g_right, gate, out):
    depth = out.shape[0]

    def one(z):
        store_tiled(out, z, load_tiled(gate, 0) * g[z + SHIFT])

    def shared(z):
        store_tiled(out, z, load_tiled(gate, 0) * (g[z + SHIFT] + g_right[z - SHIFT]))

    layers_loop(0, SHIFT, one)
    layers_loop(SHIFT, depth - SHIFT, shared)


def sum_shots(g):
    shots = lax.axis_size("shot")
    if shots != 2:
        return lax.psum_scatter(g, "shot", scatter_dimension=1, tiled=True)
    block = g.shape[1] // 2
    low, high = g[:, :block], g[:, block:]
    first = lax.axis_index("shot") == 0
    other = lax.ppermute(jnp.where(first, high, low), "shot", [(0, 1), (1, 0)])
    return jnp.where(first, low, high) + other


def snake_of(slabs):
    row = slabs // 4
    if slabs % 8:
        return list(range(slabs))
    order = []
    for i in range(slabs):
        z, (chip, core) = i // row, divmod(i % row, 2)
        order.append(z * row + 2 * (row // 2 - 1 - chip if z % 2 else chip) + core)
    return order


def on_device(fwd_last, fwd_prev, velocity, aperture, rec_index, src_index, residual):
    _, depth, width_x, width_y = fwd_last.shape
    parts = width_x // SUB
    total_steps, receivers = residual.shape[1:]
    plane = width_x * width_y
    slabs = lax.axis_size("slab")
    f32 = jnp.float32
    place = snake_of(slabs)
    slab = jnp.asarray(place, jnp.int32)[lax.axis_index("slab")]
    up = [(place[i], place[i + 1]) for i in range(slabs - 1)]
    down = [(place[i + 1], place[i]) for i in range(slabs - 1)]
    swap = [(i, place[i]) for i in range(slabs)]
    home = velocity
    if place != list(range(slabs)):
        velocity = lax.ppermute(velocity, "slab", swap)
        fwd_prev = lax.ppermute(fwd_prev, "slab", swap)
        fwd_last = lax.ppermute(fwd_last, "slab", swap)
    speed_left = lax.ppermute(home[depth - SHIFT :], "slab", [(i, place[i + 1]) for i in range(slabs - 1)])

    base = (slab * depth - SHIFT) * plane
    window = (depth + SHIFT) * plane
    local = rec_index[0] - base
    far = jnp.int32(2**30)
    keys = jnp.where((local >= 0) & (local < window), local, far)
    keys, ids = lax.sort((keys, lax.iota(jnp.int32, receivers)), num_keys=1, is_stable=False)

    def place_of(cell):
        layer = cell // plane
        x = (cell // width_y) % width_x
        return layer, x % parts, x // parts, cell % width_y

    layer, part, row, lane = place_of(keys)
    rows_of = (layer * parts + part) * SUB + row
    zones = (depth + SHIFT) // REACH
    edges = jnp.arange(zones + 1, dtype=jnp.int32) * (REACH * plane)
    starts = jnp.sum((keys[None, :] < edges[:, None]).astype(jnp.int32), axis=1)

    src = src_index[0] - base
    src_in = (src >= 0) & (src < window)
    s_layer, s_part, s_row, s_lane = place_of(jnp.where(src_in, src, 0))
    s_layer = jnp.where(src_in, s_layer, -1)
    is_last = (slab == slabs - 1).astype(jnp.int32)
    src_info = jnp.stack([is_last, s_layer, s_part, s_row, s_lane])
    info = jnp.concatenate([src_info, starts, jnp.zeros((ROWS - STARTS - zones - 1,), jnp.int32), rows_of])
    last_step = total_steps - 1

    smem = pl.BlockSpec(memory_space=pltpu.SMEM)
    vmem = pl.BlockSpec(memory_space=pltpu.VMEM)
    anym = pl.BlockSpec(memory_space=pl.ANY)

    def fields(layers):
        return jax.ShapeDtypeStruct((layers, parts, SUB, width_y), f32)

    params = pltpu.CompilerParams(vmem_limit_bytes=VMEM_BYTES)
    l_scratch = [
        pltpu.VMEM(((depth + SHIFT) * parts * SUB, width_y), f32),
        pltpu.VMEM((3, receivers, width_y), f32),
        pltpu.SemaphoreType.DMA((3, receivers // CHUNK)),
    ]

    def lane_scratch(layers):
        rows = layers * parts * SUB
        return [
            pltpu.VMEM((rows, PIECES * width_y), jnp.bfloat16),
            pltpu.VMEM((rows, width_y), f32),
            pltpu.VMEM((PIECES * width_y, width_y), jnp.bfloat16),
        ]

    block_scratch = [pltpu.VMEM((SPAN, parts, SUB, width_y), f32)] * 4 + lane_scratch(2 * SHIFT)

    def cost(layers):
        return pl.CostEstimate(
            flops=50 * layers * plane, bytes_accessed=24 * layers * plane, transcendentals=0
        )

    um, ur, f0, coef = pl.pallas_call(
        functools.partial(first_u_kernel, last_step),
        out_shape=(fields(MSG), fields(REST), fields(depth), fields(depth + SHIFT)),
        in_specs=[smem] + [vmem] * 4,
        out_specs=[vmem] * 4,
        scratch_shapes=[pltpu.VMEM((depth, parts, SUB, width_y), f32)] + lane_scratch(SHIFT),
        compiler_params=params,
        cost_estimate=cost(SHIFT),
        name="first_u",
    )(src_info, fwd_prev[0], fwd_last[0], velocity, speed_left)
    u_got = lax.ppermute(um, "slab", up)

    near, table = pl.pallas_call(
        functools.partial(table_kernel, zones),
        out_shape=(
            jax.ShapeDtypeStruct((total_steps, CHUNK, width_y), f32),
            jax.ShapeDtypeStruct((total_steps, receivers, width_y), f32),
        ),
        in_specs=[smem] + [vmem] * 5,
        out_specs=(vmem, anym),
        scratch_shapes=[
            pltpu.VMEM((receivers // CHUNK, PIECES, total_steps, CHUNK), f32),
            pltpu.VMEM((PIECES * total_steps, receivers), jnp.bfloat16),
            pltpu.VMEM((CHUNK, CHUNK), jnp.bfloat16),
            pltpu.VMEM((total_steps, CHUNK, width_y), f32),
            pltpu.SemaphoreType.DMA(()),
        ],
        compiler_params=params,
        cost_estimate=cost(SHIFT),
        name="rec_table",
    )(
        info,
        ids.reshape(receivers // CHUNK, CHUNK),
        rows_of.reshape(receivers // CHUNK, CHUNK),
        rows_of[:, None],
        lane[:, None],
        residual[0],
    )
    lm, lr, g = pl.pallas_call(
        functools.partial(first_l_kernel, last_step),
        out_shape=(fields(MSG), fields(REST), fields(depth + SHIFT)),
        in_specs=[smem, vmem, anym, vmem, vmem],
        out_specs=(vmem, vmem, vmem),
        scratch_shapes=l_scratch,
        compiler_params=params,
        cost_estimate=cost(SHIFT),
        name="first_l",
    )(info, near, table, f0, coef)
    l_got = lax.ppermute(lm, "slab", up)
    def u_block(side, n0, own, rest, recv, *vmsg):
        outs = [fields(MSG), fields(REST)] if n0 > 1 else []
        if side == 0:
            outs.append(fields(MSG))
        outs.append(fields(48))
        return pl.pallas_call(
            functools.partial(block_kernel, side, False, n0),
            out_shape=outs,
            in_specs=[smem] + [vmem] * (4 + len(vmsg)),
            out_specs=[vmem] * len(outs),
            scratch_shapes=block_scratch,
            compiler_params=params,
            cost_estimate=cost(2 * depth),
            name=f"u_block{side}",
        )(info, own, rest, recv, coef, *vmsg)

    def l_block(side, n0, own, rest, recv, vmsg, x, g):
        outs = [fields(MSG), fields(REST)] if n0 > 1 else []
        if side == 0:
            outs.append(fields(MSG))
        outs.append(fields(depth + SHIFT))
        if n0 == 1:
            outs.append(jax.ShapeDtypeStruct((depth, width_x, width_y), f32))
        return pl.pallas_call(
            functools.partial(block_kernel, side, True, n0),
            out_shape=outs,
            in_specs=[smem, vmem, anym] + [vmem] * (6 + len(vmsg)),
            out_specs=[vmem] * len(outs),
            scratch_shapes=block_scratch + l_scratch,
            compiler_params=params,
            cost_estimate=cost(2 * depth),
            name=f"l_block{side}",
        )(info, near, table, own, rest, recv, coef, *vmsg, x, g)

    for n0 in range(last_step, 0, -4):
        um, ur, uv, x = u_block(0, n0, um, ur, u_got)
        u_got = lax.ppermute(um, "slab", down)
        lm, lr, lv, g = l_block(0, n0, lm, lr, l_got, (), x, g)
        l_got = lax.ppermute(lm, "slab", down)
        g_half = g
        if n0 > 3:
            um, ur, x = u_block(1, n0 - 2, um, ur, u_got, uv)
            u_got = lax.ppermute(um, "slab", up)
            lm, lr, g = l_block(1, n0 - 2, lm, lr, l_got, (lv,), x, g)
            l_got = lax.ppermute(lm, "slab", up)
        else:
            (x,) = u_block(1, n0 - 2, um, ur, u_got, uv)
            g, adjoint_field = l_block(1, n0 - 2, lm, lr, l_got, (lv,), x, g)

    g_right = lax.ppermute(g_half[:SHIFT], "slab", down)
    terms = pl.pallas_call(
        last_kernel,
        out_shape=jax.ShapeDtypeStruct((depth, width_x, width_y), f32),
        in_specs=[vmem] * 3,
        out_specs=vmem,
        compiler_params=params,
        cost_estimate=cost(2),
        name="last_terms",
    )(g, g_right, aperture.astype(f32))
    summed = sum_shots(terms)
    if place != list(range(slabs)):
        adjoint_field = lax.ppermute(adjoint_field, "slab", swap)
        summed = lax.ppermute(summed, "slab", swap)
    block = width_x // lax.axis_size("shot")
    speed = lax.dynamic_slice_in_dim(home, lax.axis_index("shot") * block, block, 1)
    return ((-2.0 / speed) * summed, adjoint_field[None])


def solution(mesh):
    in_specs = (
        P("shot", "slab", None, None),
        P("shot", "slab", None, None),
        P("slab", None, None),
        P("shot", None, None),
        P("shot", None),
        P("shot"),
        P("shot", None, None),
    )
    out_specs = (P("slab", "shot", None), P("shot", "slab", None, None))
    return jax.shard_map(on_device, mesh=mesh, in_specs=in_specs, out_specs=out_specs, check_vma=False)
```

```python
import functools

import jax
import jax.numpy as jnp
import numpy as np
from jax import lax
from jax.experimental import pallas as pl
from jax.experimental.pallas import tpu as pltpu
from jax.sharding import PartitionSpec as P

SCALE = 5040.0
WHOLE = (-14350.0, 8064.0, -1008.0, 128.0, -9.0)
REACH = 4
SHIFT = 8
VMEM_BYTES = 14 * 1024 * 1024
MORE_BYTES = 24 * 1024 * 1024
SUB = 8
PIECES = 3
CHUNK = 256

MSG = 2 * SHIFT + REACH
REST = SHIFT + REACH
SPAN = 32
MID = 12


def wave_of(step):
    arg = (np.pi * 0.06 * (step - 10.0)) ** 2
    return float(np.float32(SCALE * 10.0 * (1.0 - 2.0 * arg) * np.exp(-arg)))


def load_tiled(field, layer):
    parts = field.shape[1] // SUB
    return jnp.stack([field[layer, pl.ds(m, SUB, stride=parts), :] for m in range(parts)])


def store_tiled(field, layer, value, first=0, count=SUB):
    parts = value.shape[0]
    for m in range(parts):
        field[layer, pl.ds(m, count, stride=parts), :] = value[m, first : first + count]


def split3(f):
    hi = f.astype(jnp.bfloat16)
    left = f - hi.astype(jnp.float32)
    mid = left.astype(jnp.bfloat16)
    return hi, mid, (left - mid.astype(jnp.float32)).astype(jnp.bfloat16)


def put_weights(weights):
    width_y = weights.shape[1]
    square = (width_y, width_y)
    away = jnp.abs(lax.broadcasted_iota(jnp.int32, square, 0) - lax.broadcasted_iota(jnp.int32, square, 1))
    once = jnp.zeros(square, jnp.float32)
    for k in range(1, 5):
        once = jnp.where(away == k, WHOLE[k], once)
    for i in range(PIECES):
        weights[i * width_y : (i + 1) * width_y, :] = once.astype(jnp.bfloat16)


def lane_pass(cur, first, count, weights, pieces, ybuf):
    parts, _, width_y = cur.shape[1:]
    rows = parts * SUB

    def one(q):
        at = pl.multiple_of(q * rows, rows)
        for i, piece in enumerate(split3(cur[first + q].reshape(rows, width_y))):
            pieces[pl.ds(at, rows), i * width_y : (i + 1) * width_y] = piece

    layers_loop(0, count, one)
    for q in range(0, count, SHIFT):
        block = slice(q * rows, min(q + SHIFT, count) * rows)
        ybuf[block, :] = jnp.dot(pieces[block, :], weights[...], preferred_element_type=jnp.float32)


def lap_maker(parts, width_y):
    row = lax.broadcasted_iota(jnp.int32, (1, SUB, width_y), 1)

    def lap(ref, j, along):
        f = ref[j]
        after = jnp.where(row == SUB - 1, 0.0, pltpu.roll(f[:REACH], SUB - 1, 1))
        before = jnp.where(row == 0, 0.0, pltpu.roll(f[parts - REACH :], 1, 1))
        wide = jnp.concatenate([before, f, after], axis=0)
        total = along + (3.0 * WHOLE[0]) * f
        for k in range(1, 5):
            pair = (ref[j + k] + ref[j - k]) + (
                wide[REACH + k : REACH + k + parts] + wide[REACH - k : REACH - k + parts]
            )
            total = total + WHOLE[k] * pair
        return f, total

    return lap


def layers_loop(first, count, body):
    def one(q, carry):
        body(first + q)
        return carry

    lax.fori_loop(0, count, one, 0, unroll=2)


STARTS = 5
ROWS = 16


def inject(rbuf, info, near, table_hbm, table, sem, step, first, last):
    low, high = info[STARTS + first], info[STARTS + last]

    def store(low, high, row_of):
        def eight(i, carry):
            for q in range(8):
                r = jnp.minimum(low + i * 8 + q, high - 1)
                rbuf[pl.ds(info[ROWS + r], 1), :] = row_of(r)
            return carry

        lax.fori_loop(0, (high - low + 7) // 8, eight, 0)

    split = jnp.clip(CHUNK, low, high)
    store(low, split, lambda r: near[step, pl.ds(r, 1), :])

    @pl.when(high > split)
    def _():
        fetch = pltpu.make_async_copy(table_hbm.at[step], table, sem)
        fetch.start()
        fetch.wait()
        store(split, high, lambda r: table[pl.ds(r, 1), :])


def chunks_of(info, zones):
    return jnp.maximum((info[STARTS + zones] + CHUNK - 1) // CHUNK, 1)


def table_kernel(zones, info, ids, rows_l, rows_s, lanes_s, res, near, out, res_cut, pieces, same, part, sem):
    steps, receivers = res.shape
    width_y = part.shape[2]
    chunks = chunks_of(info, zones)
    for i, piece in enumerate(split3(res[...])):
        pieces[i * steps : (i + 1) * steps, :] = piece

    def column(c, carry):
        who = lax.broadcasted_iota(jnp.int32, (receivers, CHUNK), 0) == ids[pl.ds(c, 1), :]
        moved = jnp.dot(
            pieces[...], jnp.where(who, 1.0, 0.0).astype(jnp.bfloat16), preferred_element_type=jnp.float32
        )
        total = SCALE * ((moved[:steps] + moved[steps : 2 * steps]) + moved[2 * steps :])
        for i, piece in enumerate(split3(total)):
            res_cut[c, i] = piece.astype(jnp.float32)
        return carry

    lax.fori_loop(0, chunks, column, 0)

    def to_chunk(c, carry):
        mine = rows_s[pl.ds(pl.multiple_of(c * CHUNK, CHUNK), CHUNK), :]

        def from_chunk(d, carry):
            same[...] = jnp.where(mine == rows_l[pl.ds(d, 1), :], 1.0, 0.0).astype(jnp.bfloat16)
            at = pl.multiple_of(d * CHUNK, CHUNK)
            lane = lax.broadcasted_iota(jnp.int32, (CHUNK, width_y), 1)
            spot = jnp.where(lane == lanes_s[pl.ds(at, CHUNK), :], 1.0, 0.0).astype(jnp.bfloat16)
            spots = jnp.concatenate([spot] * PIECES, axis=0)

            def one(n, carry):
                mixed = []
                for i in range(PIECES):
                    row = jnp.broadcast_to(res_cut[d, i, pl.ds(n, 1), :], (16, CHUNK)).astype(jnp.bfloat16)
                    mixed.append((same[...].reshape(CHUNK // 16, 16, CHUNK) * row[None]).reshape(CHUNK, CHUNK))
                total = jnp.dot(
                    jnp.concatenate(mixed, axis=1), spots, preferred_element_type=jnp.float32
                )
                part[n] = total + jnp.where(d > 0, part[n], 0.0)
                return carry

            return lax.fori_loop(0, steps, one, carry, unroll=4)

        lax.fori_loop(0, chunks, from_chunk, 0)
        return carry

    def store_chunk(c, carry):
        to_chunk(c, 0)
        at = pl.multiple_of(c * CHUNK, CHUNK)
        write = pltpu.make_async_copy(part, out.at[:, pl.ds(at, CHUNK), :], sem)
        write.start()
        write.wait()
        return carry

    to_chunk(0, 0)
    near[...] = part[...]
    lax.fori_loop(1, chunks, store_chunk, 0)


def block_kernel(side, is_l, n0, opening, *refs):
    refs = list(refs)

    def take(count):
        got = refs[:count]
        del refs[:count]
        return got

    final = n0 == 1
    (info,) = take(1)
    table_hbm = x_in = g_in = vmsg_in = None
    if is_l:
        near, table_hbm = take(2)
    own, rest, recv, coef, weights = take(5)
    if side == 1:
        (vmsg_in,) = take(1)
    if is_l:
        (x_in,) = take(1)
        if opening:
            u_msg, u_rest = take(2)
        else:
            (g_in,) = take(1)
    msg_out = rest_out = vmsg_out = x_out = g = field_out = g_left = None
    if not final:
        msg_out, rest_out = take(2)
    if side == 0:
        (vmsg_out,) = take(1)
    if is_l:
        (g,) = take(1)
        if final:
            (field_out,) = take(1)
        if n0 == 3:
            (g_left,) = take(1)
    else:
        (x_out,) = take(1)
    a, b, c, p, pieces, ybuf = take(6)
    rbuf = table = sem = None
    if is_l:
        rbuf, table, sem = take(3)

    parts, _, width_y = a.shape[1:]
    rows = parts * SUB
    zones = coef.shape[0] // REACH
    is_last, src_layer, src_part, src_row, src_lane = (info[i] for i in range(STARTS))
    off = MID - SHIFT if side == 0 else MID - 2 * SHIFT
    lap = lap_maker(parts, width_y)

    if is_l:
        rbuf[...] = jnp.zeros(rbuf.shape, jnp.float32)

    def bring(msg, low):
        if low:
            a[MID - SHIFT : MID] = msg[0:SHIFT]
            p[MID - REACH : MID] = msg[SHIFT : SHIFT + REACH]
            b[MID - SHIFT - REACH : MID - REACH] = msg[SHIFT + REACH : MSG]
        else:
            a[MID : MID + SHIFT] = msg[0:SHIFT]
            p[MID : MID + REACH] = msg[SHIFT : SHIFT + REACH]
            b[MID + REACH : MID + REACH + SHIFT] = msg[SHIFT + REACH : MSG]

    if side == 0:
        bring(recv, True)
        a[MID : MID + SHIFT] = rest[0:SHIFT]
        p[MID : MID + REACH] = rest[SHIFT:REST]
        b[MID + REACH : MID + REACH + SHIFT] = own[SHIFT + REACH : MSG]

        @pl.when(is_last == 1)
        def _():
            zero = jnp.zeros((REACH,) + a.shape[1:], jnp.float32)
            a[MID + SHIFT : MID + 2 * SHIFT] = own[0:SHIFT]
            p[MID + SHIFT + REACH : MID + 2 * SHIFT] = own[SHIFT : SHIFT + REACH]
            for field in (a, b, c):
                field[MID + 2 * SHIFT : MID + 2 * SHIFT + REACH] = zero
    else:
        a[MID - SHIFT : MID] = rest[0:SHIFT]
        p[MID - REACH : MID] = rest[SHIFT:REST]
        b[MID - SHIFT - REACH : MID - REACH] = own[SHIFT + REACH : MSG]

        @pl.when(is_last == 1)
        def _():
            bring(vmsg_in, False)

        @pl.when(is_last == 0)
        def _():
            bring(recv, False)

    def source(nxt, level, first, count):
        j = src_layer + off

        @pl.when((src_layer >= 0) & (j >= first) & (j < first + count))
        def _():
            lane = lax.broadcasted_iota(jnp.int32, (1, width_y), 1)
            spot = nxt[j, src_part, pl.ds(src_row, 1), :]
            gain = coef[src_layer, src_part, pl.ds(src_row, 1), :] * wave_of(n0 - level)
            nxt[j, src_part, pl.ds(src_row, 1), :] = spot - jnp.where(lane == src_lane, gain, 0.0)

    def advance(level, cur, nxt, first, count, x_base, outs, x_save=None):
        if is_l:
            zone = (first - off) // REACH
            inject(rbuf, info, near, table_hbm, table, sem, n0 - level, zone, zone + count // REACH)
        else:
            source(nxt, level, first, count)
        lane_pass(cur, first, count, weights, pieces, ybuf)

        def body(j):
            y_at = pl.multiple_of((j - first) * rows, rows)
            f, total = lap(cur, j, ybuf[pl.ds(y_at, rows), :].reshape(parts, SUB, width_y))
            if is_l:
                at = pl.multiple_of((j - off) * rows, rows)
                total = total + rbuf[pl.ds(at, rows), :].reshape(parts, SUB, width_y)
                rbuf[pl.ds(at, rows), :] = jnp.zeros((rows, width_y), jnp.float32)
            step = coef[j - off] * total
            new = (2.0 * f - nxt[j]) + step
            for ref, shift in outs:
                ref[j + shift] = new
            if is_l:
                g[j - off] = g[j - off] + x_in[j + (x_base - first)] * step
            else:
                x_out[j + (x_base - first)] = f

        layers_loop(first, count, body)

    if is_l and opening:
        g[...] = jnp.zeros(g.shape, jnp.float32)
        for z in range(REACH, REACH + SHIFT):
            was = u_rest[z] if z < SHIFT else u_msg[z - SHIFT]
            g[z + SHIFT] = was * own[z + SHIFT]
    elif is_l:
        g[...] = g_in[...]

    advance(0, a, p, MID - REACH, SHIFT, 0, [(b, 0)])
    if side == 0:

        @pl.when(is_last == 1)
        def _():
            advance(0, a, p, MID + SHIFT + REACH, REACH, 32, [(b, 0)])

    advance(1, b, a, MID - SHIFT, 2 * SHIFT, 8, [(c, 0)])
    if side == 0:

        @pl.when(is_last == 1)
        def _():
            advance(1, b, a, MID + SHIFT, SHIFT, 36, [(c, 0)])
            vmsg_out[0:SHIFT] = c[MID + SHIFT : MID + 2 * SHIFT]
            vmsg_out[SHIFT : SHIFT + REACH] = b[MID + SHIFT : MID + SHIFT + REACH]
            vmsg_out[SHIFT + 2 * REACH : MSG] = jnp.zeros((REACH,) + a.shape[1:], jnp.float32)

    if final:
        if is_l:
            for layer in range(2 * SHIFT):
                store_tiled(field_out, layer, c[MID - SHIFT + layer])
        return
    if side == 0:
        msg_out[0:SHIFT] = c[MID - SHIFT : MID]
        msg_out[SHIFT : SHIFT + REACH] = b[MID - SHIFT : MID - REACH]
        rest_out[0:SHIFT] = c[MID : MID + SHIFT]
        rest_out[SHIFT:REST] = b[MID + REACH : MID + SHIFT]
    else:
        msg_out[0:SHIFT] = c[MID : MID + SHIFT]
        msg_out[SHIFT : SHIFT + REACH] = b[MID + REACH : MID + SHIFT]
        rest_out[0:SHIFT] = c[MID - SHIFT : MID]
        rest_out[SHIFT:REST] = b[MID - SHIFT : MID - REACH]

    advance(2, c, b, MID - REACH, SHIFT, 24, [(msg_out, SHIFT + REACH - (MID - REACH))])
    if side == 0:

        @pl.when(is_last == 1)
        def _():
            first = MID + SHIFT + REACH
            advance(2, c, b, first, REACH, 44, [(vmsg_out, SHIFT + REACH - first)])

    if g_left is not None:
        g_left[...] = g[0:SHIFT]


def first_coef_kernel(speed, speed_left, coef, weights):
    put_weights(weights)

    def own(z):
        coef[z + SHIFT] = (0.4 * load_tiled(speed, z)) ** 2 * (1.0 / SCALE)

    def left(z):
        coef[z] = (0.4 * load_tiled(speed_left, z)) ** 2 * (1.0 / SCALE)

    layers_loop(0, speed.shape[0], own)
    layers_loop(0, SHIFT, left)


def first_u_kernel(n0, info, prev, last, coef, weights, msg_out, rest_out, f0, f1, pieces, ybuf):
    depth, parts, _, width_y = f0.shape
    rows = parts * SUB
    src_layer, src_part, src_row, src_lane = (info[i] for i in range(1, STARTS))
    lap = lap_maker(parts, width_y)

    def bring(z):
        f0[z] = load_tiled(prev, z)
        f1[z] = load_tiled(last, z)

    layers_loop(0, depth, bring)
    msg_out[0:SHIFT] = f0[depth - SHIFT : depth]
    msg_out[SHIFT : SHIFT + REACH] = f1[depth - REACH : depth]
    rest_out[0:SHIFT] = f0[0:SHIFT]
    rest_out[SHIFT:REST] = f1[0:REACH]
    lane_pass(f0, REACH, SHIFT, weights, pieces, ybuf)

    def body(j):
        y_at = pl.multiple_of((j - REACH) * rows, rows)
        f, total = lap(f0, j, ybuf[pl.ds(y_at, rows), :].reshape(parts, SUB, width_y))
        msg_out[j + SHIFT] = (2.0 * f - f1[j]) + coef[j + SHIFT] * total

    layers_loop(REACH, SHIFT, body)
    j = src_layer - SHIFT

    @pl.when((src_layer >= 0) & (j >= REACH) & (j < REACH + SHIFT))
    def _():
        lane = lax.broadcasted_iota(jnp.int32, (1, width_y), 1)
        spot = msg_out[j + SHIFT, src_part, pl.ds(src_row, 1), :]
        gain = coef[src_layer, src_part, pl.ds(src_row, 1), :] * wave_of(n0)
        msg_out[j + SHIFT, src_part, pl.ds(src_row, 1), :] = spot + jnp.where(lane == src_lane, gain, 0.0)


def first_l_kernel(n0, info, near, table_hbm, coef, msg_out, rest_out, rbuf, table, sem):
    parts, _, width_y = coef.shape[1:]
    rows = parts * SUB
    rbuf[...] = jnp.zeros(rbuf.shape, jnp.float32)
    msg_out[0 : SHIFT + REACH] = jnp.zeros((SHIFT + REACH,) + coef.shape[1:], jnp.float32)
    rest_out[...] = jnp.zeros(rest_out.shape, jnp.float32)
    zone = (SHIFT + REACH) // REACH
    inject(rbuf, info, near, table_hbm, table, sem, n0, zone, zone + SHIFT // REACH)

    def body(j):
        at = pl.multiple_of((j + SHIFT) * rows, rows)
        msg_out[j + SHIFT] = coef[j + SHIFT] * rbuf[pl.ds(at, rows), :].reshape(parts, SUB, width_y)

    layers_loop(REACH, SHIFT, body)


def last_kernel(g, g_right, gate, out):
    depth = out.shape[0]

    def one(z):
        store_tiled(out, z, load_tiled(gate, 0).astype(jnp.float32) * g[z + SHIFT])

    def shared(z):
        store_tiled(out, z, load_tiled(gate, 0).astype(jnp.float32) * (g[z + SHIFT] + g_right[z - SHIFT]))

    layers_loop(0, SHIFT, one)
    layers_loop(SHIFT, depth - SHIFT, shared)


def sum_shots(g):
    shots = lax.axis_size("shot")
    if shots != 2:
        return lax.psum_scatter(g, "shot", scatter_dimension=1, tiled=True)
    block = g.shape[1] // 2
    low, high = g[:, :block], g[:, block:]
    first = lax.axis_index("shot") == 0
    other = lax.ppermute(jnp.where(first, high, low), "shot", [(0, 1), (1, 0)])
    return jnp.where(first, low, high) + other


def snake_of(slabs):
    row = slabs // 4
    if slabs % 8:
        return list(range(slabs))
    order = []
    for i in range(slabs):
        z, (chip, core) = i // row, divmod(i % row, 2)
        order.append(z * row + 2 * (row // 2 - 1 - chip if z % 2 else chip) + core)
    return order


def on_device(fwd_last, fwd_prev, velocity, aperture, rec_index, src_index, residual):
    _, depth, width_x, width_y = fwd_last.shape
    parts = width_x // SUB
    total_steps, receivers = residual.shape[1:]
    plane = width_x * width_y
    slabs = lax.axis_size("slab")
    f32 = jnp.float32
    place = snake_of(slabs)
    slab = jnp.asarray(place, jnp.int32)[lax.axis_index("slab")]
    up = [(place[i], place[i + 1]) for i in range(slabs - 1)]
    down = [(place[i + 1], place[i]) for i in range(slabs - 1)]
    swap = [(i, place[i]) for i in range(slabs)]
    home = velocity
    if place != list(range(slabs)):
        velocity = lax.ppermute(velocity, "slab", swap)
    speed_left = lax.ppermute(home[depth - SHIFT :], "slab", [(i, place[i + 1]) for i in range(slabs - 1)])
    if place != list(range(slabs)):
        fwd_prev = lax.ppermute(fwd_prev, "slab", swap)
        fwd_last = lax.ppermute(fwd_last, "slab", swap)

    base = (slab * depth - SHIFT) * plane
    window = (depth + SHIFT) * plane
    local = rec_index[0] - base
    far = jnp.int32(2**30)
    keys = jnp.where((local >= 0) & (local < window), local, far)
    keys, ids = lax.sort((keys, lax.iota(jnp.int32, receivers)), num_keys=1, is_stable=False)

    def place_of(cell):
        layer = cell // plane
        x = (cell // width_y) % width_x
        return layer, x % parts, x // parts, cell % width_y

    layer, part, row, lane = place_of(keys)
    rows_of = (layer * parts + part) * SUB + row
    zones = (depth + SHIFT) // REACH
    edges = jnp.arange(zones + 1, dtype=jnp.int32) * (REACH * plane)
    starts = jnp.sum((keys[None, :] < edges[:, None]).astype(jnp.int32), axis=1)

    src = src_index[0] - base
    src_in = (src >= 0) & (src < window)
    s_layer, s_part, s_row, s_lane = place_of(jnp.where(src_in, src, 0))
    s_layer = jnp.where(src_in, s_layer, -1)
    is_last = (slab == slabs - 1).astype(jnp.int32)
    info = jnp.concatenate([jnp.stack([is_last, s_layer, s_part, s_row, s_lane]), starts, jnp.zeros((ROWS - STARTS - zones - 1,), jnp.int32), rows_of])
    last_step = total_steps - 1

    smem = pl.BlockSpec(memory_space=pltpu.SMEM)
    vmem = pl.BlockSpec(memory_space=pltpu.VMEM)
    anym = pl.BlockSpec(memory_space=pl.ANY)

    def fields(layers):
        return jax.ShapeDtypeStruct((layers, parts, SUB, width_y), f32)

    params = pltpu.CompilerParams(vmem_limit_bytes=VMEM_BYTES)
    once = pltpu.CompilerParams(vmem_limit_bytes=MORE_BYTES)
    l_scratch = [
        pltpu.VMEM(((depth + SHIFT) * parts * SUB, width_y), f32),
        pltpu.VMEM((receivers, width_y), f32),
        pltpu.SemaphoreType.DMA(()),
    ]

    def lane_scratch(layers):
        rows = layers * parts * SUB
        return [
            pltpu.VMEM((rows, PIECES * width_y), jnp.bfloat16),
            pltpu.VMEM((rows, width_y), f32),
        ]

    block_scratch = [pltpu.VMEM((SPAN, parts, SUB, width_y), f32)] * 4 + lane_scratch(2 * SHIFT)

    def cost(layers):
        return pl.CostEstimate(
            flops=50 * layers * plane, bytes_accessed=24 * layers * plane, transcendentals=0
        )

    near, table = pl.pallas_call(
        functools.partial(table_kernel, zones),
        out_shape=(
            jax.ShapeDtypeStruct((total_steps, CHUNK, width_y), f32),
            jax.ShapeDtypeStruct((total_steps, receivers, width_y), f32),
        ),
        in_specs=[smem] + [vmem] * 5,
        out_specs=(vmem, anym),
        scratch_shapes=[
            pltpu.VMEM((receivers // CHUNK, PIECES, total_steps, CHUNK), f32),
            pltpu.VMEM((PIECES * total_steps, receivers), jnp.bfloat16),
            pltpu.VMEM((CHUNK, CHUNK), jnp.bfloat16),
            pltpu.VMEM((total_steps, CHUNK, width_y), f32),
            pltpu.SemaphoreType.DMA(()),
        ],
        compiler_params=once,
        cost_estimate=cost(SHIFT),
        name="rec_table",
    )(
        info,
        ids.reshape(receivers // CHUNK, CHUNK),
        rows_of.reshape(receivers // CHUNK, CHUNK),
        rows_of[:, None],
        lane[:, None],
        residual[0],
    )
    coef, weights = pl.pallas_call(
        first_coef_kernel,
        out_shape=(
            fields(depth + SHIFT),
            jax.ShapeDtypeStruct((PIECES * width_y, width_y), jnp.bfloat16),
        ),
        in_specs=[vmem] * 2,
        out_specs=[vmem] * 2,
        compiler_params=once,
        cost_estimate=cost(2),
        name="first_coef",
    )(velocity, speed_left)
    lm, lr = pl.pallas_call(
        functools.partial(first_l_kernel, last_step),
        out_shape=(fields(MSG), fields(REST)),
        in_specs=[smem, vmem, anym, vmem],
        out_specs=(vmem, vmem),
        scratch_shapes=l_scratch,
        compiler_params=once,
        cost_estimate=cost(2),
        name="first_l",
    )(info, near, table, coef)
    l_got = lax.ppermute(lm, "slab", up)

    fwd_prev, fwd_last, _ = lax.optimization_barrier((fwd_prev, fwd_last, lr))
    um, ur = pl.pallas_call(
        functools.partial(first_u_kernel, last_step),
        out_shape=(fields(MSG), fields(REST)),
        in_specs=[smem] + [vmem] * 4,
        out_specs=[vmem] * 2,
        scratch_shapes=[pltpu.VMEM((depth, parts, SUB, width_y), f32)] * 2 + lane_scratch(SHIFT),
        compiler_params=once,
        cost_estimate=cost(SHIFT),
        name="first_u",
    )(info, fwd_prev[0], fwd_last[0], coef, weights)
    u_got = lax.ppermute(um, "slab", up)
    opening = (um, ur)

    def u_block(side, n0, own, rest, recv, *vmsg):
        outs = [fields(MSG), fields(REST)] if n0 > 1 else []
        if side == 0:
            outs.append(fields(MSG))
        outs.append(fields(48))
        return pl.pallas_call(
            functools.partial(block_kernel, side, False, n0, False),
            out_shape=outs,
            in_specs=[smem] + [vmem] * (5 + len(vmsg)),
            out_specs=[vmem] * len(outs),
            scratch_shapes=block_scratch,
            compiler_params=params,
            cost_estimate=cost(2 * depth),
            name=f"u_block{side}",
        )(info, own, rest, recv, coef, weights, *vmsg)

    def l_block(side, n0, own, rest, recv, vmsg, x, g):
        outs = [fields(MSG), fields(REST)] if n0 > 1 else []
        if side == 0:
            outs.append(fields(MSG))
        outs.append(fields(depth + SHIFT))
        if n0 == 1:
            outs.append(jax.ShapeDtypeStruct((depth, width_x, width_y), f32))
        if n0 == 3:
            outs.append(fields(SHIFT))
        return pl.pallas_call(
            functools.partial(block_kernel, side, True, n0, len(g) == 2),
            out_shape=outs,
            in_specs=[smem, vmem, anym] + [vmem] * (6 + len(vmsg) + len(g)),
            out_specs=[vmem] * len(outs),
            scratch_shapes=block_scratch + l_scratch,
            compiler_params=params,
            cost_estimate=cost(2 * depth),
            name=f"l_block{side}",
        )(info, near, table, own, rest, recv, coef, weights, *vmsg, x, *g)

    terms_in = opening
    for n0 in range(last_step, 0, -4):
        um, ur, uv, x = u_block(0, n0, um, ur, u_got)
        u_got = lax.ppermute(um, "slab", down)
        lm, lr, lv, g, *g_left = l_block(0, n0, lm, lr, l_got, (), x, terms_in)
        l_got = lax.ppermute(lm, "slab", down)
        if n0 > 3:
            um, ur, x = u_block(1, n0 - 2, um, ur, u_got, uv)
            u_got = lax.ppermute(um, "slab", up)
            lm, lr, g = l_block(1, n0 - 2, lm, lr, l_got, (lv,), x, (g,))
            l_got = lax.ppermute(lm, "slab", up)
            terms_in = (g,)
        else:
            g_right = lax.ppermute(g_left[0], "slab", down)
            (x,) = u_block(1, n0 - 2, um, ur, u_got, uv)
            g, adjoint_field = l_block(1, n0 - 2, lm, lr, l_got, (lv,), x, (g,))

    terms = pl.pallas_call(
        last_kernel,
        out_shape=jax.ShapeDtypeStruct((depth, width_x, width_y), f32),
        in_specs=[vmem] * 3,
        out_specs=vmem,
        compiler_params=once,
        cost_estimate=cost(2),
        name="last_terms",
    )(g, g_right, aperture)
    summed = sum_shots(terms)
    if place != list(range(slabs)):
        adjoint_field = lax.ppermute(adjoint_field, "slab", swap)
        summed = lax.ppermute(summed, "slab", swap)
    block = width_x // lax.axis_size("shot")
    speed = lax.dynamic_slice_in_dim(home, lax.axis_index("shot") * block, block, 1)
    return ((-2.0 / speed) * summed, adjoint_field[None])


def solution(mesh):
    in_specs = (
        P("shot", "slab", None, None),
        P("shot", "slab", None, None),
        P("slab", None, None),
        P("shot", None, None),
        P("shot", None),
        P("shot"),
        P("shot", None, None),
    )
    out_specs = (P("slab", "shot", None), P("shot", "slab", None, None))
    return jax.shard_map(on_device, mesh=mesh, in_specs=in_specs, out_specs=out_specs, check_vma=False)
```

```python
import functools

import jax
import jax.numpy as jnp
import numpy as np
from jax import lax
from jax.experimental import pallas as pl
from jax.experimental.pallas import tpu as pltpu
from jax.sharding import PartitionSpec as P

SCALE = 5040.0
WHOLE = (-14350.0, 8064.0, -1008.0, 128.0, -9.0)
REACH = 4
SHIFT = 8
VMEM_BYTES = 14 * 1024 * 1024
MORE_BYTES = 24 * 1024 * 1024
SUB = 8
PIECES = 3
CHUNK = 256

MSG = 2 * SHIFT
REST = 2 * SHIFT
WORK = 4 * SHIFT
WORK_ALL = 6 * SHIFT
SPAN = 32
MID = 12


def wave_of(step):
    arg = (np.pi * 0.06 * (step - 10.0)) ** 2
    return float(np.float32(SCALE * 10.0 * (1.0 - 2.0 * arg) * np.exp(-arg)))


def load_tiled(field, layer):
    parts = field.shape[1] // SUB
    return jnp.stack([field[layer, pl.ds(m, SUB, stride=parts), :] for m in range(parts)])


def store_tiled(field, layer, value, first=0, count=SUB):
    parts = value.shape[0]
    for m in range(parts):
        field[layer, pl.ds(m, count, stride=parts), :] = value[m, first : first + count]


def split3(f):
    hi = f.astype(jnp.bfloat16)
    left = f - hi.astype(jnp.float32)
    mid = left.astype(jnp.bfloat16)
    return hi, mid, (left - mid.astype(jnp.float32)).astype(jnp.bfloat16)


def put_weights(weights):
    width_y = weights.shape[1]
    square = (width_y, width_y)
    away = jnp.abs(lax.broadcasted_iota(jnp.int32, square, 0) - lax.broadcasted_iota(jnp.int32, square, 1))
    once = jnp.zeros(square, jnp.float32)
    for k in range(1, 5):
        once = jnp.where(away == k, WHOLE[k], once)
    for i in range(PIECES):
        weights[i * width_y : (i + 1) * width_y, :] = once.astype(jnp.bfloat16)


def lane_pass(cur, first, count, weights, pieces, ybuf):
    parts, _, width_y = cur.shape[1:]
    rows = parts * SUB

    def one(q):
        at = pl.multiple_of(q * rows, rows)
        for i, piece in enumerate(split3(cur[first + q].reshape(rows, width_y))):
            pieces[pl.ds(at, rows), i * width_y : (i + 1) * width_y] = piece

    layers_loop(0, count, one)
    for q in range(0, count, SHIFT):
        block = slice(q * rows, min(q + SHIFT, count) * rows)
        ybuf[block, :] = jnp.dot(pieces[block, :], weights[...], preferred_element_type=jnp.float32)


def lap_maker(parts, width_y):
    row = lax.broadcasted_iota(jnp.int32, (1, SUB, width_y), 1)

    def lap(ref, j, along):
        f = ref[j]
        after = jnp.where(row == SUB - 1, 0.0, pltpu.roll(f[:REACH], SUB - 1, 1))
        before = jnp.where(row == 0, 0.0, pltpu.roll(f[parts - REACH :], 1, 1))
        wide = jnp.concatenate([before, f, after], axis=0)
        total = along + (3.0 * WHOLE[0]) * f
        for k in range(1, 5):
            pair = (ref[j + k] + ref[j - k]) + (
                wide[REACH + k : REACH + k + parts] + wide[REACH - k : REACH - k + parts]
            )
            total = total + WHOLE[k] * pair
        return f, total

    return lap


def layers_loop(first, count, body):
    def one(q, carry):
        body(first + q)
        return carry

    lax.fori_loop(0, count, one, 0, unroll=2)


STARTS = 5
ROWS = 16


def inject(work, at, info, near, table_hbm, table, sem, step, first, last):
    low, high = info[STARTS + first], info[STARTS + last]
    rows = work.shape[1] * SUB
    shift = at * rows - first * REACH * rows
    flat = work.reshape(work.shape[0] * rows, work.shape[3])

    def store(low, high, row_of):
        def eight(i, carry):
            for q in range(8):
                r = jnp.minimum(low + i * 8 + q, high - 1)
                flat[pl.ds(info[ROWS + r] + shift, 1), :] = row_of(r)
            return carry

        lax.fori_loop(0, (high - low + 7) // 8, eight, 0)

    split = jnp.clip(CHUNK, low, high)
    store(low, split, lambda r: near[step, pl.ds(r, 1), :])

    @pl.when(high > split)
    def _():
        fetch = pltpu.make_async_copy(table_hbm.at[step], table, sem)
        fetch.start()
        fetch.wait()
        store(split, high, lambda r: table[pl.ds(r, 1), :])


def zones_of(side):
    return (1, 0, 1) if side == 0 else (3, 2, 3)


def put_rows(work, side, n0, info, near, table_hbm, table, sem):
    shared = (info, near, table_hbm, table, sem)
    zero = jnp.zeros((SHIFT,) + work.shape[1:], jnp.float32)
    for i in range(0, WORK, SHIFT):
        work[i : i + SHIFT] = zero
    for level, (at, zone, count) in enumerate(zip((0, 8, 24), zones_of(side), (2, 4, 2))):
        if n0 >= level:
            inject(work, at, *shared, n0 - level, zone, zone + count)
    if side == 0:

        @pl.when(info[0] == 1)
        def _():
            for i in range(WORK, WORK_ALL, SHIFT):
                work[i : i + SHIFT] = zero
            for level, (at, zone, count) in enumerate(((32, 5, 1), (36, 4, 2), (44, 5, 1))):
                if n0 >= level:
                    inject(work, at, *shared, n0 - level, zone, zone + count)


def add_terms(g, g_in, side, n0, is_last, x, d):
    low = 0 if side == 0 else SHIFT
    more = n0 >= 2

    def edge(at):
        def one(q):
            g[low + at + q] = g_in[low + at + q] + x[SHIFT + at + q] * d[SHIFT + at + q]

        layers_loop(0, REACH, one)

    def middle(q):
        total = x[q] * d[q] + x[SHIFT + REACH + q] * d[SHIFT + REACH + q]
        if more:
            total = total + x[3 * SHIFT + q] * d[3 * SHIFT + q]
        g[low + REACH + q] = g_in[low + REACH + q] + total

    edge(0)
    layers_loop(0, SHIFT, middle)
    edge(SHIFT + REACH)
    if side == 1:
        g[0:SHIFT] = g_in[0:SHIFT]
        return
    g[2 * SHIFT : 3 * SHIFT] = g_in[2 * SHIFT : 3 * SHIFT]

    @pl.when(is_last == 1)
    def _():
        for q in range(SHIFT):
            total = x[36 + q] * d[36 + q]
            if q >= REACH:
                total = total + x[28 + q] * d[28 + q]
                if more:
                    total = total + x[40 + q] * d[40 + q]
            g[2 * SHIFT + q] = g[2 * SHIFT + q] + total


def between_kernel(side, n0, opening, info, near, table_hbm, *refs):
    refs = list(refs)
    if n0 == opening:
        work, table, sem = refs
    elif n0 == opening - 2:
        l_msg, u_msg, u_rest, x, d, work, g, start, table, sem = refs
        start[...] = jnp.zeros(start.shape, jnp.float32)
        for z in range(REACH, REACH + SHIFT):
            was = u_rest[z] if z < SHIFT else u_msg[z - SHIFT]
            start[z + SHIFT] = was * l_msg[z - REACH + SHIFT]
        add_terms(g, start, 1 - side, n0 + 2, info[0], x, d)
    else:
        g_in, x, d, work, g, *g_left, table, sem = refs
        add_terms(g, g_in, 1 - side, n0 + 2, info[0], x, d)
        if g_left:
            g_left[0][...] = g[0:SHIFT]
    put_rows(work, side, n0, info, near, table_hbm, table, sem)


def chunks_of(info, zones):
    return jnp.maximum((info[STARTS + zones] + CHUNK - 1) // CHUNK, 1)


def table_kernel(zones, info, ids, rows_l, rows_s, lanes_s, res, near, out, res_cut, pieces, same, part, sem):
    steps, receivers = res.shape
    width_y = part.shape[2]
    chunks = chunks_of(info, zones)
    for i, piece in enumerate(split3(res[...])):
        pieces[i * steps : (i + 1) * steps, :] = piece

    def column(c, carry):
        who = lax.broadcasted_iota(jnp.int32, (receivers, CHUNK), 0) == ids[pl.ds(c, 1), :]
        moved = jnp.dot(
            pieces[...], jnp.where(who, 1.0, 0.0).astype(jnp.bfloat16), preferred_element_type=jnp.float32
        )
        total = SCALE * ((moved[:steps] + moved[steps : 2 * steps]) + moved[2 * steps :])
        for i, piece in enumerate(split3(total)):
            res_cut[c, i] = piece.astype(jnp.float32)
        return carry

    lax.fori_loop(0, chunks, column, 0)

    def to_chunk(c, carry):
        mine = rows_s[pl.ds(pl.multiple_of(c * CHUNK, CHUNK), CHUNK), :]

        def from_chunk(d, carry):
            same[...] = jnp.where(mine == rows_l[pl.ds(d, 1), :], 1.0, 0.0).astype(jnp.bfloat16)
            at = pl.multiple_of(d * CHUNK, CHUNK)
            lane = lax.broadcasted_iota(jnp.int32, (CHUNK, width_y), 1)
            spot = jnp.where(lane == lanes_s[pl.ds(at, CHUNK), :], 1.0, 0.0).astype(jnp.bfloat16)
            spots = jnp.concatenate([spot] * PIECES, axis=0)

            def one(n, carry):
                mixed = []
                for i in range(PIECES):
                    row = jnp.broadcast_to(res_cut[d, i, pl.ds(n, 1), :], (16, CHUNK)).astype(jnp.bfloat16)
                    mixed.append((same[...].reshape(CHUNK // 16, 16, CHUNK) * row[None]).reshape(CHUNK, CHUNK))
                total = jnp.dot(
                    jnp.concatenate(mixed, axis=1), spots, preferred_element_type=jnp.float32
                )
                part[n] = total + jnp.where(d > 0, part[n], 0.0)
                return carry

            return lax.fori_loop(0, steps, one, carry, unroll=4)

        lax.fori_loop(0, chunks, from_chunk, 0)
        return carry

    def store_chunk(c, carry):
        to_chunk(c, 0)
        at = pl.multiple_of(c * CHUNK, CHUNK)
        write = pltpu.make_async_copy(part, out.at[:, pl.ds(at, CHUNK), :], sem)
        write.start()
        write.wait()
        return carry

    to_chunk(0, 0)
    near[...] = part[...]
    lax.fori_loop(1, chunks, store_chunk, 0)


def block_kernel(side, is_l, n0, opening, *refs):
    refs = list(refs)

    def take(count):
        got = refs[:count]
        del refs[:count]
        return got

    final = n0 == 1
    info, own, rest, recv, coef, weights, beyond = take(7)
    work_in = msg_out = rest_out = beyond_out = field_out = None
    if is_l:
        (work_in,) = take(1)
    if not final:
        msg_out, rest_out = take(2)
        if side == 0:
            (beyond_out,) = take(1)
    elif is_l:
        (field_out,) = take(1)
    work_out, a, b, c, p, pieces, ybuf = take(7)

    parts, _, width_y = a.shape[1:]
    rows = parts * SUB
    is_last, src_layer, src_part, src_row, src_lane = (info[i] for i in range(STARTS))
    off = MID - SHIFT if side == 0 else MID - 2 * SHIFT
    lap = lap_maker(parts, width_y)

    def bring(msg, low):
        if low:
            a[MID - SHIFT : MID] = msg[0:SHIFT]
            b[MID - SHIFT - REACH : MID - REACH] = msg[SHIFT:MSG]
        else:
            a[MID : MID + SHIFT] = msg[0:SHIFT]
            b[MID + REACH : MID + REACH + SHIFT] = msg[SHIFT:MSG]

    p[MID - REACH : MID + REACH] = rest[SHIFT:REST]
    if side == 0:
        bring(recv, True)
        a[MID : MID + SHIFT] = rest[0:SHIFT]
        b[MID + REACH : MID + REACH + SHIFT] = own[SHIFT:MSG]
        if opening and not is_l:
            p[MID - REACH : MID] = recv[MSG : MSG + REACH]

        @pl.when(is_last == 1)
        def _():
            zero = jnp.zeros((REACH,) + a.shape[1:], jnp.float32)
            a[MID + SHIFT : MID + 2 * SHIFT] = own[0:SHIFT]
            p[MID + SHIFT + REACH : MID + 2 * SHIFT] = beyond[SHIFT : SHIFT + REACH]
            for field in (a, b, c):
                field[MID + 2 * SHIFT : MID + 2 * SHIFT + REACH] = zero
    else:
        a[MID - SHIFT : MID] = rest[0:SHIFT]
        b[MID - SHIFT - REACH : MID - REACH] = own[SHIFT:MSG]

        @pl.when(is_last == 1)
        def _():
            bring(beyond, False)

        @pl.when(is_last == 0)
        def _():
            bring(recv, False)

    def source(nxt, level, first, count):
        j = src_layer + off

        @pl.when((src_layer >= 0) & (j >= first) & (j < first + count))
        def _():
            lane = lax.broadcasted_iota(jnp.int32, (1, width_y), 1)
            spot = nxt[j, src_part, pl.ds(src_row, 1), :]
            gain = coef[src_layer, src_part, pl.ds(src_row, 1), :] * wave_of(n0 - level)
            nxt[j, src_part, pl.ds(src_row, 1), :] = spot - jnp.where(lane == src_lane, gain, 0.0)

    def advance(level, cur, nxt, first, count, work_at, out, shift):
        if not is_l:
            source(nxt, level, first, count)
        lane_pass(cur, first, count, weights, pieces, ybuf)

        def body(j):
            y_at = pl.multiple_of((j - first) * rows, rows)
            f, total = lap(cur, j, ybuf[pl.ds(y_at, rows), :].reshape(parts, SUB, width_y))
            if is_l:
                total = total + work_in[j + (work_at - first)]
            step = coef[j - off] * total
            out[j + shift] = (2.0 * f - nxt[j]) + step
            work_out[j + (work_at - first)] = step if is_l else f

        layers_loop(first, count, body)

    def beyond_too(*args):
        if side == 0:

            @pl.when(is_last == 1)
            def _():
                advance(*args)

    advance(0, a, p, MID - REACH, SHIFT, 0, b, 0)
    beyond_too(0, a, p, MID + SHIFT + REACH, REACH, 32, b, 0)
    advance(1, b, a, MID - SHIFT, 2 * SHIFT, 8, c, 0)
    beyond_too(1, b, a, MID + SHIFT, SHIFT, 36, c, 0)
    if final:
        if is_l:
            for layer in range(2 * SHIFT):
                store_tiled(field_out, layer, c[MID - SHIFT + layer])
        return
    advance(2, c, b, MID - REACH, SHIFT, 24, msg_out, SHIFT - (MID - REACH))
    if side == 0:
        msg_out[0:SHIFT] = c[MID - SHIFT : MID]
        rest_out[0:SHIFT] = c[MID : MID + SHIFT]
        rest_out[SHIFT:REST] = b[MID + REACH : MID + REACH + SHIFT]

        @pl.when(is_last == 1)
        def _():
            first = MID + SHIFT + REACH
            advance(2, c, b, first, REACH, 44, beyond_out, SHIFT - first)
            beyond_out[0:SHIFT] = c[MID + SHIFT : MID + 2 * SHIFT]
            beyond_out[SHIFT + REACH : MSG] = jnp.zeros((REACH,) + a.shape[1:], jnp.float32)
    else:
        msg_out[0:SHIFT] = c[MID : MID + SHIFT]
        rest_out[0:SHIFT] = c[MID - SHIFT : MID]
        rest_out[SHIFT:REST] = b[MID - SHIFT - REACH : MID - REACH]


def first_coef_kernel(speed, speed_left, coef, weights):
    put_weights(weights)

    def own(z):
        coef[z + SHIFT] = (0.4 * load_tiled(speed, z)) ** 2 * (1.0 / SCALE)

    def left(z):
        coef[z] = (0.4 * load_tiled(speed_left, z)) ** 2 * (1.0 / SCALE)

    layers_loop(0, speed.shape[0], own)
    layers_loop(0, SHIFT, left)


def first_u_kernel(n0, info, prev, last, coef, weights, msg_out, rest_out, beyond, f0, f1, pieces, ybuf):
    depth, parts, _, width_y = f0.shape
    rows = parts * SUB
    src_layer, src_part, src_row, src_lane = (info[i] for i in range(1, STARTS))
    lap = lap_maker(parts, width_y)

    def bring(z):
        f0[z] = load_tiled(prev, z)
        f1[z] = load_tiled(last, z)

    layers_loop(0, depth, bring)
    msg_out[0:SHIFT] = f0[depth - SHIFT : depth]
    msg_out[MSG : MSG + REACH] = f1[depth - REACH : depth]
    rest_out[0:SHIFT] = f0[0:SHIFT]
    rest_out[SHIFT : SHIFT + REACH] = jnp.zeros((REACH,) + f0.shape[1:], jnp.float32)
    rest_out[SHIFT + REACH : REST] = f1[0:REACH]
    beyond[...] = jnp.zeros(beyond.shape, jnp.float32)
    beyond[SHIFT : SHIFT + REACH] = f1[depth - REACH : depth]
    lane_pass(f0, REACH, SHIFT, weights, pieces, ybuf)
    to = SHIFT - REACH

    def body(j):
        y_at = pl.multiple_of((j - REACH) * rows, rows)
        f, total = lap(f0, j, ybuf[pl.ds(y_at, rows), :].reshape(parts, SUB, width_y))
        msg_out[j + to] = (2.0 * f - f1[j]) + coef[j + SHIFT] * total

    layers_loop(REACH, SHIFT, body)
    j = src_layer - SHIFT

    @pl.when((src_layer >= 0) & (j >= REACH) & (j < REACH + SHIFT))
    def _():
        lane = lax.broadcasted_iota(jnp.int32, (1, width_y), 1)
        spot = msg_out[j + to, src_part, pl.ds(src_row, 1), :]
        gain = coef[src_layer, src_part, pl.ds(src_row, 1), :] * wave_of(n0)
        msg_out[j + to, src_part, pl.ds(src_row, 1), :] = spot + jnp.where(lane == src_lane, gain, 0.0)


def first_l_kernel(n0, info, near, table_hbm, coef, msg_out, rest_out, work, table, sem):
    work[...] = jnp.zeros(work.shape, jnp.float32)
    msg_out[0:SHIFT] = jnp.zeros((SHIFT,) + coef.shape[1:], jnp.float32)
    rest_out[...] = jnp.zeros(rest_out.shape, jnp.float32)
    zone = (SHIFT + REACH) // REACH
    inject(work, 0, info, near, table_hbm, table, sem, n0, zone, zone + SHIFT // REACH)

    def body(q):
        msg_out[q + SHIFT] = coef[q + SHIFT + REACH] * work[q]

    layers_loop(0, SHIFT, body)


def last_kernel(info, g_in, x, d, g_right, gate, out, g):
    depth = out.shape[0]
    add_terms(g, g_in, 1, 1, info[0], x, d)

    def one(z):
        store_tiled(out, z, load_tiled(gate, 0).astype(jnp.float32) * g[z + SHIFT])

    def shared(z):
        store_tiled(out, z, load_tiled(gate, 0).astype(jnp.float32) * (g[z + SHIFT] + g_right[z - SHIFT]))

    layers_loop(0, SHIFT, one)
    layers_loop(SHIFT, depth - SHIFT, shared)


def sum_shots(g):
    shots = lax.axis_size("shot")
    if shots != 2:
        return lax.psum_scatter(g, "shot", scatter_dimension=1, tiled=True)
    block = g.shape[1] // 2
    low, high = g[:, :block], g[:, block:]
    first = lax.axis_index("shot") == 0
    other = lax.ppermute(jnp.where(first, high, low), "shot", [(0, 1), (1, 0)])
    return jnp.where(first, low, high) + other


def snake_of(slabs):
    row = slabs // 4
    if slabs % 8:
        return list(range(slabs))
    order = []
    for i in range(slabs):
        z, (chip, core) = i // row, divmod(i % row, 2)
        order.append(z * row + 2 * (row // 2 - 1 - chip if z % 2 else chip) + core)
    return order


def on_device(fwd_last, fwd_prev, velocity, aperture, rec_index, src_index, residual):
    _, depth, width_x, width_y = fwd_last.shape
    parts = width_x // SUB
    total_steps, receivers = residual.shape[1:]
    plane = width_x * width_y
    slabs = lax.axis_size("slab")
    f32 = jnp.float32
    place = snake_of(slabs)
    slab = jnp.asarray(place, jnp.int32)[lax.axis_index("slab")]
    up = [(place[i], place[i + 1]) for i in range(slabs - 1)]
    down = [(place[i + 1], place[i]) for i in range(slabs - 1)]
    swap = [(i, place[i]) for i in range(slabs)]
    home = velocity
    if place != list(range(slabs)):
        velocity = lax.ppermute(velocity, "slab", swap)
    speed_left = lax.ppermute(home[depth - SHIFT :], "slab", [(i, place[i + 1]) for i in range(slabs - 1)])
    if place != list(range(slabs)):
        fwd_prev = lax.ppermute(fwd_prev, "slab", swap)
        fwd_last = lax.ppermute(fwd_last, "slab", swap)

    base = (slab * depth - SHIFT) * plane
    window = (depth + SHIFT) * plane
    local = rec_index[0] - base
    far = jnp.int32(2**30)
    keys = jnp.where((local >= 0) & (local < window), local, far)
    keys, ids = lax.sort((keys, lax.iota(jnp.int32, receivers)), num_keys=1, is_stable=False)

    def place_of(cell):
        layer = cell // plane
        x = (cell // width_y) % width_x
        return layer, x % parts, x // parts, cell % width_y

    layer, part, row, lane = place_of(keys)
    rows_of = (layer * parts + part) * SUB + row
    zones = (depth + SHIFT) // REACH
    edges = jnp.arange(zones + 1, dtype=jnp.int32) * (REACH * plane)
    starts = jnp.sum((keys[None, :] < edges[:, None]).astype(jnp.int32), axis=1)

    src = src_index[0] - base
    src_in = (src >= 0) & (src < window)
    s_layer, s_part, s_row, s_lane = place_of(jnp.where(src_in, src, 0))
    s_layer = jnp.where(src_in, s_layer, -1)
    is_last = (slab == slabs - 1).astype(jnp.int32)
    info = jnp.concatenate([jnp.stack([is_last, s_layer, s_part, s_row, s_lane]), starts, jnp.zeros((ROWS - STARTS - zones - 1,), jnp.int32), rows_of])
    last_step = total_steps - 1

    smem = pl.BlockSpec(memory_space=pltpu.SMEM)
    vmem = pl.BlockSpec(memory_space=pltpu.VMEM)
    anym = pl.BlockSpec(memory_space=pl.ANY)

    def fields(layers):
        return jax.ShapeDtypeStruct((layers, parts, SUB, width_y), f32)

    params = pltpu.CompilerParams(vmem_limit_bytes=VMEM_BYTES)
    once = pltpu.CompilerParams(vmem_limit_bytes=MORE_BYTES)
    fetch_scratch = [pltpu.VMEM((receivers, width_y), f32), pltpu.SemaphoreType.DMA(())]

    def lane_scratch(layers):
        rows = layers * parts * SUB
        return [
            pltpu.VMEM((rows, PIECES * width_y), jnp.bfloat16),
            pltpu.VMEM((rows, width_y), f32),
        ]

    block_scratch = [pltpu.VMEM((SPAN, parts, SUB, width_y), f32)] * 4 + lane_scratch(2 * SHIFT)

    def cost(layers):
        return pl.CostEstimate(
            flops=50 * layers * plane, bytes_accessed=24 * layers * plane, transcendentals=0
        )

    near, table = pl.pallas_call(
        functools.partial(table_kernel, zones),
        out_shape=(
            jax.ShapeDtypeStruct((total_steps, CHUNK, width_y), f32),
            jax.ShapeDtypeStruct((total_steps, receivers, width_y), f32),
        ),
        in_specs=[smem] + [vmem] * 5,
        out_specs=(vmem, anym),
        scratch_shapes=[
            pltpu.VMEM((receivers // CHUNK, PIECES, total_steps, CHUNK), f32),
            pltpu.VMEM((PIECES * total_steps, receivers), jnp.bfloat16),
            pltpu.VMEM((CHUNK, CHUNK), jnp.bfloat16),
            pltpu.VMEM((total_steps, CHUNK, width_y), f32),
            pltpu.SemaphoreType.DMA(()),
        ],
        compiler_params=once,
        cost_estimate=cost(SHIFT),
        name="rec_table",
    )(
        info,
        ids.reshape(receivers // CHUNK, CHUNK),
        rows_of.reshape(receivers // CHUNK, CHUNK),
        rows_of[:, None],
        lane[:, None],
        residual[0],
    )
    coef, weights = pl.pallas_call(
        first_coef_kernel,
        out_shape=(
            fields(depth + SHIFT),
            jax.ShapeDtypeStruct((PIECES * width_y, width_y), jnp.bfloat16),
        ),
        in_specs=[vmem] * 2,
        out_specs=[vmem] * 2,
        compiler_params=once,
        cost_estimate=cost(2),
        name="first_coef",
    )(velocity, speed_left)
    lm, lr = pl.pallas_call(
        functools.partial(first_l_kernel, last_step),
        out_shape=(fields(MSG), fields(REST)),
        in_specs=[smem, vmem, anym, vmem],
        out_specs=(vmem, vmem),
        scratch_shapes=[pltpu.VMEM((SHIFT, parts, SUB, width_y), f32)] + fetch_scratch,
        compiler_params=once,
        cost_estimate=cost(2),
        name="first_l",
    )(info, near, table, coef)
    l_got = lax.ppermute(lm, "slab", up)

    def between(side, n0, arrays, after):
        near_now = near
        if after is not None:
            near_now, _ = lax.optimization_barrier((near, after))
        outs = [fields(WORK_ALL)]
        scratch = list(fetch_scratch)
        if n0 < last_step:
            outs.append(fields(depth + SHIFT))
            if n0 == 1:
                outs.append(fields(SHIFT))
            if n0 == last_step - 2:
                scratch = [pltpu.VMEM((depth + SHIFT, parts, SUB, width_y), f32)] + scratch
        return pl.pallas_call(
            functools.partial(between_kernel, side, n0, last_step),
            out_shape=outs,
            in_specs=[smem, vmem, anym] + [vmem] * len(arrays),
            out_specs=[vmem] * len(outs),
            scratch_shapes=scratch,
            compiler_params=params,
            cost_estimate=cost(SHIFT),
            name=f"between{side}",
        )(info, near_now, table, *arrays)

    (work,) = between(0, last_step, (), lr)

    fwd_prev, fwd_last, _ = lax.optimization_barrier((fwd_prev, fwd_last, work))
    um, ur, ub = pl.pallas_call(
        functools.partial(first_u_kernel, last_step),
        out_shape=(fields(MSG + REACH), fields(REST), fields(MSG)),
        in_specs=[smem] + [vmem] * 4,
        out_specs=[vmem] * 3,
        scratch_shapes=[pltpu.VMEM((depth, parts, SUB, width_y), f32)] * 2 + lane_scratch(SHIFT),
        compiler_params=once,
        cost_estimate=cost(SHIFT),
        name="first_u",
    )(info, fwd_prev[0], fwd_last[0], coef, weights)
    u_got = lax.ppermute(um, "slab", up)
    opening = (lm, um, ur)
    lb = lr

    def block(is_l, side, n0, own, rest, recv, beyond, *work):
        outs = []
        if n0 > 1:
            outs = [fields(MSG), fields(REST)] + ([fields(MSG)] if side == 0 else [])
        elif is_l:
            outs = [jax.ShapeDtypeStruct((depth, width_x, width_y), f32)]
        outs.append(fields(WORK_ALL))
        return pl.pallas_call(
            functools.partial(block_kernel, side, is_l, n0, n0 == last_step),
            out_shape=outs,
            in_specs=[smem] + [vmem] * (6 + len(work)),
            out_specs=[vmem] * len(outs),
            scratch_shapes=block_scratch,
            compiler_params=params,
            cost_estimate=cost(2 * depth),
            name=("l" if is_l else "u") + f"_block{side}",
        )(info, own, rest, recv, coef, weights, beyond, *work)

    g = x = d = None
    for n0 in range(last_step, 0, -2):
        side = (last_step - n0) // 2 % 2
        final = n0 == 1
        way = up if side else down
        before = x
        if final:
            (x,) = block(False, side, n0, um, ur, u_got, ub)
        else:
            um, ur, *ub_new, x = block(False, side, n0, um, ur, u_got, ub)
            ub = ub_new[0] if ub_new else ub
            u_got = lax.ppermute(um, "slab", way)
        if n0 < last_step:
            arrays = ((g,) if g is not None else opening) + (before, d)
            work, g, *g_left = between(side, n0, arrays, x)
            if final:
                g_right = lax.ppermute(g_left[0], "slab", down)
        if final:
            adjoint_field, d = block(True, side, n0, lm, lr, l_got, lb, work)
        else:
            lm, lr, *lb_new, d = block(True, side, n0, lm, lr, l_got, lb, work)
            lb = lb_new[0] if lb_new else lb
            l_got = lax.ppermute(lm, "slab", way)

    terms = pl.pallas_call(
        last_kernel,
        out_shape=jax.ShapeDtypeStruct((depth, width_x, width_y), f32),
        in_specs=[smem] + [vmem] * 5,
        out_specs=vmem,
        scratch_shapes=[pltpu.VMEM((depth + SHIFT, parts, SUB, width_y), f32)],
        compiler_params=once,
        cost_estimate=cost(SHIFT),
        name="last_terms",
    )(info, g, x, d, g_right, aperture)
    summed = sum_shots(terms)
    if place != list(range(slabs)):
        adjoint_field = lax.ppermute(adjoint_field, "slab", swap)
        summed = lax.ppermute(summed, "slab", swap)
    block = width_x // lax.axis_size("shot")
    speed = lax.dynamic_slice_in_dim(home, lax.axis_index("shot") * block, block, 1)
    return ((-2.0 / speed) * summed, adjoint_field[None])


def solution(mesh):
    in_specs = (
        P("shot", "slab", None, None),
        P("shot", "slab", None, None),
        P("slab", None, None),
        P("shot", None, None),
        P("shot", None),
        P("shot"),
        P("shot", None, None),
    )
    out_specs = (P("slab", "shot", None), P("shot", "slab", None, None))
    return jax.shard_map(on_device, mesh=mesh, in_specs=in_specs, out_specs=out_specs, check_vma=False)
```

```python
import functools

import jax
import jax.numpy as jnp
import numpy as np
from jax import lax
from jax.experimental import pallas as pl
from jax.experimental.pallas import tpu as pltpu
from jax.sharding import PartitionSpec as P

SCALE = 5040.0
WHOLE = (-14350.0, 8064.0, -1008.0, 128.0, -9.0)
REACH = 4
SHIFT = 8
VMEM_BYTES = 14 * 1024 * 1024
MORE_BYTES = 24 * 1024 * 1024
SUB = 8
PIECES = 3
CHUNK = 256

MSG = 2 * SHIFT
REST = 2 * SHIFT
WORK = 4 * SHIFT
WORK_ALL = 6 * SHIFT
SPAN = 32
MID = 12


def wave_of(step):
    arg = (np.pi * 0.06 * (step - 10.0)) ** 2
    return float(np.float32(SCALE * 10.0 * (1.0 - 2.0 * arg) * np.exp(-arg)))


def load_tiled(field, layer):
    parts = field.shape[1] // SUB
    return jnp.stack([field[layer, pl.ds(m, SUB, stride=parts), :] for m in range(parts)])


def store_tiled(field, layer, value, first=0, count=SUB):
    parts = value.shape[0]
    for m in range(parts):
        field[layer, pl.ds(m, count, stride=parts), :] = value[m, first : first + count]


def split3(f):
    hi = f.astype(jnp.bfloat16)
    left = f - hi.astype(jnp.float32)
    mid = left.astype(jnp.bfloat16)
    return hi, mid, (left - mid.astype(jnp.float32)).astype(jnp.bfloat16)


def put_weights(weights):
    width_y = weights.shape[1]
    square = (width_y, width_y)
    away = jnp.abs(lax.broadcasted_iota(jnp.int32, square, 0) - lax.broadcasted_iota(jnp.int32, square, 1))
    once = jnp.zeros(square, jnp.float32)
    for k in range(1, 5):
        once = jnp.where(away == k, WHOLE[k], once)
    for i in range(PIECES):
        weights[i * width_y : (i + 1) * width_y, :] = once.astype(jnp.bfloat16)


def lane_pass(cur, first, count, weights, pieces, ybuf):
    parts, _, width_y = cur.shape[1:]
    rows = parts * SUB

    def one(q):
        at = pl.multiple_of(q * rows, rows)
        for i, piece in enumerate(split3(cur[first + q].reshape(rows, width_y))):
            pieces[pl.ds(at, rows), i * width_y : (i + 1) * width_y] = piece

    layers_loop(0, count, one)
    for q in range(0, count, SHIFT):
        block = slice(q * rows, min(q + SHIFT, count) * rows)
        ybuf[block, :] = jnp.dot(pieces[block, :], weights[...], preferred_element_type=jnp.float32)


def lap_maker(parts, width_y):
    row = lax.broadcasted_iota(jnp.int32, (1, SUB, width_y), 1)

    def lap(ref, j, along):
        f = ref[j]
        after = jnp.where(row == SUB - 1, 0.0, pltpu.roll(f[:REACH], SUB - 1, 1))
        before = jnp.where(row == 0, 0.0, pltpu.roll(f[parts - REACH :], 1, 1))
        wide = jnp.concatenate([before, f, after], axis=0)
        total = along + (3.0 * WHOLE[0]) * f
        for k in range(1, 5):
            pair = (ref[j + k] + ref[j - k]) + (
                wide[REACH + k : REACH + k + parts] + wide[REACH - k : REACH - k + parts]
            )
            total = total + WHOLE[k] * pair
        return f, total

    return lap


def layers_loop(first, count, body):
    def one(q, carry):
        body(first + q)
        return carry

    lax.fori_loop(0, count, one, 0, unroll=2)


STARTS = 5
SHOT = 15
ROWS = 16


def inject(work, at, info, near, table_hbm, table, sem, step, first, last):
    low, high = info[STARTS + first], info[STARTS + last]
    rows = work.shape[1] * SUB
    shift = at * rows - first * REACH * rows
    flat = work.reshape(work.shape[0] * rows, work.shape[3])

    def store(low, high, row_of):
        def one(r, carry):
            flat[pl.ds(info[ROWS + r] + shift, 1), :] = row_of(r)
            return carry

        def eight(i, carry):
            for q in range(8):
                one(low + i * 8 + q, carry)
            return carry

        groups = lax.shift_right_logical(high - low, 3)
        lax.fori_loop(0, groups, eight, 0)
        lax.fori_loop(low + groups * 8, high, one, 0)

    split = jnp.clip(CHUNK, low, high)
    store(low, split, lambda r: near[step, pl.ds(r, 1), :])

    @pl.when(high > split)
    def _():
        fetch = pltpu.make_async_copy(table_hbm.at[step], table, sem)
        fetch.start()
        fetch.wait()
        store(split, high, lambda r: table[pl.ds(r, 1), :])


def zones_of(side):
    return (1, 0, 1) if side == 0 else (3, 2, 3)


def put_rows(work, side, n0, info, near, table_hbm, table, sem):
    shared = (info, near, table_hbm, table, sem)
    zero = jnp.zeros((SHIFT,) + work.shape[1:], jnp.float32)
    for i in range(0, WORK, SHIFT):
        work[i : i + SHIFT] = zero
    for level, (at, zone, count) in enumerate(zip((0, 8, 24), zones_of(side), (2, 4, 2))):
        if n0 >= level:
            inject(work, at, *shared, n0 - level, zone, zone + count)
    if side == 0:

        @pl.when(info[0] == 1)
        def _():
            for i in range(WORK, WORK_ALL, SHIFT):
                work[i : i + SHIFT] = zero
            for level, (at, zone, count) in enumerate(((32, 5, 1), (36, 4, 2), (44, 5, 1))):
                if n0 >= level:
                    inject(work, at, *shared, n0 - level, zone, zone + count)


def add_terms(g, g_in, side, n0, is_last, x, d):
    low = 0 if side == 0 else SHIFT
    more = n0 >= 2

    def edge(at):
        def one(q):
            g[low + at + q] = g_in[low + at + q] + x[SHIFT + at + q] * d[SHIFT + at + q]

        layers_loop(0, REACH, one)

    def middle(q):
        total = x[q] * d[q] + x[SHIFT + REACH + q] * d[SHIFT + REACH + q]
        if more:
            total = total + x[3 * SHIFT + q] * d[3 * SHIFT + q]
        g[low + REACH + q] = g_in[low + REACH + q] + total

    edge(0)
    layers_loop(0, SHIFT, middle)
    edge(SHIFT + REACH)
    if side == 1:
        g[0:SHIFT] = g_in[0:SHIFT]
        return
    g[2 * SHIFT : 3 * SHIFT] = g_in[2 * SHIFT : 3 * SHIFT]

    @pl.when(is_last == 1)
    def _():
        for q in range(SHIFT):
            total = x[36 + q] * d[36 + q]
            if q >= REACH:
                total = total + x[28 + q] * d[28 + q]
                if more:
                    total = total + x[40 + q] * d[40 + q]
            g[2 * SHIFT + q] = g[2 * SHIFT + q] + total


def between_kernel(side, n0, opening, info, near, table_hbm, *refs):
    if n0 == opening:
        l_msg, u_msg, u_rest, x, d, work, g, start, table, sem = refs
        start[...] = jnp.zeros(start.shape, jnp.float32)
        for z in range(REACH, REACH + SHIFT):
            was = u_rest[z] if z < SHIFT else u_msg[z - SHIFT]
            start[z + SHIFT] = was * l_msg[z - REACH + SHIFT]
        g_in = start
    else:
        g_in, x, d, work, g, *g_left, table, sem = refs
    add_terms(g, g_in, side, n0, info[0], x, d)
    if n0 == 3:
        g_left[0][...] = g[0:SHIFT]
    put_rows(work, 1 - side, n0 - 2, info, near, table_hbm, table, sem)


def chunks_of(info, zones):
    return jnp.maximum((info[STARTS + zones] + CHUNK - 1) // CHUNK, 1)


def table_kernel(zones, info, ids, rows_l, rows_s, lanes_s, res, near, out, res_cut, pieces, same, part, sem):
    steps, receivers = res.shape
    width_y = part.shape[2]
    chunks = chunks_of(info, zones)
    for i, piece in enumerate(split3(res[...])):
        pieces[i * steps : (i + 1) * steps, :] = piece

    def column(c, carry):
        who = lax.broadcasted_iota(jnp.int32, (receivers, CHUNK), 0) == ids[pl.ds(c, 1), :]
        moved = jnp.dot(
            pieces[...], jnp.where(who, 1.0, 0.0).astype(jnp.bfloat16), preferred_element_type=jnp.float32
        )
        total = SCALE * ((moved[:steps] + moved[steps : 2 * steps]) + moved[2 * steps :])
        for i, piece in enumerate(split3(total)):
            res_cut[c, i] = piece.astype(jnp.float32)
        return carry

    lax.fori_loop(0, chunks, column, 0)

    def to_chunk(c, carry):
        mine = rows_s[pl.ds(pl.multiple_of(c * CHUNK, CHUNK), CHUNK), :]

        def from_chunk(d, carry):
            same[...] = jnp.where(mine == rows_l[pl.ds(d, 1), :], 1.0, 0.0).astype(jnp.bfloat16)
            at = pl.multiple_of(d * CHUNK, CHUNK)
            lane = lax.broadcasted_iota(jnp.int32, (CHUNK, width_y), 1)
            spot = jnp.where(lane == lanes_s[pl.ds(at, CHUNK), :], 1.0, 0.0).astype(jnp.bfloat16)
            spots = jnp.concatenate([spot] * PIECES, axis=0)

            def one(n, carry):
                mixed = []
                for i in range(PIECES):
                    row = jnp.broadcast_to(res_cut[d, i, pl.ds(n, 1), :], (16, CHUNK)).astype(jnp.bfloat16)
                    mixed.append((same[...].reshape(CHUNK // 16, 16, CHUNK) * row[None]).reshape(CHUNK, CHUNK))
                total = jnp.dot(
                    jnp.concatenate(mixed, axis=1), spots, preferred_element_type=jnp.float32
                )
                part[n] = total + jnp.where(d > 0, part[n], 0.0)
                return carry

            return lax.fori_loop(0, steps, one, carry, unroll=4)

        lax.fori_loop(0, chunks, from_chunk, 0)
        return carry

    def store_chunk(c, carry):
        to_chunk(c, 0)
        at = pl.multiple_of(c * CHUNK, CHUNK)
        write = pltpu.make_async_copy(part, out.at[:, pl.ds(at, CHUNK), :], sem)
        write.start()
        write.wait()
        return carry

    to_chunk(0, 0)
    near[...] = part[...]
    lax.fori_loop(1, chunks, store_chunk, 0)


def block_kernel(side, is_l, n0, opening, *refs):
    refs = list(refs)

    def take(count):
        got = refs[:count]
        del refs[:count]
        return got

    final = n0 == 1
    info, own, rest, recv, coef, weights, beyond = take(7)
    work_in = msg_out = rest_out = beyond_out = field_out = None
    if is_l:
        (work_in,) = take(1)
    if not final:
        msg_out, rest_out = take(2)
        if side == 0:
            (beyond_out,) = take(1)
    elif is_l:
        (field_out,) = take(1)
    work_out, a, b, c, p, pieces, ybuf = take(7)

    parts, _, width_y = a.shape[1:]
    rows = parts * SUB
    is_last, src_layer, src_part, src_row, src_lane = (info[i] for i in range(STARTS))
    off = MID - SHIFT if side == 0 else MID - 2 * SHIFT
    lap = lap_maker(parts, width_y)

    def bring(msg, low):
        if low:
            a[MID - SHIFT : MID] = msg[0:SHIFT]
            b[MID - SHIFT - REACH : MID - REACH] = msg[SHIFT:MSG]
        else:
            a[MID : MID + SHIFT] = msg[0:SHIFT]
            b[MID + REACH : MID + REACH + SHIFT] = msg[SHIFT:MSG]

    p[MID - REACH : MID + REACH] = rest[SHIFT:REST]
    if side == 0:
        bring(recv, True)
        a[MID : MID + SHIFT] = rest[0:SHIFT]
        b[MID + REACH : MID + REACH + SHIFT] = own[SHIFT:MSG]
        if opening and not is_l:
            p[MID - REACH : MID] = recv[MSG : MSG + REACH]

        @pl.when(is_last == 1)
        def _():
            zero = jnp.zeros((REACH,) + a.shape[1:], jnp.float32)
            a[MID + SHIFT : MID + 2 * SHIFT] = own[0:SHIFT]
            p[MID + SHIFT + REACH : MID + 2 * SHIFT] = beyond[SHIFT : SHIFT + REACH]
            for field in (a, b, c):
                field[MID + 2 * SHIFT : MID + 2 * SHIFT + REACH] = zero
    else:
        a[MID - SHIFT : MID] = rest[0:SHIFT]
        b[MID - SHIFT - REACH : MID - REACH] = own[SHIFT:MSG]

        @pl.when(is_last == 1)
        def _():
            bring(beyond, False)

        @pl.when(is_last == 0)
        def _():
            bring(recv, False)

    def source(nxt, level, first, count):
        j = src_layer + off

        @pl.when((src_layer >= 0) & (j >= first) & (j < first + count))
        def _():
            lane = lax.broadcasted_iota(jnp.int32, (1, width_y), 1)
            spot = nxt[j, src_part, pl.ds(src_row, 1), :]
            gain = coef[src_layer, src_part, pl.ds(src_row, 1), :] * wave_of(n0 - level)
            nxt[j, src_part, pl.ds(src_row, 1), :] = spot - jnp.where(lane == src_lane, gain, 0.0)

    def advance(level, cur, nxt, first, count, work_at, out, shift):
        if not is_l:
            source(nxt, level, first, count)
        lane_pass(cur, first, count, weights, pieces, ybuf)

        def body(j):
            y_at = pl.multiple_of((j - first) * rows, rows)
            f, total = lap(cur, j, ybuf[pl.ds(y_at, rows), :].reshape(parts, SUB, width_y))
            if is_l:
                total = total + work_in[j + (work_at - first)]
            step = coef[j - off] * total
            out[j + shift] = (2.0 * f - nxt[j]) + step
            work_out[j + (work_at - first)] = step if is_l else f

        layers_loop(first, count, body)

    def beyond_too(*args):
        if side == 0:

            @pl.when(is_last == 1)
            def _():
                advance(*args)

    advance(0, a, p, MID - REACH, SHIFT, 0, b, 0)
    beyond_too(0, a, p, MID + SHIFT + REACH, REACH, 32, b, 0)
    advance(1, b, a, MID - SHIFT, 2 * SHIFT, 8, c, 0)
    beyond_too(1, b, a, MID + SHIFT, SHIFT, 36, c, 0)
    if final:
        if is_l:
            for layer in range(2 * SHIFT):
                store_tiled(field_out, layer, c[MID - SHIFT + layer])
        return
    advance(2, c, b, MID - REACH, SHIFT, 24, msg_out, SHIFT - (MID - REACH))
    if side == 0:
        msg_out[0:SHIFT] = c[MID - SHIFT : MID]
        rest_out[0:SHIFT] = c[MID : MID + SHIFT]
        rest_out[SHIFT:REST] = b[MID + REACH : MID + REACH + SHIFT]

        @pl.when(is_last == 1)
        def _():
            first = MID + SHIFT + REACH
            advance(2, c, b, first, REACH, 44, beyond_out, SHIFT - first)
            beyond_out[0:SHIFT] = c[MID + SHIFT : MID + 2 * SHIFT]
            beyond_out[SHIFT + REACH : MSG] = jnp.zeros((REACH,) + a.shape[1:], jnp.float32)
    else:
        msg_out[0:SHIFT] = c[MID : MID + SHIFT]
        rest_out[0:SHIFT] = c[MID - SHIFT : MID]
        rest_out[SHIFT:REST] = b[MID - SHIFT - REACH : MID - REACH]


def first_coef_kernel(halves, info, *refs):
    *speeds, speed_left, coef, weights = refs
    put_weights(weights)

    def fill(speed, first):
        def one(z):
            coef[z + first] = (0.4 * load_tiled(speed, z)) ** 2 * (1.0 / SCALE)

        layers_loop(0, speed.shape[0], one)

    fill(speed_left, 0)
    if not halves:
        fill(speeds[0], SHIFT)
        return
    depth = speeds[0].shape[0]

    @pl.when(info[SHOT] == 0)
    def _():
        fill(speeds[0], SHIFT)
        fill(speeds[1], SHIFT + depth)

    @pl.when(info[SHOT] != 0)
    def _():
        fill(speeds[1], SHIFT)
        fill(speeds[0], SHIFT + depth)


def first_u_kernel(n0, info, prev, last, coef, weights, msg_out, rest_out, beyond, f0, f1, pieces, ybuf):
    depth, parts, _, width_y = f0.shape
    rows = parts * SUB
    src_layer, src_part, src_row, src_lane = (info[i] for i in range(1, STARTS))
    lap = lap_maker(parts, width_y)

    def bring(z):
        f0[z] = load_tiled(prev, z)
        f1[z] = load_tiled(last, z)

    layers_loop(0, depth, bring)
    msg_out[0:SHIFT] = f0[depth - SHIFT : depth]
    msg_out[MSG : MSG + REACH] = f1[depth - REACH : depth]
    rest_out[0:SHIFT] = f0[0:SHIFT]
    rest_out[SHIFT : SHIFT + REACH] = jnp.zeros((REACH,) + f0.shape[1:], jnp.float32)
    rest_out[SHIFT + REACH : REST] = f1[0:REACH]
    beyond[...] = jnp.zeros(beyond.shape, jnp.float32)
    beyond[SHIFT : SHIFT + REACH] = f1[depth - REACH : depth]
    lane_pass(f0, REACH, SHIFT, weights, pieces, ybuf)
    to = SHIFT - REACH

    def body(j):
        y_at = pl.multiple_of((j - REACH) * rows, rows)
        f, total = lap(f0, j, ybuf[pl.ds(y_at, rows), :].reshape(parts, SUB, width_y))
        msg_out[j + to] = (2.0 * f - f1[j]) + coef[j + SHIFT] * total

    layers_loop(REACH, SHIFT, body)
    j = src_layer - SHIFT

    @pl.when((src_layer >= 0) & (j >= REACH) & (j < REACH + SHIFT))
    def _():
        lane = lax.broadcasted_iota(jnp.int32, (1, width_y), 1)
        spot = msg_out[j + to, src_part, pl.ds(src_row, 1), :]
        gain = coef[src_layer, src_part, pl.ds(src_row, 1), :] * wave_of(n0)
        msg_out[j + to, src_part, pl.ds(src_row, 1), :] = spot + jnp.where(lane == src_lane, gain, 0.0)


def first_l_kernel(n0, info, near, table_hbm, coef, msg_out, rest_out, work, table, sem):
    msg_out[...] = jnp.zeros(msg_out.shape, jnp.float32)
    rest_out[...] = jnp.zeros(rest_out.shape, jnp.float32)
    zone = (SHIFT + REACH) // REACH
    inject(msg_out, SHIFT, info, near, table_hbm, table, sem, n0, zone, zone + SHIFT // REACH)

    def body(q):
        msg_out[q + SHIFT] = coef[q + SHIFT + REACH] * msg_out[q + SHIFT]

    layers_loop(0, SHIFT, body)
    put_rows(work, 0, n0, info, near, table_hbm, table, sem)


def last_kernel(info, g_in, x, d, g_right, gate, out, g):
    depth = out.shape[0]
    add_terms(g, g_in, 1, 1, info[0], x, d)

    def one(z):
        store_tiled(out, z, load_tiled(gate, 0).astype(jnp.float32) * g[z + SHIFT])

    def shared(z):
        store_tiled(out, z, load_tiled(gate, 0).astype(jnp.float32) * (g[z + SHIFT] + g_right[z - SHIFT]))

    layers_loop(0, SHIFT, one)
    layers_loop(SHIFT, depth - SHIFT, shared)


def sum_shots(g):
    shots = lax.axis_size("shot")
    if shots != 2:
        return lax.psum_scatter(g, "shot", scatter_dimension=1, tiled=True)
    block = g.shape[1] // 2
    low, high = g[:, :block], g[:, block:]
    first = lax.axis_index("shot") == 0
    other = lax.ppermute(jnp.where(first, high, low), "shot", [(0, 1), (1, 0)])
    return jnp.where(first, low, high) + other


def snake_of(slabs):
    row = slabs // 4
    if slabs % 8:
        return list(range(slabs))
    order = []
    for i in range(slabs):
        z, (chip, core) = i // row, divmod(i % row, 2)
        order.append(z * row + 2 * (row // 2 - 1 - chip if z % 2 else chip) + core)
    return order


def on_device(fwd_last, fwd_prev, velocity, aperture, rec_index, src_index, residual):
    _, depth, width_x, width_y = fwd_last.shape
    parts = width_x // SUB
    total_steps, receivers = residual.shape[1:]
    plane = width_x * width_y
    slabs = lax.axis_size("slab")
    f32 = jnp.float32
    place = snake_of(slabs)
    at = lax.axis_index("slab")
    snake = place != list(range(slabs))
    shot = lax.axis_index("shot")
    halves = snake and lax.axis_size("shot") == 2
    slab = at
    if snake:
        row = slabs // 4
        z, chip, core = at // row, at % row // 2, at % 2
        slab = z * row + 2 * jnp.where(z % 2 == 1, row // 2 - 1 - chip, chip) + core
    up = [(place[i], place[i + 1]) for i in range(slabs - 1)]
    down = [(place[i + 1], place[i]) for i in range(slabs - 1)]
    swap = [(i, place[i]) for i in range(slabs)]
    half = depth // 2
    if halves:
        mine = jnp.where(shot == 0, velocity[:half], velocity[half:])
        mine = lax.ppermute(mine, "slab", swap)
        speeds = (mine, lax.ppermute(mine, "shot", [(0, 1), (1, 0)]))
    else:
        speeds = (lax.ppermute(velocity, "slab", swap) if snake else velocity,)
    speed_left = lax.ppermute(velocity[depth - SHIFT :], "slab", [(i, place[i + 1]) for i in range(slabs - 1)])
    if snake:
        fwd_prev = lax.ppermute(fwd_prev, "slab", swap)
        fwd_last = lax.ppermute(fwd_last, "slab", swap)

    base = (slab * depth - SHIFT) * plane
    window = (depth + SHIFT) * plane
    local = rec_index[0] - base
    far = jnp.int32(2**30)
    keys = jnp.where((local >= 0) & (local < window), local, far)
    keys, ids = lax.sort((keys, lax.iota(jnp.int32, receivers)), num_keys=1, is_stable=False)

    def place_of(cell):
        layer = cell // plane
        x = (cell // width_y) % width_x
        return layer, x % parts, x // parts, cell % width_y

    layer, part, row, lane = place_of(keys)
    rows_of = (layer * parts + part) * SUB + row
    zones = (depth + SHIFT) // REACH
    edges = jnp.arange(zones + 1, dtype=jnp.int32) * (REACH * plane)
    starts = jnp.sum((keys[None, :] < edges[:, None]).astype(jnp.int32), axis=1)

    src = src_index[0] - base
    src_in = (src >= 0) & (src < window)
    s_layer, s_part, s_row, s_lane = place_of(jnp.where(src_in, src, 0))
    s_layer = jnp.where(src_in, s_layer, -1)
    is_last = (slab == slabs - 1).astype(jnp.int32)
    scalars = [is_last, s_layer, s_part, s_row, s_lane]
    gap = [jnp.zeros((), jnp.int32)] * (SHOT - STARTS - zones - 1)
    info = jnp.concatenate([jnp.stack(scalars), starts, jnp.stack([*gap, shot]), rows_of])
    last_step = total_steps - 1

    smem = pl.BlockSpec(memory_space=pltpu.SMEM)
    vmem = pl.BlockSpec(memory_space=pltpu.VMEM)
    anym = pl.BlockSpec(memory_space=pltpu.HBM)

    def fields(layers):
        return jax.ShapeDtypeStruct((layers, parts, SUB, width_y), f32)

    params = pltpu.CompilerParams(vmem_limit_bytes=VMEM_BYTES)
    once = pltpu.CompilerParams(vmem_limit_bytes=MORE_BYTES)
    fetch_scratch = [pltpu.VMEM((receivers, width_y), f32), pltpu.SemaphoreType.DMA(())]

    def lane_scratch(layers):
        rows = layers * parts * SUB
        return [
            pltpu.VMEM((rows, PIECES * width_y), jnp.bfloat16),
            pltpu.VMEM((rows, width_y), f32),
        ]

    block_scratch = [pltpu.VMEM((SPAN, parts, SUB, width_y), f32)] * 4 + lane_scratch(2 * SHIFT)

    def cost(layers):
        return pl.CostEstimate(
            flops=50 * layers * plane, bytes_accessed=24 * layers * plane, transcendentals=0
        )

    near, table = pl.pallas_call(
        functools.partial(table_kernel, zones),
        out_shape=(
            jax.ShapeDtypeStruct((total_steps, CHUNK, width_y), f32),
            jax.ShapeDtypeStruct((total_steps, receivers, width_y), f32),
        ),
        in_specs=[smem] + [vmem] * 5,
        out_specs=(vmem, anym),
        scratch_shapes=[
            pltpu.VMEM((receivers // CHUNK, PIECES, total_steps, CHUNK), f32),
            pltpu.VMEM((PIECES * total_steps, receivers), jnp.bfloat16),
            pltpu.VMEM((CHUNK, CHUNK), jnp.bfloat16),
            pltpu.VMEM((total_steps, CHUNK, width_y), f32),
            pltpu.SemaphoreType.DMA(()),
        ],
        compiler_params=once,
        cost_estimate=cost(SHIFT),
        name="rec_table",
    )(
        info,
        ids.reshape(receivers // CHUNK, CHUNK),
        rows_of.reshape(receivers // CHUNK, CHUNK),
        rows_of[:, None],
        lane[:, None],
        residual[0],
    )
    coef, weights = pl.pallas_call(
        functools.partial(first_coef_kernel, halves),
        out_shape=(
            fields(depth + SHIFT),
            jax.ShapeDtypeStruct((PIECES * width_y, width_y), jnp.bfloat16),
        ),
        in_specs=[smem] + [vmem] * (len(speeds) + 1),
        out_specs=[vmem] * 2,
        compiler_params=once,
        cost_estimate=cost(2),
        name="first_coef",
    )(info, *speeds, speed_left)
    lm, lr, work = pl.pallas_call(
        functools.partial(first_l_kernel, last_step),
        out_shape=(fields(MSG), fields(REST), fields(WORK_ALL)),
        in_specs=[smem, vmem, anym, vmem],
        out_specs=(vmem, vmem, vmem),
        scratch_shapes=fetch_scratch,
        compiler_params=once,
        cost_estimate=cost(2),
        name="first_l",
    )(info, near, table, coef)
    l_got = lax.ppermute(lm, "slab", up)

    def between(side, n0, *arrays):
        outs = [fields(WORK_ALL), fields(depth + SHIFT)]
        scratch = list(fetch_scratch)
        if n0 == 3:
            outs.append(fields(SHIFT))
        if n0 == last_step:
            scratch = [pltpu.VMEM((depth + SHIFT, parts, SUB, width_y), f32)] + scratch
        return pl.pallas_call(
            functools.partial(between_kernel, side, n0, last_step),
            out_shape=outs,
            in_specs=[smem, vmem, anym] + [vmem] * len(arrays),
            out_specs=[vmem] * len(outs),
            scratch_shapes=scratch,
            compiler_params=params,
            cost_estimate=cost(SHIFT),
            name=f"between{side}",
        )(info, near, table, *arrays)

    fwd_prev, fwd_last, _ = lax.optimization_barrier((fwd_prev, fwd_last, work))
    um, ur, ub = pl.pallas_call(
        functools.partial(first_u_kernel, last_step),
        out_shape=(fields(MSG + REACH), fields(REST), fields(MSG)),
        in_specs=[smem] + [vmem] * 4,
        out_specs=[vmem] * 3,
        scratch_shapes=[pltpu.VMEM((depth, parts, SUB, width_y), f32)] * 2 + lane_scratch(SHIFT),
        compiler_params=once,
        cost_estimate=cost(SHIFT),
        name="first_u",
    )(info, fwd_prev[0], fwd_last[0], coef, weights)
    u_got = lax.ppermute(um, "slab", up)
    opening = (lm, um, ur)
    lb = lr

    def block(is_l, side, n0, own, rest, recv, beyond, *work):
        outs = []
        if n0 > 1:
            outs = [fields(MSG), fields(REST)] + ([fields(MSG)] if side == 0 else [])
        elif is_l:
            outs = [jax.ShapeDtypeStruct((depth, width_x, width_y), f32)]
        outs.append(fields(WORK_ALL))
        return pl.pallas_call(
            functools.partial(block_kernel, side, is_l, n0, n0 == last_step),
            out_shape=outs,
            in_specs=[smem] + [vmem] * (6 + len(work)),
            out_specs=[vmem] * len(outs),
            scratch_shapes=block_scratch,
            compiler_params=params,
            cost_estimate=cost(2 * depth),
            name=("l" if is_l else "u") + f"_block{side}",
        )(info, own, rest, recv, coef, weights, beyond, *work)

    terms_in = opening
    for n0 in range(last_step, 0, -2):
        side = (last_step - n0) // 2 % 2
        way = up if side else down
        if n0 == 1:
            adjoint_field, d = block(True, side, n0, lm, lr, l_got, lb, work)
            if snake:
                adjoint_field = lax.ppermute(adjoint_field, "slab", swap)
            (x,) = block(False, side, n0, um, ur, u_got, ub)
            break
        lm, lr, *lb_new, d = block(True, side, n0, lm, lr, l_got, lb, work)
        lb = lb_new[0] if lb_new else lb
        l_got = lax.ppermute(lm, "slab", way)
        um, ur, *ub_new, x = block(False, side, n0, um, ur, u_got, ub)
        ub = ub_new[0] if ub_new else ub
        u_got = lax.ppermute(um, "slab", way)
        work, g, *g_left = between(side, n0, *terms_in, x, d)
        terms_in = (g,)
    g_right = lax.ppermute(g_left[0], "slab", down)

    terms = pl.pallas_call(
        last_kernel,
        out_shape=jax.ShapeDtypeStruct((depth, width_x, width_y), f32),
        in_specs=[smem] + [vmem] * 5,
        out_specs=vmem,
        scratch_shapes=[pltpu.VMEM((depth + SHIFT, parts, SUB, width_y), f32)],
        compiler_params=once,
        cost_estimate=cost(SHIFT),
        name="last_terms",
    )(info, g, x, d, g_right, aperture)
    summed = sum_shots(terms)
    if snake:
        summed = lax.ppermute(summed, "slab", swap)
    block = width_x // lax.axis_size("shot")
    speed = lax.dynamic_slice_in_dim(velocity, shot * block, block, 1)
    return ((-2.0 / speed) * summed, adjoint_field[None])


def solution(mesh):
    in_specs = (
        P("shot", "slab", None, None),
        P("shot", "slab", None, None),
        P("slab", None, None),
        P("shot", None, None),
        P("shot", None),
        P("shot"),
        P("shot", None, None),
    )
    out_specs = (P("slab", "shot", None), P("shot", "slab", None, None))
    return jax.shard_map(on_device, mesh=mesh, in_specs=in_specs, out_specs=out_specs, check_vma=False)
```

```python
import functools

import jax
import jax.numpy as jnp
import numpy as np
from jax import lax
from jax.experimental import pallas as pl
from jax.experimental.pallas import tpu as pltpu
from jax.sharding import PartitionSpec as P

SCALE = 5040.0
WHOLE = (-14350.0, 8064.0, -1008.0, 128.0, -9.0)
REACH = 4
SHIFT = 8
VMEM_BYTES = 14 * 1024 * 1024
MORE_BYTES = 24 * 1024 * 1024
SUB = 8
PIECES = 3
CHUNK = 256

MSG = 2 * SHIFT
REST = 2 * SHIFT
WORK = 4 * SHIFT
WORK_ALL = 6 * SHIFT
SPAN = 32
MID = 12


def wave_of(step):
    arg = (np.pi * 0.06 * (step - 10.0)) ** 2
    return float(np.float32(SCALE * 10.0 * (1.0 - 2.0 * arg) * np.exp(-arg)))


def load_tiled(field, layer):
    parts = field.shape[1] // SUB
    return jnp.stack([field[layer, pl.ds(m, SUB, stride=parts), :] for m in range(parts)])


def store_tiled(field, layer, value, first=0, count=SUB):
    parts = value.shape[0]
    for m in range(parts):
        field[layer, pl.ds(m, count, stride=parts), :] = value[m, first : first + count]


def split3(f):
    hi = f.astype(jnp.bfloat16)
    left = f - hi.astype(jnp.float32)
    mid = left.astype(jnp.bfloat16)
    return hi, mid, (left - mid.astype(jnp.float32)).astype(jnp.bfloat16)


def put_weights(weights):
    width_y = weights.shape[1]
    square = (width_y, width_y)
    away = jnp.abs(lax.broadcasted_iota(jnp.int32, square, 0) - lax.broadcasted_iota(jnp.int32, square, 1))
    once = jnp.zeros(square, jnp.float32)
    for k in range(1, 5):
        once = jnp.where(away == k, WHOLE[k], once)
    for i in range(PIECES):
        weights[i * width_y : (i + 1) * width_y, :] = once.astype(jnp.bfloat16)


def lane_pass(cur, first, count, weights, pieces, ybuf):
    parts, _, width_y = cur.shape[1:]
    rows = parts * SUB

    def one(q):
        at = pl.multiple_of(q * rows, rows)
        for i, piece in enumerate(split3(cur[first + q].reshape(rows, width_y))):
            pieces[pl.ds(at, rows), i * width_y : (i + 1) * width_y] = piece

    layers_loop(0, count, one)
    for q in range(0, count, SHIFT):
        block = slice(q * rows, min(q + SHIFT, count) * rows)
        ybuf[block, :] = jnp.dot(pieces[block, :], weights[...], preferred_element_type=jnp.float32)


def lap_maker(parts, width_y):
    row = lax.broadcasted_iota(jnp.int32, (1, SUB, width_y), 1)

    def lap(ref, j, along):
        f = ref[j]
        after = jnp.where(row == SUB - 1, 0.0, pltpu.roll(f[:REACH], SUB - 1, 1))
        before = jnp.where(row == 0, 0.0, pltpu.roll(f[parts - REACH :], 1, 1))
        wide = jnp.concatenate([before, f, after], axis=0)
        total = along + (3.0 * WHOLE[0]) * f
        for k in range(1, 5):
            pair = (ref[j + k] + ref[j - k]) + (
                wide[REACH + k : REACH + k + parts] + wide[REACH - k : REACH - k + parts]
            )
            total = total + WHOLE[k] * pair
        return f, total

    return lap


def layers_loop(first, count, body):
    def one(q, carry):
        body(first + q)
        return carry

    lax.fori_loop(0, count, one, 0, unroll=2)


STARTS = 5
SHOT = 15
ROWS = 16


def inject(work, at, info, near, table_hbm, table, sem, step, first, last):
    low, high = info[STARTS + first], info[STARTS + last]
    rows = work.shape[1] * SUB
    shift = at * rows - first * REACH * rows
    flat = work.reshape(work.shape[0] * rows, work.shape[3])

    def store(low, high, row_of):
        def one(r, carry):
            flat[pl.ds(info[ROWS + r] + shift, 1), :] = row_of(r)
            return carry

        def eight(i, carry):
            for q in range(8):
                one(low + i * 8 + q, carry)
            return carry

        groups = lax.shift_right_logical(high - low, 3)
        lax.fori_loop(0, groups, eight, 0)
        lax.fori_loop(low + groups * 8, high, one, 0)

    split = jnp.clip(CHUNK, low, high)
    store(low, split, lambda r: near[step, pl.ds(r, 1), :])

    @pl.when(high > split)
    def _():
        fetch = pltpu.make_async_copy(table_hbm.at[step], table, sem)
        fetch.start()
        fetch.wait()
        store(split, high, lambda r: table[pl.ds(r, 1), :])


def zones_of(side):
    return (1, 0, 1) if side == 0 else (3, 2, 3)


def put_rows(work, side, n0, info, near, table_hbm, table, sem):
    shared = (info, near, table_hbm, table, sem)
    zero = jnp.zeros((SHIFT,) + work.shape[1:], jnp.float32)
    for i in range(0, WORK, SHIFT):
        work[i : i + SHIFT] = zero
    for level, (at, zone, count) in enumerate(zip((0, 8, 24), zones_of(side), (2, 4, 2))):
        if n0 >= level:
            inject(work, at, *shared, n0 - level, zone, zone + count)
    if side == 0:

        @pl.when(info[0] == 1)
        def _():
            for i in range(WORK, WORK_ALL, SHIFT):
                work[i : i + SHIFT] = zero
            for level, (at, zone, count) in enumerate(((32, 5, 1), (36, 4, 2), (44, 5, 1))):
                if n0 >= level:
                    inject(work, at, *shared, n0 - level, zone, zone + count)


def add_terms(g, g_in, side, n0, is_last, x, d):
    low = 0 if side == 0 else SHIFT
    more = n0 >= 2

    def edge(at):
        def one(q):
            g[low + at + q] = g_in[low + at + q] + x[SHIFT + at + q] * d[SHIFT + at + q]

        layers_loop(0, REACH, one)

    def middle(q):
        total = x[q] * d[q] + x[SHIFT + REACH + q] * d[SHIFT + REACH + q]
        if more:
            total = total + x[3 * SHIFT + q] * d[3 * SHIFT + q]
        g[low + REACH + q] = g_in[low + REACH + q] + total

    edge(0)
    layers_loop(0, SHIFT, middle)
    edge(SHIFT + REACH)
    if side == 1:
        g[0:SHIFT] = g_in[0:SHIFT]
        return
    g[2 * SHIFT : 3 * SHIFT] = g_in[2 * SHIFT : 3 * SHIFT]

    @pl.when(is_last == 1)
    def _():
        for q in range(SHIFT):
            total = x[36 + q] * d[36 + q]
            if q >= REACH:
                total = total + x[28 + q] * d[28 + q]
                if more:
                    total = total + x[40 + q] * d[40 + q]
            g[2 * SHIFT + q] = g[2 * SHIFT + q] + total


def between_kernel(side, n0, opening, info, near, table_hbm, *refs):
    if n0 == opening:
        l_msg, u_msg, u_rest, x, d, work, g, start, table, sem = refs
        start[...] = jnp.zeros(start.shape, jnp.float32)
        for z in range(REACH, REACH + SHIFT):
            was = u_rest[z] if z < SHIFT else u_msg[z - SHIFT]
            start[z + SHIFT] = was * l_msg[z - REACH + SHIFT]
        g_in = start
    else:
        g_in, x, d, work, g, *g_left, table, sem = refs
    add_terms(g, g_in, side, n0, info[0], x, d)
    if n0 == 3:
        g_left[0][...] = g[0:SHIFT]
    put_rows(work, 1 - side, n0 - 2, info, near, table_hbm, table, sem)


def chunks_of(info, zones):
    return jnp.maximum((info[STARTS + zones] + CHUNK - 1) // CHUNK, 1)


def table_kernel(zones, info, ids, rows_l, rows_s, lanes_s, res, near, out, res_cut, pieces, same, part, sem):
    steps, receivers = res.shape
    width_y = part.shape[2]
    chunks = chunks_of(info, zones)
    for i, piece in enumerate(split3(res[...])):
        pieces[i * steps : (i + 1) * steps, :] = piece

    def column(c, carry):
        who = lax.broadcasted_iota(jnp.int32, (receivers, CHUNK), 0) == ids[pl.ds(c, 1), :]
        moved = jnp.dot(
            pieces[...], jnp.where(who, 1.0, 0.0).astype(jnp.bfloat16), preferred_element_type=jnp.float32
        )
        total = SCALE * ((moved[:steps] + moved[steps : 2 * steps]) + moved[2 * steps :])
        for i, piece in enumerate(split3(total)):
            res_cut[c, i] = piece.astype(jnp.float32)
        return carry

    lax.fori_loop(0, chunks, column, 0)

    def to_chunk(c, carry):
        mine = rows_s[pl.ds(pl.multiple_of(c * CHUNK, CHUNK), CHUNK), :]

        def from_chunk(d, carry):
            same[...] = jnp.where(mine == rows_l[pl.ds(d, 1), :], 1.0, 0.0).astype(jnp.bfloat16)
            at = pl.multiple_of(d * CHUNK, CHUNK)
            lane = lax.broadcasted_iota(jnp.int32, (CHUNK, width_y), 1)
            spot = jnp.where(lane == lanes_s[pl.ds(at, CHUNK), :], 1.0, 0.0).astype(jnp.bfloat16)
            spots = jnp.concatenate([spot] * PIECES, axis=0)

            def one(n, carry):
                mixed = []
                for i in range(PIECES):
                    row = jnp.broadcast_to(res_cut[d, i, pl.ds(n, 1), :], (16, CHUNK)).astype(jnp.bfloat16)
                    mixed.append((same[...].reshape(CHUNK // 16, 16, CHUNK) * row[None]).reshape(CHUNK, CHUNK))
                total = jnp.dot(
                    jnp.concatenate(mixed, axis=1), spots, preferred_element_type=jnp.float32
                )
                part[n] = total + jnp.where(d > 0, part[n], 0.0)
                return carry

            return lax.fori_loop(0, steps, one, carry, unroll=4)

        lax.fori_loop(0, chunks, from_chunk, 0)
        return carry

    def store_chunk(c, carry):
        to_chunk(c, 0)
        at = pl.multiple_of(c * CHUNK, CHUNK)
        write = pltpu.make_async_copy(part, out.at[:, pl.ds(at, CHUNK), :], sem)
        write.start()
        write.wait()
        return carry

    to_chunk(0, 0)
    near[...] = part[...]
    lax.fori_loop(1, chunks, store_chunk, 0)


def block_kernel(side, is_l, n0, opening, *refs):
    refs = list(refs)

    def take(count):
        got = refs[:count]
        del refs[:count]
        return got

    final = n0 == 1
    info, own, rest, recv, coef, weights, beyond = take(7)
    work_in = msg_out = rest_out = beyond_out = field_out = None
    if is_l:
        (work_in,) = take(1)
    if not final:
        msg_out, rest_out = take(2)
        if side == 0:
            (beyond_out,) = take(1)
    elif is_l:
        (field_out,) = take(1)
    work_out, a, b, c, p, pieces, ybuf = take(7)

    parts, _, width_y = a.shape[1:]
    rows = parts * SUB
    is_last, src_layer, src_part, src_row, src_lane = (info[i] for i in range(STARTS))
    off = MID - SHIFT if side == 0 else MID - 2 * SHIFT
    lap = lap_maker(parts, width_y)

    def bring(msg, low):
        if low:
            a[MID - SHIFT : MID] = msg[0:SHIFT]
            b[MID - SHIFT - REACH : MID - REACH] = msg[SHIFT:MSG]
        else:
            a[MID : MID + SHIFT] = msg[0:SHIFT]
            b[MID + REACH : MID + REACH + SHIFT] = msg[SHIFT:MSG]

    p[MID - REACH : MID + REACH] = rest[SHIFT:REST]
    if side == 0:
        bring(recv, True)
        a[MID : MID + SHIFT] = rest[0:SHIFT]
        b[MID + REACH : MID + REACH + SHIFT] = own[SHIFT:MSG]
        if opening and not is_l:
            p[MID - REACH : MID] = recv[MSG : MSG + REACH]

        @pl.when(is_last == 1)
        def _():
            zero = jnp.zeros((REACH,) + a.shape[1:], jnp.float32)
            a[MID + SHIFT : MID + 2 * SHIFT] = own[0:SHIFT]
            p[MID + SHIFT + REACH : MID + 2 * SHIFT] = beyond[SHIFT : SHIFT + REACH]
            for field in (a, b, c):
                field[MID + 2 * SHIFT : MID + 2 * SHIFT + REACH] = zero
    else:
        a[MID - SHIFT : MID] = rest[0:SHIFT]
        b[MID - SHIFT - REACH : MID - REACH] = own[SHIFT:MSG]

        @pl.when(is_last == 1)
        def _():
            bring(beyond, False)

        @pl.when(is_last == 0)
        def _():
            bring(recv, False)

    def source(nxt, level, first, count):
        j = src_layer + off

        @pl.when((src_layer >= 0) & (j >= first) & (j < first + count))
        def _():
            lane = lax.broadcasted_iota(jnp.int32, (1, width_y), 1)
            spot = nxt[j, src_part, pl.ds(src_row, 1), :]
            gain = coef[src_layer, src_part, pl.ds(src_row, 1), :] * wave_of(n0 - level)
            nxt[j, src_part, pl.ds(src_row, 1), :] = spot - jnp.where(lane == src_lane, gain, 0.0)

    def advance(level, cur, nxt, first, count, work_at, out, shift):
        if not is_l:
            source(nxt, level, first, count)
        lane_pass(cur, first, count, weights, pieces, ybuf)

        def body(j):
            y_at = pl.multiple_of((j - first) * rows, rows)
            f, total = lap(cur, j, ybuf[pl.ds(y_at, rows), :].reshape(parts, SUB, width_y))
            if is_l:
                total = total + work_in[j + (work_at - first)]
            step = coef[j - off] * total
            out[j + shift] = (2.0 * f - nxt[j]) + step
            work_out[j + (work_at - first)] = step if is_l else f

        layers_loop(first, count, body)

    def beyond_too(*args):
        if side == 0:

            @pl.when(is_last == 1)
            def _():
                advance(*args)

    advance(0, a, p, MID - REACH, SHIFT, 0, b, 0)
    beyond_too(0, a, p, MID + SHIFT + REACH, REACH, 32, b, 0)
    advance(1, b, a, MID - SHIFT, 2 * SHIFT, 8, c, 0)
    beyond_too(1, b, a, MID + SHIFT, SHIFT, 36, c, 0)
    if final:
        if is_l:
            for layer in range(2 * SHIFT):
                store_tiled(field_out, layer, c[MID - SHIFT + layer])
        return
    advance(2, c, b, MID - REACH, SHIFT, 24, msg_out, SHIFT - (MID - REACH))
    if side == 0:
        msg_out[0:SHIFT] = c[MID - SHIFT : MID]
        rest_out[0:SHIFT] = c[MID : MID + SHIFT]
        rest_out[SHIFT:REST] = b[MID + REACH : MID + REACH + SHIFT]

        @pl.when(is_last == 1)
        def _():
            first = MID + SHIFT + REACH
            advance(2, c, b, first, REACH, 44, beyond_out, SHIFT - first)
            beyond_out[0:SHIFT] = c[MID + SHIFT : MID + 2 * SHIFT]
            beyond_out[SHIFT + REACH : MSG] = jnp.zeros((REACH,) + a.shape[1:], jnp.float32)
    else:
        msg_out[0:SHIFT] = c[MID : MID + SHIFT]
        rest_out[0:SHIFT] = c[MID - SHIFT : MID]
        rest_out[SHIFT:REST] = b[MID - SHIFT - REACH : MID - REACH]


def first_coef_kernel(halves, info, *refs):
    *speeds, speed_left, coef, weights = refs
    put_weights(weights)

    def fill(speed, first):
        def one(z):
            coef[z + first] = (0.4 * load_tiled(speed, z)) ** 2 * (1.0 / SCALE)

        layers_loop(0, speed.shape[0], one)

    fill(speed_left, 0)
    if not halves:
        fill(speeds[0], SHIFT)
        return
    depth = speeds[0].shape[0]

    @pl.when(info[SHOT] == 0)
    def _():
        fill(speeds[0], SHIFT)
        fill(speeds[1], SHIFT + depth)

    @pl.when(info[SHOT] != 0)
    def _():
        fill(speeds[1], SHIFT)
        fill(speeds[0], SHIFT + depth)


def first_u_kernel(n0, info, prev, last, coef, weights, msg_out, rest_out, beyond, f0, f1, pieces, ybuf):
    depth, parts, _, width_y = f0.shape
    rows = parts * SUB
    src_layer, src_part, src_row, src_lane = (info[i] for i in range(1, STARTS))
    lap = lap_maker(parts, width_y)

    def bring(z):
        f0[z] = load_tiled(prev, z)
        f1[z] = load_tiled(last, z)

    layers_loop(0, depth, bring)
    msg_out[0:SHIFT] = f0[depth - SHIFT : depth]
    msg_out[MSG : MSG + REACH] = f1[depth - REACH : depth]
    rest_out[0:SHIFT] = f0[0:SHIFT]
    rest_out[SHIFT : SHIFT + REACH] = jnp.zeros((REACH,) + f0.shape[1:], jnp.float32)
    rest_out[SHIFT + REACH : REST] = f1[0:REACH]
    beyond[...] = jnp.zeros(beyond.shape, jnp.float32)
    beyond[SHIFT : SHIFT + REACH] = f1[depth - REACH : depth]
    lane_pass(f0, REACH, SHIFT, weights, pieces, ybuf)
    to = SHIFT - REACH

    def body(j):
        y_at = pl.multiple_of((j - REACH) * rows, rows)
        f, total = lap(f0, j, ybuf[pl.ds(y_at, rows), :].reshape(parts, SUB, width_y))
        msg_out[j + to] = (2.0 * f - f1[j]) + coef[j + SHIFT] * total

    layers_loop(REACH, SHIFT, body)
    j = src_layer - SHIFT

    @pl.when((src_layer >= 0) & (j >= REACH) & (j < REACH + SHIFT))
    def _():
        lane = lax.broadcasted_iota(jnp.int32, (1, width_y), 1)
        spot = msg_out[j + to, src_part, pl.ds(src_row, 1), :]
        gain = coef[src_layer, src_part, pl.ds(src_row, 1), :] * wave_of(n0)
        msg_out[j + to, src_part, pl.ds(src_row, 1), :] = spot + jnp.where(lane == src_lane, gain, 0.0)


def first_l_kernel(n0, info, near, table_hbm, coef, msg_out, rest_out, work, table, sem):
    msg_out[...] = jnp.zeros(msg_out.shape, jnp.float32)
    rest_out[...] = jnp.zeros(rest_out.shape, jnp.float32)
    zone = (SHIFT + REACH) // REACH
    inject(msg_out, SHIFT, info, near, table_hbm, table, sem, n0, zone, zone + SHIFT // REACH)

    def body(q):
        msg_out[q + SHIFT] = coef[q + SHIFT + REACH] * msg_out[q + SHIFT]

    layers_loop(0, SHIFT, body)
    put_rows(work, 0, n0, info, near, table_hbm, table, sem)


def last_kernel(info, g_in, x, d, g_right, gate, out, g):
    depth = out.shape[0]
    add_terms(g, g_in, 1, 1, info[0], x, d)

    def one(z):
        store_tiled(out, z, load_tiled(gate, 0).astype(jnp.float32) * g[z + SHIFT])

    def shared(z):
        store_tiled(out, z, load_tiled(gate, 0).astype(jnp.float32) * (g[z + SHIFT] + g_right[z - SHIFT]))

    layers_loop(0, SHIFT, one)
    layers_loop(SHIFT, depth - SHIFT, shared)


def sum_shots(g):
    shots = lax.axis_size("shot")
    if shots != 2:
        return lax.psum_scatter(g, "shot", scatter_dimension=1, tiled=True)
    block = g.shape[1] // 2
    low, high = g[:, :block], g[:, block:]
    first = lax.axis_index("shot") == 0
    other = lax.ppermute(jnp.where(first, high, low), "shot", [(0, 1), (1, 0)])
    return jnp.where(first, low, high) + other


def snake_of(slabs):
    row = slabs // 4
    if slabs % 8:
        return list(range(slabs))
    order = []
    for i in range(slabs):
        z, (chip, core) = i // row, divmod(i % row, 2)
        order.append(z * row + 2 * (row // 2 - 1 - chip if z % 2 else chip) + core)
    return order


def on_device(fwd_last, fwd_prev, velocity, aperture, rec_index, src_index, residual):
    _, depth, width_x, width_y = fwd_last.shape
    parts = width_x // SUB
    total_steps, receivers = residual.shape[1:]
    plane = width_x * width_y
    slabs = lax.axis_size("slab")
    f32 = jnp.float32
    place = snake_of(slabs)
    at = lax.axis_index("slab")
    snake = place != list(range(slabs))
    shot = lax.axis_index("shot")
    halves = snake and lax.axis_size("shot") == 2
    slab = at
    if snake:
        row = slabs // 4
        z, chip, core = at // row, at % row // 2, at % 2
        slab = z * row + 2 * jnp.where(z % 2 == 1, row // 2 - 1 - chip, chip) + core
    up = [(place[i], place[i + 1]) for i in range(slabs - 1)]
    down = [(place[i + 1], place[i]) for i in range(slabs - 1)]
    swap = [(i, place[i]) for i in range(slabs)]
    half = depth // 2
    if snake:
        fwd_prev = lax.ppermute(fwd_prev, "slab", swap)
        fwd_last = lax.ppermute(fwd_last, "slab", swap)
    if halves:
        mine = jnp.where(shot == 0, velocity[:half], velocity[half:])
        mine = lax.ppermute(mine, "slab", swap)
        theirs = lax.ppermute(mine, "shot", [(0, 1), (1, 0)])
        speeds = (mine, theirs)
        upper = jnp.where(shot == 0, theirs, mine)[half - SHIFT :]
    else:
        speeds = (lax.ppermute(velocity, "slab", swap) if snake else velocity,)
        upper = speeds[0][depth - SHIFT :]
    speed_left = lax.ppermute(upper, "slab", up)

    base = (slab * depth - SHIFT) * plane
    window = (depth + SHIFT) * plane
    local = rec_index[0] - base
    far = jnp.int32(2**30)
    keys = jnp.where((local >= 0) & (local < window), local, far)
    keys, ids = lax.sort((keys, lax.iota(jnp.int32, receivers)), num_keys=1, is_stable=False)

    def place_of(cell):
        layer = cell // plane
        x = (cell // width_y) % width_x
        return layer, x % parts, x // parts, cell % width_y

    layer, part, row, lane = place_of(keys)
    rows_of = (layer * parts + part) * SUB + row
    zones = (depth + SHIFT) // REACH
    edges = jnp.arange(zones + 1, dtype=jnp.int32) * (REACH * plane)
    starts = jnp.sum((keys[None, :] < edges[:, None]).astype(jnp.int32), axis=1)

    src = src_index[0] - base
    src_in = (src >= 0) & (src < window)
    s_layer, s_part, s_row, s_lane = place_of(jnp.where(src_in, src, 0))
    s_layer = jnp.where(src_in, s_layer, -1)
    is_last = (slab == slabs - 1).astype(jnp.int32)
    scalars = [is_last, s_layer, s_part, s_row, s_lane]
    gap = [jnp.zeros((), jnp.int32)] * (SHOT - STARTS - zones - 1)
    info = jnp.concatenate([jnp.stack(scalars), starts, jnp.stack([*gap, shot]), rows_of])
    last_step = total_steps - 1

    smem = pl.BlockSpec(memory_space=pltpu.SMEM)
    vmem = pl.BlockSpec(memory_space=pltpu.VMEM)
    anym = pl.BlockSpec(memory_space=pltpu.HBM)

    def fields(layers):
        return jax.ShapeDtypeStruct((layers, parts, SUB, width_y), f32)

    params = pltpu.CompilerParams(vmem_limit_bytes=VMEM_BYTES)
    once = pltpu.CompilerParams(vmem_limit_bytes=MORE_BYTES)
    fetch_scratch = [pltpu.VMEM((receivers, width_y), f32), pltpu.SemaphoreType.DMA(())]

    def lane_scratch(layers):
        rows = layers * parts * SUB
        return [
            pltpu.VMEM((rows, PIECES * width_y), jnp.bfloat16),
            pltpu.VMEM((rows, width_y), f32),
        ]

    block_scratch = [pltpu.VMEM((SPAN, parts, SUB, width_y), f32)] * 4 + lane_scratch(2 * SHIFT)

    def cost(layers):
        return pl.CostEstimate(
            flops=50 * layers * plane, bytes_accessed=24 * layers * plane, transcendentals=0
        )

    near, table = pl.pallas_call(
        functools.partial(table_kernel, zones),
        out_shape=(
            jax.ShapeDtypeStruct((total_steps, CHUNK, width_y), f32),
            jax.ShapeDtypeStruct((total_steps, receivers, width_y), f32),
        ),
        in_specs=[smem] + [vmem] * 5,
        out_specs=(vmem, anym),
        scratch_shapes=[
            pltpu.VMEM((receivers // CHUNK, PIECES, total_steps, CHUNK), f32),
            pltpu.VMEM((PIECES * total_steps, receivers), jnp.bfloat16),
            pltpu.VMEM((CHUNK, CHUNK), jnp.bfloat16),
            pltpu.VMEM((total_steps, CHUNK, width_y), f32),
            pltpu.SemaphoreType.DMA(()),
        ],
        compiler_params=once,
        cost_estimate=cost(SHIFT),
        name="rec_table",
    )(
        info,
        ids.reshape(receivers // CHUNK, CHUNK),
        rows_of.reshape(receivers // CHUNK, CHUNK),
        rows_of[:, None],
        lane[:, None],
        residual[0],
    )
    coef, weights = pl.pallas_call(
        functools.partial(first_coef_kernel, halves),
        out_shape=(
            fields(depth + SHIFT),
            jax.ShapeDtypeStruct((PIECES * width_y, width_y), jnp.bfloat16),
        ),
        in_specs=[smem] + [vmem] * (len(speeds) + 1),
        out_specs=[vmem] * 2,
        compiler_params=once,
        cost_estimate=cost(2),
        name="first_coef",
    )(info, *speeds, speed_left)
    lm, lr, work = pl.pallas_call(
        functools.partial(first_l_kernel, last_step),
        out_shape=(fields(MSG), fields(REST), fields(WORK_ALL)),
        in_specs=[smem, vmem, anym, vmem],
        out_specs=(vmem, vmem, vmem),
        scratch_shapes=fetch_scratch,
        compiler_params=once,
        cost_estimate=cost(2),
        name="first_l",
    )(info, near, table, coef)
    l_got = lax.ppermute(lm, "slab", up)

    def between(side, n0, *arrays):
        outs = [fields(WORK_ALL), fields(depth + SHIFT)]
        scratch = list(fetch_scratch)
        if n0 == 3:
            outs.append(fields(SHIFT))
        if n0 == last_step:
            scratch = [pltpu.VMEM((depth + SHIFT, parts, SUB, width_y), f32)] + scratch
        return pl.pallas_call(
            functools.partial(between_kernel, side, n0, last_step),
            out_shape=outs,
            in_specs=[smem, vmem, anym] + [vmem] * len(arrays),
            out_specs=[vmem] * len(outs),
            scratch_shapes=scratch,
            compiler_params=params,
            cost_estimate=cost(SHIFT),
            name=f"between{side}",
        )(info, near, table, *arrays)

    fwd_prev, fwd_last, _ = lax.optimization_barrier((fwd_prev, fwd_last, work))
    um, ur, ub = pl.pallas_call(
        functools.partial(first_u_kernel, last_step),
        out_shape=(fields(MSG + REACH), fields(REST), fields(MSG)),
        in_specs=[smem] + [vmem] * 4,
        out_specs=[vmem] * 3,
        scratch_shapes=[pltpu.VMEM((depth, parts, SUB, width_y), f32)] * 2 + lane_scratch(SHIFT),
        compiler_params=once,
        cost_estimate=cost(SHIFT),
        name="first_u",
    )(info, fwd_prev[0], fwd_last[0], coef, weights)
    u_sent, l_got = lax.optimization_barrier((um, l_got))
    u_got = lax.ppermute(u_sent, "slab", up)
    opening = (lm, um, ur)
    lb = lr

    def block(is_l, side, n0, own, rest, recv, beyond, *work):
        outs = []
        if n0 > 1:
            outs = [fields(MSG), fields(REST)] + ([fields(MSG)] if side == 0 else [])
        elif is_l:
            outs = [jax.ShapeDtypeStruct((depth, width_x, width_y), f32)]
        outs.append(fields(WORK_ALL))
        return pl.pallas_call(
            functools.partial(block_kernel, side, is_l, n0, n0 == last_step),
            out_shape=outs,
            in_specs=[smem] + [vmem] * (6 + len(work)),
            out_specs=[vmem] * len(outs),
            scratch_shapes=block_scratch,
            compiler_params=params,
            cost_estimate=cost(2 * depth),
            name=("l" if is_l else "u") + f"_block{side}",
        )(info, own, rest, recv, coef, weights, beyond, *work)

    terms_in = opening
    for n0 in range(last_step, 0, -2):
        side = (last_step - n0) // 2 % 2
        way = up if side else down
        if n0 == 1:
            adjoint_field, d = block(True, side, n0, lm, lr, l_got, lb, work)
            if snake:
                adjoint_field = lax.ppermute(adjoint_field, "slab", swap)
            (x,) = block(False, side, n0, um, ur, u_got, ub)
            break
        lm, lr, *lb_new, d = block(True, side, n0, lm, lr, l_got, lb, work)
        lb = lb_new[0] if lb_new else lb
        l_got = lax.ppermute(lm, "slab", way)
        um, ur, *ub_new, x = block(False, side, n0, um, ur, u_got, ub)
        ub = ub_new[0] if ub_new else ub
        u_got = lax.ppermute(um, "slab", way)
        work, g, *g_left = between(side, n0, *terms_in, x, d)
        terms_in = (g,)
    g_right = lax.ppermute(g_left[0], "slab", down)

    terms = pl.pallas_call(
        last_kernel,
        out_shape=jax.ShapeDtypeStruct((depth, width_x, width_y), f32),
        in_specs=[smem] + [vmem] * 5,
        out_specs=vmem,
        scratch_shapes=[pltpu.VMEM((depth + SHIFT, parts, SUB, width_y), f32)],
        compiler_params=once,
        cost_estimate=cost(SHIFT),
        name="last_terms",
    )(info, g, x, d, g_right, aperture)
    summed = sum_shots(terms)
    if snake:
        summed, adjoint_field = lax.optimization_barrier((summed, adjoint_field))
        summed = lax.ppermute(summed, "slab", swap)
    block = width_x // lax.axis_size("shot")
    speed = lax.dynamic_slice_in_dim(velocity, shot * block, block, 1)
    return ((-2.0 / speed) * summed, adjoint_field[None])


def solution(mesh):
    in_specs = (
        P("shot", "slab", None, None),
        P("shot", "slab", None, None),
        P("slab", None, None),
        P("shot", None, None),
        P("shot", None),
        P("shot"),
        P("shot", None, None),
    )
    out_specs = (P("slab", "shot", None), P("shot", "slab", None, None))
    return jax.shard_map(on_device, mesh=mesh, in_specs=in_specs, out_specs=out_specs, check_vma=False)
```

```python
import functools

import jax
import jax.numpy as jnp
import numpy as np
from jax import lax
from jax.experimental import pallas as pl
from jax.experimental.pallas import tpu as pltpu
from jax.sharding import PartitionSpec as P

SCALE = 5040.0
WHOLE = (-14350.0, 8064.0, -1008.0, 128.0, -9.0)
REACH = 4
SHIFT = 8
VMEM_BYTES = 14 * 1024 * 1024
MORE_BYTES = 24 * 1024 * 1024
SUB = 8
PIECES = 3
CHUNK = 256

MSG = 2 * SHIFT
WORK = 4 * SHIFT
WORK_ALL = 6 * SHIFT
SPAN = 32
MID = 12


def wave_of(step):
    arg = (np.pi * 0.06 * (step - 10.0)) ** 2
    return float(np.float32(SCALE * 10.0 * (1.0 - 2.0 * arg) * np.exp(-arg)))


def load_tiled(field, layer):
    parts = field.shape[1] // SUB
    return jnp.stack([field[layer, pl.ds(m, SUB, stride=parts), :] for m in range(parts)])


def store_tiled(field, layer, value, first=0, count=SUB):
    parts = value.shape[0]
    for m in range(parts):
        field[layer, pl.ds(m, count, stride=parts), :] = value[m, first : first + count]


def split3(f):
    hi = f.astype(jnp.bfloat16)
    left = f - hi.astype(jnp.float32)
    mid = left.astype(jnp.bfloat16)
    return hi, mid, (left - mid.astype(jnp.float32)).astype(jnp.bfloat16)


def put_weights(weights):
    width_y = weights.shape[1]
    square = (width_y, width_y)
    away = jnp.abs(lax.broadcasted_iota(jnp.int32, square, 0) - lax.broadcasted_iota(jnp.int32, square, 1))
    once = jnp.zeros(square, jnp.float32)
    for k in range(1, 5):
        once = jnp.where(away == k, WHOLE[k], once)
    for i in range(PIECES):
        weights[i * width_y : (i + 1) * width_y, :] = once.astype(jnp.bfloat16)


def lane_pass(cur, first, count, weights, pieces, ybuf):
    parts, _, width_y = cur.shape[1:]
    rows = parts * SUB

    def one(q):
        at = pl.multiple_of(q * rows, rows)
        for i, piece in enumerate(split3(cur[first + q].reshape(rows, width_y))):
            pieces[pl.ds(at, rows), i * width_y : (i + 1) * width_y] = piece

    layers_loop(0, count, one)
    for q in range(0, count, SHIFT):
        block = slice(q * rows, min(q + SHIFT, count) * rows)
        ybuf[block, :] = jnp.dot(pieces[block, :], weights[...], preferred_element_type=jnp.float32)


def lap_maker(parts, width_y):
    row = lax.broadcasted_iota(jnp.int32, (1, SUB, width_y), 1)

    def lap(ref, j, along):
        f = ref[j]
        after = jnp.where(row == SUB - 1, 0.0, pltpu.roll(f[:REACH], SUB - 1, 1))
        before = jnp.where(row == 0, 0.0, pltpu.roll(f[parts - REACH :], 1, 1))
        wide = jnp.concatenate([before, f, after], axis=0)
        total = along + (3.0 * WHOLE[0]) * f
        for k in range(1, 5):
            pair = (ref[j + k] + ref[j - k]) + (
                wide[REACH + k : REACH + k + parts] + wide[REACH - k : REACH - k + parts]
            )
            total = total + WHOLE[k] * pair
        return f, total

    return lap


def layers_loop(first, count, body):
    def one(q, carry):
        body(first + q)
        return carry

    lax.fori_loop(0, count, one, 0, unroll=2)


STARTS = 5
SHOT = 15
ROWS = 16


def inject(work, at, info, near, table_hbm, table, sem, step, first, last):
    low, high = info[STARTS + first], info[STARTS + last]
    rows = work.shape[1] * SUB
    shift = at * rows - first * REACH * rows
    flat = work.reshape(work.shape[0] * rows, work.shape[3])

    def store(low, high, row_of):
        def one(r, carry):
            flat[pl.ds(info[ROWS + r] + shift, 1), :] = row_of(r)
            return carry

        def eight(i, carry):
            for q in range(8):
                one(low + i * 8 + q, carry)
            return carry

        groups = lax.shift_right_logical(high - low, 3)
        lax.fori_loop(0, groups, eight, 0)
        lax.fori_loop(low + groups * 8, high, one, 0)

    split = jnp.clip(CHUNK, low, high)
    store(low, split, lambda r: near[step, pl.ds(r, 1), :])

    @pl.when(high > split)
    def _():
        fetch = pltpu.make_async_copy(table_hbm.at[step], table, sem)
        fetch.start()
        fetch.wait()
        store(split, high, lambda r: table[pl.ds(r, 1), :])


def zones_of(side):
    return (1, 0, 1) if side == 0 else (3, 2, 3)


def put_rows(work, side, n0, info, near, table_hbm, table, sem):
    shared = (info, near, table_hbm, table, sem)
    zero = jnp.zeros((SHIFT,) + work.shape[1:], jnp.float32)
    for i in range(0, WORK, SHIFT):
        work[i : i + SHIFT] = zero
    for level, (at, zone, count) in enumerate(zip((0, 8, 24), zones_of(side), (2, 4, 2))):
        if n0 >= level:
            inject(work, at, *shared, n0 - level, zone, zone + count)
    if side == 0:

        @pl.when(info[0] == 1)
        def _():
            for i in range(WORK, WORK_ALL, SHIFT):
                work[i : i + SHIFT] = zero
            for level, (at, zone, count) in enumerate(((32, 5, 1), (36, 4, 2), (44, 5, 1))):
                if n0 >= level:
                    inject(work, at, *shared, n0 - level, zone, zone + count)


def add_terms(g, g_in, side, n0, is_last, x, d):
    x0, b, c = x
    low = 0 if side == 0 else SHIFT
    more = n0 >= 2

    def edge(at):
        def one(q):
            g[low + at + q] = g_in[low + at + q] + b[MID - SHIFT + at + q] * d[SHIFT + at + q]

        layers_loop(0, REACH, one)

    def middle(q):
        total = x0[q] * d[q] + b[MID - REACH + q] * d[SHIFT + REACH + q]
        if more:
            total = total + c[MID - REACH + q] * d[3 * SHIFT + q]
        g[low + REACH + q] = g_in[low + REACH + q] + total

    edge(0)
    layers_loop(0, SHIFT, middle)
    edge(SHIFT + REACH)
    if side == 1:
        g[0:SHIFT] = g_in[0:SHIFT]
        return
    g[2 * SHIFT : 3 * SHIFT] = g_in[2 * SHIFT : 3 * SHIFT]

    @pl.when(is_last == 1)
    def _():
        for q in range(SHIFT):
            total = b[MID + SHIFT + q] * d[36 + q]
            if q >= REACH:
                total = total + x0[REACH + q] * d[28 + q]
                if more:
                    total = total + c[MID + SHIFT + q] * d[40 + q]
            g[2 * SHIFT + q] = g[2 * SHIFT + q] + total


def between_kernel(side, n0, opening, info, near, table_hbm, *refs):
    if n0 == opening:
        l_msg, u_msg, u_kept, *x, d, work, g, start, table, sem = refs
        start[...] = jnp.zeros(start.shape, jnp.float32)
        for z in range(REACH, REACH + SHIFT):
            was = u_kept[MID - SHIFT + z] if z < SHIFT else u_msg[z - SHIFT]
            start[z + SHIFT] = was * l_msg[z - REACH + SHIFT]
        g_in = start
    else:
        g_in, *x, d = refs[:5]
        work, g, *g_left, table, sem = refs[5:]
    add_terms(g, g_in, side, n0, info[0], x, d)
    if n0 == 3:
        g_left[0][...] = g[0:SHIFT]
    put_rows(work, 1 - side, n0 - 2, info, near, table_hbm, table, sem)


def chunks_of(info, zones):
    return jnp.maximum((info[STARTS + zones] + CHUNK - 1) // CHUNK, 1)


def table_kernel(zones, info, ids, rows_l, rows_s, lanes_s, res, near, out, res_cut, pieces, same, part, sem):
    steps, receivers = res.shape
    width_y = part.shape[2]
    chunks = chunks_of(info, zones)
    for i, piece in enumerate(split3(res[...])):
        pieces[i * steps : (i + 1) * steps, :] = piece

    def column(c, carry):
        who = lax.broadcasted_iota(jnp.int32, (receivers, CHUNK), 0) == ids[pl.ds(c, 1), :]
        moved = jnp.dot(
            pieces[...], jnp.where(who, 1.0, 0.0).astype(jnp.bfloat16), preferred_element_type=jnp.float32
        )
        total = SCALE * ((moved[:steps] + moved[steps : 2 * steps]) + moved[2 * steps :])
        for i, piece in enumerate(split3(total)):
            res_cut[c, i] = piece.astype(jnp.float32)
        return carry

    lax.fori_loop(0, chunks, column, 0)

    def to_chunk(c, carry):
        mine = rows_s[pl.ds(pl.multiple_of(c * CHUNK, CHUNK), CHUNK), :]

        def from_chunk(d, carry):
            same[...] = jnp.where(mine == rows_l[pl.ds(d, 1), :], 1.0, 0.0).astype(jnp.bfloat16)
            at = pl.multiple_of(d * CHUNK, CHUNK)
            lane = lax.broadcasted_iota(jnp.int32, (CHUNK, width_y), 1)
            spot = jnp.where(lane == lanes_s[pl.ds(at, CHUNK), :], 1.0, 0.0).astype(jnp.bfloat16)
            spots = jnp.concatenate([spot] * PIECES, axis=0)

            def one(n, carry):
                mixed = []
                for i in range(PIECES):
                    row = jnp.broadcast_to(res_cut[d, i, pl.ds(n, 1), :], (16, CHUNK)).astype(jnp.bfloat16)
                    mixed.append((same[...].reshape(CHUNK // 16, 16, CHUNK) * row[None]).reshape(CHUNK, CHUNK))
                total = jnp.dot(
                    jnp.concatenate(mixed, axis=1), spots, preferred_element_type=jnp.float32
                )
                part[n] = total + jnp.where(d > 0, part[n], 0.0)
                return carry

            return lax.fori_loop(0, steps, one, carry, unroll=4)

        lax.fori_loop(0, chunks, from_chunk, 0)
        return carry

    def store_chunk(c, carry):
        to_chunk(c, 0)
        at = pl.multiple_of(c * CHUNK, CHUNK)
        write = pltpu.make_async_copy(part, out.at[:, pl.ds(at, CHUNK), :], sem)
        write.start()
        write.wait()
        return carry

    to_chunk(0, 0)
    near[...] = part[...]
    lax.fori_loop(1, chunks, store_chunk, 0)


def block_kernel(side, is_l, n0, opening, *refs):
    refs = list(refs)

    def take(count):
        got = refs[:count]
        del refs[:count]
        return got

    final = n0 == 1
    info, own, b_kept, c_kept, recv, coef, weights, beyond = take(8)
    work_in = work_out = x_out = msg_out = beyond_out = field_out = p = None
    if is_l:
        (work_in,) = take(1)
    if not final:
        msg_out, b, c = take(3)
        if side == 0:
            (beyond_out,) = take(1)
    elif is_l:
        (field_out,) = take(1)
    else:
        (b,) = take(1)
    if is_l:
        (work_out,) = take(1)
    else:
        (x_out,) = take(1)
    a, pieces, ybuf = take(3)
    if final and is_l:
        b, c = take(2)
    if opening and not is_l:
        (p,) = take(1)

    parts, _, width_y = a.shape[1:]
    rows = parts * SUB
    is_last, src_layer, src_part, src_row, src_lane = (info[i] for i in range(STARTS))
    off = MID - SHIFT if side == 0 else MID - 2 * SHIFT
    lap = lap_maker(parts, width_y)

    def bring(msg, low):
        if low:
            a[MID - SHIFT : MID] = msg[0:SHIFT]
            b[MID - SHIFT - REACH : MID - REACH] = msg[SHIFT:MSG]
        else:
            a[MID : MID + SHIFT] = msg[0:SHIFT]
            b[MID + REACH : MID + REACH + SHIFT] = msg[SHIFT:MSG]

    if side == 0:
        bring(recv, True)
        a[MID : MID + SHIFT] = c_kept[MID - SHIFT : MID]
        b[MID + REACH : MID + REACH + SHIFT] = own[SHIFT:MSG]

        @pl.when(is_last == 1)
        def _():
            zero = jnp.zeros((REACH,) + a.shape[1:], jnp.float32)
            a[MID + SHIFT : MID + 2 * SHIFT] = own[0:SHIFT]
            for field in (a, b, c):
                field[MID + 2 * SHIFT : MID + 2 * SHIFT + REACH] = zero
            if opening and is_l:
                a[MID + SHIFT : MID + 2 * SHIFT] = jnp.zeros((SHIFT,) + a.shape[1:], jnp.float32)

        if opening and is_l:
            a[MID - SHIFT : MID] = jnp.zeros((SHIFT,) + a.shape[1:], jnp.float32)
    else:
        a[MID - SHIFT : MID] = c_kept[MID : MID + SHIFT]
        b[MID - SHIFT - REACH : MID - REACH] = own[SHIFT:MSG]

        @pl.when(is_last == 1)
        def _():
            bring(beyond, False)

        @pl.when(is_last == 0)
        def _():
            bring(recv, False)

    before = (b_kept, -SHIFT if side == 0 else SHIFT)
    if p is not None:
        p[0:REACH] = recv[MSG : MSG + REACH]
        p[REACH:SHIFT] = b_kept[REACH:SHIFT]
        before = (p, REACH - MID)

    def source(level, first, count, out, shift):
        j = src_layer + off

        @pl.when((src_layer >= 0) & (j >= first) & (j < first + count))
        def _():
            lane = lax.broadcasted_iota(jnp.int32, (1, width_y), 1)
            spot = out[j + shift, src_part, pl.ds(src_row, 1), :]
            gain = coef[src_layer, src_part, pl.ds(src_row, 1), :] * wave_of(n0 - level)
            out[j + shift, src_part, pl.ds(src_row, 1), :] = spot + jnp.where(lane == src_lane, gain, 0.0)

    def advance(level, cur, nxt, nxt_shift, first, count, work_at, out, shift):
        lane_pass(cur, first, count, weights, pieces, ybuf)

        def body(j):
            y_at = pl.multiple_of((j - first) * rows, rows)
            f, total = lap(cur, j, ybuf[pl.ds(y_at, rows), :].reshape(parts, SUB, width_y))
            if is_l:
                total = total + work_in[j + (work_at - first)]
            step = coef[j - off] * total
            out[j + shift] = (2.0 * f - nxt[j + nxt_shift]) + step
            if is_l:
                work_out[j + (work_at - first)] = step

        layers_loop(first, count, body)
        if not is_l:
            source(level, first, count, out, shift)

    def beyond_too(*args):
        if side == 0:

            @pl.when(is_last == 1)
            def _():
                advance(*args)

    far = MID + SHIFT + REACH
    advance(0, a, *before, MID - REACH, SHIFT, 0, b, 0)
    beyond_too(0, a, beyond, SHIFT - far, far, REACH, 32, b, 0)
    if not is_l:
        x_out[0:SHIFT] = a[MID - REACH : MID + REACH]
        if side == 0:

            @pl.when(is_last == 1)
            def _():
                x_out[SHIFT : SHIFT + REACH] = a[far : far + REACH]

        if final:
            return
    advance(1, b, a, 0, MID - SHIFT, 2 * SHIFT, 8, c, 0)
    beyond_too(1, b, a, 0, MID + SHIFT, SHIFT, 36, c, 0)
    if final:
        for layer in range(2 * SHIFT):
            store_tiled(field_out, layer, c[MID - SHIFT + layer])
        return
    advance(2, c, b, 0, MID - REACH, SHIFT, 24, msg_out, SHIFT - (MID - REACH))
    if side == 1:
        msg_out[0:SHIFT] = c[MID : MID + SHIFT]
        return
    msg_out[0:SHIFT] = c[MID - SHIFT : MID]

    @pl.when(is_last == 1)
    def _():
        advance(2, c, b, 0, far, REACH, 44, beyond_out, SHIFT - far)
        beyond_out[0:SHIFT] = c[MID + SHIFT : MID + 2 * SHIFT]
        beyond_out[SHIFT + REACH : MSG] = jnp.zeros((REACH,) + a.shape[1:], jnp.float32)


def first_l_kernel(n0, halves, info, near, table_hbm, *refs):
    refs = list(refs)
    speeds = refs[: 1 + halves]
    coef, weights, msg_out, b_kept, c_kept, beyond, work, table, sem = refs[1 + halves :]
    put_weights(weights)

    def fill(speed, first):
        def one(z):
            coef[z + first] = (0.4 * load_tiled(speed, z)) ** 2 * (1.0 / SCALE)

        layers_loop(0, speed.shape[0], one)

    if halves:

        @pl.when(info[SHOT] == 0)
        def _():
            fill(speeds[0], 0)
            fill(speeds[1], SHIFT)

        @pl.when(info[SHOT] != 0)
        def _():
            fill(speeds[1], 0)
            fill(speeds[0], SHIFT)
    else:
        fill(speeds[0], 0)
    msg_out[0:SHIFT] = coef[coef.shape[0] - SHIFT :]
    msg_out[SHIFT:MSG] = jnp.zeros((SHIFT,) + coef.shape[1:], jnp.float32)
    beyond[...] = jnp.zeros(beyond.shape, jnp.float32)
    b_kept[0:SHIFT] = jnp.zeros((SHIFT,) + coef.shape[1:], jnp.float32)
    c_kept[MID - SHIFT : MID] = jnp.zeros((SHIFT,) + coef.shape[1:], jnp.float32)
    zone = (SHIFT + REACH) // REACH
    inject(msg_out, SHIFT, info, near, table_hbm, table, sem, n0, zone, zone + SHIFT // REACH)

    def body(q):
        msg_out[q + SHIFT] = coef[q + REACH] * msg_out[q + SHIFT]

    layers_loop(0, SHIFT, body)
    put_rows(work, 0, n0, info, near, table_hbm, table, sem)


def join_kernel(l_got, own, coef):
    coef[0:SHIFT] = l_got[0:SHIFT]
    coef[SHIFT:] = own[...]


def first_u_kernel(n0, info, prev, last, coef, weights, msg_out, b_kept, c_kept, beyond, f0, f1, pieces, ybuf):
    depth, parts, _, width_y = f0.shape
    rows = parts * SUB
    src_layer, src_part, src_row, src_lane = (info[i] for i in range(1, STARTS))
    lap = lap_maker(parts, width_y)

    def bring(z):
        f0[z] = load_tiled(prev, z)
        f1[z] = load_tiled(last, z)

    layers_loop(0, depth, bring)
    msg_out[0:SHIFT] = f0[depth - SHIFT : depth]
    msg_out[MSG : MSG + REACH] = f1[depth - REACH : depth]
    c_kept[MID - SHIFT : MID] = f0[0:SHIFT]
    b_kept[REACH:SHIFT] = f1[0:REACH]
    beyond[...] = jnp.zeros(beyond.shape, jnp.float32)
    beyond[SHIFT : SHIFT + REACH] = f1[depth - REACH : depth]
    lane_pass(f0, REACH, SHIFT, weights, pieces, ybuf)
    to = SHIFT - REACH

    def body(j):
        y_at = pl.multiple_of((j - REACH) * rows, rows)
        f, total = lap(f0, j, ybuf[pl.ds(y_at, rows), :].reshape(parts, SUB, width_y))
        msg_out[j + to] = (2.0 * f - f1[j]) + coef[j] * total

    layers_loop(REACH, SHIFT, body)
    j = src_layer - SHIFT

    @pl.when((src_layer >= 0) & (j >= REACH) & (j < REACH + SHIFT))
    def _():
        lane = lax.broadcasted_iota(jnp.int32, (1, width_y), 1)
        spot = msg_out[j + to, src_part, pl.ds(src_row, 1), :]
        gain = coef[j, src_part, pl.ds(src_row, 1), :] * wave_of(n0)
        msg_out[j + to, src_part, pl.ds(src_row, 1), :] = spot + jnp.where(lane == src_lane, gain, 0.0)


def last_kernel(info, g_in, x0, b, d, g_right, gate, out, g):
    depth = out.shape[0]
    add_terms(g, g_in, 1, 1, info[0], (x0, b, None), d)

    def one(z):
        store_tiled(out, z, load_tiled(gate, 0).astype(jnp.float32) * g[z + SHIFT])

    def shared(z):
        store_tiled(out, z, load_tiled(gate, 0).astype(jnp.float32) * (g[z + SHIFT] + g_right[z - SHIFT]))

    layers_loop(0, SHIFT, one)
    layers_loop(SHIFT, depth - SHIFT, shared)


def sum_shots(g):
    shots = lax.axis_size("shot")
    if shots != 2:
        return lax.psum_scatter(g, "shot", scatter_dimension=1, tiled=True)
    block = g.shape[1] // 2
    low, high = g[:, :block], g[:, block:]
    first = lax.axis_index("shot") == 0
    other = lax.ppermute(jnp.where(first, high, low), "shot", [(0, 1), (1, 0)])
    return jnp.where(first, low, high) + other


def snake_of(slabs):
    row = slabs // 4
    if slabs % 8:
        return list(range(slabs))
    order = []
    for i in range(slabs):
        z, (chip, core) = i // row, divmod(i % row, 2)
        order.append(z * row + 2 * (row // 2 - 1 - chip if z % 2 else chip) + core)
    return order


def on_device(fwd_last, fwd_prev, velocity, aperture, rec_index, src_index, residual):
    _, depth, width_x, width_y = fwd_last.shape
    parts = width_x // SUB
    total_steps, receivers = residual.shape[1:]
    plane = width_x * width_y
    slabs = lax.axis_size("slab")
    f32 = jnp.float32
    place = snake_of(slabs)
    at = lax.axis_index("slab")
    snake = place != list(range(slabs))
    shot = lax.axis_index("shot")
    halves = snake and lax.axis_size("shot") == 2
    slab = at
    if snake:
        row = slabs // 4
        z, chip, core = at // row, at % row // 2, at % 2
        slab = z * row + 2 * jnp.where(z % 2 == 1, row // 2 - 1 - chip, chip) + core
    up = [(place[i], place[i + 1]) for i in range(slabs - 1)]
    down = [(place[i + 1], place[i]) for i in range(slabs - 1)]
    swap = [(i, place[i]) for i in range(slabs)]
    half = depth // 2
    if snake:
        fwd_prev = lax.ppermute(fwd_prev, "slab", swap)
        fwd_last = lax.ppermute(fwd_last, "slab", swap)
    if halves:
        mine = jnp.where(shot == 0, velocity[:half], velocity[half:])
        mine = lax.ppermute(mine, "slab", swap)
        theirs = lax.ppermute(mine, "shot", [(0, 1), (1, 0)])
        speeds = (mine, theirs)
    else:
        speeds = (lax.ppermute(velocity, "slab", swap) if snake else velocity,)

    base = (slab * depth - SHIFT) * plane
    window = (depth + SHIFT) * plane
    local = rec_index[0] - base
    far = jnp.int32(2**30)
    keys = jnp.where((local >= 0) & (local < window), local, far)
    keys, ids = lax.sort((keys, lax.iota(jnp.int32, receivers)), num_keys=1, is_stable=False)

    def place_of(cell):
        layer = cell // plane
        x = (cell // width_y) % width_x
        return layer, x % parts, x // parts, cell % width_y

    layer, part, row, lane = place_of(keys)
    rows_of = (layer * parts + part) * SUB + row
    zones = (depth + SHIFT) // REACH
    edges = jnp.arange(zones + 1, dtype=jnp.int32) * (REACH * plane)
    starts = jnp.sum((keys[None, :] < edges[:, None]).astype(jnp.int32), axis=1)

    src = src_index[0] - base
    src_in = (src >= 0) & (src < window)
    s_layer, s_part, s_row, s_lane = place_of(jnp.where(src_in, src, 0))
    s_layer = jnp.where(src_in, s_layer, -1)
    is_last = (slab == slabs - 1).astype(jnp.int32)
    scalars = [is_last, s_layer, s_part, s_row, s_lane]
    gap = [jnp.zeros((), jnp.int32)] * (SHOT - STARTS - zones - 1)
    info = jnp.concatenate([jnp.stack(scalars), starts, jnp.stack([*gap, shot]), rows_of])
    last_step = total_steps - 1

    smem = pl.BlockSpec(memory_space=pltpu.SMEM)
    vmem = pl.BlockSpec(memory_space=pltpu.VMEM)
    anym = pl.BlockSpec(memory_space=pltpu.HBM)

    def fields(layers):
        return jax.ShapeDtypeStruct((layers, parts, SUB, width_y), f32)

    params = pltpu.CompilerParams(vmem_limit_bytes=VMEM_BYTES)
    once = pltpu.CompilerParams(vmem_limit_bytes=MORE_BYTES)
    fetch_scratch = [pltpu.VMEM((receivers, width_y), f32), pltpu.SemaphoreType.DMA(())]

    def lane_scratch(layers):
        rows = layers * parts * SUB
        return [
            pltpu.VMEM((rows, PIECES * width_y), jnp.bfloat16),
            pltpu.VMEM((rows, width_y), f32),
        ]

    span = pltpu.VMEM((SPAN, parts, SUB, width_y), f32)
    block_scratch = [span] + lane_scratch(2 * SHIFT)

    def cost(layers):
        return pl.CostEstimate(
            flops=50 * layers * plane, bytes_accessed=24 * layers * plane, transcendentals=0
        )

    near, table = pl.pallas_call(
        functools.partial(table_kernel, zones),
        out_shape=(
            jax.ShapeDtypeStruct((total_steps, CHUNK, width_y), f32),
            jax.ShapeDtypeStruct((total_steps, receivers, width_y), f32),
        ),
        in_specs=[smem] + [vmem] * 5,
        out_specs=(vmem, anym),
        scratch_shapes=[
            pltpu.VMEM((receivers // CHUNK, PIECES, total_steps, CHUNK), f32),
            pltpu.VMEM((PIECES * total_steps, receivers), jnp.bfloat16),
            pltpu.VMEM((CHUNK, CHUNK), jnp.bfloat16),
            pltpu.VMEM((total_steps, CHUNK, width_y), f32),
            pltpu.SemaphoreType.DMA(()),
        ],
        compiler_params=once,
        cost_estimate=cost(SHIFT),
        name="rec_table",
    )(
        info,
        ids.reshape(receivers // CHUNK, CHUNK),
        rows_of.reshape(receivers // CHUNK, CHUNK),
        rows_of[:, None],
        lane[:, None],
        residual[0],
    )
    coef_own, weights, lm, l_b, l_c, lb, work = pl.pallas_call(
        functools.partial(first_l_kernel, last_step, halves),
        out_shape=(
            fields(depth),
            jax.ShapeDtypeStruct((PIECES * width_y, width_y), jnp.bfloat16),
            fields(MSG),
            fields(SPAN),
            fields(SPAN),
            fields(MSG),
            fields(WORK_ALL),
        ),
        in_specs=[smem, vmem, anym] + [vmem] * len(speeds),
        out_specs=[vmem] * 7,
        scratch_shapes=fetch_scratch,
        compiler_params=once,
        cost_estimate=cost(2),
        name="first_l",
    )(info, near, table, *speeds)
    l_got = lax.ppermute(lm, "slab", up)

    def between(side, n0, *arrays):
        outs = [fields(WORK_ALL), fields(depth + SHIFT)]
        scratch = list(fetch_scratch)
        if n0 == 3:
            outs.append(fields(SHIFT))
        if n0 == last_step:
            scratch = [pltpu.VMEM((depth + SHIFT, parts, SUB, width_y), f32)] + scratch
        return pl.pallas_call(
            functools.partial(between_kernel, side, n0, last_step),
            out_shape=outs,
            in_specs=[smem, vmem, anym] + [vmem] * len(arrays),
            out_specs=[vmem] * len(outs),
            scratch_shapes=scratch,
            compiler_params=params,
            cost_estimate=cost(SHIFT),
            name=f"between{side}",
        )(info, near, table, *arrays)

    fwd_prev, fwd_last, _ = lax.optimization_barrier((fwd_prev, fwd_last, work))
    um, u_b, u_c, ub = pl.pallas_call(
        functools.partial(first_u_kernel, last_step),
        out_shape=(fields(MSG + REACH), fields(SPAN), fields(SPAN), fields(MSG)),
        in_specs=[smem] + [vmem] * 4,
        out_specs=[vmem] * 4,
        scratch_shapes=[pltpu.VMEM((depth, parts, SUB, width_y), f32)] * 2 + lane_scratch(SHIFT),
        compiler_params=once,
        cost_estimate=cost(SHIFT),
        name="first_u",
    )(info, fwd_prev[0], fwd_last[0], coef_own, weights)
    u_sent, l_got = lax.optimization_barrier((um, l_got))
    u_got = lax.ppermute(u_sent, "slab", up)
    coef = pl.pallas_call(
        join_kernel,
        out_shape=fields(depth + SHIFT),
        in_specs=[vmem] * 2,
        out_specs=vmem,
        compiler_params=once,
        cost_estimate=cost(1),
        name="join_coef",
    )(l_got, coef_own)
    opening = (lm, um, u_c)

    def block(is_l, side, n0, own, b, c, recv, beyond, *work):
        outs = []
        if n0 > 1:
            outs = [fields(MSG), fields(SPAN), fields(SPAN)] + ([fields(MSG)] if side == 0 else [])
        elif is_l:
            outs = [jax.ShapeDtypeStruct((depth, width_x, width_y), f32)]
        else:
            outs = [fields(SPAN)]
        outs.append(fields(WORK_ALL if is_l else SHIFT + REACH))
        scratch = list(block_scratch)
        if n0 == 1 and is_l:
            scratch += [span, span]
        if n0 == last_step and not is_l:
            scratch.append(pltpu.VMEM((SHIFT, parts, SUB, width_y), f32))
        return pl.pallas_call(
            functools.partial(block_kernel, side, is_l, n0, n0 == last_step),
            out_shape=outs,
            in_specs=[smem] + [vmem] * (7 + len(work)),
            out_specs=[vmem] * len(outs),
            scratch_shapes=scratch,
            compiler_params=params,
            cost_estimate=cost(2 * depth),
            name=("l" if is_l else "u") + f"_block{side}",
        )(info, own, b, c, recv, coef, weights, beyond, *work)

    terms_in = opening
    for n0 in range(last_step, 0, -2):
        side = (last_step - n0) // 2 % 2
        way = up if side else down
        if n0 == 1:
            adjoint_field, d = block(True, side, n0, lm, l_b, l_c, l_got, lb, work)
            if snake:
                adjoint_field = lax.ppermute(adjoint_field, "slab", swap)
            u_b, x0 = block(False, side, n0, um, u_b, u_c, u_got, ub)
            break
        lm, l_b, l_c, *lb_new, d = block(True, side, n0, lm, l_b, l_c, l_got, lb, work)
        lb = lb_new[0] if lb_new else lb
        l_got = lax.ppermute(lm, "slab", way)
        um, u_b, u_c, *ub_new, x0 = block(False, side, n0, um, u_b, u_c, u_got, ub)
        ub = ub_new[0] if ub_new else ub
        u_got = lax.ppermute(um, "slab", way)
        work, g, *g_left = between(side, n0, *terms_in, x0, u_b, u_c, d)
        terms_in = (g,)
    g_right = lax.ppermute(g_left[0], "slab", down)

    terms = pl.pallas_call(
        last_kernel,
        out_shape=jax.ShapeDtypeStruct((depth, width_x, width_y), f32),
        in_specs=[smem] + [vmem] * 6,
        out_specs=vmem,
        scratch_shapes=[pltpu.VMEM((depth + SHIFT, parts, SUB, width_y), f32)],
        compiler_params=once,
        cost_estimate=cost(SHIFT),
        name="last_terms",
    )(info, g, x0, u_b, d, g_right, aperture)
    summed = sum_shots(terms)
    if snake:
        summed, adjoint_field = lax.optimization_barrier((summed, adjoint_field))
        summed = lax.ppermute(summed, "slab", swap)
    block = width_x // lax.axis_size("shot")
    speed = lax.dynamic_slice_in_dim(velocity, shot * block, block, 1)
    return ((-2.0 / speed) * summed, adjoint_field[None])


def solution(mesh):
    in_specs = (
        P("shot", "slab", None, None),
        P("shot", "slab", None, None),
        P("slab", None, None),
        P("shot", None, None),
        P("shot", None),
        P("shot"),
        P("shot", None, None),
    )
    out_specs = (P("slab", "shot", None), P("shot", "slab", None, None))
    return jax.shard_map(on_device, mesh=mesh, in_specs=in_specs, out_specs=out_specs, check_vma=False)
```

```python
import functools

import jax
import jax.numpy as jnp
import numpy as np
from jax import lax
from jax.experimental import pallas as pl
from jax.experimental.pallas import tpu as pltpu
from jax.sharding import PartitionSpec as P

SCALE = 5040.0
WHOLE = (-14350.0, 8064.0, -1008.0, 128.0, -9.0)
REACH = 4
SHIFT = 8
VMEM_BYTES = 9 * 1024 * 1024
MORE_BYTES = 24 * 1024 * 1024
SUB = 8
PIECES = 3
CHUNK = 256

MSG = 2 * SHIFT
WORK = 4 * SHIFT
WORK_ALL = 6 * SHIFT
SPAN = 32
MID = 12


def wave_of(step):
    arg = (np.pi * 0.06 * (step - 10.0)) ** 2
    return float(np.float32(SCALE * 10.0 * (1.0 - 2.0 * arg) * np.exp(-arg)))


def load_tiled(field, layer):
    parts = field.shape[1] // SUB
    return jnp.stack([field[layer, pl.ds(m, SUB, stride=parts), :] for m in range(parts)])


def store_tiled(field, layer, value, first=0, count=SUB):
    parts = value.shape[0]
    for m in range(parts):
        field[layer, pl.ds(m, count, stride=parts), :] = value[m, first : first + count]


def split3(f):
    hi = f.astype(jnp.bfloat16)
    left = f - hi.astype(jnp.float32)
    mid = left.astype(jnp.bfloat16)
    return hi, mid, (left - mid.astype(jnp.float32)).astype(jnp.bfloat16)


def put_weights(weights):
    width_y = weights.shape[1]
    square = (width_y, width_y)
    away = jnp.abs(lax.broadcasted_iota(jnp.int32, square, 0) - lax.broadcasted_iota(jnp.int32, square, 1))
    once = jnp.zeros(square, jnp.float32)
    for k in range(1, 5):
        once = jnp.where(away == k, WHOLE[k], once)
    for i in range(PIECES):
        weights[i * width_y : (i + 1) * width_y, :] = once.astype(jnp.bfloat16)


def lane_pass(cur, first, count, weights, pieces, ybuf):
    parts, _, width_y = cur.shape[1:]
    rows = parts * SUB

    def one(q):
        at = pl.multiple_of(q * rows, rows)
        for i, piece in enumerate(split3(cur[first + q].reshape(rows, width_y))):
            pieces[pl.ds(at, rows), i * width_y : (i + 1) * width_y] = piece

    layers_loop(0, count, one)
    block = slice(0, count * rows)
    ybuf[block, :] = jnp.dot(pieces[block, :], weights[...], preferred_element_type=jnp.float32)


def lap_maker(parts, width_y):
    row = lax.broadcasted_iota(jnp.int32, (1, SUB, width_y), 1)

    def lap(ref, j, along):
        f = ref[j]
        after = jnp.where(row == SUB - 1, 0.0, pltpu.roll(f[:REACH], SUB - 1, 1))
        before = jnp.where(row == 0, 0.0, pltpu.roll(f[parts - REACH :], 1, 1))
        wide = jnp.concatenate([before, f, after], axis=0)
        total = along + (3.0 * WHOLE[0]) * f
        for k in range(1, 5):
            pair = (ref[j + k] + ref[j - k]) + (
                wide[REACH + k : REACH + k + parts] + wide[REACH - k : REACH - k + parts]
            )
            total = total + WHOLE[k] * pair
        return f, total

    return lap


def layers_loop(first, count, body):
    def one(q, carry):
        body(first + q)
        return carry

    lax.fori_loop(0, count, one, 0, unroll=2)


STARTS = 5
SHOT = 15
ROWS = 16


def inject(work, at, info, near, table_hbm, table, sem, step, first, last):
    low, high = info[STARTS + first], info[STARTS + last]
    rows = work.shape[1] * SUB
    shift = at * rows - first * REACH * rows
    flat = work.reshape(work.shape[0] * rows, work.shape[3])

    def store(low, high, row_of):
        def one(r, carry):
            flat[pl.ds(info[ROWS + r] + shift, 1), :] = row_of(r)
            return carry

        def eight(i, carry):
            at = [low + i * 8 + q for q in range(8)]
            values = [row_of(r) for r in at]
            for r, value in zip(at, values):
                flat[pl.ds(info[ROWS + r] + shift, 1), :] = value
            return carry

        groups = lax.shift_right_logical(high - low, 3)
        lax.fori_loop(0, groups, eight, 0)
        lax.fori_loop(low + groups * 8, high, one, 0)

    split = jnp.clip(CHUNK, low, high)
    store(low, split, lambda r: near[step, pl.ds(r, 1), :])

    @pl.when(high > split)
    def _():
        fetch = pltpu.make_async_copy(table_hbm.at[step], table, sem)
        fetch.start()
        fetch.wait()
        store(split, high, lambda r: table[pl.ds(r, 1), :])


def zones_of(side):
    return (1, 0, 1) if side == 0 else (3, 2, 3)


def put_rows(work, side, n0, info, near, table_hbm, table, sem):
    shared = (info, near, table_hbm, table, sem)
    zero = jnp.zeros((SHIFT,) + work.shape[1:], jnp.float32)
    for i in range(0, WORK, SHIFT):
        work[i : i + SHIFT] = zero
    for level, (at, zone, count) in enumerate(zip((0, 8, 24), zones_of(side), (2, 4, 2))):
        if n0 >= level:
            inject(work, at, *shared, n0 - level, zone, zone + count)
    if side == 0:

        @pl.when(info[0] == 1)
        def _():
            for i in range(WORK, WORK_ALL, SHIFT):
                work[i : i + SHIFT] = zero
            for level, (at, zone, count) in enumerate(((32, 5, 1), (36, 4, 2), (44, 5, 1))):
                if n0 >= level:
                    inject(work, at, *shared, n0 - level, zone, zone + count)


def add_terms(g, g_in, side, n0, is_last, x, d):
    x0, b, c = x
    low = 0 if side == 0 else SHIFT
    more = n0 >= 2

    def edge(at):
        def one(q):
            g[low + at + q] = g_in[low + at + q] + b[MID - SHIFT + at + q] * d[SHIFT + at + q]

        layers_loop(0, REACH, one)

    def middle(q):
        total = x0[q] * d[q] + b[MID - REACH + q] * d[SHIFT + REACH + q]
        if more:
            total = total + c[MID - REACH + q] * d[3 * SHIFT + q]
        g[low + REACH + q] = g_in[low + REACH + q] + total

    edge(0)
    layers_loop(0, SHIFT, middle)
    edge(SHIFT + REACH)
    if side == 1:
        g[0:SHIFT] = g_in[0:SHIFT]
        return
    g[2 * SHIFT : 3 * SHIFT] = g_in[2 * SHIFT : 3 * SHIFT]

    @pl.when(is_last == 1)
    def _():
        for q in range(SHIFT):
            total = b[MID + SHIFT + q] * d[36 + q]
            if q >= REACH:
                total = total + x0[REACH + q] * d[28 + q]
                if more:
                    total = total + c[MID + SHIFT + q] * d[40 + q]
            g[2 * SHIFT + q] = g[2 * SHIFT + q] + total


def between_kernel(side, n0, opening, info, near, table_hbm, *refs):
    if n0 == opening:
        l_msg, u_msg, u_kept, *x, d, work, g, start, table, sem = refs
        start[...] = jnp.zeros(start.shape, jnp.float32)
        for z in range(REACH, REACH + SHIFT):
            was = u_kept[MID - SHIFT + z] if z < SHIFT else u_msg[z - SHIFT]
            start[z + SHIFT] = was * l_msg[z - REACH + SHIFT]
        g_in = start
    else:
        g_in, *x, d = refs[:5]
        work, g, *g_left, table, sem = refs[5:]
    add_terms(g, g_in, side, n0, info[0], x, d)
    if n0 == 3:
        g_left[0][...] = g[0:SHIFT]
    put_rows(work, 1 - side, n0 - 2, info, near, table_hbm, table, sem)


def chunks_of(info, zones):
    return jnp.maximum((info[STARTS + zones] + CHUNK - 1) // CHUNK, 1)


def table_kernel(zones, info, ids, rows_l, rows_s, lanes_s, res, near, out, res_cut, pieces, same, part, sem):
    steps, receivers = res.shape
    width_y = part.shape[2]
    chunks = chunks_of(info, zones)
    for i, piece in enumerate(split3(res[...])):
        pieces[i * steps : (i + 1) * steps, :] = piece

    def column(c, carry):
        who = lax.broadcasted_iota(jnp.int32, (receivers, CHUNK), 0) == ids[pl.ds(c, 1), :]
        moved = jnp.dot(
            pieces[...], jnp.where(who, 1.0, 0.0).astype(jnp.bfloat16), preferred_element_type=jnp.float32
        )
        total = SCALE * ((moved[:steps] + moved[steps : 2 * steps]) + moved[2 * steps :])
        for i, piece in enumerate(split3(total)):
            res_cut[c, i] = piece.astype(jnp.float32)
        return carry

    lax.fori_loop(0, chunks, column, 0)

    def to_chunk(c, carry):
        mine = rows_s[pl.ds(pl.multiple_of(c * CHUNK, CHUNK), CHUNK), :]

        def from_chunk(d, carry):
            same[...] = jnp.where(mine == rows_l[pl.ds(d, 1), :], 1.0, 0.0).astype(jnp.bfloat16)
            at = pl.multiple_of(d * CHUNK, CHUNK)
            lane = lax.broadcasted_iota(jnp.int32, (CHUNK, width_y), 1)
            spot = jnp.where(lane == lanes_s[pl.ds(at, CHUNK), :], 1.0, 0.0).astype(jnp.bfloat16)
            spots = jnp.concatenate([spot] * PIECES, axis=0)

            def one(n, carry):
                mixed = []
                for i in range(PIECES):
                    row = jnp.broadcast_to(res_cut[d, i, pl.ds(n, 1), :], (16, CHUNK)).astype(jnp.bfloat16)
                    mixed.append((same[...].reshape(CHUNK // 16, 16, CHUNK) * row[None]).reshape(CHUNK, CHUNK))
                total = jnp.dot(
                    jnp.concatenate(mixed, axis=1), spots, preferred_element_type=jnp.float32
                )
                part[n] = total + jnp.where(d > 0, part[n], 0.0)
                return carry

            return lax.fori_loop(0, steps, one, carry, unroll=4)

        lax.fori_loop(0, chunks, from_chunk, 0)
        return carry

    def store_chunk(c, carry):
        to_chunk(c, 0)
        at = pl.multiple_of(c * CHUNK, CHUNK)
        write = pltpu.make_async_copy(part, out.at[:, pl.ds(at, CHUNK), :], sem)
        write.start()
        write.wait()
        return carry

    to_chunk(0, 0)
    near[...] = part[...]
    lax.fori_loop(1, chunks, store_chunk, 0)


def block_kernel(side, is_l, n0, opening, *refs):
    refs = list(refs)

    def take(count):
        got = refs[:count]
        del refs[:count]
        return got

    final = n0 == 1
    info, own, b_kept, c_kept, recv, coef, weights, beyond = take(8)
    work_in = work_out = x_out = msg_out = beyond_out = field_out = p = None
    if is_l:
        (work_in,) = take(1)
    if not final:
        msg_out, b, c = take(3)
        if side == 0:
            (beyond_out,) = take(1)
    elif is_l:
        (field_out,) = take(1)
    else:
        (b,) = take(1)
    if is_l:
        (work_out,) = take(1)
    else:
        (x_out,) = take(1)
    a, pieces, ybuf = take(3)
    if final and is_l:
        b, c = take(2)
    if opening and not is_l:
        (p,) = take(1)

    parts, _, width_y = a.shape[1:]
    rows = parts * SUB
    is_last, src_layer, src_part, src_row, src_lane = (info[i] for i in range(STARTS))
    off = MID - SHIFT if side == 0 else MID - 2 * SHIFT
    lap = lap_maker(parts, width_y)

    def bring(msg, low):
        if low:
            a[MID - SHIFT : MID] = msg[0:SHIFT]
            b[MID - SHIFT - REACH : MID - REACH] = msg[SHIFT:MSG]
        else:
            a[MID : MID + SHIFT] = msg[0:SHIFT]
            b[MID + REACH : MID + REACH + SHIFT] = msg[SHIFT:MSG]

    if side == 0:
        bring(recv, True)
        a[MID : MID + SHIFT] = c_kept[MID - SHIFT : MID]
        b[MID + REACH : MID + REACH + SHIFT] = own[SHIFT:MSG]

        @pl.when(is_last == 1)
        def _():
            zero = jnp.zeros((REACH,) + a.shape[1:], jnp.float32)
            a[MID + SHIFT : MID + 2 * SHIFT] = own[0:SHIFT]
            for field in (a, b, c):
                field[MID + 2 * SHIFT : MID + 2 * SHIFT + REACH] = zero
            if opening and is_l:
                a[MID + SHIFT : MID + 2 * SHIFT] = jnp.zeros((SHIFT,) + a.shape[1:], jnp.float32)

        if opening and is_l:
            a[MID - SHIFT : MID] = jnp.zeros((SHIFT,) + a.shape[1:], jnp.float32)
    else:
        a[MID - SHIFT : MID] = c_kept[MID : MID + SHIFT]
        b[MID - SHIFT - REACH : MID - REACH] = own[SHIFT:MSG]

        @pl.when(is_last == 1)
        def _():
            bring(beyond, False)

        @pl.when(is_last == 0)
        def _():
            bring(recv, False)

    before = (b_kept, -SHIFT if side == 0 else SHIFT)
    if p is not None:
        p[0:REACH] = recv[MSG : MSG + REACH]
        p[REACH:SHIFT] = b_kept[REACH:SHIFT]
        before = (p, REACH - MID)

    def source(level, first, count, out, shift):
        j = src_layer + off

        @pl.when((src_layer >= 0) & (j >= first) & (j < first + count))
        def _():
            lane = lax.broadcasted_iota(jnp.int32, (1, width_y), 1)
            spot = out[j + shift, src_part, pl.ds(src_row, 1), :]
            gain = coef[src_layer, src_part, pl.ds(src_row, 1), :] * wave_of(n0 - level)
            out[j + shift, src_part, pl.ds(src_row, 1), :] = spot + jnp.where(lane == src_lane, gain, 0.0)

    def advance(level, cur, nxt, nxt_shift, first, count, work_at, out, shift):
        lane_pass(cur, first, count, weights, pieces, ybuf)

        def body(j):
            y_at = pl.multiple_of((j - first) * rows, rows)
            f, total = lap(cur, j, ybuf[pl.ds(y_at, rows), :].reshape(parts, SUB, width_y))
            if is_l:
                total = total + work_in[j + (work_at - first)]
            step = coef[j - off] * total
            out[j + shift] = (2.0 * f - nxt[j + nxt_shift]) + step
            if is_l:
                work_out[j + (work_at - first)] = step

        layers_loop(first, count, body)
        if not is_l:
            source(level, first, count, out, shift)

    def beyond_too(*args):
        if side == 0:

            @pl.when(is_last == 1)
            def _():
                advance(*args)

    far = MID + SHIFT + REACH
    advance(0, a, *before, MID - REACH, SHIFT, 0, b, 0)
    beyond_too(0, a, beyond, SHIFT - far, far, REACH, 32, b, 0)
    if not is_l:
        x_out[0:SHIFT] = a[MID - REACH : MID + REACH]
        if side == 0:

            @pl.when(is_last == 1)
            def _():
                x_out[SHIFT : SHIFT + REACH] = a[far : far + REACH]

        if final:
            return
    advance(1, b, a, 0, MID - SHIFT, 2 * SHIFT, 8, c, 0)
    beyond_too(1, b, a, 0, MID + SHIFT, SHIFT, 36, c, 0)
    if final:
        for layer in range(2 * SHIFT):
            store_tiled(field_out, layer, c[MID - SHIFT + layer])
        return
    advance(2, c, b, 0, MID - REACH, SHIFT, 24, msg_out, SHIFT - (MID - REACH))
    if side == 1:
        msg_out[0:SHIFT] = c[MID : MID + SHIFT]
        return
    msg_out[0:SHIFT] = c[MID - SHIFT : MID]

    @pl.when(is_last == 1)
    def _():
        advance(2, c, b, 0, far, REACH, 44, beyond_out, SHIFT - far)
        beyond_out[0:SHIFT] = c[MID + SHIFT : MID + 2 * SHIFT]
        beyond_out[SHIFT + REACH : MSG] = jnp.zeros((REACH,) + a.shape[1:], jnp.float32)


def first_l_kernel(n0, halves, info, near, table_hbm, *refs):
    refs = list(refs)
    speeds = refs[: 1 + halves]
    coef, weights, msg_out, b_kept, c_kept, beyond, work, table, sem = refs[1 + halves :]
    put_weights(weights)

    def fill(speed, first):
        def one(z):
            coef[z + first] = (0.4 * load_tiled(speed, z)) ** 2 * (1.0 / SCALE)

        layers_loop(0, speed.shape[0], one)

    if halves:

        @pl.when(info[SHOT] == 0)
        def _():
            fill(speeds[0], 0)
            fill(speeds[1], SHIFT)

        @pl.when(info[SHOT] != 0)
        def _():
            fill(speeds[1], 0)
            fill(speeds[0], SHIFT)
    else:
        fill(speeds[0], 0)
    msg_out[0:SHIFT] = coef[coef.shape[0] - SHIFT :]
    msg_out[SHIFT:MSG] = jnp.zeros((SHIFT,) + coef.shape[1:], jnp.float32)
    beyond[...] = jnp.zeros(beyond.shape, jnp.float32)
    b_kept[0:SHIFT] = jnp.zeros((SHIFT,) + coef.shape[1:], jnp.float32)
    c_kept[MID - SHIFT : MID] = jnp.zeros((SHIFT,) + coef.shape[1:], jnp.float32)
    zone = (SHIFT + REACH) // REACH
    inject(msg_out, SHIFT, info, near, table_hbm, table, sem, n0, zone, zone + SHIFT // REACH)

    def body(q):
        msg_out[q + SHIFT] = coef[q + REACH] * msg_out[q + SHIFT]

    layers_loop(0, SHIFT, body)
    put_rows(work, 0, n0, info, near, table_hbm, table, sem)


def join_kernel(l_got, own, coef):
    coef[0:SHIFT] = l_got[0:SHIFT]
    coef[SHIFT:] = own[...]


def first_u_kernel(n0, info, prev, last, coef, weights, msg_out, b_kept, c_kept, beyond, f0, f1, pieces, ybuf):
    depth, parts, _, width_y = f0.shape
    rows = parts * SUB
    src_layer, src_part, src_row, src_lane = (info[i] for i in range(1, STARTS))
    lap = lap_maker(parts, width_y)

    def bring(z):
        f0[z] = load_tiled(prev, z)
        f1[z] = load_tiled(last, z)

    layers_loop(0, depth, bring)
    msg_out[0:SHIFT] = f0[depth - SHIFT : depth]
    msg_out[MSG : MSG + REACH] = f1[depth - REACH : depth]
    c_kept[MID - SHIFT : MID] = f0[0:SHIFT]
    b_kept[REACH:SHIFT] = f1[0:REACH]
    beyond[...] = jnp.zeros(beyond.shape, jnp.float32)
    beyond[SHIFT : SHIFT + REACH] = f1[depth - REACH : depth]
    lane_pass(f0, REACH, SHIFT, weights, pieces, ybuf)
    to = SHIFT - REACH

    def body(j):
        y_at = pl.multiple_of((j - REACH) * rows, rows)
        f, total = lap(f0, j, ybuf[pl.ds(y_at, rows), :].reshape(parts, SUB, width_y))
        msg_out[j + to] = (2.0 * f - f1[j]) + coef[j] * total

    layers_loop(REACH, SHIFT, body)
    j = src_layer - SHIFT

    @pl.when((src_layer >= 0) & (j >= REACH) & (j < REACH + SHIFT))
    def _():
        lane = lax.broadcasted_iota(jnp.int32, (1, width_y), 1)
        spot = msg_out[j + to, src_part, pl.ds(src_row, 1), :]
        gain = coef[j, src_part, pl.ds(src_row, 1), :] * wave_of(n0)
        msg_out[j + to, src_part, pl.ds(src_row, 1), :] = spot + jnp.where(lane == src_lane, gain, 0.0)


def last_kernel(info, g_in, x0, b, d, g_right, gate, out, g):
    depth = out.shape[0]
    add_terms(g, g_in, 1, 1, info[0], (x0, b, None), d)

    def one(z):
        store_tiled(out, z, load_tiled(gate, 0).astype(jnp.float32) * g[z + SHIFT])

    def shared(z):
        store_tiled(out, z, load_tiled(gate, 0).astype(jnp.float32) * (g[z + SHIFT] + g_right[z - SHIFT]))

    layers_loop(0, SHIFT, one)
    layers_loop(SHIFT, depth - SHIFT, shared)


def sum_shots(g):
    shots = lax.axis_size("shot")
    if shots != 2:
        return lax.psum_scatter(g, "shot", scatter_dimension=1, tiled=True)
    block = g.shape[1] // 2
    low, high = g[:, :block], g[:, block:]
    first = lax.axis_index("shot") == 0
    other = lax.ppermute(jnp.where(first, high, low), "shot", [(0, 1), (1, 0)])
    return jnp.where(first, low, high) + other


def snake_of(slabs):
    row = slabs // 4
    if slabs % 8:
        return list(range(slabs))
    order = []
    for i in range(slabs):
        z, (chip, core) = i // row, divmod(i % row, 2)
        order.append(z * row + 2 * (row // 2 - 1 - chip if z % 2 else chip) + core)
    return order


def on_device(fwd_last, fwd_prev, velocity, aperture, rec_index, src_index, residual):
    _, depth, width_x, width_y = fwd_last.shape
    parts = width_x // SUB
    total_steps, receivers = residual.shape[1:]
    plane = width_x * width_y
    slabs = lax.axis_size("slab")
    f32 = jnp.float32
    place = snake_of(slabs)
    at = lax.axis_index("slab")
    snake = place != list(range(slabs))
    shot = lax.axis_index("shot")
    halves = snake and lax.axis_size("shot") == 2
    slab = at
    if snake:
        row = slabs // 4
        z, chip, core = at // row, at % row // 2, at % 2
        slab = z * row + 2 * jnp.where(z % 2 == 1, row // 2 - 1 - chip, chip) + core
    up = [(place[i], place[i + 1]) for i in range(slabs - 1)]
    down = [(place[i + 1], place[i]) for i in range(slabs - 1)]
    swap = [(i, place[i]) for i in range(slabs)]
    half = depth // 2
    if snake:
        fwd_prev = lax.ppermute(fwd_prev, "slab", swap)
        fwd_last = lax.ppermute(fwd_last, "slab", swap)
    if halves:
        mine = jnp.where(shot == 0, velocity[:half], velocity[half:])
        mine = lax.ppermute(mine, "slab", swap)
        theirs = lax.ppermute(mine, "shot", [(0, 1), (1, 0)])
        speeds = (mine, theirs)
    else:
        speeds = (lax.ppermute(velocity, "slab", swap) if snake else velocity,)

    base = (slab * depth - SHIFT) * plane
    window = (depth + SHIFT) * plane
    local = rec_index[0] - base
    far = jnp.int32(2**30)
    keys = jnp.where((local >= 0) & (local < window), local, far)
    keys, ids = lax.sort((keys, lax.iota(jnp.int32, receivers)), num_keys=1, is_stable=False)

    def place_of(cell):
        layer = cell // plane
        x = (cell // width_y) % width_x
        return layer, x % parts, x // parts, cell % width_y

    layer, part, row, lane = place_of(keys)
    rows_of = (layer * parts + part) * SUB + row
    zones = (depth + SHIFT) // REACH
    edges = jnp.arange(zones + 1, dtype=jnp.int32) * (REACH * plane)
    starts = jnp.sum((keys[None, :] < edges[:, None]).astype(jnp.int32), axis=1)

    src = src_index[0] - base
    src_in = (src >= 0) & (src < window)
    s_layer, s_part, s_row, s_lane = place_of(jnp.where(src_in, src, 0))
    s_layer = jnp.where(src_in, s_layer, -1)
    is_last = (slab == slabs - 1).astype(jnp.int32)
    scalars = [is_last, s_layer, s_part, s_row, s_lane]
    gap = [jnp.zeros((), jnp.int32)] * (SHOT - STARTS - zones - 1)
    info = jnp.concatenate([jnp.stack(scalars), starts, jnp.stack([*gap, shot]), rows_of])
    last_step = total_steps - 1

    smem = pl.BlockSpec(memory_space=pltpu.SMEM)
    vmem = pl.BlockSpec(memory_space=pltpu.VMEM)
    anym = pl.BlockSpec(memory_space=pltpu.HBM)

    def fields(layers):
        return jax.ShapeDtypeStruct((layers, parts, SUB, width_y), f32)

    params = pltpu.CompilerParams(vmem_limit_bytes=VMEM_BYTES)
    once = pltpu.CompilerParams(vmem_limit_bytes=MORE_BYTES)
    fetch_scratch = [pltpu.VMEM((receivers, width_y), f32), pltpu.SemaphoreType.DMA(())]

    def lane_scratch(layers):
        rows = layers * parts * SUB
        return [
            pltpu.VMEM((rows, PIECES * width_y), jnp.bfloat16),
            pltpu.VMEM((rows, width_y), f32),
        ]

    span = pltpu.VMEM((SPAN, parts, SUB, width_y), f32)
    block_scratch = [span] + lane_scratch(2 * SHIFT)

    def cost(layers):
        return pl.CostEstimate(
            flops=50 * layers * plane, bytes_accessed=24 * layers * plane, transcendentals=0
        )

    near, table = pl.pallas_call(
        functools.partial(table_kernel, zones),
        out_shape=(
            jax.ShapeDtypeStruct((total_steps, CHUNK, width_y), f32),
            jax.ShapeDtypeStruct((total_steps, receivers, width_y), f32),
        ),
        in_specs=[smem] + [vmem] * 5,
        out_specs=(vmem, anym),
        scratch_shapes=[
            pltpu.VMEM((receivers // CHUNK, PIECES, total_steps, CHUNK), f32),
            pltpu.VMEM((PIECES * total_steps, receivers), jnp.bfloat16),
            pltpu.VMEM((CHUNK, CHUNK), jnp.bfloat16),
            pltpu.VMEM((total_steps, CHUNK, width_y), f32),
            pltpu.SemaphoreType.DMA(()),
        ],
        compiler_params=once,
        cost_estimate=cost(SHIFT),
        name="rec_table",
    )(
        info,
        ids.reshape(receivers // CHUNK, CHUNK),
        rows_of.reshape(receivers // CHUNK, CHUNK),
        rows_of[:, None],
        lane[:, None],
        residual[0],
    )
    coef_own, weights, lm, l_b, l_c, lb, work = pl.pallas_call(
        functools.partial(first_l_kernel, last_step, halves),
        out_shape=(
            fields(depth),
            jax.ShapeDtypeStruct((PIECES * width_y, width_y), jnp.bfloat16),
            fields(MSG),
            fields(SPAN),
            fields(SPAN),
            fields(MSG),
            fields(WORK_ALL),
        ),
        in_specs=[smem, vmem, anym] + [vmem] * len(speeds),
        out_specs=[vmem] * 7,
        scratch_shapes=fetch_scratch,
        compiler_params=once,
        cost_estimate=cost(2),
        name="first_l",
    )(info, near, table, *speeds)
    l_got = lax.ppermute(lm, "slab", up)

    def between(side, n0, *arrays):
        outs = [fields(WORK_ALL), fields(depth + SHIFT)]
        scratch = list(fetch_scratch)
        if n0 == 3:
            outs.append(fields(SHIFT))
        if n0 == last_step:
            scratch = [pltpu.VMEM((depth + SHIFT, parts, SUB, width_y), f32)] + scratch
        return pl.pallas_call(
            functools.partial(between_kernel, side, n0, last_step),
            out_shape=outs,
            in_specs=[smem, vmem, anym] + [vmem] * len(arrays),
            out_specs=[vmem] * len(outs),
            scratch_shapes=scratch,
            compiler_params=params,
            cost_estimate=cost(SHIFT),
            name=f"between{side}",
        )(info, near, table, *arrays)

    fwd_prev, fwd_last, _ = lax.optimization_barrier((fwd_prev, fwd_last, work))
    um, u_b, u_c, ub = pl.pallas_call(
        functools.partial(first_u_kernel, last_step),
        out_shape=(fields(MSG + REACH), fields(SPAN), fields(SPAN), fields(MSG)),
        in_specs=[smem] + [vmem] * 4,
        out_specs=[vmem] * 4,
        scratch_shapes=[pltpu.VMEM((depth, parts, SUB, width_y), f32)] * 2 + lane_scratch(SHIFT),
        compiler_params=once,
        cost_estimate=cost(SHIFT),
        name="first_u",
    )(info, fwd_prev[0], fwd_last[0], coef_own, weights)
    u_sent, l_got = lax.optimization_barrier((um, l_got))
    u_got = lax.ppermute(u_sent, "slab", up)
    coef = pl.pallas_call(
        join_kernel,
        out_shape=fields(depth + SHIFT),
        in_specs=[vmem] * 2,
        out_specs=vmem,
        compiler_params=once,
        cost_estimate=cost(1),
        name="join_coef",
    )(l_got, coef_own)
    opening = (lm, um, u_c)

    def block(is_l, side, n0, own, b, c, recv, beyond, *work):
        outs = []
        if n0 > 1:
            outs = [fields(MSG), fields(SPAN), fields(SPAN)] + ([fields(MSG)] if side == 0 else [])
        elif is_l:
            outs = [jax.ShapeDtypeStruct((depth, width_x, width_y), f32)]
        else:
            outs = [fields(SPAN)]
        outs.append(fields(WORK_ALL if is_l else SHIFT + REACH))
        scratch = list(block_scratch)
        if n0 == 1 and is_l:
            scratch += [span, span]
        if n0 == last_step and not is_l:
            scratch.append(pltpu.VMEM((SHIFT, parts, SUB, width_y), f32))
        return pl.pallas_call(
            functools.partial(block_kernel, side, is_l, n0, n0 == last_step),
            out_shape=outs,
            in_specs=[smem] + [vmem] * (7 + len(work)),
            out_specs=[vmem] * len(outs),
            scratch_shapes=scratch,
            compiler_params=params,
            cost_estimate=cost(2 * depth),
            name=("l" if is_l else "u") + f"_block{side}",
        )(info, own, b, c, recv, coef, weights, beyond, *work)

    terms_in = opening
    for n0 in range(last_step, 0, -2):
        side = (last_step - n0) // 2 % 2
        way = up if side else down
        if n0 == 1:
            adjoint_field, d = block(True, side, n0, lm, l_b, l_c, l_got, lb, work)
            if snake:
                adjoint_field = lax.ppermute(adjoint_field, "slab", swap)
            u_b, x0 = block(False, side, n0, um, u_b, u_c, u_got, ub)
            break
        lm, l_b, l_c, *lb_new, d = block(True, side, n0, lm, l_b, l_c, l_got, lb, work)
        lb = lb_new[0] if lb_new else lb
        l_got = lax.ppermute(lm, "slab", way)
        um, u_b, u_c, *ub_new, x0 = block(False, side, n0, um, u_b, u_c, u_got, ub)
        ub = ub_new[0] if ub_new else ub
        u_got = lax.ppermute(um, "slab", way)
        work, g, *g_left = between(side, n0, *terms_in, x0, u_b, u_c, d)
        terms_in = (g,)
    g_right = lax.ppermute(g_left[0], "slab", down)

    terms = pl.pallas_call(
        last_kernel,
        out_shape=jax.ShapeDtypeStruct((depth, width_x, width_y), f32),
        in_specs=[smem] + [vmem] * 6,
        out_specs=vmem,
        scratch_shapes=[pltpu.VMEM((depth + SHIFT, parts, SUB, width_y), f32)],
        compiler_params=once,
        cost_estimate=cost(SHIFT),
        name="last_terms",
    )(info, g, x0, u_b, d, g_right, aperture)
    summed = sum_shots(terms)
    if snake:
        summed, adjoint_field = lax.optimization_barrier((summed, adjoint_field))
        summed = lax.ppermute(summed, "slab", swap)
    block = width_x // lax.axis_size("shot")
    speed = lax.dynamic_slice_in_dim(velocity, shot * block, block, 1)
    return ((-2.0 / speed) * summed, adjoint_field[None])


def solution(mesh):
    in_specs = (
        P("shot", "slab", None, None),
        P("shot", "slab", None, None),
        P("slab", None, None),
        P("shot", None, None),
        P("shot", None),
        P("shot"),
        P("shot", None, None),
    )
    out_specs = (P("slab", "shot", None), P("shot", "slab", None, None))
    return jax.shard_map(on_device, mesh=mesh, in_specs=in_specs, out_specs=out_specs, check_vma=False)
```

```python
import functools

import jax
import jax.numpy as jnp
import numpy as np
from jax import lax
from jax.experimental import pallas as pl
from jax.experimental.pallas import tpu as pltpu
from jax.sharding import PartitionSpec as P

SCALE = 5040.0
WHOLE = (-14350.0, 8064.0, -1008.0, 128.0, -9.0)
REACH = 4
SHIFT = 8
VMEM_BYTES = 9 * 1024 * 1024
MORE_BYTES = 24 * 1024 * 1024
SUB = 8
PIECES = 3
CHUNK = 256
FAR = 2

MSG = 2 * SHIFT
WORK = 4 * SHIFT
WORK_ALL = 6 * SHIFT
SPAN = 32
MID = 12


def wave_of(step):
    arg = (np.pi * 0.06 * (step - 10.0)) ** 2
    return float(np.float32(SCALE * 10.0 * (1.0 - 2.0 * arg) * np.exp(-arg)))


def load_tiled(field, layer):
    parts = field.shape[1] // SUB
    return jnp.stack([field[layer, pl.ds(m, SUB, stride=parts), :] for m in range(parts)])


def store_tiled(field, layer, value, first=0, count=SUB):
    parts = value.shape[0]
    for m in range(parts):
        field[layer, pl.ds(m, count, stride=parts), :] = value[m, first : first + count]


def split3(f):
    hi = f.astype(jnp.bfloat16)
    left = f - hi.astype(jnp.float32)
    mid = left.astype(jnp.bfloat16)
    return hi, mid, (left - mid.astype(jnp.float32)).astype(jnp.bfloat16)


def put_weights(weights):
    width_y = weights.shape[1]
    square = (width_y, width_y)
    away = jnp.abs(lax.broadcasted_iota(jnp.int32, square, 0) - lax.broadcasted_iota(jnp.int32, square, 1))
    once = jnp.zeros(square, jnp.float32)
    for k in range(1, 5):
        once = jnp.where(away == k, WHOLE[k], once)
    for i in range(PIECES):
        weights[i * width_y : (i + 1) * width_y, :] = once.astype(jnp.bfloat16)


def lane_pass(cur, first, count, weights, pieces, ybuf):
    parts, _, width_y = cur.shape[1:]
    rows = parts * SUB

    def one(q):
        at = pl.multiple_of(q * rows, rows)
        for i, piece in enumerate(split3(cur[first + q].reshape(rows, width_y))):
            pieces[pl.ds(at, rows), i * width_y : (i + 1) * width_y] = piece

    layers_loop(0, count, one)
    block = slice(0, count * rows)
    ybuf[block, :] = jnp.dot(pieces[block, :], weights[...], preferred_element_type=jnp.float32)


def lap_maker(parts, width_y):
    row = lax.broadcasted_iota(jnp.int32, (1, SUB, width_y), 1)

    def lap(ref, j, along):
        f = ref[j]
        after = jnp.where(row == SUB - 1, 0.0, pltpu.roll(f[:REACH], SUB - 1, 1))
        before = jnp.where(row == 0, 0.0, pltpu.roll(f[parts - REACH :], 1, 1))
        wide = jnp.concatenate([before, f, after], axis=0)
        total = along + (3.0 * WHOLE[0]) * f
        for k in range(1, 5):
            pair = (ref[j + k] + ref[j - k]) + (
                wide[REACH + k : REACH + k + parts] + wide[REACH - k : REACH - k + parts]
            )
            total = total + WHOLE[k] * pair
        return f, total

    return lap


def layers_loop(first, count, body):
    def one(q, carry):
        body(first + q)
        return carry

    lax.fori_loop(0, count, one, 0, unroll=2)


STARTS = 5
SHOT = 15
ROWS = 16


def inject(work, at, info, near, table_hbm, table, sem, step, first, last):
    low, high = info[STARTS + first], info[STARTS + last]
    rows = work.shape[1] * SUB
    shift = at * rows - first * REACH * rows
    flat = work.reshape(work.shape[0] * rows, work.shape[3])

    def store(low, high, row_of):
        def one(r, carry):
            flat[pl.ds(info[ROWS + r] + shift, 1), :] = row_of(r)
            return carry

        def eight(i, carry):
            at = [low + i * 8 + q for q in range(8)]
            values = [row_of(r) for r in at]
            for r, value in zip(at, values):
                flat[pl.ds(info[ROWS + r] + shift, 1), :] = value
            return carry

        groups = lax.shift_right_logical(high - low, 3)
        lax.fori_loop(0, groups, eight, 0)
        lax.fori_loop(low + groups * 8, high, one, 0)

    split = jnp.clip(CHUNK, low, high)
    store(low, split, lambda r: near[step, pl.ds(r, 1), :])

    @pl.when(high > split)
    def _():
        fetch = pltpu.make_async_copy(table_hbm.at[step, pl.ds(0, table.shape[0]), :], table, sem)
        fetch.start()
        fetch.wait()
        store(split, high, lambda r: table[pl.ds(r, 1), :])


def zones_of(side):
    return (1, 0, 1) if side == 0 else (3, 2, 3)


def put_rows(work, side, n0, info, near, table_hbm, table, sem):
    shared = (info, near, table_hbm, table, sem)
    zero = jnp.zeros((SHIFT,) + work.shape[1:], jnp.float32)
    for i in range(0, WORK, SHIFT):
        work[i : i + SHIFT] = zero
    for level, (at, zone, count) in enumerate(zip((0, 8, 24), zones_of(side), (2, 4, 2))):
        if n0 >= level:
            inject(work, at, *shared, n0 - level, zone, zone + count)
    if side == 0:

        @pl.when(info[0] == 1)
        def _():
            for i in range(WORK, WORK_ALL, SHIFT):
                work[i : i + SHIFT] = zero
            for level, (at, zone, count) in enumerate(((32, 5, 1), (36, 4, 2), (44, 5, 1))):
                if n0 >= level:
                    inject(work, at, *shared, n0 - level, zone, zone + count)


def add_terms(g, g_in, side, n0, is_last, x, d):
    x0, b, c = x
    low = 0 if side == 0 else SHIFT
    more = n0 >= 2

    def edge(at):
        def one(q):
            g[low + at + q] = g_in[low + at + q] + b[MID - SHIFT + at + q] * d[SHIFT + at + q]

        layers_loop(0, REACH, one)

    def middle(q):
        total = x0[q] * d[q] + b[MID - REACH + q] * d[SHIFT + REACH + q]
        if more:
            total = total + c[MID - REACH + q] * d[3 * SHIFT + q]
        g[low + REACH + q] = g_in[low + REACH + q] + total

    edge(0)
    layers_loop(0, SHIFT, middle)
    edge(SHIFT + REACH)
    if side == 1:
        g[0:SHIFT] = g_in[0:SHIFT]
        return
    g[2 * SHIFT : 3 * SHIFT] = g_in[2 * SHIFT : 3 * SHIFT]

    @pl.when(is_last == 1)
    def _():
        for q in range(SHIFT):
            total = b[MID + SHIFT + q] * d[36 + q]
            if q >= REACH:
                total = total + x0[REACH + q] * d[28 + q]
                if more:
                    total = total + c[MID + SHIFT + q] * d[40 + q]
            g[2 * SHIFT + q] = g[2 * SHIFT + q] + total


def between_kernel(side, n0, opening, info, near, table_hbm, *refs):
    if n0 == opening:
        l_msg, u_msg, u_kept, *x, d, work, g, start, table, sem = refs
        start[...] = jnp.zeros(start.shape, jnp.float32)
        for z in range(REACH, REACH + SHIFT):
            was = u_kept[MID - SHIFT + z] if z < SHIFT else u_msg[z - SHIFT]
            start[z + SHIFT] = was * l_msg[z - REACH + SHIFT]
        g_in = start
    else:
        g_in, *x, d = refs[:5]
        work, g, *g_left, table, sem = refs[5:]
    add_terms(g, g_in, side, n0, info[0], x, d)
    if n0 == 3:
        g_left[0][...] = g[0:SHIFT]
    put_rows(work, 1 - side, n0 - 2, info, near, table_hbm, table, sem)


def chunks_of(info, zones):
    return jnp.maximum((info[STARTS + zones] + CHUNK - 1) // CHUNK, 1)


def table_kernel(zones, info, ids, rows_l, rows_s, lanes_s, res, near, out, res_cut, pieces, same, part, sem):
    steps, receivers = res.shape
    width_y = part.shape[2]
    chunks = chunks_of(info, zones)
    for i, piece in enumerate(split3(res[...])):
        pieces[i * steps : (i + 1) * steps, :] = piece

    def column(c, carry):
        who = lax.broadcasted_iota(jnp.int32, (receivers, CHUNK), 0) == ids[pl.ds(c, 1), :]
        moved = jnp.dot(
            pieces[...], jnp.where(who, 1.0, 0.0).astype(jnp.bfloat16), preferred_element_type=jnp.float32
        )
        total = SCALE * ((moved[:steps] + moved[steps : 2 * steps]) + moved[2 * steps :])
        for i, piece in enumerate(split3(total)):
            res_cut[c, i] = piece.astype(jnp.float32)
        return carry

    lax.fori_loop(0, chunks, column, 0)

    def to_chunk(c, carry):
        mine = rows_s[pl.ds(pl.multiple_of(c * CHUNK, CHUNK), CHUNK), :]

        def from_chunk(d, carry):
            same[...] = jnp.where(mine == rows_l[pl.ds(d, 1), :], 1.0, 0.0).astype(jnp.bfloat16)
            at = pl.multiple_of(d * CHUNK, CHUNK)
            lane = lax.broadcasted_iota(jnp.int32, (CHUNK, width_y), 1)
            spot = jnp.where(lane == lanes_s[pl.ds(at, CHUNK), :], 1.0, 0.0).astype(jnp.bfloat16)
            spots = jnp.concatenate([spot] * PIECES, axis=0)

            def one(n, carry):
                mixed = []
                for i in range(PIECES):
                    row = jnp.broadcast_to(res_cut[d, i, pl.ds(n, 1), :], (16, CHUNK)).astype(jnp.bfloat16)
                    mixed.append((same[...].reshape(CHUNK // 16, 16, CHUNK) * row[None]).reshape(CHUNK, CHUNK))
                total = jnp.dot(
                    jnp.concatenate(mixed, axis=1), spots, preferred_element_type=jnp.float32
                )
                part[n] = total + jnp.where(d > 0, part[n], 0.0)
                return carry

            return lax.fori_loop(0, steps, one, carry, unroll=4)

        lax.fori_loop(0, chunks, from_chunk, 0)
        return carry

    def store_chunk(c, carry):
        to_chunk(c, 0)
        at = pl.multiple_of(c * CHUNK, CHUNK)
        write = pltpu.make_async_copy(part, out.at[:, pl.ds(at, CHUNK), :], sem)
        write.start()
        write.wait()
        return carry

    to_chunk(0, 0)
    near[...] = part[...]
    lax.fori_loop(1, chunks, store_chunk, 0)


def block_kernel(side, is_l, n0, opening, *refs):
    refs = list(refs)

    def take(count):
        got = refs[:count]
        del refs[:count]
        return got

    final = n0 == 1
    info, own, b_kept, c_kept, recv, coef, weights, beyond = take(8)
    work_in = work_out = x_out = msg_out = beyond_out = field_out = p = None
    if is_l:
        (work_in,) = take(1)
    if not final:
        msg_out, b, c = take(3)
        if side == 0:
            (beyond_out,) = take(1)
    elif is_l:
        (field_out,) = take(1)
    else:
        (b,) = take(1)
    if is_l:
        (work_out,) = take(1)
    else:
        (x_out,) = take(1)
    a, pieces, ybuf = take(3)
    if final and is_l:
        b, c = take(2)
    if opening and not is_l:
        (p,) = take(1)

    parts, _, width_y = a.shape[1:]
    rows = parts * SUB
    is_last, src_layer, src_part, src_row, src_lane = (info[i] for i in range(STARTS))
    off = MID - SHIFT if side == 0 else MID - 2 * SHIFT
    lap = lap_maker(parts, width_y)

    def bring(msg, low):
        if low:
            a[MID - SHIFT : MID] = msg[0:SHIFT]
            b[MID - SHIFT - REACH : MID - REACH] = msg[SHIFT:MSG]
        else:
            a[MID : MID + SHIFT] = msg[0:SHIFT]
            b[MID + REACH : MID + REACH + SHIFT] = msg[SHIFT:MSG]

    if side == 0:
        bring(recv, True)
        a[MID : MID + SHIFT] = c_kept[MID - SHIFT : MID]
        b[MID + REACH : MID + REACH + SHIFT] = own[SHIFT:MSG]

        @pl.when(is_last == 1)
        def _():
            zero = jnp.zeros((REACH,) + a.shape[1:], jnp.float32)
            a[MID + SHIFT : MID + 2 * SHIFT] = own[0:SHIFT]
            for field in (a, b, c):
                field[MID + 2 * SHIFT : MID + 2 * SHIFT + REACH] = zero
            if opening and is_l:
                a[MID + SHIFT : MID + 2 * SHIFT] = jnp.zeros((SHIFT,) + a.shape[1:], jnp.float32)

        if opening and is_l:
            a[MID - SHIFT : MID] = jnp.zeros((SHIFT,) + a.shape[1:], jnp.float32)
    else:
        a[MID - SHIFT : MID] = c_kept[MID : MID + SHIFT]
        b[MID - SHIFT - REACH : MID - REACH] = own[SHIFT:MSG]

        @pl.when(is_last == 1)
        def _():
            bring(beyond, False)

        @pl.when(is_last == 0)
        def _():
            bring(recv, False)

    before = (b_kept, -SHIFT if side == 0 else SHIFT)
    if p is not None:
        p[0:REACH] = recv[MSG : MSG + REACH]
        p[REACH:SHIFT] = b_kept[REACH:SHIFT]
        before = (p, REACH - MID)

    def source(level, first, count, out, shift):
        j = src_layer + off

        @pl.when((src_layer >= 0) & (j >= first) & (j < first + count))
        def _():
            lane = lax.broadcasted_iota(jnp.int32, (1, width_y), 1)
            spot = out[j + shift, src_part, pl.ds(src_row, 1), :]
            gain = coef[src_layer, src_part, pl.ds(src_row, 1), :] * wave_of(n0 - level)
            out[j + shift, src_part, pl.ds(src_row, 1), :] = spot + jnp.where(lane == src_lane, gain, 0.0)

    def advance(level, cur, nxt, nxt_shift, first, count, work_at, out, shift):
        lane_pass(cur, first, count, weights, pieces, ybuf)

        def body(j):
            y_at = pl.multiple_of((j - first) * rows, rows)
            f, total = lap(cur, j, ybuf[pl.ds(y_at, rows), :].reshape(parts, SUB, width_y))
            if is_l:
                total = total + work_in[j + (work_at - first)]
            step = coef[j - off] * total
            out[j + shift] = (2.0 * f - nxt[j + nxt_shift]) + step
            if is_l:
                work_out[j + (work_at - first)] = step

        layers_loop(first, count, body)
        if not is_l:
            source(level, first, count, out, shift)

    def beyond_too(*args):
        if side == 0:

            @pl.when(is_last == 1)
            def _():
                advance(*args)

    far = MID + SHIFT + REACH
    advance(0, a, *before, MID - REACH, SHIFT, 0, b, 0)
    beyond_too(0, a, beyond, SHIFT - far, far, REACH, 32, b, 0)
    if not is_l:
        x_out[0:SHIFT] = a[MID - REACH : MID + REACH]
        if side == 0:

            @pl.when(is_last == 1)
            def _():
                x_out[SHIFT : SHIFT + REACH] = a[far : far + REACH]

        if final:
            return
    advance(1, b, a, 0, MID - SHIFT, 2 * SHIFT, 8, c, 0)
    beyond_too(1, b, a, 0, MID + SHIFT, SHIFT, 36, c, 0)
    if final:
        for layer in range(2 * SHIFT):
            store_tiled(field_out, layer, c[MID - SHIFT + layer])
        return
    advance(2, c, b, 0, MID - REACH, SHIFT, 24, msg_out, SHIFT - (MID - REACH))
    if side == 1:
        msg_out[0:SHIFT] = c[MID : MID + SHIFT]
        return
    msg_out[0:SHIFT] = c[MID - SHIFT : MID]

    @pl.when(is_last == 1)
    def _():
        advance(2, c, b, 0, far, REACH, 44, beyond_out, SHIFT - far)
        beyond_out[0:SHIFT] = c[MID + SHIFT : MID + 2 * SHIFT]
        beyond_out[SHIFT + REACH : MSG] = jnp.zeros((REACH,) + a.shape[1:], jnp.float32)


def first_l_kernel(n0, halves, info, near, table_hbm, *refs):
    refs = list(refs)
    speeds = refs[: 1 + halves]
    coef, weights, msg_out, b_kept, c_kept, beyond, work, table, sem = refs[1 + halves :]
    put_weights(weights)

    def fill(speed, first):
        def one(z):
            coef[z + first] = (0.4 * load_tiled(speed, z)) ** 2 * (1.0 / SCALE)

        layers_loop(0, speed.shape[0], one)

    if halves:

        @pl.when(info[SHOT] == 0)
        def _():
            fill(speeds[0], 0)
            fill(speeds[1], SHIFT)

        @pl.when(info[SHOT] != 0)
        def _():
            fill(speeds[1], 0)
            fill(speeds[0], SHIFT)
    else:
        fill(speeds[0], 0)
    msg_out[0:SHIFT] = coef[coef.shape[0] - SHIFT :]
    msg_out[SHIFT:MSG] = jnp.zeros((SHIFT,) + coef.shape[1:], jnp.float32)
    beyond[...] = jnp.zeros(beyond.shape, jnp.float32)
    b_kept[0:SHIFT] = jnp.zeros((SHIFT,) + coef.shape[1:], jnp.float32)
    c_kept[MID - SHIFT : MID] = jnp.zeros((SHIFT,) + coef.shape[1:], jnp.float32)
    zone = (SHIFT + REACH) // REACH
    inject(msg_out, SHIFT, info, near, table_hbm, table, sem, n0, zone, zone + SHIFT // REACH)

    def body(q):
        msg_out[q + SHIFT] = coef[q + REACH] * msg_out[q + SHIFT]

    layers_loop(0, SHIFT, body)
    put_rows(work, 0, n0, info, near, table_hbm, table, sem)


def join_kernel(l_got, own, coef):
    coef[0:SHIFT] = l_got[0:SHIFT]
    coef[SHIFT:] = own[...]


def first_u_kernel(n0, info, prev, last, coef, weights, msg_out, b_kept, c_kept, beyond, f0, f1, pieces, ybuf):
    depth, parts, _, width_y = f0.shape
    rows = parts * SUB
    src_layer, src_part, src_row, src_lane = (info[i] for i in range(1, STARTS))
    lap = lap_maker(parts, width_y)

    def bring(z):
        f0[z] = load_tiled(prev, z)
        f1[z] = load_tiled(last, z)

    layers_loop(0, depth, bring)
    msg_out[0:SHIFT] = f0[depth - SHIFT : depth]
    msg_out[MSG : MSG + REACH] = f1[depth - REACH : depth]
    c_kept[MID - SHIFT : MID] = f0[0:SHIFT]
    b_kept[REACH:SHIFT] = f1[0:REACH]
    beyond[...] = jnp.zeros(beyond.shape, jnp.float32)
    beyond[SHIFT : SHIFT + REACH] = f1[depth - REACH : depth]
    lane_pass(f0, REACH, SHIFT, weights, pieces, ybuf)
    to = SHIFT - REACH

    def body(j):
        y_at = pl.multiple_of((j - REACH) * rows, rows)
        f, total = lap(f0, j, ybuf[pl.ds(y_at, rows), :].reshape(parts, SUB, width_y))
        msg_out[j + to] = (2.0 * f - f1[j]) + coef[j] * total

    layers_loop(REACH, SHIFT, body)
    j = src_layer - SHIFT

    @pl.when((src_layer >= 0) & (j >= REACH) & (j < REACH + SHIFT))
    def _():
        lane = lax.broadcasted_iota(jnp.int32, (1, width_y), 1)
        spot = msg_out[j + to, src_part, pl.ds(src_row, 1), :]
        gain = coef[j, src_part, pl.ds(src_row, 1), :] * wave_of(n0)
        msg_out[j + to, src_part, pl.ds(src_row, 1), :] = spot + jnp.where(lane == src_lane, gain, 0.0)


def last_kernel(info, g_in, x0, b, d, g_right, gate, out, g):
    depth = out.shape[0]
    add_terms(g, g_in, 1, 1, info[0], (x0, b, None), d)

    def one(z):
        store_tiled(out, z, load_tiled(gate, 0).astype(jnp.float32) * g[z + SHIFT])

    def shared(z):
        store_tiled(out, z, load_tiled(gate, 0).astype(jnp.float32) * (g[z + SHIFT] + g_right[z - SHIFT]))

    layers_loop(0, SHIFT, one)
    layers_loop(SHIFT, depth - SHIFT, shared)


def sum_shots(g):
    shots = lax.axis_size("shot")
    if shots != 2:
        return lax.psum_scatter(g, "shot", scatter_dimension=1, tiled=True)
    block = g.shape[1] // 2
    low, high = g[:, :block], g[:, block:]
    first = lax.axis_index("shot") == 0
    other = lax.ppermute(jnp.where(first, high, low), "shot", [(0, 1), (1, 0)])
    return jnp.where(first, low, high) + other


def snake_of(slabs):
    row = slabs // 4
    if slabs % 8:
        return list(range(slabs))
    order = []
    for i in range(slabs):
        z, (chip, core) = i // row, divmod(i % row, 2)
        order.append(z * row + 2 * (row // 2 - 1 - chip if z % 2 else chip) + core)
    return order


def on_device(fwd_last, fwd_prev, velocity, aperture, rec_index, src_index, residual):
    _, depth, width_x, width_y = fwd_last.shape
    parts = width_x // SUB
    total_steps, receivers = residual.shape[1:]
    plane = width_x * width_y
    slabs = lax.axis_size("slab")
    f32 = jnp.float32
    place = snake_of(slabs)
    at = lax.axis_index("slab")
    snake = place != list(range(slabs))
    shot = lax.axis_index("shot")
    halves = snake and lax.axis_size("shot") == 2
    slab = at
    if snake:
        row = slabs // 4
        z, chip, core = at // row, at % row // 2, at % 2
        slab = z * row + 2 * jnp.where(z % 2 == 1, row // 2 - 1 - chip, chip) + core
    up = [(place[i], place[i + 1]) for i in range(slabs - 1)]
    down = [(place[i + 1], place[i]) for i in range(slabs - 1)]
    swap = [(i, place[i]) for i in range(slabs)]
    half = depth // 2
    if snake:
        fwd_prev = lax.ppermute(fwd_prev, "slab", swap)
        fwd_last = lax.ppermute(fwd_last, "slab", swap)
    if halves:
        mine = jnp.where(shot == 0, velocity[:half], velocity[half:])
        mine = lax.ppermute(mine, "slab", swap)
        theirs = lax.ppermute(mine, "shot", [(0, 1), (1, 0)])
        speeds = (mine, theirs)
    else:
        speeds = (lax.ppermute(velocity, "slab", swap) if snake else velocity,)

    base = (slab * depth - SHIFT) * plane
    window = (depth + SHIFT) * plane
    local = rec_index[0] - base
    far = jnp.int32(2**30)
    keys = jnp.where((local >= 0) & (local < window), local, far)
    keys, ids = lax.sort((keys, lax.iota(jnp.int32, receivers)), num_keys=1, is_stable=False)

    def place_of(cell):
        layer = cell // plane
        x = (cell // width_y) % width_x
        return layer, x % parts, x // parts, cell % width_y

    layer, part, row, lane = place_of(keys)
    rows_of = (layer * parts + part) * SUB + row
    zones = (depth + SHIFT) // REACH
    edges = jnp.arange(zones + 1, dtype=jnp.int32) * (REACH * plane)
    starts = jnp.sum((keys[None, :] < edges[:, None]).astype(jnp.int32), axis=1)

    src = src_index[0] - base
    src_in = (src >= 0) & (src < window)
    s_layer, s_part, s_row, s_lane = place_of(jnp.where(src_in, src, 0))
    s_layer = jnp.where(src_in, s_layer, -1)
    is_last = (slab == slabs - 1).astype(jnp.int32)
    scalars = [is_last, s_layer, s_part, s_row, s_lane]
    gap = [jnp.zeros((), jnp.int32)] * (SHOT - STARTS - zones - 1)
    info = jnp.concatenate([jnp.stack(scalars), starts, jnp.stack([*gap, shot]), rows_of])
    last_step = total_steps - 1

    smem = pl.BlockSpec(memory_space=pltpu.SMEM)
    vmem = pl.BlockSpec(memory_space=pltpu.VMEM)
    anym = pl.BlockSpec(memory_space=pltpu.HBM)

    def fields(layers):
        return jax.ShapeDtypeStruct((layers, parts, SUB, width_y), f32)

    params = pltpu.CompilerParams(vmem_limit_bytes=VMEM_BYTES)
    once = pltpu.CompilerParams(vmem_limit_bytes=MORE_BYTES)
    fetch_scratch = [pltpu.VMEM((receivers, width_y), f32), pltpu.SemaphoreType.DMA(())]

    def lane_scratch(layers):
        rows = layers * parts * SUB
        return [
            pltpu.VMEM((rows, PIECES * width_y), jnp.bfloat16),
            pltpu.VMEM((rows, width_y), f32),
        ]

    span = pltpu.VMEM((SPAN, parts, SUB, width_y), f32)
    block_scratch = [span] + lane_scratch(2 * SHIFT)

    def cost(layers):
        return pl.CostEstimate(
            flops=50 * layers * plane, bytes_accessed=24 * layers * plane, transcendentals=0
        )

    near, table = pl.pallas_call(
        functools.partial(table_kernel, zones),
        out_shape=(
            jax.ShapeDtypeStruct((total_steps, CHUNK, width_y), f32),
            jax.ShapeDtypeStruct((total_steps, FAR * receivers, width_y), f32),
        ),
        in_specs=[smem] + [vmem] * 5,
        out_specs=(vmem, anym),
        scratch_shapes=[
            pltpu.VMEM((receivers // CHUNK, PIECES, total_steps, CHUNK), f32),
            pltpu.VMEM((PIECES * total_steps, receivers), jnp.bfloat16),
            pltpu.VMEM((CHUNK, CHUNK), jnp.bfloat16),
            pltpu.VMEM((total_steps, CHUNK, width_y), f32),
            pltpu.SemaphoreType.DMA(()),
        ],
        compiler_params=once,
        cost_estimate=cost(SHIFT),
        name="rec_table",
    )(
        info,
        ids.reshape(receivers // CHUNK, CHUNK),
        rows_of.reshape(receivers // CHUNK, CHUNK),
        rows_of[:, None],
        lane[:, None],
        residual[0],
    )
    coef_own, weights, lm, l_b, l_c, lb, work = pl.pallas_call(
        functools.partial(first_l_kernel, last_step, halves),
        out_shape=(
            fields(depth),
            jax.ShapeDtypeStruct((PIECES * width_y, width_y), jnp.bfloat16),
            fields(MSG),
            fields(SPAN),
            fields(SPAN),
            fields(MSG),
            fields(WORK_ALL),
        ),
        in_specs=[smem, vmem, anym] + [vmem] * len(speeds),
        out_specs=[vmem] * 7,
        scratch_shapes=fetch_scratch,
        compiler_params=once,
        cost_estimate=cost(2),
        name="first_l",
    )(info, near, table, *speeds)
    l_got = lax.ppermute(lm, "slab", up)

    def between(side, n0, *arrays):
        outs = [fields(WORK_ALL), fields(depth + SHIFT)]
        scratch = list(fetch_scratch)
        if n0 == 3:
            outs.append(fields(SHIFT))
        if n0 == last_step:
            scratch = [pltpu.VMEM((depth + SHIFT, parts, SUB, width_y), f32)] + scratch
        return pl.pallas_call(
            functools.partial(between_kernel, side, n0, last_step),
            out_shape=outs,
            in_specs=[smem, vmem, anym] + [vmem] * len(arrays),
            out_specs=[vmem] * len(outs),
            scratch_shapes=scratch,
            compiler_params=params,
            cost_estimate=cost(SHIFT),
            name=f"between{side}",
        )(info, near, table, *arrays)

    fwd_prev, fwd_last, _ = lax.optimization_barrier((fwd_prev, fwd_last, work))
    um, u_b, u_c, ub = pl.pallas_call(
        functools.partial(first_u_kernel, last_step),
        out_shape=(fields(MSG + REACH), fields(SPAN), fields(SPAN), fields(MSG)),
        in_specs=[smem] + [vmem] * 4,
        out_specs=[vmem] * 4,
        scratch_shapes=[pltpu.VMEM((depth, parts, SUB, width_y), f32)] * 2 + lane_scratch(SHIFT),
        compiler_params=once,
        cost_estimate=cost(SHIFT),
        name="first_u",
    )(info, fwd_prev[0], fwd_last[0], coef_own, weights)
    u_sent, l_got = lax.optimization_barrier((um, l_got))
    u_got = lax.ppermute(u_sent, "slab", up)
    coef = pl.pallas_call(
        join_kernel,
        out_shape=fields(depth + SHIFT),
        in_specs=[vmem] * 2,
        out_specs=vmem,
        compiler_params=once,
        cost_estimate=cost(1),
        name="join_coef",
    )(l_got, coef_own)
    opening = (lm, um, u_c)

    def block(is_l, side, n0, own, b, c, recv, beyond, *work):
        outs = []
        if n0 > 1:
            outs = [fields(MSG), fields(SPAN), fields(SPAN)] + ([fields(MSG)] if side == 0 else [])
        elif is_l:
            outs = [jax.ShapeDtypeStruct((depth, width_x, width_y), f32)]
        else:
            outs = [fields(SPAN)]
        outs.append(fields(WORK_ALL if is_l else SHIFT + REACH))
        scratch = list(block_scratch)
        if n0 == 1 and is_l:
            scratch += [span, span]
        if n0 == last_step and not is_l:
            scratch.append(pltpu.VMEM((SHIFT, parts, SUB, width_y), f32))
        return pl.pallas_call(
            functools.partial(block_kernel, side, is_l, n0, n0 == last_step),
            out_shape=outs,
            in_specs=[smem] + [vmem] * (7 + len(work)),
            out_specs=[vmem] * len(outs),
            scratch_shapes=scratch,
            compiler_params=params,
            cost_estimate=cost(2 * depth),
            name=("l" if is_l else "u") + f"_block{side}",
        )(info, own, b, c, recv, coef, weights, beyond, *work)

    terms_in = opening
    for n0 in range(last_step, 0, -2):
        side = (last_step - n0) // 2 % 2
        way = up if side else down
        if n0 == 1:
            adjoint_field, d = block(True, side, n0, lm, l_b, l_c, l_got, lb, work)
            if snake:
                adjoint_field = lax.ppermute(adjoint_field, "slab", swap)
            u_b, x0 = block(False, side, n0, um, u_b, u_c, u_got, ub)
            break
        lm, l_b, l_c, *lb_new, d = block(True, side, n0, lm, l_b, l_c, l_got, lb, work)
        lb = lb_new[0] if lb_new else lb
        l_got = lax.ppermute(lm, "slab", way)
        um, u_b, u_c, *ub_new, x0 = block(False, side, n0, um, u_b, u_c, u_got, ub)
        ub = ub_new[0] if ub_new else ub
        u_got = lax.ppermute(um, "slab", way)
        work, g, *g_left = between(side, n0, *terms_in, x0, u_b, u_c, d)
        terms_in = (g,)
    g_right = lax.ppermute(g_left[0], "slab", down)

    terms = pl.pallas_call(
        last_kernel,
        out_shape=jax.ShapeDtypeStruct((depth, width_x, width_y), f32),
        in_specs=[smem] + [vmem] * 6,
        out_specs=vmem,
        scratch_shapes=[pltpu.VMEM((depth + SHIFT, parts, SUB, width_y), f32)],
        compiler_params=once,
        cost_estimate=cost(SHIFT),
        name="last_terms",
    )(info, g, x0, u_b, d, g_right, aperture)
    summed = sum_shots(terms)
    if snake:
        summed, adjoint_field = lax.optimization_barrier((summed, adjoint_field))
        summed = lax.ppermute(summed, "slab", swap)
    block = width_x // lax.axis_size("shot")
    speed = lax.dynamic_slice_in_dim(velocity, shot * block, block, 1)
    return ((-2.0 / speed) * summed, adjoint_field[None])


def solution(mesh):
    in_specs = (
        P("shot", "slab", None, None),
        P("shot", "slab", None, None),
        P("slab", None, None),
        P("shot", None, None),
        P("shot", None),
        P("shot"),
        P("shot", None, None),
    )
    out_specs = (P("slab", "shot", None), P("shot", "slab", None, None))
    return jax.shard_map(on_device, mesh=mesh, in_specs=in_specs, out_specs=out_specs, check_vma=False)
```

```python
import functools

import jax
import jax.numpy as jnp
import numpy as np
from jax import lax
from jax.experimental import pallas as pl
from jax.experimental.pallas import tpu as pltpu
from jax.sharding import PartitionSpec as P

SCALE = 5040.0
WHOLE = (-14350.0, 8064.0, -1008.0, 128.0, -9.0)
REACH = 4
SHIFT = 8
VMEM_BYTES = 9 * 1024 * 1024
MORE_BYTES = 24 * 1024 * 1024
SUB = 8
PIECES = 3
CHUNK = 256
FAR = 2

MSG = 2 * SHIFT
WORK = 4 * SHIFT
WORK_ALL = 6 * SHIFT
SPAN = 32
MID = 12


def wave_of(step):
    arg = (np.pi * 0.06 * (step - 10.0)) ** 2
    return float(np.float32(SCALE * 10.0 * (1.0 - 2.0 * arg) * np.exp(-arg)))


def load_tiled(field, layer):
    parts = field.shape[1] // SUB
    return jnp.stack([field[layer, pl.ds(m, SUB, stride=parts), :] for m in range(parts)])


def store_tiled(field, layer, value, first=0, count=SUB):
    parts = value.shape[0]
    for m in range(parts):
        field[layer, pl.ds(m, count, stride=parts), :] = value[m, first : first + count]


def split3(f):
    hi = f.astype(jnp.bfloat16)
    left = f - hi.astype(jnp.float32)
    mid = left.astype(jnp.bfloat16)
    return hi, mid, (left - mid.astype(jnp.float32)).astype(jnp.bfloat16)


def put_weights(weights):
    width_y = weights.shape[1]
    square = (width_y, width_y)
    away = jnp.abs(lax.broadcasted_iota(jnp.int32, square, 0) - lax.broadcasted_iota(jnp.int32, square, 1))
    once = jnp.zeros(square, jnp.float32)
    for k in range(1, 5):
        once = jnp.where(away == k, WHOLE[k], once)
    for i in range(PIECES):
        weights[i * width_y : (i + 1) * width_y, :] = once.astype(jnp.bfloat16)


def lane_pass(cur, first, count, weights, pieces, ybuf):
    parts, _, width_y = cur.shape[1:]
    rows = parts * SUB

    def one(q):
        at = pl.multiple_of(q * rows, rows)
        for i, piece in enumerate(split3(cur[first + q].reshape(rows, width_y))):
            pieces[pl.ds(at, rows), i * width_y : (i + 1) * width_y] = piece

    layers_loop(0, count, one)
    block = slice(0, count * rows)
    ybuf[block, :] = jnp.dot(pieces[block, :], weights[...], preferred_element_type=jnp.float32)


def lap_maker(parts, width_y):
    row = lax.broadcasted_iota(jnp.int32, (SUB, width_y), 0)

    def lap(ref, j, along):
        f = ([], [])
        total = ([], [])
        for m in range(parts):
            column = [ref[j + d, m] for d in range(-REACH, REACH + 2)]
            for t in range(2):
                mid = REACH + t
                f[t].append(column[mid])
                value = along[t, m] + (3.0 * WHOLE[0]) * column[mid]
                total[t].append((value, [column[mid + k] + column[mid - k] for k in range(1, 5)]))
        for t in range(2):
            after = [jnp.where(row == SUB - 1, 0.0, pltpu.roll(v, SUB - 1, 0)) for v in f[t][:REACH]]
            before = [jnp.where(row == 0, 0.0, pltpu.roll(v, 1, 0)) for v in f[t][parts - REACH :]]
            wide = before + f[t] + after
            for m in range(parts):
                value, pairs = total[t][m]
                for k in range(1, 5):
                    value = value + WHOLE[k] * (pairs[k - 1] + (wide[REACH + m + k] + wide[REACH + m - k]))
                total[t][m] = value
        return f, total

    return lap


def layers_loop(first, count, body):
    def one(q, carry):
        body(first + q)
        return carry

    lax.fori_loop(0, count, one, 0, unroll=2)


STARTS = 5
SHOT = 15
ROWS = 16


def inject(work, at, info, near, table_hbm, table, sem, step, first, last):
    low, high = info[STARTS + first], info[STARTS + last]
    rows = work.shape[1] * SUB
    shift = at * rows - first * REACH * rows
    flat = work.reshape(work.shape[0] * rows, work.shape[3])

    def store(low, high, row_of):
        def one(r, carry):
            flat[pl.ds(info[ROWS + r] + shift, 1), :] = row_of(r)
            return carry

        def eight(i, carry):
            at = [low + i * 8 + q for q in range(8)]
            values = [row_of(r) for r in at]
            for r, value in zip(at, values):
                flat[pl.ds(info[ROWS + r] + shift, 1), :] = value
            return carry

        groups = lax.shift_right_logical(high - low, 3)
        lax.fori_loop(0, groups, eight, 0)
        lax.fori_loop(low + groups * 8, high, one, 0)

    split = jnp.clip(CHUNK, low, high)
    store(low, split, lambda r: near[step, pl.ds(r, 1), :])

    @pl.when(high > split)
    def _():
        fetch = pltpu.make_async_copy(table_hbm.at[step, pl.ds(0, table.shape[0]), :], table, sem)
        fetch.start()
        fetch.wait()
        store(split, high, lambda r: table[pl.ds(r, 1), :])


def zones_of(side):
    return (1, 0, 1) if side == 0 else (3, 2, 3)


def put_rows(work, side, n0, info, near, table_hbm, table, sem):
    shared = (info, near, table_hbm, table, sem)
    zero = jnp.zeros((SHIFT,) + work.shape[1:], jnp.float32)
    for i in range(0, WORK, SHIFT):
        work[i : i + SHIFT] = zero
    for level, (at, zone, count) in enumerate(zip((0, 8, 24), zones_of(side), (2, 4, 2))):
        if n0 >= level:
            inject(work, at, *shared, n0 - level, zone, zone + count)
    if side == 0:

        @pl.when(info[0] == 1)
        def _():
            for i in range(WORK, WORK_ALL, SHIFT):
                work[i : i + SHIFT] = zero
            for level, (at, zone, count) in enumerate(((32, 5, 1), (36, 4, 2), (44, 5, 1))):
                if n0 >= level:
                    inject(work, at, *shared, n0 - level, zone, zone + count)


def add_terms(g, g_in, side, n0, is_last, x, d):
    x0, b, c = x
    low = 0 if side == 0 else SHIFT
    more = n0 >= 2

    def edge(at):
        def one(q):
            g[low + at + q] = g_in[low + at + q] + b[MID - SHIFT + at + q] * d[SHIFT + at + q]

        layers_loop(0, REACH, one)

    def middle(q):
        total = x0[q] * d[q] + b[MID - REACH + q] * d[SHIFT + REACH + q]
        if more:
            total = total + c[MID - REACH + q] * d[3 * SHIFT + q]
        g[low + REACH + q] = g_in[low + REACH + q] + total

    edge(0)
    layers_loop(0, SHIFT, middle)
    edge(SHIFT + REACH)
    if side == 1:
        g[0:SHIFT] = g_in[0:SHIFT]
        return
    g[2 * SHIFT : 3 * SHIFT] = g_in[2 * SHIFT : 3 * SHIFT]

    @pl.when(is_last == 1)
    def _():
        for q in range(SHIFT):
            total = b[MID + SHIFT + q] * d[36 + q]
            if q >= REACH:
                total = total + x0[REACH + q] * d[28 + q]
                if more:
                    total = total + c[MID + SHIFT + q] * d[40 + q]
            g[2 * SHIFT + q] = g[2 * SHIFT + q] + total


def between_kernel(side, n0, opening, info, near, table_hbm, *refs):
    if n0 == opening:
        l_msg, u_msg, u_kept, *x, d, work, g, start, table, sem = refs
        start[...] = jnp.zeros(start.shape, jnp.float32)
        for z in range(REACH, REACH + SHIFT):
            was = u_kept[MID - SHIFT + z] if z < SHIFT else u_msg[z - SHIFT]
            start[z + SHIFT] = was * l_msg[z - REACH + SHIFT]
        g_in = start
    else:
        g_in, *x, d = refs[:5]
        work, g, *g_left, table, sem = refs[5:]
    add_terms(g, g_in, side, n0, info[0], x, d)
    if n0 == 3:
        g_left[0][...] = g[0:SHIFT]
    put_rows(work, 1 - side, n0 - 2, info, near, table_hbm, table, sem)


def chunks_of(info, zones):
    return jnp.maximum((info[STARTS + zones] + CHUNK - 1) // CHUNK, 1)


def table_kernel(zones, info, ids, rows_l, rows_s, lanes_s, res, near, out, res_cut, pieces, same, part, sem):
    steps, receivers = res.shape
    width_y = part.shape[2]
    chunks = chunks_of(info, zones)
    for i, piece in enumerate(split3(res[...])):
        pieces[i * steps : (i + 1) * steps, :] = piece

    def column(c, carry):
        who = lax.broadcasted_iota(jnp.int32, (receivers, CHUNK), 0) == ids[pl.ds(c, 1), :]
        moved = jnp.dot(
            pieces[...], jnp.where(who, 1.0, 0.0).astype(jnp.bfloat16), preferred_element_type=jnp.float32
        )
        total = SCALE * ((moved[:steps] + moved[steps : 2 * steps]) + moved[2 * steps :])
        for i, piece in enumerate(split3(total)):
            res_cut[c, i] = piece.astype(jnp.float32)
        return carry

    lax.fori_loop(0, chunks, column, 0)

    def to_chunk(c, carry):
        mine = rows_s[pl.ds(pl.multiple_of(c * CHUNK, CHUNK), CHUNK), :]

        def from_chunk(d, carry):
            same[...] = jnp.where(mine == rows_l[pl.ds(d, 1), :], 1.0, 0.0).astype(jnp.bfloat16)
            at = pl.multiple_of(d * CHUNK, CHUNK)
            lane = lax.broadcasted_iota(jnp.int32, (CHUNK, width_y), 1)
            spot = jnp.where(lane == lanes_s[pl.ds(at, CHUNK), :], 1.0, 0.0).astype(jnp.bfloat16)
            spots = jnp.concatenate([spot] * PIECES, axis=0)

            def one(n, carry):
                mixed = []
                for i in range(PIECES):
                    row = jnp.broadcast_to(res_cut[d, i, pl.ds(n, 1), :], (16, CHUNK)).astype(jnp.bfloat16)
                    mixed.append((same[...].reshape(CHUNK // 16, 16, CHUNK) * row[None]).reshape(CHUNK, CHUNK))
                total = jnp.dot(
                    jnp.concatenate(mixed, axis=1), spots, preferred_element_type=jnp.float32
                )
                part[n] = total + jnp.where(d > 0, part[n], 0.0)
                return carry

            return lax.fori_loop(0, steps, one, carry, unroll=4)

        lax.fori_loop(0, chunks, from_chunk, 0)
        return carry

    def store_chunk(c, carry):
        to_chunk(c, 0)
        at = pl.multiple_of(c * CHUNK, CHUNK)
        write = pltpu.make_async_copy(part, out.at[:, pl.ds(at, CHUNK), :], sem)
        write.start()
        write.wait()
        return carry

    to_chunk(0, 0)
    near[...] = part[...]
    lax.fori_loop(1, chunks, store_chunk, 0)


def block_kernel(side, is_l, n0, opening, *refs):
    refs = list(refs)

    def take(count):
        got = refs[:count]
        del refs[:count]
        return got

    final = n0 == 1
    info, own, b_kept, c_kept, recv, coef, weights, beyond = take(8)
    work_in = work_out = x_out = msg_out = beyond_out = field_out = p = None
    if is_l:
        (work_in,) = take(1)
    if not final:
        msg_out, b, c = take(3)
        if side == 0:
            (beyond_out,) = take(1)
    elif is_l:
        (field_out,) = take(1)
    else:
        (b,) = take(1)
    if is_l:
        (work_out,) = take(1)
    else:
        (x_out,) = take(1)
    a, pieces, ybuf = take(3)
    if final and is_l:
        b, c = take(2)
    if opening and not is_l:
        (p,) = take(1)

    parts, _, width_y = a.shape[1:]
    rows = parts * SUB
    is_last, src_layer, src_part, src_row, src_lane = (info[i] for i in range(STARTS))
    off = MID - SHIFT if side == 0 else MID - 2 * SHIFT
    lap = lap_maker(parts, width_y)

    def bring(msg, low):
        if low:
            a[MID - SHIFT : MID] = msg[0:SHIFT]
            b[MID - SHIFT - REACH : MID - REACH] = msg[SHIFT:MSG]
        else:
            a[MID : MID + SHIFT] = msg[0:SHIFT]
            b[MID + REACH : MID + REACH + SHIFT] = msg[SHIFT:MSG]

    if side == 0:
        bring(recv, True)
        a[MID : MID + SHIFT] = c_kept[MID - SHIFT : MID]
        b[MID + REACH : MID + REACH + SHIFT] = own[SHIFT:MSG]

        @pl.when(is_last == 1)
        def _():
            zero = jnp.zeros((REACH,) + a.shape[1:], jnp.float32)
            a[MID + SHIFT : MID + 2 * SHIFT] = own[0:SHIFT]
            for field in (a, b, c):
                field[MID + 2 * SHIFT : MID + 2 * SHIFT + REACH] = zero
            if opening and is_l:
                a[MID + SHIFT : MID + 2 * SHIFT] = jnp.zeros((SHIFT,) + a.shape[1:], jnp.float32)

        if opening and is_l:
            a[MID - SHIFT : MID] = jnp.zeros((SHIFT,) + a.shape[1:], jnp.float32)
    else:
        a[MID - SHIFT : MID] = c_kept[MID : MID + SHIFT]
        b[MID - SHIFT - REACH : MID - REACH] = own[SHIFT:MSG]

        @pl.when(is_last == 1)
        def _():
            bring(beyond, False)

        @pl.when(is_last == 0)
        def _():
            bring(recv, False)

    before = (b_kept, -SHIFT if side == 0 else SHIFT)
    if p is not None:
        p[0:REACH] = recv[MSG : MSG + REACH]
        p[REACH:SHIFT] = b_kept[REACH:SHIFT]
        before = (p, REACH - MID)

    def source(level, first, count, out, shift):
        j = src_layer + off

        @pl.when((src_layer >= 0) & (j >= first) & (j < first + count))
        def _():
            lane = lax.broadcasted_iota(jnp.int32, (1, width_y), 1)
            spot = out[j + shift, src_part, pl.ds(src_row, 1), :]
            gain = coef[src_layer, src_part, pl.ds(src_row, 1), :] * wave_of(n0 - level)
            out[j + shift, src_part, pl.ds(src_row, 1), :] = spot + jnp.where(lane == src_lane, gain, 0.0)

    def advance(level, cur, nxt, nxt_shift, first, count, work_at, out, shift):
        lane_pass(cur, first, count, weights, pieces, ybuf)

        def body(q):
            j = first + 2 * q
            y_at = pl.multiple_of(q * 2 * rows, 2 * rows)
            f, total = lap(cur, j, ybuf[pl.ds(y_at, 2 * rows), :].reshape(2, parts, SUB, width_y))
            for t in range(2):
                for m in range(parts):
                    value = total[t][m]
                    if is_l:
                        value = value + work_in[work_at + 2 * q + t, m]
                    step = coef[j + t - off, m] * value
                    out[j + t + shift, m] = (2.0 * f[t][m] - nxt[j + t + nxt_shift, m]) + step
                    if is_l:
                        work_out[work_at + 2 * q + t, m] = step

        layers_loop(0, count // 2, body)
        if not is_l:
            source(level, first, count, out, shift)

    def beyond_too(*args):
        if side == 0:

            @pl.when(is_last == 1)
            def _():
                advance(*args)

    far = MID + SHIFT + REACH
    advance(0, a, *before, MID - REACH, SHIFT, 0, b, 0)
    beyond_too(0, a, beyond, SHIFT - far, far, REACH, 32, b, 0)
    if not is_l:
        x_out[0:SHIFT] = a[MID - REACH : MID + REACH]
        if side == 0:

            @pl.when(is_last == 1)
            def _():
                x_out[SHIFT : SHIFT + REACH] = a[far : far + REACH]

        if final:
            return
    advance(1, b, a, 0, MID - SHIFT, 2 * SHIFT, 8, c, 0)
    beyond_too(1, b, a, 0, MID + SHIFT, SHIFT, 36, c, 0)
    if final:
        for layer in range(2 * SHIFT):
            store_tiled(field_out, layer, c[MID - SHIFT + layer])
        return
    advance(2, c, b, 0, MID - REACH, SHIFT, 24, msg_out, SHIFT - (MID - REACH))
    if side == 1:
        msg_out[0:SHIFT] = c[MID : MID + SHIFT]
        return
    msg_out[0:SHIFT] = c[MID - SHIFT : MID]

    @pl.when(is_last == 1)
    def _():
        advance(2, c, b, 0, far, REACH, 44, beyond_out, SHIFT - far)
        beyond_out[0:SHIFT] = c[MID + SHIFT : MID + 2 * SHIFT]
        beyond_out[SHIFT + REACH : MSG] = jnp.zeros((REACH,) + a.shape[1:], jnp.float32)


def first_l_kernel(n0, halves, info, near, table_hbm, *refs):
    refs = list(refs)
    speeds = refs[: 1 + halves]
    coef, weights, msg_out, b_kept, c_kept, beyond, work, table, sem = refs[1 + halves :]
    put_weights(weights)

    def fill(speed, first):
        def one(z):
            coef[z + first] = (0.4 * load_tiled(speed, z)) ** 2 * (1.0 / SCALE)

        layers_loop(0, speed.shape[0], one)

    if halves:

        @pl.when(info[SHOT] == 0)
        def _():
            fill(speeds[0], 0)
            fill(speeds[1], SHIFT)

        @pl.when(info[SHOT] != 0)
        def _():
            fill(speeds[1], 0)
            fill(speeds[0], SHIFT)
    else:
        fill(speeds[0], 0)
    msg_out[0:SHIFT] = coef[coef.shape[0] - SHIFT :]
    msg_out[SHIFT:MSG] = jnp.zeros((SHIFT,) + coef.shape[1:], jnp.float32)
    beyond[...] = jnp.zeros(beyond.shape, jnp.float32)
    b_kept[0:SHIFT] = jnp.zeros((SHIFT,) + coef.shape[1:], jnp.float32)
    c_kept[MID - SHIFT : MID] = jnp.zeros((SHIFT,) + coef.shape[1:], jnp.float32)
    zone = (SHIFT + REACH) // REACH
    inject(msg_out, SHIFT, info, near, table_hbm, table, sem, n0, zone, zone + SHIFT // REACH)

    def body(q):
        msg_out[q + SHIFT] = coef[q + REACH] * msg_out[q + SHIFT]

    layers_loop(0, SHIFT, body)
    put_rows(work, 0, n0, info, near, table_hbm, table, sem)


def join_kernel(l_got, own, coef):
    coef[0:SHIFT] = l_got[0:SHIFT]
    coef[SHIFT:] = own[...]


def first_u_kernel(n0, info, prev, last, coef, weights, msg_out, b_kept, c_kept, beyond, f0, f1, pieces, ybuf):
    depth, parts, _, width_y = f0.shape
    rows = parts * SUB
    src_layer, src_part, src_row, src_lane = (info[i] for i in range(1, STARTS))
    lap = lap_maker(parts, width_y)

    def bring(z):
        f0[z] = load_tiled(prev, z)
        f1[z] = load_tiled(last, z)

    layers_loop(0, depth, bring)
    msg_out[0:SHIFT] = f0[depth - SHIFT : depth]
    msg_out[MSG : MSG + REACH] = f1[depth - REACH : depth]
    c_kept[MID - SHIFT : MID] = f0[0:SHIFT]
    b_kept[REACH:SHIFT] = f1[0:REACH]
    beyond[...] = jnp.zeros(beyond.shape, jnp.float32)
    beyond[SHIFT : SHIFT + REACH] = f1[depth - REACH : depth]
    lane_pass(f0, REACH, SHIFT, weights, pieces, ybuf)
    to = SHIFT - REACH

    def body(q):
        j = REACH + 2 * q
        y_at = pl.multiple_of(q * 2 * rows, 2 * rows)
        f, total = lap(f0, j, ybuf[pl.ds(y_at, 2 * rows), :].reshape(2, parts, SUB, width_y))
        for t in range(2):
            for m in range(parts):
                msg_out[j + t + to, m] = (2.0 * f[t][m] - f1[j + t, m]) + coef[j + t, m] * total[t][m]

    layers_loop(0, SHIFT // 2, body)
    j = src_layer - SHIFT

    @pl.when((src_layer >= 0) & (j >= REACH) & (j < REACH + SHIFT))
    def _():
        lane = lax.broadcasted_iota(jnp.int32, (1, width_y), 1)
        spot = msg_out[j + to, src_part, pl.ds(src_row, 1), :]
        gain = coef[j, src_part, pl.ds(src_row, 1), :] * wave_of(n0)
        msg_out[j + to, src_part, pl.ds(src_row, 1), :] = spot + jnp.where(lane == src_lane, gain, 0.0)


def last_kernel(info, g_in, x0, b, d, g_right, gate, out, g):
    depth = out.shape[0]
    add_terms(g, g_in, 1, 1, info[0], (x0, b, None), d)

    def one(z):
        store_tiled(out, z, load_tiled(gate, 0).astype(jnp.float32) * g[z + SHIFT])

    def shared(z):
        store_tiled(out, z, load_tiled(gate, 0).astype(jnp.float32) * (g[z + SHIFT] + g_right[z - SHIFT]))

    layers_loop(0, SHIFT, one)
    layers_loop(SHIFT, depth - SHIFT, shared)


def sum_shots(g):
    shots = lax.axis_size("shot")
    if shots != 2:
        return lax.psum_scatter(g, "shot", scatter_dimension=1, tiled=True)
    block = g.shape[1] // 2
    low, high = g[:, :block], g[:, block:]
    first = lax.axis_index("shot") == 0
    other = lax.ppermute(jnp.where(first, high, low), "shot", [(0, 1), (1, 0)])
    return jnp.where(first, low, high) + other


def snake_of(slabs):
    row = slabs // 4
    if slabs % 8:
        return list(range(slabs))
    order = []
    for i in range(slabs):
        z, (chip, core) = i // row, divmod(i % row, 2)
        order.append(z * row + 2 * (row // 2 - 1 - chip if z % 2 else chip) + core)
    return order


def on_device(fwd_last, fwd_prev, velocity, aperture, rec_index, src_index, residual):
    _, depth, width_x, width_y = fwd_last.shape
    parts = width_x // SUB
    total_steps, receivers = residual.shape[1:]
    plane = width_x * width_y
    slabs = lax.axis_size("slab")
    f32 = jnp.float32
    place = snake_of(slabs)
    at = lax.axis_index("slab")
    snake = place != list(range(slabs))
    shot = lax.axis_index("shot")
    halves = snake and lax.axis_size("shot") == 2
    slab = at
    if snake:
        row = slabs // 4
        z, chip, core = at // row, at % row // 2, at % 2
        slab = z * row + 2 * jnp.where(z % 2 == 1, row // 2 - 1 - chip, chip) + core
    up = [(place[i], place[i + 1]) for i in range(slabs - 1)]
    down = [(place[i + 1], place[i]) for i in range(slabs - 1)]
    swap = [(i, place[i]) for i in range(slabs)]
    half = depth // 2
    if snake:
        fwd_prev = lax.ppermute(fwd_prev, "slab", swap)
        fwd_last = lax.ppermute(fwd_last, "slab", swap)
    if halves:
        mine = jnp.where(shot == 0, velocity[:half], velocity[half:])
        mine = lax.ppermute(mine, "slab", swap)
        theirs = lax.ppermute(mine, "shot", [(0, 1), (1, 0)])
        speeds = (mine, theirs)
    else:
        speeds = (lax.ppermute(velocity, "slab", swap) if snake else velocity,)

    base = (slab * depth - SHIFT) * plane
    window = (depth + SHIFT) * plane
    local = rec_index[0] - base
    far = jnp.int32(2**30)
    keys = jnp.where((local >= 0) & (local < window), local, far)
    keys, ids = lax.sort((keys, lax.iota(jnp.int32, receivers)), num_keys=1, is_stable=False)

    def place_of(cell):
        layer = cell // plane
        x = (cell // width_y) % width_x
        return layer, x % parts, x // parts, cell % width_y

    layer, part, row, lane = place_of(keys)
    rows_of = (layer * parts + part) * SUB + row
    zones = (depth + SHIFT) // REACH
    edges = jnp.arange(zones + 1, dtype=jnp.int32) * (REACH * plane)
    starts = jnp.sum((keys[None, :] < edges[:, None]).astype(jnp.int32), axis=1)

    src = src_index[0] - base
    src_in = (src >= 0) & (src < window)
    s_layer, s_part, s_row, s_lane = place_of(jnp.where(src_in, src, 0))
    s_layer = jnp.where(src_in, s_layer, -1)
    is_last = (slab == slabs - 1).astype(jnp.int32)
    scalars = [is_last, s_layer, s_part, s_row, s_lane]
    gap = [jnp.zeros((), jnp.int32)] * (SHOT - STARTS - zones - 1)
    info = jnp.concatenate([jnp.stack(scalars), starts, jnp.stack([*gap, shot]), rows_of])
    last_step = total_steps - 1

    smem = pl.BlockSpec(memory_space=pltpu.SMEM)
    vmem = pl.BlockSpec(memory_space=pltpu.VMEM)
    anym = pl.BlockSpec(memory_space=pltpu.HBM)

    def fields(layers):
        return jax.ShapeDtypeStruct((layers, parts, SUB, width_y), f32)

    params = pltpu.CompilerParams(vmem_limit_bytes=VMEM_BYTES)
    once = pltpu.CompilerParams(vmem_limit_bytes=MORE_BYTES)
    fetch_scratch = [pltpu.VMEM((receivers, width_y), f32), pltpu.SemaphoreType.DMA(())]

    def lane_scratch(layers):
        rows = layers * parts * SUB
        return [
            pltpu.VMEM((rows, PIECES * width_y), jnp.bfloat16),
            pltpu.VMEM((rows, width_y), f32),
        ]

    span = pltpu.VMEM((SPAN, parts, SUB, width_y), f32)
    block_scratch = [span] + lane_scratch(2 * SHIFT)

    def cost(layers):
        return pl.CostEstimate(
            flops=50 * layers * plane, bytes_accessed=24 * layers * plane, transcendentals=0
        )

    near, table = pl.pallas_call(
        functools.partial(table_kernel, zones),
        out_shape=(
            jax.ShapeDtypeStruct((total_steps, CHUNK, width_y), f32),
            jax.ShapeDtypeStruct((total_steps, FAR * receivers, width_y), f32),
        ),
        in_specs=[smem] + [vmem] * 5,
        out_specs=(vmem, anym),
        scratch_shapes=[
            pltpu.VMEM((receivers // CHUNK, PIECES, total_steps, CHUNK), f32),
            pltpu.VMEM((PIECES * total_steps, receivers), jnp.bfloat16),
            pltpu.VMEM((CHUNK, CHUNK), jnp.bfloat16),
            pltpu.VMEM((total_steps, CHUNK, width_y), f32),
            pltpu.SemaphoreType.DMA(()),
        ],
        compiler_params=once,
        cost_estimate=cost(SHIFT),
        name="rec_table",
    )(
        info,
        ids.reshape(receivers // CHUNK, CHUNK),
        rows_of.reshape(receivers // CHUNK, CHUNK),
        rows_of[:, None],
        lane[:, None],
        residual[0],
    )
    coef_own, weights, lm, l_b, l_c, lb, work = pl.pallas_call(
        functools.partial(first_l_kernel, last_step, halves),
        out_shape=(
            fields(depth),
            jax.ShapeDtypeStruct((PIECES * width_y, width_y), jnp.bfloat16),
            fields(MSG),
            fields(SPAN),
            fields(SPAN),
            fields(MSG),
            fields(WORK_ALL),
        ),
        in_specs=[smem, vmem, anym] + [vmem] * len(speeds),
        out_specs=[vmem] * 7,
        scratch_shapes=fetch_scratch,
        compiler_params=once,
        cost_estimate=cost(2),
        name="first_l",
    )(info, near, table, *speeds)
    l_got = lax.ppermute(lm, "slab", up)

    def between(side, n0, *arrays):
        outs = [fields(WORK_ALL), fields(depth + SHIFT)]
        scratch = list(fetch_scratch)
        if n0 == 3:
            outs.append(fields(SHIFT))
        if n0 == last_step:
            scratch = [pltpu.VMEM((depth + SHIFT, parts, SUB, width_y), f32)] + scratch
        return pl.pallas_call(
            functools.partial(between_kernel, side, n0, last_step),
            out_shape=outs,
            in_specs=[smem, vmem, anym] + [vmem] * len(arrays),
            out_specs=[vmem] * len(outs),
            scratch_shapes=scratch,
            compiler_params=params,
            cost_estimate=cost(SHIFT),
            name=f"between{side}",
        )(info, near, table, *arrays)

    fwd_prev, fwd_last, _ = lax.optimization_barrier((fwd_prev, fwd_last, work))
    um, u_b, u_c, ub = pl.pallas_call(
        functools.partial(first_u_kernel, last_step),
        out_shape=(fields(MSG + REACH), fields(SPAN), fields(SPAN), fields(MSG)),
        in_specs=[smem] + [vmem] * 4,
        out_specs=[vmem] * 4,
        scratch_shapes=[pltpu.VMEM((depth, parts, SUB, width_y), f32)] * 2 + lane_scratch(SHIFT),
        compiler_params=once,
        cost_estimate=cost(SHIFT),
        name="first_u",
    )(info, fwd_prev[0], fwd_last[0], coef_own, weights)
    u_sent, l_got = lax.optimization_barrier((um, l_got))
    u_got = lax.ppermute(u_sent, "slab", up)
    coef = pl.pallas_call(
        join_kernel,
        out_shape=fields(depth + SHIFT),
        in_specs=[vmem] * 2,
        out_specs=vmem,
        compiler_params=once,
        cost_estimate=cost(1),
        name="join_coef",
    )(l_got, coef_own)
    opening = (lm, um, u_c)

    def block(is_l, side, n0, own, b, c, recv, beyond, *work):
        outs = []
        if n0 > 1:
            outs = [fields(MSG), fields(SPAN), fields(SPAN)] + ([fields(MSG)] if side == 0 else [])
        elif is_l:
            outs = [jax.ShapeDtypeStruct((depth, width_x, width_y), f32)]
        else:
            outs = [fields(SPAN)]
        outs.append(fields(WORK_ALL if is_l else SHIFT + REACH))
        scratch = list(block_scratch)
        if n0 == 1 and is_l:
            scratch += [span, span]
        if n0 == last_step and not is_l:
            scratch.append(pltpu.VMEM((SHIFT, parts, SUB, width_y), f32))
        return pl.pallas_call(
            functools.partial(block_kernel, side, is_l, n0, n0 == last_step),
            out_shape=outs,
            in_specs=[smem] + [vmem] * (7 + len(work)),
            out_specs=[vmem] * len(outs),
            scratch_shapes=scratch,
            compiler_params=params,
            cost_estimate=cost(2 * depth),
            name=("l" if is_l else "u") + f"_block{side}",
        )(info, own, b, c, recv, coef, weights, beyond, *work)

    terms_in = opening
    for n0 in range(last_step, 0, -2):
        side = (last_step - n0) // 2 % 2
        way = up if side else down
        if n0 == 1:
            adjoint_field, d = block(True, side, n0, lm, l_b, l_c, l_got, lb, work)
            if snake:
                adjoint_field = lax.ppermute(adjoint_field, "slab", swap)
            u_b, x0 = block(False, side, n0, um, u_b, u_c, u_got, ub)
            break
        lm, l_b, l_c, *lb_new, d = block(True, side, n0, lm, l_b, l_c, l_got, lb, work)
        lb = lb_new[0] if lb_new else lb
        l_got = lax.ppermute(lm, "slab", way)
        um, u_b, u_c, *ub_new, x0 = block(False, side, n0, um, u_b, u_c, u_got, ub)
        ub = ub_new[0] if ub_new else ub
        u_got = lax.ppermute(um, "slab", way)
        work, g, *g_left = between(side, n0, *terms_in, x0, u_b, u_c, d)
        terms_in = (g,)
    g_right = lax.ppermute(g_left[0], "slab", down)

    terms = pl.pallas_call(
        last_kernel,
        out_shape=jax.ShapeDtypeStruct((depth, width_x, width_y), f32),
        in_specs=[smem] + [vmem] * 6,
        out_specs=vmem,
        scratch_shapes=[pltpu.VMEM((depth + SHIFT, parts, SUB, width_y), f32)],
        compiler_params=once,
        cost_estimate=cost(SHIFT),
        name="last_terms",
    )(info, g, x0, u_b, d, g_right, aperture)
    summed = sum_shots(terms)
    if snake:
        summed, adjoint_field = lax.optimization_barrier((summed, adjoint_field))
        summed = lax.ppermute(summed, "slab", swap)
    block = width_x // lax.axis_size("shot")
    speed = lax.dynamic_slice_in_dim(velocity, shot * block, block, 1)
    return ((-2.0 / speed) * summed, adjoint_field[None])


def solution(mesh):
    in_specs = (
        P("shot", "slab", None, None),
        P("shot", "slab", None, None),
        P("slab", None, None),
        P("shot", None, None),
        P("shot", None),
        P("shot"),
        P("shot", None, None),
    )
    out_specs = (P("slab", "shot", None), P("shot", "slab", None, None))
    return jax.shard_map(on_device, mesh=mesh, in_specs=in_specs, out_specs=out_specs, check_vma=False)
```

```python
import functools

import jax
import jax.numpy as jnp
import numpy as np
from jax import lax
from jax.experimental import pallas as pl
from jax.experimental.pallas import tpu as pltpu
from jax.sharding import PartitionSpec as P

SCALE = 5040.0
WHOLE = (-14350.0, 8064.0, -1008.0, 128.0, -9.0)
REACH = 4
SHIFT = 8
VMEM_BYTES = 9 * 1024 * 1024
MORE_BYTES = 24 * 1024 * 1024
SUB = 8
PIECES = 3
CHUNK = 256
FAR = 2

MSG = 2 * SHIFT
WORK = 4 * SHIFT
WORK_ALL = 6 * SHIFT
SPAN = 32
MID = 12


def wave_of(step):
    arg = (np.pi * 0.06 * (step - 10.0)) ** 2
    return float(np.float32(SCALE * 10.0 * (1.0 - 2.0 * arg) * np.exp(-arg)))


def load_tiled(field, layer):
    parts = field.shape[1] // SUB
    return jnp.stack([field[layer, pl.ds(m, SUB, stride=parts), :] for m in range(parts)])


def store_tiled(field, layer, value, first=0, count=SUB):
    parts = value.shape[0]
    for m in range(parts):
        field[layer, pl.ds(m, count, stride=parts), :] = value[m, first : first + count]


def split3(f):
    hi = f.astype(jnp.bfloat16)
    left = f - hi.astype(jnp.float32)
    mid = left.astype(jnp.bfloat16)
    return hi, mid, (left - mid.astype(jnp.float32)).astype(jnp.bfloat16)


def put_weights(weights):
    width_y = weights.shape[1]
    square = (width_y, width_y)
    away = jnp.abs(lax.broadcasted_iota(jnp.int32, square, 0) - lax.broadcasted_iota(jnp.int32, square, 1))
    once = jnp.zeros(square, jnp.float32)
    for k in range(1, 5):
        once = jnp.where(away == k, WHOLE[k], once)
    for i in range(PIECES):
        weights[i * width_y : (i + 1) * width_y, :] = once.astype(jnp.bfloat16)


def lane_pass(cur, first, count, weights, pieces, ybuf):
    parts, _, width_y = cur.shape[1:]
    rows = parts * SUB

    def one(q):
        at = pl.multiple_of(q * rows, rows)
        for i, piece in enumerate(split3(cur[first + q].reshape(rows, width_y))):
            pieces[pl.ds(at, rows), i * width_y : (i + 1) * width_y] = piece

    layers_loop(0, count, one)
    block = slice(0, count * rows)
    ybuf[block, :] = jnp.dot(pieces[block, :], weights[...], preferred_element_type=jnp.float32)


def lap_maker(parts, width_y):
    row = lax.broadcasted_iota(jnp.int32, (SUB, width_y), 0)

    def lap(ref, j, along):
        f = ([], [])
        total = ([], [])
        for m in range(parts):
            column = [ref[j + d, m] for d in range(-REACH, REACH + 2)]
            for t in range(2):
                mid = REACH + t
                f[t].append(column[mid])
                value = along[t, m] + (3.0 * WHOLE[0]) * column[mid]
                total[t].append((value, [column[mid + k] + column[mid - k] for k in range(1, 5)]))
        for t in range(2):
            after = [jnp.where(row == SUB - 1, 0.0, pltpu.roll(v, SUB - 1, 0)) for v in f[t][:REACH]]
            before = [jnp.where(row == 0, 0.0, pltpu.roll(v, 1, 0)) for v in f[t][parts - REACH :]]
            wide = before + f[t] + after
            for m in range(parts):
                value, pairs = total[t][m]
                for k in range(1, 5):
                    value = value + WHOLE[k] * (pairs[k - 1] + (wide[REACH + m + k] + wide[REACH + m - k]))
                total[t][m] = value
        return f, total

    return lap


def layers_loop(first, count, body):
    def one(q, carry):
        body(first + q)
        return carry

    lax.fori_loop(0, count, one, 0, unroll=2)


STARTS = 5
SHOT = 15
ROWS = 16


def inject(work, at, info, near, table_hbm, table, sem, step, first, last):
    low, high = info[STARTS + first], info[STARTS + last]
    rows = work.shape[1] * SUB
    shift = at * rows - first * REACH * rows
    flat = work.reshape(work.shape[0] * rows, work.shape[3])

    def store(low, high, row_of):
        def one(r, carry):
            flat[pl.ds(info[ROWS + r] + shift, 1), :] = row_of(r)
            return carry

        def eight(i, carry):
            at = [low + i * 8 + q for q in range(8)]
            values = [row_of(r) for r in at]
            for r, value in zip(at, values):
                flat[pl.ds(info[ROWS + r] + shift, 1), :] = value
            return carry

        groups = lax.shift_right_logical(high - low, 3)
        lax.fori_loop(0, groups, eight, 0)
        lax.fori_loop(low + groups * 8, high, one, 0)

    split = jnp.clip(CHUNK, low, high)
    store(low, split, lambda r: near[step, pl.ds(r, 1), :])

    @pl.when(high > split)
    def _():
        fetch = pltpu.make_async_copy(table_hbm.at[step, pl.ds(0, table.shape[0]), :], table, sem)
        fetch.start()
        fetch.wait()
        store(split, high, lambda r: table[pl.ds(r, 1), :])


def zones_of(side):
    return (1, 0, 1) if side == 0 else (3, 2, 3)


def put_rows(work, side, n0, is_last, info, near, table_hbm, table, sem):
    shared = (info, near, table_hbm, table, sem)
    zero = jnp.zeros((SHIFT,) + work.shape[1:], jnp.float32)
    for i in range(0, WORK, SHIFT):
        work[i : i + SHIFT] = zero
    for level, (at, zone, count) in enumerate(zip((0, 8, 24), zones_of(side), (2, 4, 2))):
        if n0 >= level:
            inject(work, at, *shared, n0 - level, zone, zone + count)
    if side == 0:

        @pl.when(is_last)
        def _():
            for i in range(WORK, WORK_ALL, SHIFT):
                work[i : i + SHIFT] = zero
            for level, (at, zone, count) in enumerate(((32, 5, 1), (36, 4, 2), (44, 5, 1))):
                if n0 >= level:
                    inject(work, at, *shared, n0 - level, zone, zone + count)


def add_terms(g, g_in, side, n0, is_last, x, d):
    x0, b, c = x
    low = 0 if side == 0 else SHIFT
    more = n0 >= 2

    def edge(at):
        def one(q):
            g[low + at + q] = g_in[low + at + q] + b[MID - SHIFT + at + q] * d[SHIFT + at + q]

        layers_loop(0, REACH, one)

    def middle(q):
        total = x0[q] * d[q] + b[MID - REACH + q] * d[SHIFT + REACH + q]
        if more:
            total = total + c[MID - REACH + q] * d[3 * SHIFT + q]
        g[low + REACH + q] = g_in[low + REACH + q] + total

    edge(0)
    layers_loop(0, SHIFT, middle)
    edge(SHIFT + REACH)
    if side == 1:
        g[0:SHIFT] = g_in[0:SHIFT]
        return
    g[2 * SHIFT : 3 * SHIFT] = g_in[2 * SHIFT : 3 * SHIFT]

    @pl.when(is_last)
    def _():
        for q in range(SHIFT):
            total = b[MID + SHIFT + q] * d[36 + q]
            if q >= REACH:
                total = total + x0[REACH + q] * d[28 + q]
                if more:
                    total = total + c[MID + SHIFT + q] * d[40 + q]
            g[2 * SHIFT + q] = g[2 * SHIFT + q] + total


def between_kernel(side, n0, opening, last_place, info_any, near, table_hbm, *refs):
    if n0 == opening:
        l_msg, u_msg, u_kept, *x, d, work, g, start, table, sem, info, info_sem = refs
        start[...] = jnp.zeros(start.shape, jnp.float32)
        for z in range(REACH, REACH + SHIFT):
            was = u_kept[MID - SHIFT + z] if z < SHIFT else u_msg[z - SHIFT]
            start[z + SHIFT] = was * l_msg[z - REACH + SHIFT]
        g_in = start
    else:
        g_in, *x, d = refs[:5]
        work, g, *g_left, table, sem, info, info_sem = refs[5:]
    fetch = pltpu.make_async_copy(info_any, info, info_sem)
    fetch.start()
    is_last = lax.axis_index("slab") == last_place
    add_terms(g, g_in, side, n0, is_last, x, d)
    if n0 == 3:
        g_left[0][...] = g[0:SHIFT]
    fetch.wait()
    put_rows(work, 1 - side, n0 - 2, is_last, info, near, table_hbm, table, sem)


def chunks_of(info, zones):
    return jnp.maximum((info[STARTS + zones] + CHUNK - 1) // CHUNK, 1)


def table_kernel(zones, info, ids, rows_l, rows_s, lanes_s, res, near, out, res_cut, pieces, same, part, sem):
    steps, receivers = res.shape
    width_y = part.shape[2]
    chunks = chunks_of(info, zones)
    for i, piece in enumerate(split3(res[...])):
        pieces[i * steps : (i + 1) * steps, :] = piece

    def column(c, carry):
        who = lax.broadcasted_iota(jnp.int32, (receivers, CHUNK), 0) == ids[pl.ds(c, 1), :]
        moved = jnp.dot(
            pieces[...], jnp.where(who, 1.0, 0.0).astype(jnp.bfloat16), preferred_element_type=jnp.float32
        )
        total = SCALE * ((moved[:steps] + moved[steps : 2 * steps]) + moved[2 * steps :])
        for i, piece in enumerate(split3(total)):
            res_cut[c, i] = piece.astype(jnp.float32)
        return carry

    lax.fori_loop(0, chunks, column, 0)

    def to_chunk(c, carry):
        mine = rows_s[pl.ds(pl.multiple_of(c * CHUNK, CHUNK), CHUNK), :]

        def from_chunk(d, carry):
            same[...] = jnp.where(mine == rows_l[pl.ds(d, 1), :], 1.0, 0.0).astype(jnp.bfloat16)
            at = pl.multiple_of(d * CHUNK, CHUNK)
            lane = lax.broadcasted_iota(jnp.int32, (CHUNK, width_y), 1)
            spot = jnp.where(lane == lanes_s[pl.ds(at, CHUNK), :], 1.0, 0.0).astype(jnp.bfloat16)
            spots = jnp.concatenate([spot] * PIECES, axis=0)

            def one(n, carry):
                mixed = []
                for i in range(PIECES):
                    row = jnp.broadcast_to(res_cut[d, i, pl.ds(n, 1), :], (16, CHUNK)).astype(jnp.bfloat16)
                    mixed.append((same[...].reshape(CHUNK // 16, 16, CHUNK) * row[None]).reshape(CHUNK, CHUNK))
                total = jnp.dot(
                    jnp.concatenate(mixed, axis=1), spots, preferred_element_type=jnp.float32
                )
                part[n] = total + jnp.where(d > 0, part[n], 0.0)
                return carry

            return lax.fori_loop(0, steps, one, carry, unroll=4)

        lax.fori_loop(0, chunks, from_chunk, 0)
        return carry

    def store_chunk(c, carry):
        to_chunk(c, 0)
        at = pl.multiple_of(c * CHUNK, CHUNK)
        write = pltpu.make_async_copy(part, out.at[:, pl.ds(at, CHUNK), :], sem)
        write.start()
        write.wait()
        return carry

    to_chunk(0, 0)
    near[...] = part[...]
    lax.fori_loop(1, chunks, store_chunk, 0)


def block_kernel(side, is_l, n0, opening, last_place, *refs):
    refs = list(refs)

    def take(count):
        got = refs[:count]
        del refs[:count]
        return got

    final = n0 == 1
    own, b_kept, c_kept, recv, coef, weights, beyond, extra = take(8)
    work_out = x_out = msg_out = beyond_out = field_out = p = None
    if not final:
        msg_out, b, c = take(3)
        if side == 0:
            (beyond_out,) = take(1)
    elif is_l:
        (field_out,) = take(1)
    else:
        (b,) = take(1)
    if is_l:
        (work_out,) = take(1)
    else:
        (x_out,) = take(1)
    a, pieces, ybuf = take(3)
    if final and is_l:
        b, c = take(2)
    if opening and not is_l:
        (p,) = take(1)

    parts, _, width_y = a.shape[1:]
    rows = parts * SUB
    is_last = lax.axis_index("slab") == last_place
    off = MID - SHIFT if side == 0 else MID - 2 * SHIFT
    lap = lap_maker(parts, width_y)

    def bring(msg, low):
        if low:
            a[MID - SHIFT : MID] = msg[0:SHIFT]
            b[MID - SHIFT - REACH : MID - REACH] = msg[SHIFT:MSG]
        else:
            a[MID : MID + SHIFT] = msg[0:SHIFT]
            b[MID + REACH : MID + REACH + SHIFT] = msg[SHIFT:MSG]

    if side == 0:
        bring(recv, True)
        a[MID : MID + SHIFT] = c_kept[MID - SHIFT : MID]
        b[MID + REACH : MID + REACH + SHIFT] = own[SHIFT:MSG]

        @pl.when(is_last)
        def _():
            zero = jnp.zeros((REACH,) + a.shape[1:], jnp.float32)
            a[MID + SHIFT : MID + 2 * SHIFT] = own[0:SHIFT]
            for field in (a, b, c):
                field[MID + 2 * SHIFT : MID + 2 * SHIFT + REACH] = zero
            if opening and is_l:
                a[MID + SHIFT : MID + 2 * SHIFT] = jnp.zeros((SHIFT,) + a.shape[1:], jnp.float32)

        if opening and is_l:
            a[MID - SHIFT : MID] = jnp.zeros((SHIFT,) + a.shape[1:], jnp.float32)
    else:
        a[MID - SHIFT : MID] = c_kept[MID : MID + SHIFT]
        b[MID - SHIFT - REACH : MID - REACH] = own[SHIFT:MSG]

        @pl.when(is_last)
        def _():
            bring(beyond, False)

        @pl.when(jnp.logical_not(is_last))
        def _():
            bring(recv, False)

    before = (b_kept, -SHIFT if side == 0 else SHIFT)
    if p is not None:
        p[0:REACH] = recv[MSG : MSG + REACH]
        p[REACH:SHIFT] = b_kept[REACH:SHIFT]
        before = (p, REACH - MID)

    def advance(level, cur, nxt, nxt_shift, first, count, work_at, out, shift):
        lane_pass(cur, first, count, weights, pieces, ybuf)

        def body(q):
            j = first + 2 * q
            y_at = pl.multiple_of(q * 2 * rows, 2 * rows)
            f, total = lap(cur, j, ybuf[pl.ds(y_at, 2 * rows), :].reshape(2, parts, SUB, width_y))
            for t in range(2):
                for m in range(parts):
                    value = total[t][m]
                    if is_l:
                        value = value + extra[work_at + 2 * q + t, m]
                    else:
                        value = value + wave_of(n0 - level) * extra[j + t - off, m]
                    step = coef[j + t - off, m] * value
                    out[j + t + shift, m] = (2.0 * f[t][m] - nxt[j + t + nxt_shift, m]) + step
                    if is_l:
                        work_out[work_at + 2 * q + t, m] = step

        layers_loop(0, count // 2, body)

    def beyond_too(*args):
        if side == 0:

            @pl.when(is_last)
            def _():
                advance(*args)

    far = MID + SHIFT + REACH
    advance(0, a, *before, MID - REACH, SHIFT, 0, b, 0)
    beyond_too(0, a, beyond, SHIFT - far, far, REACH, 32, b, 0)
    if not is_l:
        x_out[0:SHIFT] = a[MID - REACH : MID + REACH]
        if side == 0:

            @pl.when(is_last)
            def _():
                x_out[SHIFT : SHIFT + REACH] = a[far : far + REACH]

        if final:
            return
    advance(1, b, a, 0, MID - SHIFT, 2 * SHIFT, 8, c, 0)
    beyond_too(1, b, a, 0, MID + SHIFT, SHIFT, 36, c, 0)
    if final:
        for layer in range(2 * SHIFT):
            store_tiled(field_out, layer, c[MID - SHIFT + layer])
        return
    advance(2, c, b, 0, MID - REACH, SHIFT, 24, msg_out, SHIFT - (MID - REACH))
    if side == 1:
        msg_out[0:SHIFT] = c[MID : MID + SHIFT]
        return
    msg_out[0:SHIFT] = c[MID - SHIFT : MID]

    @pl.when(is_last)
    def _():
        advance(2, c, b, 0, far, REACH, 44, beyond_out, SHIFT - far)
        beyond_out[0:SHIFT] = c[MID + SHIFT : MID + 2 * SHIFT]
        beyond_out[SHIFT + REACH : MSG] = jnp.zeros((REACH,) + a.shape[1:], jnp.float32)


def first_l_kernel(n0, halves, info, near, table_hbm, *refs):
    refs = list(refs)
    speeds = refs[: 1 + halves]
    coef, weights, msg_out, b_kept, c_kept, beyond, work, table, sem = refs[1 + halves :]
    put_weights(weights)

    def fill(speed, first):
        def one(z):
            coef[z + first] = (0.4 * load_tiled(speed, z)) ** 2 * (1.0 / SCALE)

        layers_loop(0, speed.shape[0], one)

    if halves:

        @pl.when(info[SHOT] == 0)
        def _():
            fill(speeds[0], 0)
            fill(speeds[1], SHIFT)

        @pl.when(info[SHOT] != 0)
        def _():
            fill(speeds[1], 0)
            fill(speeds[0], SHIFT)
    else:
        fill(speeds[0], 0)
    msg_out[0:SHIFT] = coef[coef.shape[0] - SHIFT :]
    msg_out[SHIFT:MSG] = jnp.zeros((SHIFT,) + coef.shape[1:], jnp.float32)
    beyond[...] = jnp.zeros(beyond.shape, jnp.float32)
    b_kept[0:SHIFT] = jnp.zeros((SHIFT,) + coef.shape[1:], jnp.float32)
    c_kept[MID - SHIFT : MID] = jnp.zeros((SHIFT,) + coef.shape[1:], jnp.float32)
    zone = (SHIFT + REACH) // REACH
    inject(msg_out, SHIFT, info, near, table_hbm, table, sem, n0, zone, zone + SHIFT // REACH)

    def body(q):
        msg_out[q + SHIFT] = coef[q + REACH] * msg_out[q + SHIFT]

    layers_loop(0, SHIFT, body)
    put_rows(work, 0, n0, info[0] == 1, info, near, table_hbm, table, sem)


def join_kernel(l_got, own, coef):
    coef[0:SHIFT] = l_got[0:SHIFT]
    coef[SHIFT:] = own[...]


def first_u_kernel(n0, info, prev, last, coef, weights, msg_out, b_kept, c_kept, beyond, cell, f0, f1, pieces, ybuf):
    depth, parts, _, width_y = f0.shape
    rows = parts * SUB
    src_layer, src_part, src_row, src_lane = (info[i] for i in range(1, STARTS))
    lap = lap_maker(parts, width_y)

    def bring(z):
        f0[z] = load_tiled(prev, z)
        f1[z] = load_tiled(last, z)

    layers_loop(0, depth, bring)
    msg_out[0:SHIFT] = f0[depth - SHIFT : depth]
    msg_out[MSG : MSG + REACH] = f1[depth - REACH : depth]
    c_kept[MID - SHIFT : MID] = f0[0:SHIFT]
    b_kept[REACH:SHIFT] = f1[0:REACH]
    beyond[...] = jnp.zeros(beyond.shape, jnp.float32)
    beyond[SHIFT : SHIFT + REACH] = f1[depth - REACH : depth]
    lane_pass(f0, REACH, SHIFT, weights, pieces, ybuf)
    to = SHIFT - REACH

    def body(q):
        j = REACH + 2 * q
        y_at = pl.multiple_of(q * 2 * rows, 2 * rows)
        f, total = lap(f0, j, ybuf[pl.ds(y_at, 2 * rows), :].reshape(2, parts, SUB, width_y))
        for t in range(2):
            for m in range(parts):
                msg_out[j + t + to, m] = (2.0 * f[t][m] - f1[j + t, m]) + coef[j + t, m] * total[t][m]

    layers_loop(0, SHIFT // 2, body)
    j = src_layer - SHIFT
    here = lax.broadcasted_iota(jnp.int32, (1, width_y), 1) == src_lane
    cell[...] = jnp.zeros(cell.shape, jnp.float32)

    @pl.when(src_layer >= 0)
    def _():
        cell[src_layer, src_part, pl.ds(src_row, 1), :] = jnp.where(here, 1.0, 0.0)

    @pl.when((src_layer >= 0) & (j >= REACH) & (j < REACH + SHIFT))
    def _():
        spot = msg_out[j + to, src_part, pl.ds(src_row, 1), :]
        gain = coef[j, src_part, pl.ds(src_row, 1), :] * wave_of(n0)
        msg_out[j + to, src_part, pl.ds(src_row, 1), :] = spot + jnp.where(here, gain, 0.0)


def last_kernel(g_in, x0, b, d, g_right, gate, out, g):
    depth = out.shape[0]
    add_terms(g, g_in, 1, 1, False, (x0, b, None), d)

    def one(z):
        store_tiled(out, z, load_tiled(gate, 0).astype(jnp.float32) * g[z + SHIFT])

    def shared(z):
        store_tiled(out, z, load_tiled(gate, 0).astype(jnp.float32) * (g[z + SHIFT] + g_right[z - SHIFT]))

    layers_loop(0, SHIFT, one)
    layers_loop(SHIFT, depth - SHIFT, shared)


def sum_shots(g):
    shots = lax.axis_size("shot")
    if shots != 2:
        return lax.psum_scatter(g, "shot", scatter_dimension=1, tiled=True)
    block = g.shape[1] // 2
    low, high = g[:, :block], g[:, block:]
    first = lax.axis_index("shot") == 0
    other = lax.ppermute(jnp.where(first, high, low), "shot", [(0, 1), (1, 0)])
    return jnp.where(first, low, high) + other


def snake_of(slabs):
    row = slabs // 4
    if slabs % 8:
        return list(range(slabs))
    order = []
    for i in range(slabs):
        z, (chip, core) = i // row, divmod(i % row, 2)
        order.append(z * row + 2 * (row // 2 - 1 - chip if z % 2 else chip) + core)
    return order


def on_device(fwd_last, fwd_prev, velocity, aperture, rec_index, src_index, residual):
    _, depth, width_x, width_y = fwd_last.shape
    parts = width_x // SUB
    total_steps, receivers = residual.shape[1:]
    plane = width_x * width_y
    slabs = lax.axis_size("slab")
    f32 = jnp.float32
    place = snake_of(slabs)
    at = lax.axis_index("slab")
    snake = place != list(range(slabs))
    shot = lax.axis_index("shot")
    halves = snake and lax.axis_size("shot") == 2
    slab = at
    if snake:
        row = slabs // 4
        z, chip, core = at // row, at % row // 2, at % 2
        slab = z * row + 2 * jnp.where(z % 2 == 1, row // 2 - 1 - chip, chip) + core
    up = [(place[i], place[i + 1]) for i in range(slabs - 1)]
    down = [(place[i + 1], place[i]) for i in range(slabs - 1)]
    swap = [(i, place[i]) for i in range(slabs)]
    half = depth // 2
    if snake:
        fwd_prev = lax.ppermute(fwd_prev, "slab", swap)
        fwd_last = lax.ppermute(fwd_last, "slab", swap)
    if halves:
        mine = jnp.where(shot == 0, velocity[:half], velocity[half:])
        mine = lax.ppermute(mine, "slab", swap)
        theirs = lax.ppermute(mine, "shot", [(0, 1), (1, 0)])
        speeds = (mine, theirs)
    else:
        speeds = (lax.ppermute(velocity, "slab", swap) if snake else velocity,)

    base = (slab * depth - SHIFT) * plane
    window = (depth + SHIFT) * plane
    local = rec_index[0] - base
    far = jnp.int32(2**30)
    keys = jnp.where((local >= 0) & (local < window), local, far)
    keys, ids = lax.sort((keys, lax.iota(jnp.int32, receivers)), num_keys=1, is_stable=False)

    def place_of(cell):
        layer = cell // plane
        x = (cell // width_y) % width_x
        return layer, x % parts, x // parts, cell % width_y

    layer, part, row, lane = place_of(keys)
    rows_of = (layer * parts + part) * SUB + row
    zones = (depth + SHIFT) // REACH
    edges = jnp.arange(zones + 1, dtype=jnp.int32) * (REACH * plane)
    starts = jnp.sum((keys[None, :] < edges[:, None]).astype(jnp.int32), axis=1)

    src = src_index[0] - base
    src_in = (src >= 0) & (src < window)
    s_layer, s_part, s_row, s_lane = place_of(jnp.where(src_in, src, 0))
    s_layer = jnp.where(src_in, s_layer, -1)
    is_last = (slab == slabs - 1).astype(jnp.int32)
    scalars = [is_last, s_layer, s_part, s_row, s_lane]
    gap = [jnp.zeros((), jnp.int32)] * (SHOT - STARTS - zones - 1)
    fill = jnp.zeros((-(ROWS + receivers) % 1024,), jnp.int32)
    info = jnp.concatenate([jnp.stack(scalars), starts, jnp.stack([*gap, shot]), rows_of, fill])
    last_step = total_steps - 1

    smem = pl.BlockSpec(memory_space=pltpu.SMEM)
    vmem = pl.BlockSpec(memory_space=pltpu.VMEM)
    anym = pl.BlockSpec(memory_space=pltpu.HBM)

    def fields(layers):
        return jax.ShapeDtypeStruct((layers, parts, SUB, width_y), f32)

    params = pltpu.CompilerParams(vmem_limit_bytes=VMEM_BYTES)
    once = pltpu.CompilerParams(vmem_limit_bytes=MORE_BYTES)
    fetch_scratch = [pltpu.VMEM((receivers, width_y), f32), pltpu.SemaphoreType.DMA(())]

    def lane_scratch(layers):
        rows = layers * parts * SUB
        return [
            pltpu.VMEM((rows, PIECES * width_y), jnp.bfloat16),
            pltpu.VMEM((rows, width_y), f32),
        ]

    span = pltpu.VMEM((SPAN, parts, SUB, width_y), f32)
    block_scratch = [span] + lane_scratch(2 * SHIFT)

    def cost(layers):
        return pl.CostEstimate(
            flops=50 * layers * plane, bytes_accessed=24 * layers * plane, transcendentals=0
        )

    near, table = pl.pallas_call(
        functools.partial(table_kernel, zones),
        out_shape=(
            jax.ShapeDtypeStruct((total_steps, CHUNK, width_y), f32),
            jax.ShapeDtypeStruct((total_steps, FAR * receivers, width_y), f32),
        ),
        in_specs=[smem] + [vmem] * 5,
        out_specs=(vmem, anym),
        scratch_shapes=[
            pltpu.VMEM((receivers // CHUNK, PIECES, total_steps, CHUNK), f32),
            pltpu.VMEM((PIECES * total_steps, receivers), jnp.bfloat16),
            pltpu.VMEM((CHUNK, CHUNK), jnp.bfloat16),
            pltpu.VMEM((total_steps, CHUNK, width_y), f32),
            pltpu.SemaphoreType.DMA(()),
        ],
        compiler_params=once,
        cost_estimate=cost(SHIFT),
        name="rec_table",
    )(
        info,
        ids.reshape(receivers // CHUNK, CHUNK),
        rows_of.reshape(receivers // CHUNK, CHUNK),
        rows_of[:, None],
        lane[:, None],
        residual[0],
    )
    coef_own, weights, lm, l_b, l_c, lb, work = pl.pallas_call(
        functools.partial(first_l_kernel, last_step, halves),
        out_shape=(
            fields(depth),
            jax.ShapeDtypeStruct((PIECES * width_y, width_y), jnp.bfloat16),
            fields(MSG),
            fields(SPAN),
            fields(SPAN),
            fields(MSG),
            fields(WORK_ALL),
        ),
        in_specs=[smem, vmem, anym] + [vmem] * len(speeds),
        out_specs=[vmem] * 7,
        scratch_shapes=fetch_scratch,
        compiler_params=once,
        cost_estimate=cost(2),
        name="first_l",
    )(info, near, table, *speeds)
    l_got = lax.ppermute(lm, "slab", up)

    def between(side, n0, *arrays):
        outs = [fields(WORK_ALL), fields(depth + SHIFT)]
        scratch = fetch_scratch + [pltpu.SMEM(info.shape, jnp.int32), pltpu.SemaphoreType.DMA(())]
        if n0 == 3:
            outs.append(fields(SHIFT))
        if n0 == last_step:
            scratch = [pltpu.VMEM((depth + SHIFT, parts, SUB, width_y), f32)] + scratch
        return pl.pallas_call(
            functools.partial(between_kernel, side, n0, last_step, place[-1]),
            out_shape=outs,
            in_specs=[pl.BlockSpec(memory_space=pl.ANY), vmem, anym] + [vmem] * len(arrays),
            out_specs=[vmem] * len(outs),
            scratch_shapes=scratch,
            compiler_params=params,
            cost_estimate=cost(SHIFT),
            name=f"between{side}",
        )(info, near, table, *arrays)

    fwd_prev, fwd_last, _ = lax.optimization_barrier((fwd_prev, fwd_last, work))
    um, u_b, u_c, ub, cell = pl.pallas_call(
        functools.partial(first_u_kernel, last_step),
        out_shape=(fields(MSG + REACH), fields(SPAN), fields(SPAN), fields(MSG), fields(depth + SHIFT)),
        in_specs=[smem] + [vmem] * 4,
        out_specs=[vmem] * 5,
        scratch_shapes=[pltpu.VMEM((depth, parts, SUB, width_y), f32)] * 2 + lane_scratch(SHIFT),
        compiler_params=once,
        cost_estimate=cost(SHIFT),
        name="first_u",
    )(info, fwd_prev[0], fwd_last[0], coef_own, weights)
    u_sent, l_got = lax.optimization_barrier((um, l_got))
    u_got = lax.ppermute(u_sent, "slab", up)
    coef = pl.pallas_call(
        join_kernel,
        out_shape=fields(depth + SHIFT),
        in_specs=[vmem] * 2,
        out_specs=vmem,
        compiler_params=once,
        cost_estimate=cost(1),
        name="join_coef",
    )(l_got, coef_own)
    opening = (lm, um, u_c)

    def block(is_l, side, n0, own, b, c, recv, beyond, extra):
        outs = []
        if n0 > 1:
            outs = [fields(MSG), fields(SPAN), fields(SPAN)] + ([fields(MSG)] if side == 0 else [])
        elif is_l:
            outs = [jax.ShapeDtypeStruct((depth, width_x, width_y), f32)]
        else:
            outs = [fields(SPAN)]
        outs.append(fields(WORK_ALL if is_l else SHIFT + REACH))
        scratch = list(block_scratch)
        if n0 == 1 and is_l:
            scratch += [span, span]
        if n0 == last_step and not is_l:
            scratch.append(pltpu.VMEM((SHIFT, parts, SUB, width_y), f32))
        return pl.pallas_call(
            functools.partial(block_kernel, side, is_l, n0, n0 == last_step, place[-1]),
            out_shape=outs,
            in_specs=[vmem] * 8,
            out_specs=[vmem] * len(outs),
            scratch_shapes=scratch,
            compiler_params=params,
            cost_estimate=cost(2 * depth),
            name=("l" if is_l else "u") + f"_block{side}",
        )(own, b, c, recv, coef, weights, beyond, extra)

    terms_in = opening
    for n0 in range(last_step, 0, -2):
        side = (last_step - n0) // 2 % 2
        way = up if side else down
        if n0 == 1:
            adjoint_field, d = block(True, side, n0, lm, l_b, l_c, l_got, lb, work)
            if snake:
                adjoint_field = lax.ppermute(adjoint_field, "slab", swap)
            u_b, x0 = block(False, side, n0, um, u_b, u_c, u_got, ub, cell)
            break
        lm, l_b, l_c, *lb_new, d = block(True, side, n0, lm, l_b, l_c, l_got, lb, work)
        lb = lb_new[0] if lb_new else lb
        l_got = lax.ppermute(lm, "slab", way)
        um, u_b, u_c, *ub_new, x0 = block(False, side, n0, um, u_b, u_c, u_got, ub, cell)
        ub = ub_new[0] if ub_new else ub
        u_got = lax.ppermute(um, "slab", way)
        work, g, *g_left = between(side, n0, *terms_in, x0, u_b, u_c, d)
        terms_in = (g,)
    g_right = lax.ppermute(g_left[0], "slab", down)

    terms = pl.pallas_call(
        last_kernel,
        out_shape=jax.ShapeDtypeStruct((depth, width_x, width_y), f32),
        in_specs=[vmem] * 6,
        out_specs=vmem,
        scratch_shapes=[pltpu.VMEM((depth + SHIFT, parts, SUB, width_y), f32)],
        compiler_params=once,
        cost_estimate=cost(SHIFT),
        name="last_terms",
    )(g, x0, u_b, d, g_right, aperture)
    summed = sum_shots(terms)
    if snake:
        summed, adjoint_field = lax.optimization_barrier((summed, adjoint_field))
        summed = lax.ppermute(summed, "slab", swap)
    block = width_x // lax.axis_size("shot")
    speed = lax.dynamic_slice_in_dim(velocity, shot * block, block, 1)
    return ((-2.0 / speed) * summed, adjoint_field[None])


def solution(mesh):
    in_specs = (
        P("shot", "slab", None, None),
        P("shot", "slab", None, None),
        P("slab", None, None),
        P("shot", None, None),
        P("shot", None),
        P("shot"),
        P("shot", None, None),
    )
    out_specs = (P("slab", "shot", None), P("shot", "slab", None, None))
    return jax.shard_map(on_device, mesh=mesh, in_specs=in_specs, out_specs=out_specs, check_vma=False)
```

```python
import functools

import jax
import jax.numpy as jnp
import numpy as np
from jax import lax
from jax.experimental import pallas as pl
from jax.experimental.pallas import tpu as pltpu
from jax.sharding import PartitionSpec as P

SCALE = 5040.0
WHOLE = (-14350.0, 8064.0, -1008.0, 128.0, -9.0)
REACH = 4
SHIFT = 8
VMEM_BYTES = 9 * 1024 * 1024
MORE_BYTES = 24 * 1024 * 1024
SUB = 8
PIECES = 3
CHUNK = 256
FAR = 2

MSG = 2 * SHIFT
WORK = 4 * SHIFT
WORK_ALL = 6 * SHIFT
SPAN = 32
MID = 12


def wave_of(step):
    arg = (np.pi * 0.06 * (step - 10.0)) ** 2
    return float(np.float32(SCALE * 10.0 * (1.0 - 2.0 * arg) * np.exp(-arg)))


def load_tiled(field, layer):
    parts = field.shape[1] // SUB
    return jnp.stack([field[layer, pl.ds(m, SUB, stride=parts), :] for m in range(parts)])


def store_tiled(field, layer, value, first=0, count=SUB):
    parts = value.shape[0]
    for m in range(parts):
        field[layer, pl.ds(m, count, stride=parts), :] = value[m, first : first + count]


def split3(f):
    hi = f.astype(jnp.bfloat16)
    left = f - hi.astype(jnp.float32)
    mid = left.astype(jnp.bfloat16)
    return hi, mid, (left - mid.astype(jnp.float32)).astype(jnp.bfloat16)


def put_weights(weights):
    width_y = weights.shape[1]
    square = (width_y, width_y)
    away = jnp.abs(lax.broadcasted_iota(jnp.int32, square, 0) - lax.broadcasted_iota(jnp.int32, square, 1))
    once = jnp.zeros(square, jnp.float32)
    for k in range(1, 5):
        once = jnp.where(away == k, WHOLE[k], once)
    for i in range(PIECES):
        weights[i * width_y : (i + 1) * width_y, :] = once.astype(jnp.bfloat16)


def lane_pass(cur, first, count, weights, pieces, ybuf):
    parts, _, width_y = cur.shape[1:]
    rows = parts * SUB

    def one(q):
        at = pl.multiple_of(q * rows, rows)
        for i, piece in enumerate(split3(cur[first + q].reshape(rows, width_y))):
            pieces[pl.ds(at, rows), i * width_y : (i + 1) * width_y] = piece

    layers_loop(0, count, one)
    block = slice(0, count * rows)
    ybuf[block, :] = jnp.dot(pieces[block, :], weights[...], preferred_element_type=jnp.float32)


def lap_maker(parts, width_y):
    row = lax.broadcasted_iota(jnp.int32, (SUB, width_y), 0)

    def lap(ref, j, along):
        f = ([], [])
        total = ([], [])
        for m in range(parts):
            column = [ref[j + d, m] for d in range(-REACH, REACH + 2)]
            for t in range(2):
                mid = REACH + t
                f[t].append(column[mid])
                value = along[t, m] + (3.0 * WHOLE[0]) * column[mid]
                total[t].append((value, [column[mid + k] + column[mid - k] for k in range(1, 5)]))
        for t in range(2):
            after = [jnp.where(row == SUB - 1, 0.0, pltpu.roll(v, SUB - 1, 0)) for v in f[t][:REACH]]
            before = [jnp.where(row == 0, 0.0, pltpu.roll(v, 1, 0)) for v in f[t][parts - REACH :]]
            wide = before + f[t] + after
            for m in range(parts):
                value, pairs = total[t][m]
                for k in range(1, 5):
                    value = value + WHOLE[k] * (pairs[k - 1] + (wide[REACH + m + k] + wide[REACH + m - k]))
                total[t][m] = value
        return f, total

    return lap


def layers_loop(first, count, body):
    def one(q, carry):
        body(first + q)
        return carry

    lax.fori_loop(0, count, one, 0, unroll=2)


STARTS = 5
SHOT = 15
ROWS = 16


def inject(work, at, info, near, table_hbm, table, sem, step, first, last):
    low, high = info[STARTS + first], info[STARTS + last]
    rows = work.shape[1] * SUB
    shift = at * rows - first * REACH * rows
    flat = work.reshape(work.shape[0] * rows, work.shape[3])

    def store(low, high, row_of):
        def one(r, carry):
            flat[pl.ds(info[ROWS + r] + shift, 1), :] = row_of(r)
            return carry

        def eight(i, carry):
            at = [low + i * 8 + q for q in range(8)]
            values = [row_of(r) for r in at]
            for r, value in zip(at, values):
                flat[pl.ds(info[ROWS + r] + shift, 1), :] = value
            return carry

        groups = lax.shift_right_logical(high - low, 3)
        lax.fori_loop(0, groups, eight, 0)
        lax.fori_loop(low + groups * 8, high, one, 0)

    split = jnp.clip(CHUNK, low, high)
    store(low, split, lambda r: near[step, pl.ds(r, 1), :])

    @pl.when(high > split)
    def _():
        fetch = pltpu.make_async_copy(table_hbm.at[step, pl.ds(0, table.shape[0]), :], table, sem)
        fetch.start()
        fetch.wait()
        store(split, high, lambda r: table[pl.ds(r, 1), :])


def zones_of(side):
    return (1, 0, 1) if side == 0 else (3, 2, 3)


def put_rows(work, side, n0, is_last, info, near, table_hbm, table, sem):
    shared = (info, near, table_hbm, table, sem)
    zero = jnp.zeros((SHIFT,) + work.shape[1:], jnp.float32)
    for i in range(0, WORK, SHIFT):
        work[i : i + SHIFT] = zero
    for level, (at, zone, count) in enumerate(zip((0, 8, 24), zones_of(side), (2, 4, 2))):
        if n0 >= level:
            inject(work, at, *shared, n0 - level, zone, zone + count)
    if side == 0:

        @pl.when(is_last)
        def _():
            for i in range(WORK, WORK_ALL, SHIFT):
                work[i : i + SHIFT] = zero
            for level, (at, zone, count) in enumerate(((32, 5, 1), (36, 4, 2), (44, 5, 1))):
                if n0 >= level:
                    inject(work, at, *shared, n0 - level, zone, zone + count)


def add_terms(g, g_in, side, n0, is_last, x, d):
    x0, b, c = x
    low = 0 if side == 0 else SHIFT
    more = n0 >= 2

    def edge(at):
        def one(q):
            g[low + at + q] = g_in[low + at + q] + b[MID - SHIFT + at + q] * d[SHIFT + at + q]

        layers_loop(0, REACH, one)

    def middle(q):
        total = x0[q] * d[q] + b[MID - REACH + q] * d[SHIFT + REACH + q]
        if more:
            total = total + c[MID - REACH + q] * d[3 * SHIFT + q]
        g[low + REACH + q] = g_in[low + REACH + q] + total

    edge(0)
    layers_loop(0, SHIFT, middle)
    edge(SHIFT + REACH)
    if side == 1:
        g[0:SHIFT] = g_in[0:SHIFT]
        return
    g[2 * SHIFT : 3 * SHIFT] = g_in[2 * SHIFT : 3 * SHIFT]

    @pl.when(is_last)
    def _():
        for q in range(SHIFT):
            total = b[MID + SHIFT + q] * d[36 + q]
            if q >= REACH:
                total = total + x0[REACH + q] * d[28 + q]
                if more:
                    total = total + c[MID + SHIFT + q] * d[40 + q]
            g[2 * SHIFT + q] = g[2 * SHIFT + q] + total


def between_kernel(side, n0, opening, last_place, info_any, near, table_hbm, *refs):
    if n0 == opening:
        l_msg, u_msg, u_kept, *x, d, work, g, start, table, sem, info, info_sem = refs
        start[...] = jnp.zeros(start.shape, jnp.float32)
        for z in range(REACH, REACH + SHIFT):
            was = u_kept[MID - SHIFT + z] if z < SHIFT else u_msg[z - SHIFT]
            start[z + SHIFT] = was * l_msg[z - REACH + SHIFT]
        g_in = start
    else:
        g_in, *x, d = refs[:5]
        work, g, *g_left, table, sem, info, info_sem = refs[5:]
    fetch = pltpu.make_async_copy(info_any, info, info_sem)
    fetch.start()
    is_last = lax.axis_index("slab") == last_place
    add_terms(g, g_in, side, n0, is_last, x, d)
    if n0 == 3:
        g_left[0][...] = g[0:SHIFT]
    fetch.wait()
    put_rows(work, 1 - side, n0 - 2, is_last, info, near, table_hbm, table, sem)


def chunks_of(info, zones):
    return jnp.maximum((info[STARTS + zones] + CHUNK - 1) // CHUNK, 1)


def table_kernel(zones, info, ids, rows_l, rows_s, lanes_s, res, near, out, res_cut, pieces, same, part, sem):
    steps, receivers = res.shape
    width_y = part.shape[2]
    chunks = chunks_of(info, zones)
    for i, piece in enumerate(split3(res[...])):
        pieces[i * steps : (i + 1) * steps, :] = piece

    def column(c, carry):
        who = lax.broadcasted_iota(jnp.int32, (receivers, CHUNK), 0) == ids[pl.ds(c, 1), :]
        moved = jnp.dot(
            pieces[...], jnp.where(who, 1.0, 0.0).astype(jnp.bfloat16), preferred_element_type=jnp.float32
        )
        total = SCALE * ((moved[:steps] + moved[steps : 2 * steps]) + moved[2 * steps :])
        for i, piece in enumerate(split3(total)):
            res_cut[c, i] = piece.astype(jnp.float32)
        return carry

    lax.fori_loop(0, chunks, column, 0)

    def to_chunk(c, carry):
        mine = rows_s[pl.ds(pl.multiple_of(c * CHUNK, CHUNK), CHUNK), :]

        def from_chunk(d, carry):
            same[...] = jnp.where(mine == rows_l[pl.ds(d, 1), :], 1.0, 0.0).astype(jnp.bfloat16)
            at = pl.multiple_of(d * CHUNK, CHUNK)
            lane = lax.broadcasted_iota(jnp.int32, (CHUNK, width_y), 1)
            spot = jnp.where(lane == lanes_s[pl.ds(at, CHUNK), :], 1.0, 0.0).astype(jnp.bfloat16)
            spots = jnp.concatenate([spot] * PIECES, axis=0)

            def one(n, carry):
                mixed = []
                for i in range(PIECES):
                    row = jnp.broadcast_to(res_cut[d, i, pl.ds(n, 1), :], (16, CHUNK)).astype(jnp.bfloat16)
                    mixed.append((same[...].reshape(CHUNK // 16, 16, CHUNK) * row[None]).reshape(CHUNK, CHUNK))
                total = jnp.dot(
                    jnp.concatenate(mixed, axis=1), spots, preferred_element_type=jnp.float32
                )
                part[n] = total + jnp.where(d > 0, part[n], 0.0)
                return carry

            return lax.fori_loop(0, steps, one, carry, unroll=4)

        lax.fori_loop(0, chunks, from_chunk, 0)
        return carry

    def store_chunk(c, carry):
        to_chunk(c, 0)
        at = pl.multiple_of(c * CHUNK, CHUNK)
        write = pltpu.make_async_copy(part, out.at[:, pl.ds(at, CHUNK), :], sem)
        write.start()
        write.wait()
        return carry

    to_chunk(0, 0)
    near[...] = part[...]
    lax.fori_loop(1, chunks, store_chunk, 0)


def block_kernel(side, is_l, n0, opening, last_place, *refs):
    refs = list(refs)

    def take(count):
        got = refs[:count]
        del refs[:count]
        return got

    final = n0 == 1
    own, b_kept, c_kept, recv, coef, weights, beyond, extra = take(8)
    work_out = x_out = msg_out = beyond_out = field_out = p = None
    if not final:
        msg_out, b, c = take(3)
        if side == 0:
            (beyond_out,) = take(1)
    elif is_l:
        field_out = take(2)
    else:
        (b,) = take(1)
    if is_l:
        (work_out,) = take(1)
    else:
        (x_out,) = take(1)
    a, pieces, ybuf = take(3)
    if final and is_l:
        b, c = take(2)
    if opening and not is_l:
        (p,) = take(1)

    parts, _, width_y = a.shape[1:]
    rows = parts * SUB
    is_last = lax.axis_index("slab") == last_place
    off = MID - SHIFT if side == 0 else MID - 2 * SHIFT
    lap = lap_maker(parts, width_y)

    def bring(msg, low):
        if low:
            a[MID - SHIFT : MID] = msg[0:SHIFT]
            b[MID - SHIFT - REACH : MID - REACH] = msg[SHIFT:MSG]
        else:
            a[MID : MID + SHIFT] = msg[0:SHIFT]
            b[MID + REACH : MID + REACH + SHIFT] = msg[SHIFT:MSG]

    if side == 0:
        bring(recv, True)
        a[MID : MID + SHIFT] = c_kept[MID - SHIFT : MID]
        b[MID + REACH : MID + REACH + SHIFT] = own[SHIFT:MSG]

        @pl.when(is_last)
        def _():
            zero = jnp.zeros((REACH,) + a.shape[1:], jnp.float32)
            a[MID + SHIFT : MID + 2 * SHIFT] = own[0:SHIFT]
            for field in (a, b, c):
                field[MID + 2 * SHIFT : MID + 2 * SHIFT + REACH] = zero
            if opening and is_l:
                a[MID + SHIFT : MID + 2 * SHIFT] = jnp.zeros((SHIFT,) + a.shape[1:], jnp.float32)

        if opening and is_l:
            a[MID - SHIFT : MID] = jnp.zeros((SHIFT,) + a.shape[1:], jnp.float32)
    else:
        a[MID - SHIFT : MID] = c_kept[MID : MID + SHIFT]
        b[MID - SHIFT - REACH : MID - REACH] = own[SHIFT:MSG]

        @pl.when(is_last)
        def _():
            bring(beyond, False)

        @pl.when(jnp.logical_not(is_last))
        def _():
            bring(recv, False)

    before = (b_kept, -SHIFT if side == 0 else SHIFT)
    if p is not None:
        p[0:REACH] = recv[MSG : MSG + REACH]
        p[REACH:SHIFT] = b_kept[REACH:SHIFT]
        before = (p, REACH - MID)

    def advance(level, cur, nxt, nxt_shift, first, count, work_at, out, shift):
        lane_pass(cur, first, count, weights, pieces, ybuf)

        def body(q):
            j = first + 2 * q
            y_at = pl.multiple_of(q * 2 * rows, 2 * rows)
            f, total = lap(cur, j, ybuf[pl.ds(y_at, 2 * rows), :].reshape(2, parts, SUB, width_y))
            for t in range(2):
                for m in range(parts):
                    value = total[t][m]
                    if is_l:
                        value = value + extra[work_at + 2 * q + t, m]
                    else:
                        value = value + wave_of(n0 - level) * extra[j + t - off, m]
                    step = coef[j + t - off, m] * value
                    out[j + t + shift, m] = (2.0 * f[t][m] - nxt[j + t + nxt_shift, m]) + step
                    if is_l:
                        work_out[work_at + 2 * q + t, m] = step

        layers_loop(0, count // 2, body)

    def beyond_too(*args):
        if side == 0:

            @pl.when(is_last)
            def _():
                advance(*args)

    far = MID + SHIFT + REACH
    advance(0, a, *before, MID - REACH, SHIFT, 0, b, 0)
    beyond_too(0, a, beyond, SHIFT - far, far, REACH, 32, b, 0)
    if not is_l:
        x_out[0:SHIFT] = a[MID - REACH : MID + REACH]
        if side == 0:

            @pl.when(is_last)
            def _():
                x_out[SHIFT : SHIFT + REACH] = a[far : far + REACH]

        if final:
            return
    advance(1, b, a, 0, MID - SHIFT, 2 * SHIFT, 8, c, 0)
    beyond_too(1, b, a, 0, MID + SHIFT, SHIFT, 36, c, 0)
    if final:
        for layer in range(2 * SHIFT):
            store_tiled(field_out[layer // SHIFT], layer % SHIFT, c[MID - SHIFT + layer])
        return
    advance(2, c, b, 0, MID - REACH, SHIFT, 24, msg_out, SHIFT - (MID - REACH))
    if side == 1:
        msg_out[0:SHIFT] = c[MID : MID + SHIFT]
        return
    msg_out[0:SHIFT] = c[MID - SHIFT : MID]

    @pl.when(is_last)
    def _():
        advance(2, c, b, 0, far, REACH, 44, beyond_out, SHIFT - far)
        beyond_out[0:SHIFT] = c[MID + SHIFT : MID + 2 * SHIFT]
        beyond_out[SHIFT + REACH : MSG] = jnp.zeros((REACH,) + a.shape[1:], jnp.float32)


def first_l_kernel(n0, halves, info, near, table_hbm, *refs):
    refs = list(refs)
    speeds = refs[: 1 + halves]
    coef, weights, msg_out, b_kept, c_kept, beyond, work, cell, table, sem = refs[1 + halves :]
    put_weights(weights)
    src_layer, src_part, src_row, src_lane = (info[i] for i in range(1, STARTS))
    cell[...] = jnp.zeros(cell.shape, jnp.float32)

    @pl.when(src_layer >= 0)
    def _():
        here = lax.broadcasted_iota(jnp.int32, (1, cell.shape[3]), 1) == src_lane
        cell[src_layer, src_part, pl.ds(src_row, 1), :] = jnp.where(here, 1.0, 0.0)

    def fill(speed, first):
        def one(z):
            coef[z + first] = (0.4 * load_tiled(speed, z)) ** 2 * (1.0 / SCALE)

        layers_loop(0, speed.shape[0], one)

    if halves:

        @pl.when(info[SHOT] == 0)
        def _():
            fill(speeds[0], 0)
            fill(speeds[1], SHIFT)

        @pl.when(info[SHOT] != 0)
        def _():
            fill(speeds[1], 0)
            fill(speeds[0], SHIFT)
    else:
        fill(speeds[0], 0)
    msg_out[0:SHIFT] = coef[coef.shape[0] - SHIFT :]
    msg_out[SHIFT:MSG] = jnp.zeros((SHIFT,) + coef.shape[1:], jnp.float32)
    beyond[...] = jnp.zeros(beyond.shape, jnp.float32)
    b_kept[0:SHIFT] = jnp.zeros((SHIFT,) + coef.shape[1:], jnp.float32)
    c_kept[MID - SHIFT : MID] = jnp.zeros((SHIFT,) + coef.shape[1:], jnp.float32)
    zone = (SHIFT + REACH) // REACH
    inject(msg_out, SHIFT, info, near, table_hbm, table, sem, n0, zone, zone + SHIFT // REACH)

    def body(q):
        msg_out[q + SHIFT] = coef[q + REACH] * msg_out[q + SHIFT]

    layers_loop(0, SHIFT, body)
    put_rows(work, 0, n0, info[0] == 1, info, near, table_hbm, table, sem)


def join_kernel(l_got, own, coef):
    coef[0:SHIFT] = l_got[0:SHIFT]
    coef[SHIFT:] = own[...]


def first_u_kernel(n0, prev, last, coef, weights, cell, msg_out, b_kept, c_kept, beyond, f0, f1, pieces, ybuf):
    depth, parts, _, width_y = f0.shape
    rows = parts * SUB
    lap = lap_maker(parts, width_y)

    def bring(z):
        f0[z] = load_tiled(prev, z)
        f1[z] = load_tiled(last, z)

    layers_loop(0, depth, bring)
    msg_out[0:SHIFT] = f0[depth - SHIFT : depth]
    msg_out[MSG : MSG + REACH] = f1[depth - REACH : depth]
    c_kept[MID - SHIFT : MID] = f0[0:SHIFT]
    b_kept[REACH:SHIFT] = f1[0:REACH]
    beyond[...] = jnp.zeros(beyond.shape, jnp.float32)
    beyond[SHIFT : SHIFT + REACH] = f1[depth - REACH : depth]
    lane_pass(f0, REACH, SHIFT, weights, pieces, ybuf)
    to = SHIFT - REACH

    def body(q):
        j = REACH + 2 * q
        y_at = pl.multiple_of(q * 2 * rows, 2 * rows)
        f, total = lap(f0, j, ybuf[pl.ds(y_at, 2 * rows), :].reshape(2, parts, SUB, width_y))
        for t in range(2):
            for m in range(parts):
                value = total[t][m] + wave_of(n0) * cell[j + t + SHIFT, m]
                msg_out[j + t + to, m] = (2.0 * f[t][m] - f1[j + t, m]) + coef[j + t, m] * value

    layers_loop(0, SHIFT // 2, body)


def last_kernel(g_in, x0, b, d, g_right, gate, out, g):
    depth = out.shape[0]
    add_terms(g, g_in, 1, 1, False, (x0, b, None), d)

    def one(z):
        store_tiled(out, z, load_tiled(gate, 0).astype(jnp.float32) * g[z + SHIFT])

    def shared(z):
        store_tiled(out, z, load_tiled(gate, 0).astype(jnp.float32) * (g[z + SHIFT] + g_right[z - SHIFT]))

    layers_loop(0, SHIFT, one)
    layers_loop(SHIFT, depth - SHIFT, shared)


def sum_shots(g):
    shots = lax.axis_size("shot")
    if shots != 2:
        return lax.psum_scatter(g, "shot", scatter_dimension=1, tiled=True)
    block = g.shape[1] // 2
    low, high = g[:, :block], g[:, block:]
    first = lax.axis_index("shot") == 0
    other = lax.ppermute(jnp.where(first, high, low), "shot", [(0, 1), (1, 0)])
    return jnp.where(first, low, high) + other


def snake_of(slabs):
    row = slabs // 4
    if slabs % 8:
        return list(range(slabs))
    order = []
    for i in range(slabs):
        z, (chip, core) = i // row, divmod(i % row, 2)
        order.append(z * row + 2 * (row // 2 - 1 - chip if z % 2 else chip) + core)
    return order


def on_device(fwd_last, fwd_prev, velocity, aperture, rec_index, src_index, residual):
    _, depth, width_x, width_y = fwd_last.shape
    parts = width_x // SUB
    total_steps, receivers = residual.shape[1:]
    plane = width_x * width_y
    slabs = lax.axis_size("slab")
    f32 = jnp.float32
    place = snake_of(slabs)
    at = lax.axis_index("slab")
    snake = place != list(range(slabs))
    shot = lax.axis_index("shot")
    halves = snake and lax.axis_size("shot") == 2
    slab = at
    if snake:
        row = slabs // 4
        z, chip, core = at // row, at % row // 2, at % 2
        slab = z * row + 2 * jnp.where(z % 2 == 1, row // 2 - 1 - chip, chip) + core
    up = [(place[i], place[i + 1]) for i in range(slabs - 1)]
    down = [(place[i + 1], place[i]) for i in range(slabs - 1)]
    swap = [(i, place[i]) for i in range(slabs)]
    half = depth // 2
    if snake:
        fwd_prev = lax.ppermute(fwd_prev, "slab", swap)
        fwd_last = lax.ppermute(fwd_last, "slab", swap)
    if halves:
        mine = jnp.where(shot == 0, velocity[:half], velocity[half:])
        mine = lax.ppermute(mine, "slab", swap)
        theirs = lax.ppermute(mine, "shot", [(0, 1), (1, 0)])
        speeds = (mine, theirs)
    else:
        speeds = (lax.ppermute(velocity, "slab", swap) if snake else velocity,)

    base = (slab * depth - SHIFT) * plane
    window = (depth + SHIFT) * plane
    local = rec_index[0] - base
    far = jnp.int32(2**30)
    keys = jnp.where((local >= 0) & (local < window), local, far)
    keys, ids = lax.sort((keys, lax.iota(jnp.int32, receivers)), num_keys=1, is_stable=False)

    def place_of(cell):
        layer = cell // plane
        x = (cell // width_y) % width_x
        return layer, x % parts, x // parts, cell % width_y

    layer, part, row, lane = place_of(keys)
    rows_of = (layer * parts + part) * SUB + row
    zones = (depth + SHIFT) // REACH
    edges = jnp.arange(zones + 1, dtype=jnp.int32) * (REACH * plane)
    starts = jnp.sum((keys[None, :] < edges[:, None]).astype(jnp.int32), axis=1)

    src = src_index[0] - base
    src_in = (src >= 0) & (src < window)
    s_layer, s_part, s_row, s_lane = place_of(jnp.where(src_in, src, 0))
    s_layer = jnp.where(src_in, s_layer, -1)
    is_last = (slab == slabs - 1).astype(jnp.int32)
    scalars = [is_last, s_layer, s_part, s_row, s_lane]
    gap = [jnp.zeros((), jnp.int32)] * (SHOT - STARTS - zones - 1)
    fill = jnp.zeros((-(ROWS + receivers) % 1024,), jnp.int32)
    info = jnp.concatenate([jnp.stack(scalars), starts, jnp.stack([*gap, shot]), rows_of, fill])
    last_step = total_steps - 1

    smem = pl.BlockSpec(memory_space=pltpu.SMEM)
    vmem = pl.BlockSpec(memory_space=pltpu.VMEM)
    anym = pl.BlockSpec(memory_space=pltpu.HBM)

    def fields(layers):
        return jax.ShapeDtypeStruct((layers, parts, SUB, width_y), f32)

    params = pltpu.CompilerParams(vmem_limit_bytes=VMEM_BYTES)
    once = pltpu.CompilerParams(vmem_limit_bytes=MORE_BYTES)
    fetch_scratch = [pltpu.VMEM((receivers, width_y), f32), pltpu.SemaphoreType.DMA(())]

    def lane_scratch(layers):
        rows = layers * parts * SUB
        return [
            pltpu.VMEM((rows, PIECES * width_y), jnp.bfloat16),
            pltpu.VMEM((rows, width_y), f32),
        ]

    span = pltpu.VMEM((SPAN, parts, SUB, width_y), f32)
    block_scratch = [span] + lane_scratch(2 * SHIFT)

    def cost(layers):
        return pl.CostEstimate(
            flops=50 * layers * plane, bytes_accessed=24 * layers * plane, transcendentals=0
        )

    near, table = pl.pallas_call(
        functools.partial(table_kernel, zones),
        out_shape=(
            jax.ShapeDtypeStruct((total_steps, CHUNK, width_y), f32),
            jax.ShapeDtypeStruct((total_steps, FAR * receivers, width_y), f32),
        ),
        in_specs=[smem] + [vmem] * 5,
        out_specs=(vmem, anym),
        scratch_shapes=[
            pltpu.VMEM((receivers // CHUNK, PIECES, total_steps, CHUNK), f32),
            pltpu.VMEM((PIECES * total_steps, receivers), jnp.bfloat16),
            pltpu.VMEM((CHUNK, CHUNK), jnp.bfloat16),
            pltpu.VMEM((total_steps, CHUNK, width_y), f32),
            pltpu.SemaphoreType.DMA(()),
        ],
        compiler_params=once,
        cost_estimate=cost(SHIFT),
        name="rec_table",
    )(
        info,
        ids.reshape(receivers // CHUNK, CHUNK),
        rows_of.reshape(receivers // CHUNK, CHUNK),
        rows_of[:, None],
        lane[:, None],
        residual[0],
    )
    coef_own, weights, lm, l_b, l_c, lb, work, cell = pl.pallas_call(
        functools.partial(first_l_kernel, last_step, halves),
        out_shape=(
            fields(depth),
            jax.ShapeDtypeStruct((PIECES * width_y, width_y), jnp.bfloat16),
            fields(MSG),
            fields(SPAN),
            fields(SPAN),
            fields(MSG),
            fields(WORK_ALL),
            fields(depth + SHIFT),
        ),
        in_specs=[smem, vmem, anym] + [vmem] * len(speeds),
        out_specs=[vmem] * 8,
        scratch_shapes=fetch_scratch,
        compiler_params=once,
        cost_estimate=cost(2),
        name="first_l",
    )(info, near, table, *speeds)
    l_got = lax.ppermute(lm, "slab", up)

    def between(side, n0, *arrays):
        outs = [fields(WORK_ALL), fields(depth + SHIFT)]
        scratch = fetch_scratch + [pltpu.SMEM(info.shape, jnp.int32), pltpu.SemaphoreType.DMA(())]
        if n0 == 3:
            outs.append(fields(SHIFT))
        if n0 == last_step:
            scratch = [pltpu.VMEM((depth + SHIFT, parts, SUB, width_y), f32)] + scratch
        return pl.pallas_call(
            functools.partial(between_kernel, side, n0, last_step, place[-1]),
            out_shape=outs,
            in_specs=[pl.BlockSpec(memory_space=pl.ANY), vmem, anym] + [vmem] * len(arrays),
            out_specs=[vmem] * len(outs),
            scratch_shapes=scratch,
            compiler_params=params,
            cost_estimate=cost(SHIFT),
            name=f"between{side}",
        )(info, near, table, *arrays)

    fwd_prev, fwd_last, _ = lax.optimization_barrier((fwd_prev, fwd_last, work))
    um, u_b, u_c, ub = pl.pallas_call(
        functools.partial(first_u_kernel, last_step),
        out_shape=(fields(MSG + REACH), fields(SPAN), fields(SPAN), fields(MSG)),
        in_specs=[vmem] * 5,
        out_specs=[vmem] * 4,
        scratch_shapes=[pltpu.VMEM((depth, parts, SUB, width_y), f32)] * 2 + lane_scratch(SHIFT),
        compiler_params=once,
        cost_estimate=cost(SHIFT),
        name="first_u",
    )(fwd_prev[0], fwd_last[0], coef_own, weights, cell)
    u_sent, l_got = lax.optimization_barrier((um, l_got))
    u_got = lax.ppermute(u_sent, "slab", up)
    coef = pl.pallas_call(
        join_kernel,
        out_shape=fields(depth + SHIFT),
        in_specs=[vmem] * 2,
        out_specs=vmem,
        compiler_params=once,
        cost_estimate=cost(1),
        name="join_coef",
    )(l_got, coef_own)
    opening = (lm, um, u_c)

    def block(is_l, side, n0, own, b, c, recv, beyond, extra):
        outs = []
        if n0 > 1:
            outs = [fields(MSG), fields(SPAN), fields(SPAN)] + ([fields(MSG)] if side == 0 else [])
        elif is_l:
            outs = [jax.ShapeDtypeStruct((SHIFT, width_x, width_y), f32)] * 2
        else:
            outs = [fields(SPAN)]
        outs.append(fields(WORK_ALL if is_l else SHIFT + REACH))
        scratch = list(block_scratch)
        if n0 == 1 and is_l:
            scratch += [span, span]
        if n0 == last_step and not is_l:
            scratch.append(pltpu.VMEM((SHIFT, parts, SUB, width_y), f32))
        return pl.pallas_call(
            functools.partial(block_kernel, side, is_l, n0, n0 == last_step, place[-1]),
            out_shape=outs,
            in_specs=[vmem] * 8,
            out_specs=[vmem] * len(outs),
            scratch_shapes=scratch,
            compiler_params=params,
            cost_estimate=cost(2 * depth),
            name=("l" if is_l else "u") + f"_block{side}",
        )(own, b, c, recv, coef, weights, beyond, extra)

    terms_in = opening
    for n0 in range(last_step, 0, -2):
        side = (last_step - n0) // 2 % 2
        way = up if side else down
        if n0 == 1:
            low, high, d = block(True, side, n0, lm, l_b, l_c, l_got, lb, work)
            if snake:
                low = lax.ppermute(low, "slab", swap)
                high = lax.ppermute(high, "slab", swap)
            u_b, x0 = block(False, side, n0, um, u_b, u_c, u_got, ub, cell)
            break
        lm, l_b, l_c, *lb_new, d = block(True, side, n0, lm, l_b, l_c, l_got, lb, work)
        lb = lb_new[0] if lb_new else lb
        l_got = lax.ppermute(lm, "slab", way)
        um, u_b, u_c, *ub_new, x0 = block(False, side, n0, um, u_b, u_c, u_got, ub, cell)
        ub = ub_new[0] if ub_new else ub
        u_got = lax.ppermute(um, "slab", way)
        work, g, *g_left = between(side, n0, *terms_in, x0, u_b, u_c, d)
        terms_in = (g,)
    g_right = lax.ppermute(g_left[0], "slab", down)

    terms = pl.pallas_call(
        last_kernel,
        out_shape=jax.ShapeDtypeStruct((depth, width_x, width_y), f32),
        in_specs=[vmem] * 6,
        out_specs=vmem,
        scratch_shapes=[pltpu.VMEM((depth + SHIFT, parts, SUB, width_y), f32)],
        compiler_params=once,
        cost_estimate=cost(SHIFT),
        name="last_terms",
    )(g, x0, u_b, d, g_right, aperture)
    summed = sum_shots(terms)
    if snake:
        summed, low = lax.optimization_barrier((summed, low))
        summed = lax.ppermute(summed, "slab", swap)
    adjoint_field = jnp.concatenate([low, high], axis=0)
    block = width_x // lax.axis_size("shot")
    speed = lax.dynamic_slice_in_dim(velocity, shot * block, block, 1)
    return ((-2.0 / speed) * summed, adjoint_field[None])


def solution(mesh):
    in_specs = (
        P("shot", "slab", None, None),
        P("shot", "slab", None, None),
        P("slab", None, None),
        P("shot", None, None),
        P("shot", None),
        P("shot"),
        P("shot", None, None),
    )
    out_specs = (P("slab", "shot", None), P("shot", "slab", None, None))
    return jax.shard_map(on_device, mesh=mesh, in_specs=in_specs, out_specs=out_specs, check_vma=False)
```
